128 devices in a mesh: fsdp: 16 (over y, z), ctx: 8 (over x, core).
Axes of the slice: x: 4, y: 4, z: 4, core: 2. Of those that a mesh axis runs over, the one named last changes fastest.
Arguments:
- tokens: bfloat16 [16, 1024, 1152], P('fsdp', 'ctx'), may hold values from -6 to 6
- norm_gains: bfloat16 [4, 1152], P(None, 'fsdp'), may hold values from 0.099609375 to 1.8984375
- qk_gains: bfloat16 [2, 256], P(None, 'fsdp'), may hold values from 0.099609375 to 1.8984375
- qkv_weight: bfloat16 [1152, 1536], P('fsdp'), may hold values from -0.1875 to 0.1875
- out_weight: bfloat16 [1024, 1152], P('fsdp'), may hold values from -0.1875 to 0.1875
- gate_weight: bfloat16 [6912, 1152], P('fsdp'), may hold values from -0.1875 to 0.1875
- up_weight: bfloat16 [6912, 1152], P('fsdp'), may hold values from -0.1875 to 0.1875
- down_weight: bfloat16 [6912, 1152], P('fsdp'), may hold values from -0.078125 to 0.078125
- segments: int32 [16, 1024], P('fsdp', 'ctx'), may hold values from 0 to 8, as said below
- cotangent: bfloat16 [16, 1024, 1152], P('fsdp', 'ctx'), may hold values from -6 to 6
Outputs:
- out: bfloat16 [16, 1024, 1152], P('fsdp', 'ctx')
- grad_tokens: float32 [16, 1024, 1152], P('fsdp', 'ctx')
- grad_norm_gains: float32 [4, 1152], P(None, 'fsdp')
- grad_qk_gains: float32 [2, 256], P(None, 'fsdp')
- grad_qkv_weight: float32 [1152, 1536], P('fsdp')
- grad_out_weight: float32 [1024, 1152], P('fsdp')
- grad_gate_weight: float32 [6912, 1152], P('fsdp')
- grad_up_weight: float32 [6912, 1152], P('fsdp')
- grad_down_weight: float32 [6912, 1152], P('fsdp')
The draws below stay inside these ranges and needn't reach their ends.
Inputs may be any that keep to these rules, and one draw needn't show every extreme that they name: `segments`: along each sequence the segment numbers never fall.
All inputs are finite; a program needn't handle non-finite values.
Results may differ from the reference program's by a relative error of at most 0.024.
Values may be sent and summed in bfloat16 or wider, within the bound.
A program may use at most 320 MiB of HBM per device.

```python
import math
import jax
import jax.numpy as jnp
from jax import lax

D = 1152
NH = 4
HD = 256
FF = 6912
WINDOW = 512
LEN = 1024
CH = 128
SEQUENCES = 16


def draw_segments(key, part):
    key = jax.random.fold_in(key, 11)
    key_pick, key_cut, key_edge = jax.random.split(key, 3)
    order = jax.random.permutation(key_pick, jnp.arange(SEQUENCES, dtype=jnp.int32))
    chosen = (order < (SEQUENCES + 1) // 2)[:, None]
    free_cuts = jax.random.randint(key_cut, (SEQUENCES, 8), 1, LEN)
    edge_draw = jax.random.randint(key_edge, (SEQUENCES, 8), 1, 2 * CH - 1)
    edge_cuts = jnp.where(edge_draw < CH, edge_draw, LEN - 2 * CH + 1 + edge_draw)
    all_cuts = jnp.where(chosen, edge_cuts, free_cuts)
    token_index = jnp.arange(LEN, dtype=jnp.int32)
    return jnp.sum((all_cuts[:, :, None] <= token_index[None, None, :]).astype(jnp.int32), axis=1)


def steps_of(key, shape, cuts, least, top_value):
    def one(axis_at, parts):
        heights = jax.random.uniform(jax.random.fold_in(jax.random.fold_in(key, 6), axis_at), (parts,), jnp.float32, least / len(cuts), top_value / len(cuts))
        return jnp.repeat(jnp.exp(heights), shape[axis_at] // parts).reshape((-1,) + (1,) * (len(shape) - axis_at - 1))

    level = one(*cuts[0])
    for cut in cuts[1:]:
        level = level * one(*cut)
    return level


def gaussian(own_key, extent, width, reach, pieces=(), kind=jnp.bfloat16):
    entries = jax.random.normal(own_key, extent, jnp.float32) * width
    if len(pieces) > 0:
        entries = steps_of(own_key, extent, pieces, -0.22, 0.18) * entries
    return jnp.clip(entries, min=-reach, max=reach).astype(kind)


def setup_inputs(seed: int = 0) -> dict:
    streams_of = jax.random.split(jax.random.key(seed), 11)
    tokens = gaussian(streams_of[0], (SEQUENCES, LEN, D), 1.0, 6.0, ((0, 16), (1, 8)))
    norm_gains = jnp.clip(1.0 + 0.18 * jax.random.normal(streams_of[1], (4, D), jnp.float32), 0.099609375, 1.8984375).astype(jnp.bfloat16)
    qk_gains = jnp.clip(1.0 + 0.18 * jax.random.normal(streams_of[2], (2, HD), jnp.float32), 0.099609375, 1.8984375).astype(jnp.bfloat16)
    qkv_weight = gaussian(streams_of[3], (D, NH * HD + 2 * HD), D ** -0.5, 0.1875, ((0, 16),))
    out_weight = gaussian(streams_of[4], (NH * HD, D), (NH * HD) ** -0.5, 0.1875, ((0, 16),))
    gate_weight = gaussian(streams_of[5], (FF, D), D ** -0.5, 0.1875, ((0, 16),))
    up_weight = gaussian(streams_of[6], (FF, D), D ** -0.5, 0.1875, ((0, 16),))
    down_weight = gaussian(streams_of[7], (FF, D), FF ** -0.5, 0.078125, ((0, 16),))
    segments = draw_segments(jax.random.fold_in(streams_of[10], 71), 0)
    cotangent = gaussian(streams_of[9], (SEQUENCES, LEN, D), 1.0, 6.0, ((0, 16), (1, 8)))
    return {"tokens": tokens, "norm_gains": norm_gains, "qk_gains": qk_gains, "qkv_weight": qkv_weight, "out_weight": out_weight, "gate_weight": gate_weight, "up_weight": up_weight, "down_weight": down_weight, "segments": segments, "cotangent": cotangent}


EPS = 1e-06
ROPE_BASE = 10000.0
NEG_FILL = -1e+30
HIGH = lax.Precision.HIGHEST

@jax.custom_vjp
def low(v):
    return lax.optimization_barrier(v.astype(jnp.bfloat16)).astype(jnp.float32)

@jax.custom_vjp
def low_back(v):
    return v

def low_keep(v):
    return (low(v), None)

def low_pass(kept, grad):
    return (grad,)

def back_keep(v):
    return (v, None)

def back_low(kept, grad):
    return (low(grad),)
low.defvjp(low_keep, low_pass)
low_back.defvjp(back_keep, back_low)

def rms_norm(values, gain_vec):
    return values * lax.rsqrt(lax.optimization_barrier(jnp.mean(values * values, axis=-1, keepdims=True)) + EPS) * gain_vec

def hi_dot(left, right):
    return jnp.dot(left, right, precision=HIGH)

def rotate(values, cos_table, sin_table):
    half_size = values.shape[-1] // 2
    first_half = values[..., :half_size]
    second_half = values[..., half_size:]
    return jnp.concatenate([first_half * cos_table - second_half * sin_table, second_half * cos_table + first_half * sin_table], axis=-1)

def rope_tables(positions):
    frequency = ROPE_BASE ** (-(2.0 * jnp.arange(HD // 2).astype(jnp.float32)) / HD)
    angles = positions.astype(jnp.float32)[..., None] * frequency
    return (jnp.cos(angles), jnp.sin(angles))

def positions_of(seg_row):
    token_index = jnp.arange(LEN, dtype=jnp.int32)
    change = jnp.concatenate([jnp.ones((1,), jnp.bool_), seg_row[1:] != seg_row[:-1]])
    return token_index - lax.cummax(jnp.where(change, token_index, 0))

def sequence_layer(stream_row, pos_row, weights):
    norm_gains, qk_gains, qkv_w, out_w, gate_w, up_w, down_w = weights
    cos_table, sin_table = rope_tables(pos_row)
    normed = low(rms_norm(stream_row, norm_gains[0]))
    projected = low_back(hi_dot(normed, qkv_w))
    q_raw = projected[:, :NH * HD].reshape(LEN, NH, HD)
    k_raw = projected[:, NH * HD:NH * HD + HD]
    values = low(projected[:, NH * HD + HD:])
    queries = low(rotate(rms_norm(q_raw, qk_gains[0]), cos_table[:, None, :], sin_table[:, None, :]))
    key_rows = low(rotate(rms_norm(k_raw, qk_gains[1]), cos_table, sin_table))
    raw_scores = jnp.einsum('qhd,kd->hqk', queries, key_rows, precision=HIGH)
    scores = low_back(raw_scores * HD ** (-0.5))
    token_index = jnp.arange(LEN, dtype=jnp.int32)
    distance = token_index[:, None] - token_index[None, :]
    allowed = (distance >= 0) & (distance < WINDOW) & (distance <= pos_row[:, None])
    scores = jnp.where(allowed[None], scores, NEG_FILL)
    top_score = lax.optimization_barrier(jnp.max(scores, axis=-1, keepdims=True))
    expo = jnp.exp(scores - top_score)
    probs = low(expo / lax.optimization_barrier(jnp.sum(expo, axis=-1, keepdims=True)))
    attended = low_back(low(jnp.einsum('hqk,kd->qhd', probs, values, precision=HIGH))).reshape(LEN, NH * HD)
    attn = low_back(hi_dot(attended, out_w))
    mid = stream_row + rms_norm(attn, norm_gains[1])
    normed_two = low(rms_norm(mid, norm_gains[2]))
    gate_pre = low_back(hi_dot(normed_two, gate_w.T))
    up_pre = low_back(hi_dot(normed_two, up_w.T))
    hidden = low(jax.nn.gelu(gate_pre, approximate=True) * up_pre)
    mlp_out = low_back(hi_dot(hidden, down_w))
    return mid + rms_norm(mlp_out, norm_gains[3])

def reference(tokens, norm_gains, qk_gains, qkv_weight, out_weight, gate_weight, up_weight, down_weight, segments, cotangent):
    positions = jax.vmap(positions_of)(segments)
    params = tuple((weight_arg.astype(jnp.float32) for weight_arg in (norm_gains, qk_gains, qkv_weight, out_weight, gate_weight, up_weight, down_weight)))
    group_size = math.gcd(SEQUENCES, 4)

    def run_block(weights, block_pair):
        return jax.vmap(sequence_layer, in_axes=(0, 0, None))(block_pair[0], block_pair[1], weights)
    checked = jax.checkpoint(run_block)

    def forward(stream, weights):
        blocks = stream.reshape(SEQUENCES // group_size, group_size, LEN, D)
        pos_blocks = positions.reshape(SEQUENCES // group_size, group_size, LEN)
        result = lax.map(lambda block_pair: checked(weights, block_pair), (blocks, pos_blocks))
        return result.reshape(SEQUENCES, LEN, D)
    result, pullback = jax.vjp(forward, tokens.astype(jnp.float32), params)
    grad_tokens, grads = pullback(cotangent.astype(jnp.float32))
    return (result.astype(jnp.bfloat16), grad_tokens, grads[0], grads[1], grads[2], grads[3], grads[4], grads[5], grads[6])
```

```python
from functools import partial

import jax
import jax.numpy as jnp
from jax import lax
from jax.sharding import PartitionSpec as P

D = 1152
NH = 4
HD = 256
WINDOW = 512


EPS = 1e-06
ROPE_BASE = 10000.0
NEG_FILL = -1e30
CONTRACT_LAST = (((1,), (1,)), ((), ()))
CONTRACT_FIRST = (((0,), (0,)), ((), ()))


def from_behind(array, axis, by):
    devices = lax.axis_size(axis)
    pairs = [(i, i + by) for i in range(devices) if 0 <= i + by < devices]
    return lax.ppermute(array, axis, pairs)


def rms_norm(values, gain_vec):
    return values * lax.rsqrt(jnp.mean(values * values, axis=-1, keepdims=True) + EPS) * gain_vec


def rotate(values, cos_table, sin_table):
    half_size = values.shape[-1] // 2
    first_half = values[..., :half_size]
    second_half = values[..., half_size:]
    return jnp.concatenate(
        [
            first_half * cos_table - second_half * sin_table,
            second_half * cos_table + first_half * sin_table,
        ],
        axis=-1,
    )


def rope_tables(positions):
    frequency = ROPE_BASE ** (-(2.0 * jnp.arange(HD // 2).astype(jnp.float32)) / HD)
    angles = positions.astype(jnp.float32)[..., None] * frequency
    return (jnp.cos(angles), jnp.sin(angles))


def head_prep(q_raw, k_raw, q_gain, k_gain, cos_table, sin_table):
    queries = rotate(rms_norm(q_raw, q_gain), cos_table[:, None, :], sin_table[:, None, :])
    key_rows = rotate(rms_norm(k_raw, k_gain), cos_table, sin_table)
    return (queries, key_rows)


def gelu_product(gate_pre, up_pre):
    return jax.nn.gelu(gate_pre, approximate=True) * up_pre


def on_device(
    tokens,
    norm_gains,
    qk_gains,
    qkv_weight,
    out_weight,
    gate_weight,
    up_weight,
    down_weight,
    segments,
    cotangent,
):
    local_len = tokens.shape[1]
    scale = HD ** (-0.5)
    ctx_index = lax.axis_index("ctx")
    ctx_size = lax.axis_size("ctx")
    own_rows = gate_weight.shape[0]
    slice_rows = own_rows // ctx_size
    padded = -(-slice_rows // 16) * 16
    gains_flat = jnp.concatenate([norm_gains.reshape(-1), qk_gains.reshape(-1)])
    gains_got = lax.all_gather(gains_flat, "fsdp")
    n_gain = norm_gains.size
    gains_all = (
        gains_got[:, :n_gain]
        .reshape(-1, 4, norm_gains.shape[1])
        .transpose(1, 0, 2)
        .reshape(4, D)
        .astype(jnp.float32)
    )
    qk_all = (
        gains_got[:, n_gain:]
        .reshape(-1, 2, qk_gains.shape[1])
        .transpose(1, 0, 2)
        .reshape(2, HD)
        .astype(jnp.float32)
    )
    seg_all = lax.all_gather(segments[0], "ctx", axis=0, tiled=True)
    qkv_full = lax.all_gather(qkv_weight, "fsdp", axis=0, tiled=True)
    out_full = lax.all_gather(out_weight, "fsdp", axis=0, tiled=True)

    def my_slice(weight):
        part = lax.dynamic_index_in_dim(
            weight.reshape(ctx_size, slice_rows, D), ctx_index, 0, False
        )
        return jnp.pad(part, ((0, padded - slice_rows), (0, 0)))

    gate_full = lax.all_gather(my_slice(gate_weight), "fsdp", axis=0, tiled=True)
    up_full = lax.all_gather(my_slice(up_weight), "fsdp", axis=0, tiled=True)
    down_full = lax.all_gather(my_slice(down_weight), "fsdp", axis=0, tiled=True)

    offset = ctx_index * local_len
    positions = offset + jnp.arange(local_len, dtype=jnp.int32)
    cos_table, sin_table = rope_tables(positions)
    stream = tokens.astype(jnp.float32).reshape(local_len, D)
    flat_normed = rms_norm(stream, gains_all[0]).astype(jnp.bfloat16)
    projected = jnp.dot(flat_normed, qkv_full, preferred_element_type=jnp.float32)
    q_raw = projected[:, : NH * HD].reshape(local_len, NH, HD)
    k_raw = projected[:, NH * HD : NH * HD + HD]
    values = projected[:, NH * HD + HD :].astype(jnp.bfloat16)
    prep_fixed = partial(head_prep, cos_table=cos_table, sin_table=sin_table)
    (q_rot, k_rot), prep_back = jax.vjp(prep_fixed, q_raw, k_raw, qk_all[0], qk_all[1])
    queries = q_rot.astype(jnp.bfloat16)
    own_pair = jnp.concatenate([k_rot.astype(jnp.bfloat16), values], axis=-1)
    reach = min(-(-(WINDOW - 1) // local_len), ctx_size - 1)
    pieces = [own_pair]
    for distance in range(1, reach + 1):
        pieces.insert(0, from_behind(own_pair, "ctx", distance))
    pair_all = jnp.concatenate(pieces, axis=0)
    key_all = pair_all[:, :HD]
    value_all = pair_all[:, HD:]
    key_index = offset - reach * local_len + jnp.arange((reach + 1) * local_len, dtype=jnp.int32)
    seg_padded = jnp.concatenate([jnp.full((reach * local_len,), -1, jnp.int32), seg_all])
    key_seg = lax.dynamic_slice_in_dim(seg_padded, offset, (reach + 1) * local_len, 0)
    spacing = positions[:, None] - key_index[None, :]
    allowed = (
        (spacing >= 0) & (spacing < WINDOW) & (segments[0][:, None] == key_seg[None, :])
    )
    raw_scores = (
        jnp.einsum("qhd,kd->hqk", queries, key_all, preferred_element_type=jnp.float32) * scale
    )
    scores = jnp.where(allowed[None], raw_scores, NEG_FILL)
    top_score = jnp.max(scores, axis=-1, keepdims=True)
    expo = jnp.exp(scores - top_score)
    probs = expo / jnp.sum(expo, axis=-1, keepdims=True)
    probs_low = probs.astype(jnp.bfloat16)
    attended = (
        jnp.einsum("hqk,kd->qhd", probs_low, value_all, preferred_element_type=jnp.float32)
        .astype(jnp.bfloat16)
        .reshape(local_len, NH * HD)
    )
    attn = jnp.dot(attended, out_full, preferred_element_type=jnp.float32)
    mid_stream = stream + rms_norm(attn, gains_all[1])
    normed_two = rms_norm(mid_stream, gains_all[2]).astype(jnp.bfloat16)

    normed_seq = lax.all_gather(normed_two, "ctx", axis=0, tiled=True)
    gate_pre = lax.dot_general(
        normed_seq, gate_full, CONTRACT_LAST, preferred_element_type=jnp.float32
    )
    up_pre = lax.dot_general(normed_seq, up_full, CONTRACT_LAST, preferred_element_type=jnp.float32)
    hidden_value, hidden_back = jax.vjp(gelu_product, gate_pre, up_pre)
    hidden_low = hidden_value.astype(jnp.bfloat16)
    mlp_part = jnp.dot(hidden_low, down_full, preferred_element_type=jnp.float32)
    mlp_out = lax.psum_scatter(
        mlp_part.astype(jnp.bfloat16), "ctx", scatter_dimension=0, tiled=True
    ).astype(jnp.float32)
    final = mid_stream + rms_norm(mlp_out, gains_all[3])
    output = final.reshape(1, local_len, D).astype(jnp.bfloat16)
    grad_final = cotangent.astype(jnp.float32).reshape(local_len, D)
    grad_mlp, grad_gain_three = jax.vjp(rms_norm, mlp_out, gains_all[3])[1](grad_final)
    grad_mlp_seq = lax.all_gather(grad_mlp.astype(jnp.bfloat16), "ctx", axis=0, tiled=True)
    grad_hidden = lax.dot_general(
        grad_mlp_seq, down_full, CONTRACT_LAST, preferred_element_type=jnp.float32
    )
    grad_gate, grad_up = hidden_back(grad_hidden)
    grad_gate_low = grad_gate.astype(jnp.bfloat16)
    grad_up_low = grad_up.astype(jnp.bfloat16)
    grad_normed_part = jnp.dot(
        grad_gate_low, gate_full, preferred_element_type=jnp.float32
    ) + jnp.dot(grad_up_low, up_full, preferred_element_type=jnp.float32)
    grad_normed_two = lax.psum_scatter(
        grad_normed_part.astype(jnp.bfloat16), "ctx", scatter_dimension=0, tiled=True
    ).astype(jnp.float32)
    mlp_grads = jnp.concatenate(
        [
            lax.dot_general(
                grad_gate_low, normed_seq, CONTRACT_FIRST, preferred_element_type=jnp.float32
            ),
            lax.dot_general(
                grad_up_low, normed_seq, CONTRACT_FIRST, preferred_element_type=jnp.float32
            ),
            lax.dot_general(
                hidden_low, grad_mlp_seq, CONTRACT_FIRST, preferred_element_type=jnp.float32
            ),
        ],
        axis=1,
    ).astype(jnp.bfloat16)
    mlp_share = lax.psum_scatter(mlp_grads, "fsdp", scatter_dimension=0, tiled=True)
    mlp_total = lax.all_gather(mlp_share[:slice_rows], "ctx", axis=0, tiled=True).astype(
        jnp.float32
    )

    grad_mid_part, grad_gain_two = jax.vjp(rms_norm, mid_stream, gains_all[2])[1](grad_normed_two)
    grad_mid = grad_final + grad_mid_part
    grad_attn, grad_gain_one = jax.vjp(rms_norm, attn, gains_all[1])[1](grad_mid)
    grad_attn_low = grad_attn.astype(jnp.bfloat16)
    grad_attended = lax.dot_general(
        grad_attn_low, out_full, CONTRACT_LAST, preferred_element_type=jnp.float32
    ).astype(jnp.bfloat16)
    grad_out_weight = lax.dot_general(
        attended, grad_attn_low, CONTRACT_FIRST, preferred_element_type=jnp.float32
    )
    grad_heads = grad_attended.reshape(local_len, NH, HD)
    grad_probs = jnp.einsum(
        "qhd,kd->hqk", grad_heads, value_all, preferred_element_type=jnp.float32
    )
    row_total = jnp.sum(probs * grad_probs, axis=-1, keepdims=True)
    grad_scores = (probs * (grad_probs - row_total)).astype(jnp.bfloat16)
    grad_queries = (
        jnp.einsum("hqk,kd->qhd", grad_scores, key_all, preferred_element_type=jnp.float32) * scale
    )
    grad_keys = (
        jnp.einsum("hqk,qhd->kd", grad_scores, queries, preferred_element_type=jnp.float32) * scale
    )
    grad_values = jnp.einsum(
        "hqk,qhd->kd", probs_low, grad_heads, preferred_element_type=jnp.float32
    )
    grad_pairs = jnp.concatenate([grad_keys, grad_values], axis=-1)
    own_grad = grad_pairs[reach * local_len :]
    for distance in range(1, reach + 1):
        block_grad = grad_pairs[(reach - distance) * local_len : (reach - distance + 1) * local_len]
        own_grad = own_grad + from_behind(block_grad.astype(jnp.bfloat16), "ctx", -distance).astype(
            jnp.float32
        )
    grad_q_raw, grad_k_raw, grad_q_gain, grad_k_gain = prep_back((grad_queries, own_grad[:, :HD]))
    grad_projected = jnp.concatenate(
        [grad_q_raw.reshape(local_len, NH * HD), grad_k_raw, own_grad[:, HD:]], axis=1
    ).astype(jnp.bfloat16)
    grad_normed = lax.dot_general(
        grad_projected, qkv_full, CONTRACT_LAST, preferred_element_type=jnp.float32
    )
    grad_qkv_weight = lax.dot_general(
        flat_normed, grad_projected, CONTRACT_FIRST, preferred_element_type=jnp.float32
    )
    grad_input_part, grad_gain_zero = jax.vjp(rms_norm, stream, gains_all[0])[1](grad_normed)
    grad_tokens = (grad_mid + grad_input_part).reshape(1, local_len, D)
    gain_grads = jnp.stack([grad_gain_zero, grad_gain_one, grad_gain_two, grad_gain_three])
    qk_grads = jnp.stack([grad_q_gain, grad_k_gain])
    fsdp_size = lax.axis_size("fsdp")
    small = jnp.concatenate(
        [
            gain_grads.reshape(4, fsdp_size, -1).transpose(1, 0, 2).reshape(fsdp_size, -1),
            qk_grads.reshape(2, fsdp_size, -1).transpose(1, 0, 2).reshape(fsdp_size, -1),
        ],
        axis=1,
    )
    small_total = lax.psum(small, ("fsdp", "ctx"))
    small_own = lax.dynamic_index_in_dim(small_total, lax.axis_index("fsdp"), 0, False)
    total_gains = small_own[:n_gain].reshape(norm_gains.shape)
    total_qk = small_own[n_gain:].reshape(qk_gains.shape)
    share_qkv = lax.psum_scatter(
        grad_qkv_weight.astype(jnp.bfloat16), "fsdp", scatter_dimension=0, tiled=True
    )
    share_out = lax.psum_scatter(
        grad_out_weight.astype(jnp.bfloat16), "fsdp", scatter_dimension=0, tiled=True
    )
    total_qkv = lax.psum(share_qkv, "ctx").astype(jnp.float32)
    total_out = lax.psum(share_out, "ctx").astype(jnp.float32)
    return (
        output,
        grad_tokens,
        total_gains,
        total_qk,
        total_qkv,
        total_out,
        mlp_total[:, :D],
        mlp_total[:, D : 2 * D],
        mlp_total[:, 2 * D :],
    )


def solution(mesh):
    in_specs = (
        P("fsdp", "ctx", None),
        P(None, "fsdp"),
        P(None, "fsdp"),
        P("fsdp", None),
        P("fsdp", None),
        P("fsdp", None),
        P("fsdp", None),
        P("fsdp", None),
        P("fsdp", "ctx"),
        P("fsdp", "ctx", None),
    )
    out_specs = (
        P("fsdp", "ctx", None),
        P("fsdp", "ctx", None),
        P(None, "fsdp"),
        P(None, "fsdp"),
        P("fsdp", None),
        P("fsdp", None),
        P("fsdp", None),
        P("fsdp", None),
        P("fsdp", None),
    )
    return jax.shard_map(
        on_device, mesh=mesh, in_specs=in_specs, out_specs=out_specs, check_vma=False
    )
```

```python
from functools import partial

import jax
import jax.numpy as jnp
from jax import lax
from jax.experimental import pallas as pl
from jax.experimental.pallas import tpu as pltpu
from jax.sharding import PartitionSpec as P

D = 1152
NH = 4
HD = 256
WINDOW = 512


EPS = 1e-06
ROPE_BASE = 10000.0
NEG_FILL = -1e30
CONTRACT_LAST = (((1,), (1,)), ((), ()))
CONTRACT_FIRST = (((0,), (0,)), ((), ()))


def from_behind(array, axis, by):
    devices = lax.axis_size(axis)
    pairs = [(i, i + by) for i in range(devices) if 0 <= i + by < devices]
    return lax.ppermute(array, axis, pairs)


def rms_norm(values, gain_vec):
    return values * lax.rsqrt(jnp.mean(values * values, axis=-1, keepdims=True) + EPS) * gain_vec


def rotate(values, cos_table, sin_table):
    half_size = values.shape[-1] // 2
    first_half = values[..., :half_size]
    second_half = values[..., half_size:]
    return jnp.concatenate(
        [
            first_half * cos_table - second_half * sin_table,
            second_half * cos_table + first_half * sin_table,
        ],
        axis=-1,
    )


def rope_tables(positions):
    frequency = ROPE_BASE ** (-(2.0 * jnp.arange(HD // 2).astype(jnp.float32)) / HD)
    angles = positions.astype(jnp.float32)[..., None] * frequency
    return (jnp.cos(angles), jnp.sin(angles))


def head_prep(q_raw, k_raw, q_gain, k_gain, cos_table, sin_table):
    queries = rotate(rms_norm(q_raw, q_gain), cos_table[:, None, :], sin_table[:, None, :])
    key_rows = rotate(rms_norm(k_raw, k_gain), cos_table, sin_table)
    return (queries, key_rows)


def gelu_product(gate_pre, up_pre):
    return jax.nn.gelu(gate_pre, approximate=True) * up_pre


MESH = pl.DeviceIdType.MESH
NT = (((1,), (1,)), ((), ()))
NN = (((1,), (0,)), ((), ()))
TN = (((0,), (0,)), ((), ()))
GELU_C = 0.7978845608028654
GELU_A = 0.044715


def dot32(left, right, dims):
    return lax.dot_general(left, right, dims, preferred_element_type=jnp.float32)


def ffn_kernel(
    normed_ref, mid_ref, cot_ref, gain_ref, wg_hbm, wu_hbm, wd_hbm,
    out_ref, gn_ref, ggain_ref, dg_hbm, du_hbm, dd_hbm,
    wg, wu, wd, seq, gseq, act_a, act_b, hid, dgate, dup, part,
    d2d_snd, d2d_in, ici_snd, ici_in, dw,
    w_sem, o_sem, ag_s, ag_r, rd_s, rd_r, ri_s, ri_r,
):
    rows = normed_ref.shape[0]
    units = wg.shape[0]
    tile = 256
    me = lax.axis_index("ctx")
    chip, core = me // 2, lax.rem(me, 2)
    partner = {"ctx": chip * 2 + 1 - core}
    chips = {k: {"ctx": lax.rem(chip + k, 4) * 2 + core} for k in (1, 2, 3)}
    order = (0, 1, 3, 2)

    loads = [
        pltpu.make_async_copy(src, dst, w_sem.at[i])
        for i, (src, dst) in enumerate(((wg_hbm, wg), (wu_hbm, wu), (wd_hbm, wd)))
    ]
    for load in loads:
        load.start()

    barrier = pltpu.get_barrier_semaphore()
    for peer in (partner, chips[1], chips[2], chips[3]):
        pl.semaphore_signal(barrier, inc=1, device_id=peer, device_id_type=MESH)
    pl.semaphore_wait(barrier, 4)

    started = []

    def send(src, dst, s_sem, r_sem, peer):
        copy = pltpu.make_async_remote_copy(
            src_ref=src, dst_ref=dst, send_sem=s_sem, recv_sem=r_sem,
            device_id=peer, device_id_type=MESH,
        )
        copy.start()
        started.append(copy)
        return copy

    def mine(k):
        return pl.ds(k * 2 * rows, rows)

    def other(k):
        return pl.ds(k * 2 * rows + rows, rows)

    def pair(k):
        return pl.ds(k * 2 * rows, 2 * rows)

    def spread(buf, ph):
        own = buf.at[mine(0)]
        got = {}
        for k in (1, 3, 2):
            back = 4 - k
            got[back] = send(own, buf.at[mine(back)], ag_s.at[ph, k], ag_r.at[ph, back], chips[k])
        got[0] = send(own, buf.at[other(0)], ag_s.at[ph, 0], ag_r.at[ph, 0], partner)
        return got

    def relay(buf, ph, got, k):
        got[k].wait_recv()
        got[k] = send(
            buf.at[mine(k)], buf.at[other(k)], ag_s.at[ph, 4 + k], ag_r.at[ph, 4 + k], partner
        )

    def sum_out(ph, k):
        d2d_snd[ph, k] = part[pl.ds(rows, rows), :].astype(jnp.bfloat16)
        copy = send(
            d2d_snd.at[ph, k], d2d_in.at[ph, k], rd_s.at[ph, k], rd_r.at[ph, k], partner
        )
        copy.wait_recv()
        total = part[pl.ds(0, rows), :] + d2d_in[ph, k].astype(jnp.float32)
        if k == 0:
            return total
        ici_snd[ph, k - 1] = total.astype(jnp.bfloat16)
        back = 4 - k
        return send(
            ici_snd.at[ph, k - 1], ici_in.at[ph, back - 1], ri_s.at[ph, k], ri_r.at[ph, back],
            chips[k],
        )

    def phase(buf, ph, work):
        got = spread(buf, ph)
        if ph == 0:
            for load in loads:
                load.wait()
        sums = {}
        for k in order:
            if k == 1:
                relay(buf, ph, got, 1)
                relay(buf, ph, got, 3)
            if k == 2:
                relay(buf, ph, got, 2)
            got[k].wait_recv()
            work(k)
            sums[k] = sum_out(ph, k)
        return sums

    def collect(ph, sums):
        total = sums[0]
        for k in (1, 3, 2):
            sums[k].wait_recv()
        for k in (1, 2, 3):
            total = total + ici_in[ph, k - 1].astype(jnp.float32)
        return total

    def forward(k):
        def one(t, carry):
            cols = pl.ds(pl.multiple_of(t * tile, tile), tile)
            block = seq[pair(k), :]
            gate = dot32(block, wg[cols, :], NT)
            up = dot32(block, wu[cols, :], NT)
            square = gate * gate
            th = jnp.tanh(GELU_C * gate * (1.0 + GELU_A * square))
            half = 0.5 * (1.0 + th)
            gelu = gate * half
            slope = half + (0.5 * GELU_C) * gate * (1.0 - th * th) * (1.0 + 3.0 * GELU_A * square)
            hid[pair(k), cols] = (gelu * up).astype(jnp.bfloat16)
            act_a[pair(k), cols] = up * slope
            act_b[pair(k), cols] = gelu
            return carry

        lax.fori_loop(0, units // tile, one, 0)
        part[...] = dot32(hid[pair(k), :], wd[...], NN)

    seq[mine(0), :] = normed_ref[...]
    sums = phase(seq, 0, forward)
    mlp = collect(0, sums)
    r = lax.rsqrt(jnp.mean(mlp * mlp, axis=-1, keepdims=True) + EPS)
    n = mlp * r
    gain = gain_ref[...]
    out_ref[...] = (mid_ref[...] + n * gain).astype(jnp.bfloat16)
    dy = cot_ref[...].astype(jnp.float32)
    ggain_ref[...] = jnp.sum(dy * n, axis=0, keepdims=True)
    dyg = dy * gain
    dv = r * (dyg - n * jnp.mean(dyg * n, axis=-1, keepdims=True))
    gseq[mine(0), :] = dv.astype(jnp.bfloat16)

    def backward(k):
        def one(t, carry):
            cols = pl.ds(pl.multiple_of(t * tile, tile), tile)
            gh = dot32(gseq[pair(k), :], wd[cols, :], NT)
            dgate[pair(k), cols] = (gh * act_a[pair(k), cols]).astype(jnp.bfloat16)
            dup[pair(k), cols] = (gh * act_b[pair(k), cols]).astype(jnp.bfloat16)
            return carry

        lax.fori_loop(0, units // tile, one, 0)
        part[...] = dot32(dgate[pair(k), :], wg[...], NN) + dot32(dup[pair(k), :], wu[...], NN)

    sums = phase(gseq, 1, backward)
    stores = []
    for i, (left, right, dst) in enumerate(
        ((hid, gseq, dd_hbm), (dgate, seq, dg_hbm), (dup, seq, du_hbm))
    ):
        def one(t, carry, i=i, left=left, right=right):
            cols = pl.ds(pl.multiple_of(t * tile, tile), tile)
            dw[i, cols, :] = dot32(left[:, cols], right[...], TN).astype(jnp.bfloat16)
            return carry

        lax.fori_loop(0, units // tile, one, 0)
        store = pltpu.make_async_copy(dw.at[i], dst, o_sem.at[i])
        store.start()
        stores.append(store)
    gn_ref[...] = collect(1, sums)
    for copy in started:
        copy.wait_send()
    for store in stores:
        store.wait()


def ffn(normed_two, mid, cot, gain, wg, wu, wd):
    rows = normed_two.shape[0]
    units = wg.shape[0]
    seq_rows = rows * 8
    bf, f32 = jnp.bfloat16, jnp.float32
    vm = pl.BlockSpec(memory_space=pltpu.VMEM)
    hbm = pl.BlockSpec(memory_space=pl.ANY)
    dma = pltpu.SemaphoreType.DMA
    weight = jax.ShapeDtypeStruct((units, D), bf)
    return pl.pallas_call(
        ffn_kernel,
        out_shape=(
            jax.ShapeDtypeStruct((rows, D), bf),
            jax.ShapeDtypeStruct((rows, D), f32),
            jax.ShapeDtypeStruct((1, D), f32),
            weight, weight, weight,
        ),
        in_specs=[vm] * 4 + [hbm] * 3,
        out_specs=(vm, vm, vm, hbm, hbm, hbm),
        scratch_shapes=[
            pltpu.VMEM((units, D), bf),
            pltpu.VMEM((units, D), bf),
            pltpu.VMEM((units, D), bf),
            pltpu.VMEM((seq_rows, D), bf),
            pltpu.VMEM((seq_rows, D), bf),
            pltpu.VMEM((seq_rows, units), f32),
            pltpu.VMEM((seq_rows, units), f32),
            pltpu.VMEM((seq_rows, units), bf),
            pltpu.VMEM((seq_rows, units), bf),
            pltpu.VMEM((seq_rows, units), bf),
            pltpu.VMEM((2 * rows, D), f32),
            pltpu.VMEM((2, 4, rows, D), bf),
            pltpu.VMEM((2, 4, rows, D), bf),
            pltpu.VMEM((2, 3, rows, D), bf),
            pltpu.VMEM((2, 3, rows, D), bf),
            pltpu.VMEM((3, units, D), bf),
            dma((3,)), dma((3,)),
            dma((2, 8)), dma((2, 8)),
            dma((2, 4)), dma((2, 4)),
            dma((2, 4)), dma((2, 4)),
        ],
        compiler_params=pltpu.CompilerParams(
            collective_id=1, has_side_effects=True, vmem_limit_bytes=58 * 1024 * 1024
        ),
        cost_estimate=pl.CostEstimate(
            flops=18 * seq_rows * units * D, bytes_accessed=14 * units * D, transcendentals=0
        ),
    )(normed_two, mid, cot, gain, wg, wu, wd)


def on_device(
    tokens,
    norm_gains,
    qk_gains,
    qkv_weight,
    out_weight,
    gate_weight,
    up_weight,
    down_weight,
    segments,
    cotangent,
):
    local_len = tokens.shape[1]
    scale = HD ** (-0.5)
    ctx_index = lax.axis_index("ctx")
    ctx_size = lax.axis_size("ctx")
    own_rows = gate_weight.shape[0]
    slice_rows = own_rows // ctx_size
    padded = -(-slice_rows // 16) * 16
    gains_flat = jnp.concatenate([norm_gains.reshape(-1), qk_gains.reshape(-1)])
    gains_got = lax.all_gather(gains_flat, "fsdp")
    n_gain = norm_gains.size
    gains_all = (
        gains_got[:, :n_gain]
        .reshape(-1, 4, norm_gains.shape[1])
        .transpose(1, 0, 2)
        .reshape(4, D)
        .astype(jnp.float32)
    )
    qk_all = (
        gains_got[:, n_gain:]
        .reshape(-1, 2, qk_gains.shape[1])
        .transpose(1, 0, 2)
        .reshape(2, HD)
        .astype(jnp.float32)
    )
    seg_all = lax.all_gather(segments[0], "ctx", axis=0, tiled=True)
    qkv_full = lax.all_gather(qkv_weight, "fsdp", axis=0, tiled=True)
    out_full = lax.all_gather(out_weight, "fsdp", axis=0, tiled=True)

    def my_slice(weight):
        part = lax.dynamic_index_in_dim(
            weight.reshape(ctx_size, slice_rows, D), ctx_index, 0, False
        )
        return jnp.pad(part, ((0, padded - slice_rows), (0, 0)))

    gate_full = lax.all_gather(my_slice(gate_weight), "fsdp", axis=0, tiled=True)
    up_full = lax.all_gather(my_slice(up_weight), "fsdp", axis=0, tiled=True)
    down_full = lax.all_gather(my_slice(down_weight), "fsdp", axis=0, tiled=True)

    offset = ctx_index * local_len
    positions = offset + jnp.arange(local_len, dtype=jnp.int32)
    cos_table, sin_table = rope_tables(positions)
    stream = tokens.astype(jnp.float32).reshape(local_len, D)
    flat_normed = rms_norm(stream, gains_all[0]).astype(jnp.bfloat16)
    projected = jnp.dot(flat_normed, qkv_full, preferred_element_type=jnp.float32)
    q_raw = projected[:, : NH * HD].reshape(local_len, NH, HD)
    k_raw = projected[:, NH * HD : NH * HD + HD]
    values = projected[:, NH * HD + HD :].astype(jnp.bfloat16)
    prep_fixed = partial(head_prep, cos_table=cos_table, sin_table=sin_table)
    (q_rot, k_rot), prep_back = jax.vjp(prep_fixed, q_raw, k_raw, qk_all[0], qk_all[1])
    queries = q_rot.astype(jnp.bfloat16)
    own_pair = jnp.concatenate([k_rot.astype(jnp.bfloat16), values], axis=-1)
    reach = min(-(-(WINDOW - 1) // local_len), ctx_size - 1)
    pieces = [own_pair]
    for distance in range(1, reach + 1):
        pieces.insert(0, from_behind(own_pair, "ctx", distance))
    pair_all = jnp.concatenate(pieces, axis=0)
    key_all = pair_all[:, :HD]
    value_all = pair_all[:, HD:]
    key_index = offset - reach * local_len + jnp.arange((reach + 1) * local_len, dtype=jnp.int32)
    seg_padded = jnp.concatenate([jnp.full((reach * local_len,), -1, jnp.int32), seg_all])
    key_seg = lax.dynamic_slice_in_dim(seg_padded, offset, (reach + 1) * local_len, 0)
    spacing = positions[:, None] - key_index[None, :]
    allowed = (
        (spacing >= 0) & (spacing < WINDOW) & (segments[0][:, None] == key_seg[None, :])
    )
    raw_scores = (
        jnp.einsum("qhd,kd->hqk", queries, key_all, preferred_element_type=jnp.float32) * scale
    )
    scores = jnp.where(allowed[None], raw_scores, NEG_FILL)
    top_score = jnp.max(scores, axis=-1, keepdims=True)
    expo = jnp.exp(scores - top_score)
    probs = expo / jnp.sum(expo, axis=-1, keepdims=True)
    probs_low = probs.astype(jnp.bfloat16)
    attended = (
        jnp.einsum("hqk,kd->qhd", probs_low, value_all, preferred_element_type=jnp.float32)
        .astype(jnp.bfloat16)
        .reshape(local_len, NH * HD)
    )
    attn = jnp.dot(attended, out_full, preferred_element_type=jnp.float32)
    mid_stream = stream + rms_norm(attn, gains_all[1])
    normed_two = rms_norm(mid_stream, gains_all[2]).astype(jnp.bfloat16)

    grad_final = cotangent.astype(jnp.float32).reshape(local_len, D)
    output, grad_normed_two, grad_gain_three, d_gate, d_up, d_down = ffn(
        normed_two,
        mid_stream,
        cotangent.reshape(local_len, D),
        gains_all[3:4],
        gate_full,
        up_full,
        down_full,
    )
    output = output.reshape(1, local_len, D)
    grad_gain_three = grad_gain_three[0]
    mlp_grads = jnp.concatenate([d_gate, d_up, d_down], axis=1)
    mlp_share = lax.psum_scatter(mlp_grads, "fsdp", scatter_dimension=0, tiled=True)
    mlp_total = lax.all_gather(mlp_share[:slice_rows], "ctx", axis=0, tiled=True).astype(
        jnp.float32
    )

    grad_mid_part, grad_gain_two = jax.vjp(rms_norm, mid_stream, gains_all[2])[1](grad_normed_two)
    grad_mid = grad_final + grad_mid_part
    grad_attn, grad_gain_one = jax.vjp(rms_norm, attn, gains_all[1])[1](grad_mid)
    grad_attn_low = grad_attn.astype(jnp.bfloat16)
    grad_attended = lax.dot_general(
        grad_attn_low, out_full, CONTRACT_LAST, preferred_element_type=jnp.float32
    ).astype(jnp.bfloat16)
    grad_out_weight = lax.dot_general(
        attended, grad_attn_low, CONTRACT_FIRST, preferred_element_type=jnp.float32
    )
    grad_heads = grad_attended.reshape(local_len, NH, HD)
    grad_probs = jnp.einsum(
        "qhd,kd->hqk", grad_heads, value_all, preferred_element_type=jnp.float32
    )
    row_total = jnp.sum(probs * grad_probs, axis=-1, keepdims=True)
    grad_scores = (probs * (grad_probs - row_total)).astype(jnp.bfloat16)
    grad_queries = (
        jnp.einsum("hqk,kd->qhd", grad_scores, key_all, preferred_element_type=jnp.float32) * scale
    )
    grad_keys = (
        jnp.einsum("hqk,qhd->kd", grad_scores, queries, preferred_element_type=jnp.float32) * scale
    )
    grad_values = jnp.einsum(
        "hqk,qhd->kd", probs_low, grad_heads, preferred_element_type=jnp.float32
    )
    grad_pairs = jnp.concatenate([grad_keys, grad_values], axis=-1)
    own_grad = grad_pairs[reach * local_len :]
    for distance in range(1, reach + 1):
        block_grad = grad_pairs[(reach - distance) * local_len : (reach - distance + 1) * local_len]
        own_grad = own_grad + from_behind(block_grad.astype(jnp.bfloat16), "ctx", -distance).astype(
            jnp.float32
        )
    grad_q_raw, grad_k_raw, grad_q_gain, grad_k_gain = prep_back((grad_queries, own_grad[:, :HD]))
    grad_projected = jnp.concatenate(
        [grad_q_raw.reshape(local_len, NH * HD), grad_k_raw, own_grad[:, HD:]], axis=1
    ).astype(jnp.bfloat16)
    grad_normed = lax.dot_general(
        grad_projected, qkv_full, CONTRACT_LAST, preferred_element_type=jnp.float32
    )
    grad_qkv_weight = lax.dot_general(
        flat_normed, grad_projected, CONTRACT_FIRST, preferred_element_type=jnp.float32
    )
    grad_input_part, grad_gain_zero = jax.vjp(rms_norm, stream, gains_all[0])[1](grad_normed)
    grad_tokens = (grad_mid + grad_input_part).reshape(1, local_len, D)
    gain_grads = jnp.stack([grad_gain_zero, grad_gain_one, grad_gain_two, grad_gain_three])
    qk_grads = jnp.stack([grad_q_gain, grad_k_gain])
    fsdp_size = lax.axis_size("fsdp")
    small = jnp.concatenate(
        [
            gain_grads.reshape(4, fsdp_size, -1).transpose(1, 0, 2).reshape(fsdp_size, -1),
            qk_grads.reshape(2, fsdp_size, -1).transpose(1, 0, 2).reshape(fsdp_size, -1),
        ],
        axis=1,
    )
    small_total = lax.psum(small, ("fsdp", "ctx"))
    small_own = lax.dynamic_index_in_dim(small_total, lax.axis_index("fsdp"), 0, False)
    total_gains = small_own[:n_gain].reshape(norm_gains.shape)
    total_qk = small_own[n_gain:].reshape(qk_gains.shape)
    share_qkv = lax.psum_scatter(
        grad_qkv_weight.astype(jnp.bfloat16), "fsdp", scatter_dimension=0, tiled=True
    )
    share_out = lax.psum_scatter(
        grad_out_weight.astype(jnp.bfloat16), "fsdp", scatter_dimension=0, tiled=True
    )
    total_qkv = lax.psum(share_qkv, "ctx").astype(jnp.float32)
    total_out = lax.psum(share_out, "ctx").astype(jnp.float32)
    return (
        output,
        grad_tokens,
        total_gains,
        total_qk,
        total_qkv,
        total_out,
        mlp_total[:, :D],
        mlp_total[:, D : 2 * D],
        mlp_total[:, 2 * D :],
    )


def solution(mesh):
    in_specs = (
        P("fsdp", "ctx", None),
        P(None, "fsdp"),
        P(None, "fsdp"),
        P("fsdp", None),
        P("fsdp", None),
        P("fsdp", None),
        P("fsdp", None),
        P("fsdp", None),
        P("fsdp", "ctx"),
        P("fsdp", "ctx", None),
    )
    out_specs = (
        P("fsdp", "ctx", None),
        P("fsdp", "ctx", None),
        P(None, "fsdp"),
        P(None, "fsdp"),
        P("fsdp", None),
        P("fsdp", None),
        P("fsdp", None),
        P("fsdp", None),
        P("fsdp", None),
    )
    return jax.shard_map(
        on_device, mesh=mesh, in_specs=in_specs, out_specs=out_specs, check_vma=False
    )
```

```python
from functools import partial

import jax
import jax.numpy as jnp
from jax import lax
from jax.experimental import pallas as pl
from jax.experimental.pallas import tpu as pltpu
from jax.sharding import PartitionSpec as P

D = 1152
NH = 4
HD = 256
WINDOW = 512


EPS = 1e-06
ROPE_BASE = 10000.0
NEG_FILL = -1e30
CONTRACT_LAST = (((1,), (1,)), ((), ()))
CONTRACT_FIRST = (((0,), (0,)), ((), ()))


def from_behind(array, axis, by):
    devices = lax.axis_size(axis)
    pairs = [(i, i + by) for i in range(devices) if 0 <= i + by < devices]
    return lax.ppermute(array, axis, pairs)


def rms_norm(values, gain_vec):
    return values * lax.rsqrt(jnp.mean(values * values, axis=-1, keepdims=True) + EPS) * gain_vec


def rotate(values, cos_table, sin_table):
    half_size = values.shape[-1] // 2
    first_half = values[..., :half_size]
    second_half = values[..., half_size:]
    return jnp.concatenate(
        [
            first_half * cos_table - second_half * sin_table,
            second_half * cos_table + first_half * sin_table,
        ],
        axis=-1,
    )


def rope_tables(positions):
    frequency = ROPE_BASE ** (-(2.0 * jnp.arange(HD // 2).astype(jnp.float32)) / HD)
    angles = positions.astype(jnp.float32)[..., None] * frequency
    return (jnp.cos(angles), jnp.sin(angles))


def head_prep(q_raw, k_raw, q_gain, k_gain, cos_table, sin_table):
    queries = rotate(rms_norm(q_raw, q_gain), cos_table[:, None, :], sin_table[:, None, :])
    key_rows = rotate(rms_norm(k_raw, k_gain), cos_table, sin_table)
    return (queries, key_rows)


def gelu_product(gate_pre, up_pre):
    return jax.nn.gelu(gate_pre, approximate=True) * up_pre


MESH = pl.DeviceIdType.MESH
NT = (((1,), (1,)), ((), ()))
NN = (((1,), (0,)), ((), ()))
TN = (((0,), (0,)), ((), ()))
GELU_C = 0.7978845608028654
GELU_A = 0.044715


def dot32(left, right, dims):
    return lax.dot_general(left, right, dims, preferred_element_type=jnp.float32)


def ffn_kernel(
    normed_ref, mid_ref, cot_ref, gain_ref, w_hbm,
    out_ref, gn_ref, ggain_ref, dg_hbm, du_hbm, dd_hbm,
    wg, wu, wd, seq, gseq, act_a, act_b, hid, dgate, dup, part,
    d2d_snd, d2d_in, ici_snd, ici_in, dw,
    w_sem, o_sem, ag_s, ag_r, rd_s, rd_r, ri_s, ri_r,
):
    rows = normed_ref.shape[0]
    units = wg.shape[0]
    share = units // w_hbm.shape[0]
    tile = 256
    me = lax.axis_index("ctx")
    chip, core = me // 2, lax.rem(me, 2)
    partner = {"ctx": chip * 2 + 1 - core}
    chips = {k: {"ctx": lax.rem(chip + k, 4) * 2 + core} for k in (1, 2, 3)}
    order = (0, 1, 3, 2)

    loads = [
        pltpu.make_async_copy(
            w_hbm.at[f, pl.ds(i * share, share), :], dst.at[pl.ds(f * share, share), :], w_sem.at[i, f]
        )
        for i, dst in enumerate((wg, wu, wd))
        for f in range(w_hbm.shape[0])
    ]
    for load in loads:
        load.start()

    barrier = pltpu.get_barrier_semaphore()
    for peer in (partner, chips[1], chips[2], chips[3]):
        pl.semaphore_signal(barrier, inc=1, device_id=peer, device_id_type=MESH)
    pl.semaphore_wait(barrier, 4)

    started = []

    def send(src, dst, s_sem, r_sem, peer):
        copy = pltpu.make_async_remote_copy(
            src_ref=src, dst_ref=dst, send_sem=s_sem, recv_sem=r_sem,
            device_id=peer, device_id_type=MESH,
        )
        copy.start()
        started.append(copy)
        return copy

    def mine(k):
        return pl.ds(k * 2 * rows, rows)

    def other(k):
        return pl.ds(k * 2 * rows + rows, rows)

    def pair(k):
        return pl.ds(k * 2 * rows, 2 * rows)

    def spread(buf, ph):
        own = buf.at[mine(0)]
        got = {}
        for k in (1, 3, 2):
            back = 4 - k
            got[back] = send(own, buf.at[mine(back)], ag_s.at[ph, k], ag_r.at[ph, back], chips[k])
        got[0] = send(own, buf.at[other(0)], ag_s.at[ph, 0], ag_r.at[ph, 0], partner)
        return got

    def relay(buf, ph, got, k):
        got[k].wait_recv()
        got[k] = send(
            buf.at[mine(k)], buf.at[other(k)], ag_s.at[ph, 4 + k], ag_r.at[ph, 4 + k], partner
        )

    def sum_out(ph, k):
        d2d_snd[ph, k] = part[pl.ds(rows, rows), :].astype(jnp.bfloat16)
        copy = send(
            d2d_snd.at[ph, k], d2d_in.at[ph, k], rd_s.at[ph, k], rd_r.at[ph, k], partner
        )
        copy.wait_recv()
        total = part[pl.ds(0, rows), :] + d2d_in[ph, k].astype(jnp.float32)
        if k == 0:
            return total
        ici_snd[ph, k - 1] = total.astype(jnp.bfloat16)
        back = 4 - k
        return send(
            ici_snd.at[ph, k - 1], ici_in.at[ph, back - 1], ri_s.at[ph, k], ri_r.at[ph, back],
            chips[k],
        )

    def phase(buf, ph, work):
        got = spread(buf, ph)
        if ph == 0:
            for load in loads:
                load.wait()
        sums = {}
        for k in order:
            if k == 1:
                relay(buf, ph, got, 1)
                relay(buf, ph, got, 3)
            if k == 2:
                relay(buf, ph, got, 2)
            got[k].wait_recv()
            work(k)
            sums[k] = sum_out(ph, k)
        return sums

    def collect(ph, sums):
        total = sums[0]
        for k in (1, 3, 2):
            sums[k].wait_recv()
        for k in (1, 2, 3):
            total = total + ici_in[ph, k - 1].astype(jnp.float32)
        return total

    def forward(k):
        def one(t, carry):
            cols = pl.ds(pl.multiple_of(t * tile, tile), tile)
            block = seq[pair(k), :]
            gate = dot32(block, wg[cols, :], NT)
            up = dot32(block, wu[cols, :], NT)
            square = gate * gate
            th = jnp.tanh(GELU_C * gate * (1.0 + GELU_A * square))
            half = 0.5 * (1.0 + th)
            gelu = gate * half
            slope = half + (0.5 * GELU_C) * gate * (1.0 - th * th) * (1.0 + 3.0 * GELU_A * square)
            hid[pair(k), cols] = (gelu * up).astype(jnp.bfloat16)
            act_a[pair(k), cols] = up * slope
            act_b[pair(k), cols] = gelu
            return carry

        lax.fori_loop(0, units // tile, one, 0)
        part[...] = dot32(hid[pair(k), :], wd[...], NN)

    seq[mine(0), :] = normed_ref[...]
    sums = phase(seq, 0, forward)
    mlp = collect(0, sums)
    r = lax.rsqrt(jnp.mean(mlp * mlp, axis=-1, keepdims=True) + EPS)
    n = mlp * r
    gain = gain_ref[...]
    out_ref[...] = (mid_ref[...] + n * gain).astype(jnp.bfloat16)
    dy = cot_ref[...].astype(jnp.float32)
    ggain_ref[...] = jnp.sum(dy * n, axis=0, keepdims=True)
    dyg = dy * gain
    dv = r * (dyg - n * jnp.mean(dyg * n, axis=-1, keepdims=True))
    gseq[mine(0), :] = dv.astype(jnp.bfloat16)

    def backward(k):
        def one(t, carry):
            cols = pl.ds(pl.multiple_of(t * tile, tile), tile)
            gh = dot32(gseq[pair(k), :], wd[cols, :], NT)
            dgate[pair(k), cols] = (gh * act_a[pair(k), cols]).astype(jnp.bfloat16)
            dup[pair(k), cols] = (gh * act_b[pair(k), cols]).astype(jnp.bfloat16)
            return carry

        lax.fori_loop(0, units // tile, one, 0)
        part[...] = dot32(dgate[pair(k), :], wg[...], NN) + dot32(dup[pair(k), :], wu[...], NN)

    sums = phase(gseq, 1, backward)
    stores = []
    for i, (left, right, dst) in enumerate(
        ((hid, gseq, dd_hbm), (dgate, seq, dg_hbm), (dup, seq, du_hbm))
    ):
        def one(t, carry, i=i, left=left, right=right):
            cols = pl.ds(pl.multiple_of(t * tile, tile), tile)
            dw[i, cols, :] = dot32(left[:, cols], right[...], TN).astype(jnp.bfloat16)
            return carry

        lax.fori_loop(0, units // tile, one, 0)
        store = pltpu.make_async_copy(dw.at[i], dst, o_sem.at[i])
        store.start()
        stores.append(store)
    gn_ref[...] = collect(1, sums)
    for copy in started:
        copy.wait_send()
    for store in stores:
        store.wait()


def ffn(normed_two, mid, cot, gain, weights):
    rows = normed_two.shape[0]
    owners, lines = weights.shape[:2]
    units = owners * lines // 3
    seq_rows = rows * 8
    bf, f32 = jnp.bfloat16, jnp.float32
    vm = pl.BlockSpec(memory_space=pltpu.VMEM)
    hbm = pl.BlockSpec(memory_space=pl.ANY)
    dma = pltpu.SemaphoreType.DMA
    weight = jax.ShapeDtypeStruct((units, D), bf)
    return pl.pallas_call(
        ffn_kernel,
        out_shape=(
            jax.ShapeDtypeStruct((rows, D), bf),
            jax.ShapeDtypeStruct((rows, D), f32),
            jax.ShapeDtypeStruct((1, D), f32),
            weight, weight, weight,
        ),
        in_specs=[vm] * 4 + [hbm],
        out_specs=(vm, vm, vm, hbm, hbm, hbm),
        scratch_shapes=[
            pltpu.VMEM((units, D), bf),
            pltpu.VMEM((units, D), bf),
            pltpu.VMEM((units, D), bf),
            pltpu.VMEM((seq_rows, D), bf),
            pltpu.VMEM((seq_rows, D), bf),
            pltpu.VMEM((seq_rows, units), f32),
            pltpu.VMEM((seq_rows, units), f32),
            pltpu.VMEM((seq_rows, units), bf),
            pltpu.VMEM((seq_rows, units), bf),
            pltpu.VMEM((seq_rows, units), bf),
            pltpu.VMEM((2 * rows, D), f32),
            pltpu.VMEM((2, 4, rows, D), bf),
            pltpu.VMEM((2, 4, rows, D), bf),
            pltpu.VMEM((2, 3, rows, D), bf),
            pltpu.VMEM((2, 3, rows, D), bf),
            pltpu.VMEM((3, units, D), bf),
            dma((3, owners)), dma((3,)),
            dma((2, 8)), dma((2, 8)),
            dma((2, 4)), dma((2, 4)),
            dma((2, 4)), dma((2, 4)),
        ],
        compiler_params=pltpu.CompilerParams(
            collective_id=1, has_side_effects=True, vmem_limit_bytes=58 * 1024 * 1024
        ),
        cost_estimate=pl.CostEstimate(
            flops=18 * seq_rows * units * D, bytes_accessed=14 * units * D, transcendentals=0
        ),
    )(normed_two, mid, cot, gain, weights)


def place():
    fsdp = lax.axis_index("fsdp")
    ctx = lax.axis_index("ctx")
    y, z = fsdp // 4, lax.rem(fsdp, 4)
    chip, core = ctx // 2, lax.rem(ctx, 2)
    return y, z, chip, core


def shape_of(y, z, core):
    first = (1 - core) * y + core * z
    second = (1 - core) * z + core * y

    def block(i, j):
        return (1 - core) * (4 * i + j) + core * (4 * j + i)

    return first, second, block


def remote(src, dst, s_sem, r_sem, peer):
    return pltpu.make_async_remote_copy(
        src_ref=src, dst_ref=dst, send_sem=s_sem, recv_sem=r_sem,
        device_id=peer, device_id_type=MESH,
    )


def greet(peers):
    barrier = pltpu.get_barrier_semaphore()
    for peer in peers:
        pl.semaphore_signal(barrier, inc=1, device_id=peer, device_id_type=MESH)
    pl.semaphore_wait(barrier, len(peers))


def gather_kernel(
    qkv_ref, wo_ref, qkv_out, wo_all, rows_out, qkv_all,
    l_sem, s1, r1, s2, r2, sd, rd,
):
    y, z, chip, core = place()
    a, b, block = shape_of(y, z, core)
    _, _, block_there = shape_of(y, z, 1 - core)
    q_rows, width = qkv_ref.shape
    o_rows = wo_ref.shape[0]
    q_half, o_half = width // 2, o_rows // 2
    partner = {"ctx": chip * 2 + 1 - core}

    def views(f, half):
        return (
            qkv_all.at[
                pl.ds(pl.multiple_of(f * q_rows, 16), q_rows),
                pl.ds(pl.multiple_of(half * q_half, 128), q_half),
            ],
            wo_all.at[pl.ds(pl.multiple_of(f * o_rows + half * o_half, 16), o_half), :],
        )

    mine = (
        qkv_ref.at[:, pl.ds(pl.multiple_of(core * q_half, 128), q_half)],
        wo_ref.at[pl.ds(pl.multiple_of(core * o_half, 16), o_half), :],
    )
    here = block(a, b)
    locals_ = [
        pltpu.make_async_copy(
            qkv_ref, qkv_all.at[pl.ds(pl.multiple_of(here * q_rows, 16), q_rows), :], l_sem.at[0]
        ),
        pltpu.make_async_copy(
            wo_ref, wo_all.at[pl.ds(pl.multiple_of(here * o_rows, 16), o_rows), :], l_sem.at[1]
        ),
    ]
    for copy in locals_:
        copy.start()

    def first_peer(k):
        return {"fsdp": block(lax.rem(a + k, 4), b)}

    def second_peer(k):
        return {"fsdp": block(a, lax.rem(b + k, 4))}

    greet([first_peer(k) for k in (1, 2, 3)] + [second_peer(k) for k in (1, 2, 3)] + [partner])

    def hop_one(k, t):
        return remote(mine[t], views(here, core)[t], s1.at[k, t], r1.at[4 - k, t], first_peer(k))

    def hop_two(j, k, t):
        f = block(lax.rem(a + j, 4), b)
        dst = views(f, core)[t]
        src = dst if j else mine[t]
        return remote(src, dst, s2.at[j, k, t], r2.at[j, 4 - k, t], second_peer(k))

    def arrive_one(j, t):
        dst = views(block(lax.rem(a + j, 4), b), core)[t]
        return remote(dst, dst, s1.at[j, t], r1.at[j, t], partner)

    def arrive_two(j, m, t):
        dst = views(block(lax.rem(a + j, 4), lax.rem(b + m, 4)), core)[t]
        return remote(dst, dst, s2.at[j, m, t], r2.at[j, m, t], partner)

    def cross(j, m, t):
        dst = views(block(lax.rem(a + j, 4), lax.rem(b + m, 4)), core)[t]
        return remote(dst, dst, sd.at[j, m, t], rd.at[j, m, t], partner)

    def arrive_cross(j, m, t):
        dst = views(block_there(lax.rem(b + j, 4), lax.rem(a + m, 4)), 1 - core)[t]
        return remote(dst, dst, sd.at[j, m, t], rd.at[j, m, t], partner)

    both = (0, 1)
    for k in (1, 3, 2):
        for t in both:
            hop_one(k, t).start()
    for k in (1, 3, 2):
        for t in both:
            hop_two(0, k, t).start()
    for j in (1, 3, 2):
        for t in both:
            arrive_one(j, t).wait_recv()
            for k in (1, 3, 2):
                hop_two(j, k, t).start()
            cross(j, 0, t).start()

    def pass_on(i, carry):
        m, j = i // 4 + 1, lax.rem(i, 4)
        for t in both:
            arrive_two(j, m, t).wait_recv()
            cross(j, m, t).start()
        return carry

    lax.fori_loop(0, 12, pass_on, 0)

    def land(i, carry):
        m, j = i // 4, lax.rem(i, 4)
        for t in both:
            arrive_cross(j, m, t).wait_recv()
            cross(j, m, t).wait_send()
        return carry

    lax.fori_loop(1, 16, land, 0)
    for copy in locals_:
        copy.wait()
    for k in (1, 2, 3):
        for t in both:
            hop_one(k, t).wait_send()
            for j in range(4):
                hop_two(j, k, t).wait_send()

    keep = qkv_out.shape[0] // 16
    for f in range(0, 16, 2):
        left = qkv_all[pl.ds(f * q_rows, q_rows), :].astype(jnp.float32)
        right = qkv_all[pl.ds((f + 1) * q_rows, q_rows), :].astype(jnp.float32)
        qkv_out[pl.ds(f * keep, 2 * keep), :] = jnp.concatenate(
            [left[:keep], right[:keep]], axis=0
        ).astype(jnp.bfloat16)
        rows_out[f] = left[keep:, : rows_out.shape[2]]
        rows_out[f + 1] = right[keep:, : rows_out.shape[2]]


def gather_attention(qkv_shard, wo_shard, keep, extra):
    bf = jnp.bfloat16
    vm = pl.BlockSpec(memory_space=pltpu.VMEM)
    dma = pltpu.SemaphoreType.DMA
    q_rows, width = qkv_shard.shape
    o_rows, o_width = wo_shard.shape
    return pl.pallas_call(
        gather_kernel,
        out_shape=(
            jax.ShapeDtypeStruct((16 * keep, width), bf),
            jax.ShapeDtypeStruct((16 * o_rows, o_width), bf),
            jax.ShapeDtypeStruct((16, q_rows - keep, extra), jnp.float32),
        ),
        in_specs=[vm] * 2,
        out_specs=(vm,) * 3,
        scratch_shapes=[
            pltpu.VMEM((16 * q_rows, width), bf),
            dma((2,)),
            dma((4, 2)), dma((4, 2)),
            dma((4, 4, 2)), dma((4, 4, 2)),
            dma((4, 4, 2)), dma((4, 4, 2)),
        ],
        compiler_params=pltpu.CompilerParams(
            collective_id=2, has_side_effects=True, vmem_limit_bytes=40 * 1024 * 1024
        ),
        cost_estimate=pl.CostEstimate(
            flops=0, bytes_accessed=64 * (q_rows * width + o_rows * o_width), transcendentals=0
        ),
    )(qkv_shard, wo_shard)


def scatter_kernel(
    gq_ref, small_ref, go_ref, oq_ref, oo_ref,
    stage, dq, do, sq, so, iq1, io1, tq, to, iq2, io2, xq, xo,
    sd, rd, s1, r1, s2, r2, sx, rx, sf, rf,
):
    y, z, chip, core = place()
    a, b, block = shape_of(y, z, core)
    _, _, block_there = shape_of(y, z, 1 - core)
    q_rows, width = oq_ref.shape
    keep = gq_ref.shape[0] // 16
    o_rows = oo_ref.shape[0]
    q_half, o_half = width // 2, o_rows // 2
    chips = xq.shape[0]
    f32, bf = jnp.float32, jnp.bfloat16
    partner = {"ctx": chip * 2 + 1 - core}

    def first_peer(k):
        return {"fsdp": block(lax.rem(a + k, 4), b)}

    def second_peer(k):
        return {"fsdp": block(a, lax.rem(b + k, 4))}

    def chip_peer(k):
        return {"ctx": lax.rem(chip + k, chips) * 2 + core}

    def q_cols(half):
        return pl.ds(pl.multiple_of(half * q_half, 128), q_half)

    def o_lines(half):
        return pl.ds(pl.multiple_of(half * o_half, 16), o_half)

    for f in range(16):
        stage[f] = jnp.concatenate(
            [
                gq_ref[pl.ds(f * keep, keep), :],
                jnp.concatenate(
                    [
                        small_ref[f],
                        jnp.zeros((q_rows - keep, width - small_ref.shape[2]), f32),
                    ],
                    axis=1,
                ),
            ],
            axis=0,
        ).astype(bf)

    greet(
        [first_peer(k) for k in (1, 2, 3)]
        + [second_peer(k) for k in (1, 2, 3)]
        + [chip_peer(k) for k in range(1, chips)]
        + [partner]
    )

    def away(i, t):
        k, j = lax.rem(i // 4 + 1, 4), lax.rem(i, 4)
        line = lax.rem(b + k, 4)
        f = block_there(line, j)
        slot = line * 4 + j
        if t == 0:
            src, dst = stage.at[f, :, q_cols(1 - core)], dq.at[slot]
        else:
            src, dst = go_ref.at[f, o_lines(1 - core), :], do.at[slot]
        return remote(src, dst, sd.at[i, t], rd.at[i, t], partner)

    def home(i, t):
        k, j = lax.rem(i // 4 + 1, 4), lax.rem(i, 4)
        slot = lax.rem(a + k, 4) * 4 + j
        dst = (dq, do)[t].at[slot]
        return remote(dst, dst, sd.at[i, t], rd.at[i, t], partner)

    def start_away(i, carry):
        for t in (0, 1):
            away(i, t).start()
        return carry

    lax.fori_loop(0, 16, start_away, 0)

    def hop_one(k, t):
        src, dst = ((sq, iq1), (so, io1))[t]
        line = pl.ds(lax.rem(a + k, 4) * 4, 4)
        return remote(
            src.at[line], dst.at[3 - k], s1.at[k, t], r1.at[4 - k, t], first_peer(k)
        )

    for k in (1, 2, 3, 0):
        def add(j, carry, k=k):
            i = (k + 3) % 4 * 4 + j
            line = lax.rem(a + k, 4)
            slot = line * 4 + j
            f = block(line, j)
            home(i, 0).wait_recv()
            sq[slot] = (stage[f, :, q_cols(core)].astype(f32) + dq[slot].astype(f32)).astype(bf)
            home(i, 1).wait_recv()
            so[slot] = (go_ref[f, o_lines(core), :].astype(f32) + do[slot].astype(f32)).astype(bf)
            return carry

        lax.fori_loop(0, 4, add, 0)
        if k:
            for t in (0, 1):
                hop_one(k, t).start()

    for k in (1, 3, 2):
        for t in (0, 1):
            hop_one(4 - k, t).wait_recv()

    def hop_two(k, t):
        src, dst = ((tq, iq2), (to, io2))[t]
        return remote(
            src.at[lax.rem(b + k, 4)], dst.at[3 - k], s2.at[k, t], r2.at[4 - k, t], second_peer(k)
        )

    for k in (2, 1, 3, 0):
        j = lax.rem(b + k, 4)
        slot = a * 4 + j
        for t, (own, got, dst) in enumerate(((sq, iq1, tq), (so, io1, to))):
            total = own[slot].astype(f32)
            for m in range(3):
                total = total + got[m, j].astype(f32)
            dst[j] = total.astype(bf)
            if k:
                hop_two(k, t).start()

    def hop_chip(k, t):
        buf = (xq, xo)[t]
        return remote(
            buf.at[chip], buf.at[chip], sx.at[k, t], rx.at[chips - k, t], chip_peer(k)
        )

    for t, (own, got, dst) in enumerate(((tq, iq2, xq), (to, io2, xo))):
        for k in (1, 3, 2):
            hop_two(4 - k, t).wait_recv()
        total = own[b].astype(f32)
        for m in range(3):
            total = total + got[m].astype(f32)
        dst[chip] = total.astype(bf)
        for k in range(1, chips):
            hop_chip(k, t).start()

    def last(t):
        part = (oq_ref.at[:, q_cols(core)], oo_ref.at[o_lines(core), :])[t]
        return remote(part, part, sf.at[t], rf.at[t], partner)

    def last_home(t):
        part = (oq_ref.at[:, q_cols(1 - core)], oo_ref.at[o_lines(1 - core), :])[t]
        return remote(part, part, sf.at[t], rf.at[t], partner)

    for t, buf in enumerate((xq, xo)):
        for k in range(1, chips):
            dst = buf.at[lax.rem(chip + k, chips)]
            remote(dst, dst, sx.at[k, t], rx.at[k, t], partner).wait_recv()
        total = buf[0].astype(f32)
        for m in range(1, chips):
            total = total + buf[m].astype(f32)
        if t == 0:
            oq_ref[:, q_cols(core)] = total
        else:
            oo_ref[o_lines(core), :] = total
        last(t).start()

    def end_away(i, carry):
        for t in (0, 1):
            away(i, t).wait_send()
        return carry

    lax.fori_loop(0, 16, end_away, 0)
    for t in (0, 1):
        for k in (1, 2, 3):
            hop_one(k, t).wait_send()
            hop_two(k, t).wait_send()
        for k in range(1, chips):
            hop_chip(k, t).wait_send()
        last(t).wait_send()
        last_home(t).wait_recv()


def scatter_attention(gq, small, go):
    f32, bf = jnp.float32, jnp.bfloat16
    vm = pl.BlockSpec(memory_space=pltpu.VMEM)
    dma = pltpu.SemaphoreType.DMA
    keep, width = gq.shape[0] // 16, gq.shape[1]
    q_rows = keep + small.shape[1]
    o_rows, o_width = go.shape[1:]
    q_half, o_half = width // 2, o_rows // 2
    chips = lax.axis_size("ctx") // 2

    def two(*lead):
        return [pltpu.VMEM(lead + (q_rows, q_half), bf), pltpu.VMEM(lead + (o_half, o_width), bf)]

    return pl.pallas_call(
        scatter_kernel,
        out_shape=(
            jax.ShapeDtypeStruct((q_rows, width), f32),
            jax.ShapeDtypeStruct((o_rows, o_width), f32),
        ),
        in_specs=[vm] * 3,
        out_specs=(vm,) * 2,
        scratch_shapes=[
            pltpu.VMEM((16, q_rows, width), bf),
            *two(16), *two(16), *two(3, 4), *two(4), *two(3), *two(chips),
            dma((16, 2)), dma((16, 2)),
            dma((4, 2)), dma((4, 2)),
            dma((4, 2)), dma((4, 2)),
            dma((4, 2)), dma((4, 2)),
            dma((2,)), dma((2,)),
        ],
        compiler_params=pltpu.CompilerParams(
            collective_id=3, has_side_effects=True, vmem_limit_bytes=48 * 1024 * 1024
        ),
        cost_estimate=pl.CostEstimate(
            flops=0, bytes_accessed=64 * (q_rows * width + o_rows * o_width), transcendentals=0
        ),
    )(gq, small, go)


def on_device(
    tokens,
    norm_gains,
    qk_gains,
    qkv_weight,
    out_weight,
    gate_weight,
    up_weight,
    down_weight,
    segments,
    cotangent,
):
    local_len = tokens.shape[1]
    scale = HD ** (-0.5)
    ctx_index = lax.axis_index("ctx")
    ctx_size = lax.axis_size("ctx")
    own_rows = gate_weight.shape[0]
    slice_rows = own_rows // ctx_size
    padded = -(-slice_rows // 16) * 16
    n_gain, n_qk = norm_gains.size, qk_gains.size
    extra = -(-n_gain // 128) * 128
    gain_rows = jnp.zeros((8, qkv_weight.shape[1]), jnp.bfloat16)
    gain_rows = gain_rows.at[0, :n_gain].set(norm_gains.reshape(-1))
    gain_rows = gain_rows.at[1, :n_qk].set(qk_gains.reshape(-1))
    qkv_full, out_full, gain_got = gather_attention(
        jnp.concatenate([qkv_weight, gain_rows], axis=0), out_weight, qkv_weight.shape[0], extra
    )
    gains_all = (
        gain_got[:, 0, :n_gain]
        .reshape(-1, 4, norm_gains.shape[1])
        .transpose(1, 0, 2)
        .reshape(4, D)
    )
    qk_all = (
        gain_got[:, 1, :n_qk]
        .reshape(-1, 2, qk_gains.shape[1])
        .transpose(1, 0, 2)
        .reshape(2, HD)
    )
    seg_all = lax.all_gather(segments[0], "ctx", axis=0, tiled=True)

    def my_slice(weight):
        part = lax.dynamic_index_in_dim(
            weight.reshape(ctx_size, slice_rows, D), ctx_index, 0, False
        )
        return jnp.pad(part, ((0, padded - slice_rows), (0, 0)))

    ffn_shard = jnp.concatenate(
        [my_slice(gate_weight), my_slice(up_weight), my_slice(down_weight)], axis=0
    )
    ffn_full = lax.all_gather(ffn_shard, "fsdp")

    offset = ctx_index * local_len
    positions = offset + jnp.arange(local_len, dtype=jnp.int32)
    cos_table, sin_table = rope_tables(positions)
    stream = tokens.astype(jnp.float32).reshape(local_len, D)
    flat_normed = rms_norm(stream, gains_all[0]).astype(jnp.bfloat16)
    projected = jnp.dot(flat_normed, qkv_full, preferred_element_type=jnp.float32)
    q_raw = projected[:, : NH * HD].reshape(local_len, NH, HD)
    k_raw = projected[:, NH * HD : NH * HD + HD]
    values = projected[:, NH * HD + HD :].astype(jnp.bfloat16)
    prep_fixed = partial(head_prep, cos_table=cos_table, sin_table=sin_table)
    (q_rot, k_rot), prep_back = jax.vjp(prep_fixed, q_raw, k_raw, qk_all[0], qk_all[1])
    queries = q_rot.astype(jnp.bfloat16)
    own_pair = jnp.concatenate([k_rot.astype(jnp.bfloat16), values], axis=-1)
    reach = min(-(-(WINDOW - 1) // local_len), ctx_size - 1)
    pieces = [own_pair]
    for distance in range(1, reach + 1):
        pieces.insert(0, from_behind(own_pair, "ctx", distance))
    pair_all = jnp.concatenate(pieces, axis=0)
    key_all = pair_all[:, :HD]
    value_all = pair_all[:, HD:]
    key_index = offset - reach * local_len + jnp.arange((reach + 1) * local_len, dtype=jnp.int32)
    seg_padded = jnp.concatenate([jnp.full((reach * local_len,), -1, jnp.int32), seg_all])
    key_seg = lax.dynamic_slice_in_dim(seg_padded, offset, (reach + 1) * local_len, 0)
    spacing = positions[:, None] - key_index[None, :]
    allowed = (
        (spacing >= 0) & (spacing < WINDOW) & (segments[0][:, None] == key_seg[None, :])
    )
    raw_scores = (
        jnp.einsum("qhd,kd->hqk", queries, key_all, preferred_element_type=jnp.float32) * scale
    )
    scores = jnp.where(allowed[None], raw_scores, NEG_FILL)
    top_score = jnp.max(scores, axis=-1, keepdims=True)
    expo = jnp.exp(scores - top_score)
    probs = expo / jnp.sum(expo, axis=-1, keepdims=True)
    probs_low = probs.astype(jnp.bfloat16)
    attended = (
        jnp.einsum("hqk,kd->qhd", probs_low, value_all, preferred_element_type=jnp.float32)
        .astype(jnp.bfloat16)
        .reshape(local_len, NH * HD)
    )
    attn = jnp.dot(attended, out_full, preferred_element_type=jnp.float32)
    mid_stream = stream + rms_norm(attn, gains_all[1])
    normed_two = rms_norm(mid_stream, gains_all[2]).astype(jnp.bfloat16)

    grad_final = cotangent.astype(jnp.float32).reshape(local_len, D)
    output, grad_normed_two, grad_gain_three, d_gate, d_up, d_down = ffn(
        normed_two,
        mid_stream,
        cotangent.reshape(local_len, D),
        gains_all[3:4],
        ffn_full,
    )
    output = output.reshape(1, local_len, D)
    grad_gain_three = grad_gain_three[0]
    mlp_grads = jnp.concatenate([d_gate, d_up, d_down], axis=1)
    mlp_share = lax.psum_scatter(mlp_grads, "fsdp", scatter_dimension=0, tiled=True)
    mlp_total = lax.all_gather(mlp_share[:slice_rows], "ctx", axis=0, tiled=True).astype(
        jnp.float32
    )

    grad_mid_part, grad_gain_two = jax.vjp(rms_norm, mid_stream, gains_all[2])[1](grad_normed_two)
    grad_mid = grad_final + grad_mid_part
    grad_attn, grad_gain_one = jax.vjp(rms_norm, attn, gains_all[1])[1](grad_mid)
    grad_attn_low = grad_attn.astype(jnp.bfloat16)
    grad_attended = lax.dot_general(
        grad_attn_low, out_full, CONTRACT_LAST, preferred_element_type=jnp.float32
    ).astype(jnp.bfloat16)
    grad_out_weight = lax.dot_general(
        attended, grad_attn_low, CONTRACT_FIRST, preferred_element_type=jnp.float32
    )
    grad_heads = grad_attended.reshape(local_len, NH, HD)
    grad_probs = jnp.einsum(
        "qhd,kd->hqk", grad_heads, value_all, preferred_element_type=jnp.float32
    )
    row_total = jnp.sum(probs * grad_probs, axis=-1, keepdims=True)
    grad_scores = (probs * (grad_probs - row_total)).astype(jnp.bfloat16)
    grad_queries = (
        jnp.einsum("hqk,kd->qhd", grad_scores, key_all, preferred_element_type=jnp.float32) * scale
    )
    grad_keys = (
        jnp.einsum("hqk,qhd->kd", grad_scores, queries, preferred_element_type=jnp.float32) * scale
    )
    grad_values = jnp.einsum(
        "hqk,qhd->kd", probs_low, grad_heads, preferred_element_type=jnp.float32
    )
    grad_pairs = jnp.concatenate([grad_keys, grad_values], axis=-1)
    own_grad = grad_pairs[reach * local_len :]
    for distance in range(1, reach + 1):
        block_grad = grad_pairs[(reach - distance) * local_len : (reach - distance + 1) * local_len]
        own_grad = own_grad + from_behind(block_grad.astype(jnp.bfloat16), "ctx", -distance).astype(
            jnp.float32
        )
    grad_q_raw, grad_k_raw, grad_q_gain, grad_k_gain = prep_back((grad_queries, own_grad[:, :HD]))
    grad_projected = jnp.concatenate(
        [grad_q_raw.reshape(local_len, NH * HD), grad_k_raw, own_grad[:, HD:]], axis=1
    ).astype(jnp.bfloat16)
    grad_normed = lax.dot_general(
        grad_projected, qkv_full, CONTRACT_LAST, preferred_element_type=jnp.float32
    )
    grad_qkv_weight = lax.dot_general(
        flat_normed, grad_projected, CONTRACT_FIRST, preferred_element_type=jnp.float32
    )
    grad_input_part, grad_gain_zero = jax.vjp(rms_norm, stream, gains_all[0])[1](grad_normed)
    grad_tokens = (grad_mid + grad_input_part).reshape(1, local_len, D)
    gain_grads = jnp.stack([grad_gain_zero, grad_gain_one, grad_gain_two, grad_gain_three])
    qk_grads = jnp.stack([grad_q_gain, grad_k_gain])
    owners = lax.axis_size("fsdp")

    def by_owner(grads):
        lines = grads.shape[0]
        flat = grads.reshape(lines, owners, -1).transpose(1, 0, 2).reshape(owners, 1, -1)
        return jnp.pad(flat, ((0, 0), (0, 0), (0, extra - flat.shape[2])))

    small = jnp.concatenate(
        [by_owner(gain_grads), by_owner(qk_grads), jnp.zeros((owners, 6, extra), jnp.float32)],
        axis=1,
    )
    own_qkv, total_out = scatter_attention(
        grad_qkv_weight,
        small,
        grad_out_weight.astype(jnp.bfloat16).reshape(owners, out_weight.shape[0], D),
    )
    total_qkv = own_qkv[: qkv_weight.shape[0]]
    total_gains = own_qkv[qkv_weight.shape[0], :n_gain].reshape(norm_gains.shape)
    total_qk = own_qkv[qkv_weight.shape[0] + 1, :n_qk].reshape(qk_gains.shape)
    return (
        output,
        grad_tokens,
        total_gains,
        total_qk,
        total_qkv,
        total_out,
        mlp_total[:, :D],
        mlp_total[:, D : 2 * D],
        mlp_total[:, 2 * D :],
    )


def solution(mesh):
    in_specs = (
        P("fsdp", "ctx", None),
        P(None, "fsdp"),
        P(None, "fsdp"),
        P("fsdp", None),
        P("fsdp", None),
        P("fsdp", None),
        P("fsdp", None),
        P("fsdp", None),
        P("fsdp", "ctx"),
        P("fsdp", "ctx", None),
    )
    out_specs = (
        P("fsdp", "ctx", None),
        P("fsdp", "ctx", None),
        P(None, "fsdp"),
        P(None, "fsdp"),
        P("fsdp", None),
        P("fsdp", None),
        P("fsdp", None),
        P("fsdp", None),
        P("fsdp", None),
    )
    return jax.shard_map(
        on_device, mesh=mesh, in_specs=in_specs, out_specs=out_specs, check_vma=False
    )
```

```python
from functools import partial

import jax
import jax.numpy as jnp
from jax import lax
from jax.experimental import pallas as pl
from jax.experimental.pallas import tpu as pltpu
from jax.sharding import PartitionSpec as P

D = 1152
NH = 4
HD = 256
WINDOW = 512


EPS = 1e-06
ROPE_BASE = 10000.0
NEG_FILL = -1e30
CONTRACT_LAST = (((1,), (1,)), ((), ()))
CONTRACT_FIRST = (((0,), (0,)), ((), ()))


def from_behind(array, axis, by):
    devices = lax.axis_size(axis)
    pairs = [(i, i + by) for i in range(devices) if 0 <= i + by < devices]
    return lax.ppermute(array, axis, pairs)


def rms_norm(values, gain_vec):
    return values * lax.rsqrt(jnp.mean(values * values, axis=-1, keepdims=True) + EPS) * gain_vec


def rotate(values, cos_table, sin_table):
    half_size = values.shape[-1] // 2
    first_half = values[..., :half_size]
    second_half = values[..., half_size:]
    return jnp.concatenate(
        [
            first_half * cos_table - second_half * sin_table,
            second_half * cos_table + first_half * sin_table,
        ],
        axis=-1,
    )


def rope_tables(positions):
    frequency = ROPE_BASE ** (-(2.0 * jnp.arange(HD // 2).astype(jnp.float32)) / HD)
    angles = positions.astype(jnp.float32)[..., None] * frequency
    return (jnp.cos(angles), jnp.sin(angles))


def head_prep(q_raw, k_raw, q_gain, k_gain, cos_table, sin_table):
    queries = rotate(rms_norm(q_raw, q_gain), cos_table[:, None, :], sin_table[:, None, :])
    key_rows = rotate(rms_norm(k_raw, k_gain), cos_table, sin_table)
    return (queries, key_rows)


def gelu_product(gate_pre, up_pre):
    return jax.nn.gelu(gate_pre, approximate=True) * up_pre


MESH = pl.DeviceIdType.MESH
NT = (((1,), (1,)), ((), ()))
NN = (((1,), (0,)), ((), ()))
TN = (((0,), (0,)), ((), ()))
GELU_C = 0.7978845608028654
GELU_A = 0.044715


def dot32(left, right, dims):
    return lax.dot_general(left, right, dims, preferred_element_type=jnp.float32)


def ffn_kernel(
    normed_ref, mid_ref, cot_ref, gain_ref, w_hbm,
    out_ref, gn_ref, ggain_ref, gff_hbm,
    wg, wu, wd, seq, gseq, act_a, act_b, hid, dgate, dup, part,
    d2d_snd, d2d_in, ici_snd, ici_in, dw,
    w_sem, o_sem, ag_s, ag_r, rd_s, rd_r, ri_s, ri_r,
):
    rows = normed_ref.shape[0]
    units = wg.shape[0]
    share = units // w_hbm.shape[0]
    tile = 256
    me = lax.axis_index("ctx")
    chip, core = me // 2, lax.rem(me, 2)
    partner = {"ctx": chip * 2 + 1 - core}
    chips = {k: {"ctx": lax.rem(chip + k, 4) * 2 + core} for k in (1, 2, 3)}
    order = (0, 1, 3, 2)

    loads = [
        pltpu.make_async_copy(
            w_hbm.at[f, pl.ds(i * share, share), :], dst.at[pl.ds(f * share, share), :], w_sem.at[i, f]
        )
        for i, dst in enumerate((wg, wu, wd))
        for f in range(w_hbm.shape[0])
    ]
    for load in loads:
        load.start()

    barrier = pltpu.get_barrier_semaphore()
    for peer in (partner, chips[1], chips[2], chips[3]):
        pl.semaphore_signal(barrier, inc=1, device_id=peer, device_id_type=MESH)
    pl.semaphore_wait(barrier, 4)

    started = []

    def send(src, dst, s_sem, r_sem, peer):
        copy = pltpu.make_async_remote_copy(
            src_ref=src, dst_ref=dst, send_sem=s_sem, recv_sem=r_sem,
            device_id=peer, device_id_type=MESH,
        )
        copy.start()
        started.append(copy)
        return copy

    def mine(k):
        return pl.ds(k * 2 * rows, rows)

    def other(k):
        return pl.ds(k * 2 * rows + rows, rows)

    def pair(k):
        return pl.ds(k * 2 * rows, 2 * rows)

    def spread(buf, ph):
        own = buf.at[mine(0)]
        got = {}
        for k in (1, 3, 2):
            back = 4 - k
            got[back] = send(own, buf.at[mine(back)], ag_s.at[ph, k], ag_r.at[ph, back], chips[k])
        got[0] = send(own, buf.at[other(0)], ag_s.at[ph, 0], ag_r.at[ph, 0], partner)
        return got

    def relay(buf, ph, got, k):
        got[k].wait_recv()
        got[k] = send(
            buf.at[mine(k)], buf.at[other(k)], ag_s.at[ph, 4 + k], ag_r.at[ph, 4 + k], partner
        )

    def sum_out(ph, k):
        d2d_snd[ph, k] = part[pl.ds(rows, rows), :].astype(jnp.bfloat16)
        copy = send(
            d2d_snd.at[ph, k], d2d_in.at[ph, k], rd_s.at[ph, k], rd_r.at[ph, k], partner
        )
        copy.wait_recv()
        total = part[pl.ds(0, rows), :] + d2d_in[ph, k].astype(jnp.float32)
        if k == 0:
            return total
        ici_snd[ph, k - 1] = total.astype(jnp.bfloat16)
        back = 4 - k
        return send(
            ici_snd.at[ph, k - 1], ici_in.at[ph, back - 1], ri_s.at[ph, k], ri_r.at[ph, back],
            chips[k],
        )

    def phase(buf, ph, work):
        got = spread(buf, ph)
        if ph == 0:
            for load in loads:
                load.wait()
        sums = {}
        for k in order:
            if k == 1:
                relay(buf, ph, got, 1)
                relay(buf, ph, got, 3)
            if k == 2:
                relay(buf, ph, got, 2)
            got[k].wait_recv()
            work(k)
            sums[k] = sum_out(ph, k)
        return sums

    def collect(ph, sums):
        total = sums[0]
        for k in (1, 3, 2):
            sums[k].wait_recv()
        for k in (1, 2, 3):
            total = total + ici_in[ph, k - 1].astype(jnp.float32)
        return total

    def forward(k):
        def one(t, carry):
            cols = pl.ds(pl.multiple_of(t * tile, tile), tile)
            block = seq[pair(k), :]
            gate = dot32(block, wg[cols, :], NT)
            up = dot32(block, wu[cols, :], NT)
            square = gate * gate
            th = jnp.tanh(GELU_C * gate * (1.0 + GELU_A * square))
            half = 0.5 * (1.0 + th)
            gelu = gate * half
            slope = half + (0.5 * GELU_C) * gate * (1.0 - th * th) * (1.0 + 3.0 * GELU_A * square)
            hid[pair(k), cols] = (gelu * up).astype(jnp.bfloat16)
            act_a[pair(k), cols] = up * slope
            act_b[pair(k), cols] = gelu
            return carry

        lax.fori_loop(0, units // tile, one, 0)
        part[...] = dot32(hid[pair(k), :], wd[...], NN)

    seq[mine(0), :] = normed_ref[...]
    sums = phase(seq, 0, forward)
    mlp = collect(0, sums)
    r = lax.rsqrt(jnp.mean(mlp * mlp, axis=-1, keepdims=True) + EPS)
    n = mlp * r
    gain = gain_ref[...]
    out_ref[...] = (mid_ref[...] + n * gain).astype(jnp.bfloat16)
    dy = cot_ref[...].astype(jnp.float32)
    ggain_ref[...] = jnp.sum(dy * n, axis=0, keepdims=True)
    dyg = dy * gain
    dv = r * (dyg - n * jnp.mean(dyg * n, axis=-1, keepdims=True))
    gseq[mine(0), :] = dv.astype(jnp.bfloat16)

    def backward(k):
        def one(t, carry):
            cols = pl.ds(pl.multiple_of(t * tile, tile), tile)
            gh = dot32(gseq[pair(k), :], wd[cols, :], NT)
            dgate[pair(k), cols] = (gh * act_a[pair(k), cols]).astype(jnp.bfloat16)
            dup[pair(k), cols] = (gh * act_b[pair(k), cols]).astype(jnp.bfloat16)
            return carry

        lax.fori_loop(0, units // tile, one, 0)
        part[...] = dot32(dgate[pair(k), :], wg[...], NN) + dot32(dup[pair(k), :], wu[...], NN)

    sums = phase(gseq, 1, backward)
    for i, (left, right) in enumerate(((dgate, seq), (dup, seq), (hid, gseq))):
        def one(t, carry, i=i, left=left, right=right):
            cols = pl.ds(pl.multiple_of(t * tile, tile), tile)
            group = tile // share
            dw[pl.ds(t * group, group), pl.ds(i * share, share), :] = (
                dot32(left[:, cols], right[...], TN).reshape(group, share, -1).astype(jnp.bfloat16)
            )
            return carry

        lax.fori_loop(0, units // tile, one, 0)
    store = pltpu.make_async_copy(dw, gff_hbm, o_sem)
    store.start()
    gn_ref[...] = collect(1, sums)
    for copy in started:
        copy.wait_send()
    store.wait()


def ffn(normed_two, mid, cot, gain, weights):
    rows = normed_two.shape[0]
    owners, lines = weights.shape[:2]
    units = owners * lines // 3
    seq_rows = rows * 8
    bf, f32 = jnp.bfloat16, jnp.float32
    vm = pl.BlockSpec(memory_space=pltpu.VMEM)
    hbm = pl.BlockSpec(memory_space=pl.ANY)
    dma = pltpu.SemaphoreType.DMA
    return pl.pallas_call(
        ffn_kernel,
        out_shape=(
            jax.ShapeDtypeStruct((rows, D), bf),
            jax.ShapeDtypeStruct((rows, D), f32),
            jax.ShapeDtypeStruct((1, D), f32),
            jax.ShapeDtypeStruct(weights.shape, bf),
        ),
        in_specs=[vm] * 4 + [hbm],
        out_specs=(vm, vm, vm, hbm),
        scratch_shapes=[
            pltpu.VMEM((units, D), bf),
            pltpu.VMEM((units, D), bf),
            pltpu.VMEM((units, D), bf),
            pltpu.VMEM((seq_rows, D), bf),
            pltpu.VMEM((seq_rows, D), bf),
            pltpu.VMEM((seq_rows, units), f32),
            pltpu.VMEM((seq_rows, units), f32),
            pltpu.VMEM((seq_rows, units), bf),
            pltpu.VMEM((seq_rows, units), bf),
            pltpu.VMEM((seq_rows, units), bf),
            pltpu.VMEM((2 * rows, D), f32),
            pltpu.VMEM((2, 4, rows, D), bf),
            pltpu.VMEM((2, 4, rows, D), bf),
            pltpu.VMEM((2, 3, rows, D), bf),
            pltpu.VMEM((2, 3, rows, D), bf),
            pltpu.VMEM(weights.shape, bf),
            dma((3, owners)), dma,
            dma((2, 8)), dma((2, 8)),
            dma((2, 4)), dma((2, 4)),
            dma((2, 4)), dma((2, 4)),
        ],
        compiler_params=pltpu.CompilerParams(
            collective_id=1, has_side_effects=True, vmem_limit_bytes=58 * 1024 * 1024
        ),
        cost_estimate=pl.CostEstimate(
            flops=18 * seq_rows * units * D, bytes_accessed=14 * units * D, transcendentals=0
        ),
    )(normed_two, mid, cot, gain, weights)


def place():
    fsdp = lax.axis_index("fsdp")
    ctx = lax.axis_index("ctx")
    y, z = fsdp // 4, lax.rem(fsdp, 4)
    chip, core = ctx // 2, lax.rem(ctx, 2)
    return y, z, chip, core


def shape_of(y, z, core):
    first = (1 - core) * y + core * z
    second = (1 - core) * z + core * y

    def block(i, j):
        return (1 - core) * (4 * i + j) + core * (4 * j + i)

    return first, second, block


def remote(src, dst, s_sem, r_sem, peer):
    return pltpu.make_async_remote_copy(
        src_ref=src, dst_ref=dst, send_sem=s_sem, recv_sem=r_sem,
        device_id=peer, device_id_type=MESH,
    )


def greet(peers):
    barrier = pltpu.get_barrier_semaphore()
    for peer in peers:
        pl.semaphore_signal(barrier, inc=1, device_id=peer, device_id_type=MESH)
    pl.semaphore_wait(barrier, len(peers))


def gather_kernel(
    qkv_ref, wo_ref, qkv_out, wo_all, rows_out, qkv_all,
    l_sem, s1, r1, s2, r2, sd, rd,
):
    y, z, chip, core = place()
    a, b, block = shape_of(y, z, core)
    _, _, block_there = shape_of(y, z, 1 - core)
    q_rows, width = qkv_ref.shape
    o_rows = wo_ref.shape[0]
    q_half, o_half = width // 2, o_rows // 2
    partner = {"ctx": chip * 2 + 1 - core}

    def views(f, half):
        return (
            qkv_all.at[
                pl.ds(pl.multiple_of(f * q_rows, 16), q_rows),
                pl.ds(pl.multiple_of(half * q_half, 128), q_half),
            ],
            wo_all.at[pl.ds(pl.multiple_of(f * o_rows + half * o_half, 16), o_half), :],
        )

    mine = (
        qkv_ref.at[:, pl.ds(pl.multiple_of(core * q_half, 128), q_half)],
        wo_ref.at[pl.ds(pl.multiple_of(core * o_half, 16), o_half), :],
    )
    here = block(a, b)
    locals_ = [
        pltpu.make_async_copy(
            qkv_ref, qkv_all.at[pl.ds(pl.multiple_of(here * q_rows, 16), q_rows), :], l_sem.at[0]
        ),
        pltpu.make_async_copy(
            wo_ref, wo_all.at[pl.ds(pl.multiple_of(here * o_rows, 16), o_rows), :], l_sem.at[1]
        ),
    ]
    for copy in locals_:
        copy.start()

    def first_peer(k):
        return {"fsdp": block(lax.rem(a + k, 4), b)}

    def second_peer(k):
        return {"fsdp": block(a, lax.rem(b + k, 4))}

    greet([first_peer(k) for k in (1, 2, 3)] + [second_peer(k) for k in (1, 2, 3)] + [partner])

    def hop_one(k, t):
        return remote(mine[t], views(here, core)[t], s1.at[k, t], r1.at[4 - k, t], first_peer(k))

    def hop_two(j, k, t):
        f = block(lax.rem(a + j, 4), b)
        dst = views(f, core)[t]
        src = dst if j else mine[t]
        return remote(src, dst, s2.at[j, k, t], r2.at[j, 4 - k, t], second_peer(k))

    def arrive_one(j, t):
        dst = views(block(lax.rem(a + j, 4), b), core)[t]
        return remote(dst, dst, s1.at[j, t], r1.at[j, t], partner)

    def arrive_two(j, m, t):
        dst = views(block(lax.rem(a + j, 4), lax.rem(b + m, 4)), core)[t]
        return remote(dst, dst, s2.at[j, m, t], r2.at[j, m, t], partner)

    def cross(j, m, t):
        dst = views(block(lax.rem(a + j, 4), lax.rem(b + m, 4)), core)[t]
        return remote(dst, dst, sd.at[j, m, t], rd.at[j, m, t], partner)

    def arrive_cross(j, m, t):
        dst = views(block_there(lax.rem(b + j, 4), lax.rem(a + m, 4)), 1 - core)[t]
        return remote(dst, dst, sd.at[j, m, t], rd.at[j, m, t], partner)

    both = (0, 1)
    for k in (1, 3, 2):
        for t in both:
            hop_one(k, t).start()
    for k in (1, 3, 2):
        for t in both:
            hop_two(0, k, t).start()
    for j in (1, 3, 2):
        for t in both:
            arrive_one(j, t).wait_recv()
            for k in (1, 3, 2):
                hop_two(j, k, t).start()
            cross(j, 0, t).start()

    def pass_on(i, carry):
        m, j = i // 4 + 1, lax.rem(i, 4)
        for t in both:
            arrive_two(j, m, t).wait_recv()
            cross(j, m, t).start()
        return carry

    lax.fori_loop(0, 12, pass_on, 0)

    def land(i, carry):
        m, j = i // 4, lax.rem(i, 4)
        for t in both:
            arrive_cross(j, m, t).wait_recv()
            cross(j, m, t).wait_send()
        return carry

    lax.fori_loop(1, 16, land, 0)
    for copy in locals_:
        copy.wait()
    for k in (1, 2, 3):
        for t in both:
            hop_one(k, t).wait_send()
            for j in range(4):
                hop_two(j, k, t).wait_send()

    keep = qkv_out.shape[0] // 16
    for f in range(0, 16, 2):
        left = qkv_all[pl.ds(f * q_rows, q_rows), :].astype(jnp.float32)
        right = qkv_all[pl.ds((f + 1) * q_rows, q_rows), :].astype(jnp.float32)
        qkv_out[pl.ds(f * keep, 2 * keep), :] = jnp.concatenate(
            [left[:keep], right[:keep]], axis=0
        ).astype(jnp.bfloat16)
        rows_out[f] = left[keep:, : rows_out.shape[2]]
        rows_out[f + 1] = right[keep:, : rows_out.shape[2]]


def gather_attention(qkv_shard, wo_shard, keep, extra):
    bf = jnp.bfloat16
    vm = pl.BlockSpec(memory_space=pltpu.VMEM)
    dma = pltpu.SemaphoreType.DMA
    q_rows, width = qkv_shard.shape
    o_rows, o_width = wo_shard.shape
    return pl.pallas_call(
        gather_kernel,
        out_shape=(
            jax.ShapeDtypeStruct((16 * keep, width), bf),
            jax.ShapeDtypeStruct((16 * o_rows, o_width), bf),
            jax.ShapeDtypeStruct((16, q_rows - keep, extra), jnp.float32),
        ),
        in_specs=[vm] * 2,
        out_specs=(vm,) * 3,
        scratch_shapes=[
            pltpu.VMEM((16 * q_rows, width), bf),
            dma((2,)),
            dma((4, 2)), dma((4, 2)),
            dma((4, 4, 2)), dma((4, 4, 2)),
            dma((4, 4, 2)), dma((4, 4, 2)),
        ],
        compiler_params=pltpu.CompilerParams(
            collective_id=2, has_side_effects=True, vmem_limit_bytes=40 * 1024 * 1024
        ),
        cost_estimate=pl.CostEstimate(
            flops=0, bytes_accessed=64 * (q_rows * width + o_rows * o_width), transcendentals=0
        ),
    )(qkv_shard, wo_shard)


def rms_back(values, grad, gain):
    r = lax.rsqrt(jnp.mean(values * values, axis=-1, keepdims=True) + EPS)
    n = values * r
    dyg = grad * gain
    return (
        r * (dyg - n * jnp.mean(dyg * n, axis=-1, keepdims=True)),
        jnp.sum(grad * n, axis=0, keepdims=True),
    )


def stack_heads(values):
    return jnp.concatenate([values[:, h * HD : (h + 1) * HD] for h in range(NH)], axis=0)


def turn_back(grad, cos_table, sin_table):
    left, right = grad[:, : HD // 2], grad[:, HD // 2 :]
    return jnp.concatenate(
        [left * cos_table + right * sin_table, right * cos_table - left * sin_table], axis=1
    )


def back_kernel(
    gff, gn_ref, mid_ref, attn_ref, cot_ref, tok_ref, gains_ref, qk_ref, proj_ref, q_ref,
    pair_ref, att_ref, normed_ref, qkv_ref, wo_ref, cos_ref, sin_ref, bias_ref, g3_ref,
    gt_ref, oq_ref, oo_ref, og_ref, ou_ref, od_ref,
    own_ff, in1_ff, t_ff, in2_ff, all_ff, kv_snd, kv_in, gmid, gpair, gproj, tail,
    stage, go, dq, do, sq, so, iq1, io1, tq, to, iq2, io2, xq, xo,
    l_sem, s1f, r1f, s2f, r2f, sag, rag, skv, rkv,
    sd, rd, s1, r1, s2, r2, sx, rx, sf, rf,
):
    y, z, chip, core = place()
    a, b, block = shape_of(y, z, core)
    _, _, block_there = shape_of(y, z, 1 - core)
    me = chip * 2 + core
    rows = gn_ref.shape[0]
    q_rows, width = oq_ref.shape
    keep = normed_ref.shape[1] // 16
    o_rows = oo_ref.shape[0]
    q_half, o_half = width // 2, o_rows // 2
    chips = xq.shape[0]
    members = 2 * chips
    reach = kv_in.shape[0]
    scale = HD ** (-0.5)
    f32, bf = jnp.float32, jnp.bfloat16
    partner = {"ctx": chip * 2 + 1 - core}

    def first_peer(k):
        return {"fsdp": block(lax.rem(a + k, 4), b)}

    def second_peer(k):
        return {"fsdp": block(a, lax.rem(b + k, 4))}

    def chip_peer(k):
        return {"ctx": lax.rem(chip + k, chips) * 2 + core}

    def member(k):
        return {"ctx": lax.rem(me + k, members)}

    def q_cols(half):
        return pl.ds(pl.multiple_of(half * q_half, 128), q_half)

    def o_lines(half):
        return pl.ds(pl.multiple_of(half * o_half, 16), o_half)

    own_loads = [
        pltpu.make_async_copy(gff.at[block(a, j)], own_ff.at[j], l_sem.at[j]) for j in range(4)
    ]
    for copy in own_loads:
        copy.start()
    greet(
        [first_peer(k) for k in (1, 2, 3)]
        + [second_peer(k) for k in (1, 2, 3)]
        + [member(k) for k in range(1, members)]
    )

    def ff_one(k, j):
        return remote(
            gff.at[block(lax.rem(a + k, 4), j)], in1_ff.at[3 - k, j],
            s1f.at[k, j], r1f.at[4 - k, j], first_peer(k),
        )

    for i in (2, 1, 3, 0):
        for k in (1, 3, 2):
            ff_one(k, lax.rem(b + i, 4)).start()

    grad_final = cot_ref[...].astype(f32)
    part, gain_two = rms_back(mid_ref[...], gn_ref[...], gains_ref[2:3, :])
    grad_mid = grad_final + part
    gmid[...] = grad_mid
    grad_attn, gain_one = rms_back(attn_ref[...], grad_mid, gains_ref[1:2, :])
    grad_attn_low = grad_attn.astype(bf)
    grad_attended = dot32(grad_attn_low, wo_ref[...], NT).astype(bf)

    def out_tile(t, carry):
        cols = pl.ds(pl.multiple_of(t * 256, 256), 256)
        go[pl.ds(t * 4, 4)] = (
            dot32(att_ref[:, cols], grad_attn_low, TN).reshape(4, 64, D).astype(bf)
        )
        return carry

    lax.fori_loop(0, NH * HD // 256, out_tile, 0)

    def away(i, t):
        k, j = lax.rem(i // 4 + 1, 4), lax.rem(i, 4)
        line = lax.rem(b + k, 4)
        f = block_there(line, j)
        slot = line * 4 + j
        if t == 0:
            src, dst = stage.at[f, :, q_cols(1 - core)], dq.at[slot]
        else:
            src, dst = go.at[f, o_lines(1 - core), :], do.at[slot]
        return remote(src, dst, sd.at[i, t], rd.at[i, t], partner)

    def home(i, t):
        k, j = lax.rem(i // 4 + 1, 4), lax.rem(i, 4)
        slot = lax.rem(a + k, 4) * 4 + j
        dst = (dq, do)[t].at[slot]
        return remote(dst, dst, sd.at[i, t], rd.at[i, t], partner)

    def start_away(t):
        def one(i, carry):
            away(i, t).start()
            return carry

        lax.fori_loop(0, 16, one, 0)

    start_away(1)

    keys, vals = pair_ref[:, :HD], pair_ref[:, HD:]
    queries = stack_heads(q_ref[...])
    grad_heads = stack_heads(grad_attended)
    scores = dot32(queries, keys, NT) * scale + jnp.concatenate([bias_ref[...]] * NH, axis=0)
    expo = jnp.exp(scores - jnp.max(scores, axis=-1, keepdims=True))
    probs = expo / jnp.sum(expo, axis=-1, keepdims=True)
    grad_probs = dot32(grad_heads, vals, NT)
    row_total = jnp.sum(probs * grad_probs, axis=-1, keepdims=True)
    grad_scores = (probs * (grad_probs - row_total)).astype(bf)
    gpair[:, HD:] = dot32(probs.astype(bf), grad_heads, TN)
    gpair[:, :HD] = dot32(grad_scores, queries, TN) * scale

    def kv_send(d):
        return remote(
            kv_snd.at[d - 1], kv_in.at[d - 1], skv.at[d - 1], rkv.at[d - 1], member(members - d)
        )

    for d in range(1, reach + 1):
        kv_snd[d - 1] = gpair[pl.ds((reach - d) * rows, rows), :].astype(bf)
        kv_send(d).start()

    cos_all = jnp.concatenate([cos_ref[...]] * NH, axis=0)
    sin_all = jnp.concatenate([sin_ref[...]] * NH, axis=0)
    grad_queries = dot32(grad_scores, keys, NN) * scale
    grad_q, qk_gain_q = rms_back(
        stack_heads(proj_ref[:, : NH * HD]),
        turn_back(grad_queries, cos_all, sin_all),
        qk_ref[0:1, :],
    )
    for h in range(NH):
        gproj[:, h * HD : (h + 1) * HD] = grad_q[h * rows : (h + 1) * rows].astype(bf)

    def hop_one(k, t):
        src, dst = ((sq, iq1), (so, io1))[t]
        line = pl.ds(lax.rem(a + k, 4) * 4, 4)
        return remote(
            src.at[line], dst.at[3 - k], s1.at[k, t], r1.at[4 - k, t], first_peer(k)
        )

    def fold_cores(t):
        for k in (1, 2, 3, 0):
            def add(j, carry, k=k):
                line = lax.rem(a + k, 4)
                slot = line * 4 + j
                f = block(line, j)
                home((k + 3) % 4 * 4 + j, t).wait_recv()
                if t == 0:
                    sq[slot] = (
                        stage[f, :, q_cols(core)].astype(f32) + dq[slot].astype(f32)
                    ).astype(bf)
                else:
                    so[slot] = (
                        go[f, o_lines(core), :].astype(f32) + do[slot].astype(f32)
                    ).astype(bf)
                return carry

            lax.fori_loop(0, 4, add, 0)
            if k:
                hop_one(k, t).start()

    fold_cores(1)

    total = gpair[pl.ds(reach * rows, rows), :]
    for d in range(1, reach + 1):
        kv_send(d).wait_recv()
        total = total + kv_in[d - 1].astype(f32)
    grad_k, qk_gain_k = rms_back(
        proj_ref[:, NH * HD : NH * HD + HD],
        turn_back(total[:, :HD], cos_ref[...], sin_ref[...]),
        qk_ref[1:2, :],
    )
    gproj[:, NH * HD : NH * HD + HD] = grad_k.astype(bf)
    gproj[:, NH * HD + HD :] = total[:, HD:].astype(bf)
    stream = tok_ref[...].astype(f32)
    grad_in, gain_zero = rms_back(stream, dot32(gproj[...], qkv_ref[...], NT), gains_ref[0:1, :])
    gt_ref[...] = gmid[...] + grad_in
    tail[...] = jnp.zeros_like(tail)
    for i, line in enumerate((gain_zero, gain_one, gain_two, g3_ref[...])):
        tail[i : i + 1, :D] = line
    tail[4:5, :HD] = qk_gain_q
    tail[5:6, :HD] = qk_gain_k

    def qkv_tile(t, carry):
        cols = pl.ds(pl.multiple_of(t * 256, 256), 256)
        res = dot32(normed_ref[...], gproj[:, cols], TN)
        low = tail[:, cols]
        for f in range(16):
            stage[f, :, cols] = jnp.concatenate(
                [res[f * keep : (f + 1) * keep], low], axis=0
            ).astype(bf)
        return carry

    lax.fori_loop(0, width // 256, qkv_tile, 0)
    start_away(0)
    fold_cores(0)

    for copy in own_loads:
        copy.wait()

    def ff_two(k):
        return remote(
            t_ff.at[lax.rem(b + k, 4)], in2_ff.at[3 - k], s2f.at[k], r2f.at[4 - k], second_peer(k)
        )

    for k in (2, 1, 3, 0):
        j = lax.rem(b + k, 4)
        for m in (1, 2, 3):
            dst = in1_ff.at[m - 1, j]
            remote(dst, dst, s1f.at[m, j], r1f.at[m, j], partner).wait_recv()
        total = own_ff[j].astype(f32)
        for m in range(3):
            total = total + in1_ff[m, j].astype(f32)
        t_ff[j] = total.astype(bf)
        if k:
            ff_two(k).start()

    def hop_two(k, t):
        src, dst = ((tq, iq2), (to, io2))[t]
        return remote(
            src.at[lax.rem(b + k, 4)], dst.at[3 - k], s2.at[k, t], r2.at[4 - k, t], second_peer(k)
        )

    for t in (1, 0):
        own, got, dst = ((sq, iq1, tq), (so, io1, to))[t]
        for k in (1, 3, 2):
            hop_one(4 - k, t).wait_recv()
        for k in (2, 1, 3, 0):
            j = lax.rem(b + k, 4)
            total = own[a * 4 + j].astype(f32)
            for m in range(3):
                total = total + got[m, j].astype(f32)
            dst[j] = total.astype(bf)
            if k:
                hop_two(k, t).start()

    for k in (1, 3, 2):
        ff_two(4 - k).wait_recv()
    total = t_ff[b].astype(f32)
    for m in range(3):
        total = total + in2_ff[m].astype(f32)
    all_ff[me] = total.astype(bf)

    def ff_all(k):
        peer = chip_peer(k) if k else partner
        return remote(
            all_ff.at[me], all_ff.at[me], sag.at[k], rag.at[(chips - k) % chips], peer
        )

    def ff_from(k):
        dst = all_ff.at[lax.rem(chip + k, chips) * 2 + core]
        return remote(dst, dst, sag.at[chips + k], rag.at[k], partner)

    def ff_cross(k):
        dst = all_ff.at[lax.rem(chip + k, chips) * 2 + core]
        return remote(dst, dst, sag.at[chips + k], rag.at[chips + k], partner)

    def ff_crossed(k):
        dst = all_ff.at[lax.rem(chip + k, chips) * 2 + 1 - core]
        return remote(dst, dst, sag.at[k], rag.at[chips + k if k else 0], partner)

    for k in (*range(1, chips), 0):
        ff_all(k).start()

    def hop_chip(k, t):
        buf = (xq, xo)[t]
        return remote(
            buf.at[chip], buf.at[chip], sx.at[k, t], rx.at[chips - k, t], chip_peer(k)
        )

    for t in (1, 0):
        own, got, dst = ((tq, iq2, xq), (to, io2, xo))[t]
        for k in (1, 3, 2):
            hop_two(4 - k, t).wait_recv()
        total = own[b].astype(f32)
        for m in range(3):
            total = total + got[m].astype(f32)
        dst[chip] = total.astype(bf)
        for k in range(1, chips):
            hop_chip(k, t).start()

    def last(t, half):
        part = (oq_ref.at[:, q_cols(half)], oo_ref.at[o_lines(half), :])[t]
        return remote(part, part, sf.at[t], rf.at[t], partner)

    for k in range(1, chips):
        ff_from(k).wait_recv()
        ff_cross(k).start()

    for t in (1, 0):
        buf = (xq, xo)[t]
        for k in range(1, chips):
            dst = buf.at[lax.rem(chip + k, chips)]
            remote(dst, dst, sx.at[k, t], rx.at[k, t], partner).wait_recv()
        total = buf[0].astype(f32)
        for m in range(1, chips):
            total = total + buf[m].astype(f32)
        if t == 0:
            oq_ref[:, q_cols(core)] = total
        else:
            oo_ref[o_lines(core), :] = total
        last(t, core).start()

    for k in range(chips):
        ff_crossed(k).wait_recv()
    lines = og_ref.shape[0] // members
    share = all_ff.shape[1] // 3
    for i, dst in enumerate((og_ref, ou_ref, od_ref)):
        for m in range(members):
            dst[m * lines : (m + 1) * lines, :] = all_ff[
                m, i * share : (i + 1) * share, :
            ].astype(f32)[:lines]

    def end_away(i, carry):
        for t in (0, 1):
            away(i, t).wait_send()
        return carry

    lax.fori_loop(0, 16, end_away, 0)
    for k in (1, 2, 3):
        for j in range(4):
            ff_one(k, j).wait_send()
        ff_two(k).wait_send()
    for d in range(1, reach + 1):
        kv_send(d).wait_send()
    for k in range(chips):
        ff_all(k).wait_send()
        if k:
            ff_cross(k).wait_send()
    for t in (0, 1):
        for k in (1, 2, 3):
            hop_one(k, t).wait_send()
            hop_two(k, t).wait_send()
        for k in range(1, chips):
            hop_chip(k, t).wait_send()
        last(t, core).wait_send()
        last(t, 1 - core).wait_recv()


def backward_rest(gff, values, keep, lines):
    f32, bf = jnp.float32, jnp.bfloat16
    vm = pl.BlockSpec(memory_space=pltpu.VMEM)
    hbm = pl.BlockSpec(memory_space=pl.ANY)
    dma = pltpu.SemaphoreType.DMA
    rows = values[0].shape[0]
    owners, ff_rows = gff.shape[:2]
    q_rows, width = keep + 8, (NH + 2) * HD
    o_rows, o_width = NH * HD // owners, D
    q_half, o_half = width // 2, o_rows // 2
    chips = lax.axis_size("ctx") // 2
    pairs = values[9].shape[0]
    reach = pairs // rows - 1

    def two(*lead):
        return [pltpu.VMEM(lead + (q_rows, q_half), bf), pltpu.VMEM(lead + (o_half, o_width), bf)]

    def ff(*lead):
        return pltpu.VMEM(lead + (ff_rows, D), bf)

    weight = jax.ShapeDtypeStruct((lines, D), f32)
    return pl.pallas_call(
        back_kernel,
        out_shape=(
            jax.ShapeDtypeStruct((rows, D), f32),
            jax.ShapeDtypeStruct((q_rows, width), f32),
            jax.ShapeDtypeStruct((o_rows, o_width), f32),
            weight, weight, weight,
        ),
        in_specs=[hbm] + [vm] * len(values),
        out_specs=(vm,) * 6,
        scratch_shapes=[
            ff(4), ff(3, 4), ff(4), ff(3), ff(2 * chips),
            pltpu.VMEM((reach, rows, 2 * HD), bf),
            pltpu.VMEM((reach, rows, 2 * HD), bf),
            pltpu.VMEM((rows, D), f32),
            pltpu.VMEM((pairs, 2 * HD), f32),
            pltpu.VMEM((rows, width), bf),
            pltpu.VMEM((8, width), f32),
            pltpu.VMEM((16, q_rows, width), bf),
            pltpu.VMEM((16, o_rows, o_width), bf),
            *two(16), *two(16), *two(3, 4), *two(4), *two(3), *two(chips),
            dma((4,)),
            dma((4, 4)), dma((4, 4)),
            dma((4,)), dma((4,)),
            dma((2 * chips,)), dma((2 * chips,)),
            dma((reach,)), dma((reach,)),
            dma((16, 2)), dma((16, 2)),
            dma((4, 2)), dma((4, 2)),
            dma((4, 2)), dma((4, 2)),
            dma((4, 2)), dma((4, 2)),
            dma((2,)), dma((2,)),
        ],
        compiler_params=pltpu.CompilerParams(
            collective_id=3, has_side_effects=True, vmem_limit_bytes=62 * 1024 * 1024
        ),
        cost_estimate=pl.CostEstimate(
            flops=12 * rows * width * D, bytes_accessed=64 * ff_rows * D, transcendentals=0
        ),
    )(gff, *values)


def on_device(
    tokens,
    norm_gains,
    qk_gains,
    qkv_weight,
    out_weight,
    gate_weight,
    up_weight,
    down_weight,
    segments,
    cotangent,
):
    local_len = tokens.shape[1]
    scale = HD ** (-0.5)
    ctx_index = lax.axis_index("ctx")
    ctx_size = lax.axis_size("ctx")
    own_rows = gate_weight.shape[0]
    slice_rows = own_rows // ctx_size
    padded = -(-slice_rows // 16) * 16
    n_gain, n_qk = norm_gains.size, qk_gains.size
    extra = -(-n_gain // 128) * 128
    gain_rows = jnp.zeros((8, qkv_weight.shape[1]), jnp.bfloat16)
    gain_rows = gain_rows.at[0, :n_gain].set(norm_gains.reshape(-1))
    gain_rows = gain_rows.at[1, :n_qk].set(qk_gains.reshape(-1))
    qkv_full, out_full, gain_got = gather_attention(
        jnp.concatenate([qkv_weight, gain_rows], axis=0), out_weight, qkv_weight.shape[0], extra
    )
    gains_all = (
        gain_got[:, 0, :n_gain]
        .reshape(-1, 4, norm_gains.shape[1])
        .transpose(1, 0, 2)
        .reshape(4, D)
    )
    qk_all = (
        gain_got[:, 1, :n_qk]
        .reshape(-1, 2, qk_gains.shape[1])
        .transpose(1, 0, 2)
        .reshape(2, HD)
    )
    seg_all = lax.all_gather(segments[0], "ctx", axis=0, tiled=True)

    def my_slice(weight):
        part = lax.dynamic_index_in_dim(
            weight.reshape(ctx_size, slice_rows, D), ctx_index, 0, False
        )
        return jnp.pad(part, ((0, padded - slice_rows), (0, 0)))

    ffn_shard = jnp.concatenate(
        [my_slice(gate_weight), my_slice(up_weight), my_slice(down_weight)], axis=0
    )
    ffn_full = lax.all_gather(ffn_shard, "fsdp")

    offset = ctx_index * local_len
    positions = offset + jnp.arange(local_len, dtype=jnp.int32)
    cos_table, sin_table = rope_tables(positions)
    stream = tokens.astype(jnp.float32).reshape(local_len, D)
    flat_normed = rms_norm(stream, gains_all[0]).astype(jnp.bfloat16)
    projected = jnp.dot(flat_normed, qkv_full, preferred_element_type=jnp.float32)
    q_raw = projected[:, : NH * HD].reshape(local_len, NH, HD)
    k_raw = projected[:, NH * HD : NH * HD + HD]
    values = projected[:, NH * HD + HD :].astype(jnp.bfloat16)
    prep_fixed = partial(head_prep, cos_table=cos_table, sin_table=sin_table)
    q_rot, k_rot = prep_fixed(q_raw, k_raw, qk_all[0], qk_all[1])
    queries = q_rot.astype(jnp.bfloat16)
    own_pair = jnp.concatenate([k_rot.astype(jnp.bfloat16), values], axis=-1)
    reach = min(-(-(WINDOW - 1) // local_len), ctx_size - 1)
    pieces = [own_pair]
    for distance in range(1, reach + 1):
        pieces.insert(0, from_behind(own_pair, "ctx", distance))
    pair_all = jnp.concatenate(pieces, axis=0)
    key_all = pair_all[:, :HD]
    value_all = pair_all[:, HD:]
    key_index = offset - reach * local_len + jnp.arange((reach + 1) * local_len, dtype=jnp.int32)
    seg_padded = jnp.concatenate([jnp.full((reach * local_len,), -1, jnp.int32), seg_all])
    key_seg = lax.dynamic_slice_in_dim(seg_padded, offset, (reach + 1) * local_len, 0)
    spacing = positions[:, None] - key_index[None, :]
    allowed = (
        (spacing >= 0) & (spacing < WINDOW) & (segments[0][:, None] == key_seg[None, :])
    )
    raw_scores = (
        jnp.einsum("qhd,kd->hqk", queries, key_all, preferred_element_type=jnp.float32) * scale
    )
    scores = jnp.where(allowed[None], raw_scores, NEG_FILL)
    top_score = jnp.max(scores, axis=-1, keepdims=True)
    expo = jnp.exp(scores - top_score)
    probs = expo / jnp.sum(expo, axis=-1, keepdims=True)
    probs_low = probs.astype(jnp.bfloat16)
    attended = (
        jnp.einsum("hqk,kd->qhd", probs_low, value_all, preferred_element_type=jnp.float32)
        .astype(jnp.bfloat16)
        .reshape(local_len, NH * HD)
    )
    attn = jnp.dot(attended, out_full, preferred_element_type=jnp.float32)
    mid_stream = stream + rms_norm(attn, gains_all[1])
    normed_two = rms_norm(mid_stream, gains_all[2]).astype(jnp.bfloat16)

    cot = cotangent.reshape(local_len, D)
    output, grad_normed_two, grad_gain_three, ffn_grads = ffn(
        normed_two, mid_stream, cot, gains_all[3:4], ffn_full
    )
    bias = jnp.where(allowed, 0.0, NEG_FILL)
    keep = qkv_weight.shape[0]
    grad_tokens, own_qkv, total_out, total_gate, total_up, total_down = backward_rest(
        ffn_grads,
        (
            grad_normed_two, mid_stream, attn, cot, tokens.reshape(local_len, D), gains_all,
            qk_all, projected, queries.reshape(local_len, NH * HD), pair_all, attended,
            flat_normed, qkv_full, out_full, cos_table, sin_table, bias, grad_gain_three,
        ),
        keep,
        own_rows,
    )
    owner = lax.axis_index("fsdp")
    gain_lines, qk_lines = norm_gains.shape, qk_gains.shape
    total_gains = lax.dynamic_slice(
        own_qkv[keep : keep + 4, :D], (0, owner * gain_lines[1]), gain_lines
    )
    total_qk = lax.dynamic_slice(
        own_qkv[keep + 4 : keep + 6, :HD], (0, owner * qk_lines[1]), qk_lines
    )
    return (
        output.reshape(tokens.shape),
        grad_tokens.reshape(tokens.shape),
        total_gains,
        total_qk,
        own_qkv[:keep],
        total_out,
        total_gate,
        total_up,
        total_down,
    )


def solution(mesh):
    in_specs = (
        P("fsdp", "ctx", None),
        P(None, "fsdp"),
        P(None, "fsdp"),
        P("fsdp", None),
        P("fsdp", None),
        P("fsdp", None),
        P("fsdp", None),
        P("fsdp", None),
        P("fsdp", "ctx"),
        P("fsdp", "ctx", None),
    )
    out_specs = (
        P("fsdp", "ctx", None),
        P("fsdp", "ctx", None),
        P(None, "fsdp"),
        P(None, "fsdp"),
        P("fsdp", None),
        P("fsdp", None),
        P("fsdp", None),
        P("fsdp", None),
        P("fsdp", None),
    )
    return jax.shard_map(
        on_device, mesh=mesh, in_specs=in_specs, out_specs=out_specs, check_vma=False
    )
```

```python
import jax
import numpy as np
import jax.numpy as jnp
from jax import lax
from jax.experimental import pallas as pl
from jax.experimental.pallas import tpu as pltpu
from jax.sharding import PartitionSpec as P

D = 1152
NH = 4
HD = 256
WINDOW = 512


EPS = 1e-06
ROPE_BASE = 10000.0
NEG_FILL = -1e30


def rms_norm(values, gain_vec):
    return values * lax.rsqrt(jnp.mean(values * values, axis=-1, keepdims=True) + EPS) * gain_vec


MESH = pl.DeviceIdType.MESH
NT = (((1,), (1,)), ((), ()))
NN = (((1,), (0,)), ((), ()))
TN = (((0,), (0,)), ((), ()))
GELU_C = 0.7978845608028654
GELU_A = 0.044715


def dot32(left, right, dims):
    return lax.dot_general(left, right, dims, preferred_element_type=jnp.float32)


def ffn_kernel(
    normed_ref, mid_ref, cot_ref, gain_ref, w_hbm,
    out_ref, gn_ref, ggain_ref, gff_hbm,
    wg, wu, wd, seq, gseq, act_a, act_b, hid, dgate, dup, part,
    d2d_snd, d2d_in, ici_snd, ici_in, dw,
    w_sem, o_sem, ag_s, ag_r, rd_s, rd_r, ri_s, ri_r,
):
    rows = normed_ref.shape[0]
    units = wg.shape[0]
    share = units // w_hbm.shape[0]
    tile = 256
    me = lax.axis_index("ctx")
    chip, core = me // 2, lax.rem(me, 2)
    partner = {"ctx": chip * 2 + 1 - core}
    chips = {k: {"ctx": lax.rem(chip + k, 4) * 2 + core} for k in (1, 2, 3)}
    order = (0, 1, 3, 2)

    loads = [
        pltpu.make_async_copy(
            w_hbm.at[f, pl.ds(i * share, share), :], dst.at[pl.ds(f * share, share), :], w_sem.at[i, f]
        )
        for i, dst in enumerate((wg, wu, wd))
        for f in range(w_hbm.shape[0])
    ]
    for load in loads:
        load.start()

    barrier = pltpu.get_barrier_semaphore()
    for peer in (partner, chips[1], chips[2], chips[3]):
        pl.semaphore_signal(barrier, inc=1, device_id=peer, device_id_type=MESH)
    pl.semaphore_wait(barrier, 4)

    started = []

    def send(src, dst, s_sem, r_sem, peer):
        copy = pltpu.make_async_remote_copy(
            src_ref=src, dst_ref=dst, send_sem=s_sem, recv_sem=r_sem,
            device_id=peer, device_id_type=MESH,
        )
        copy.start()
        started.append(copy)
        return copy

    def mine(k):
        return pl.ds(k * 2 * rows, rows)

    def other(k):
        return pl.ds(k * 2 * rows + rows, rows)

    def pair(k):
        return pl.ds(k * 2 * rows, 2 * rows)

    def spread(buf, ph):
        own = buf.at[mine(0)]
        got = {}
        for k in (1, 3, 2):
            back = 4 - k
            got[back] = send(own, buf.at[mine(back)], ag_s.at[ph, k], ag_r.at[ph, back], chips[k])
        got[0] = send(own, buf.at[other(0)], ag_s.at[ph, 0], ag_r.at[ph, 0], partner)
        return got

    def relay(buf, ph, got, k):
        got[k].wait_recv()
        got[k] = send(
            buf.at[mine(k)], buf.at[other(k)], ag_s.at[ph, 4 + k], ag_r.at[ph, 4 + k], partner
        )

    def sum_out(ph, k):
        d2d_snd[ph, k] = part[pl.ds(rows, rows), :].astype(jnp.bfloat16)
        copy = send(
            d2d_snd.at[ph, k], d2d_in.at[ph, k], rd_s.at[ph, k], rd_r.at[ph, k], partner
        )
        copy.wait_recv()
        total = part[pl.ds(0, rows), :] + d2d_in[ph, k].astype(jnp.float32)
        if k == 0:
            return total
        ici_snd[ph, k - 1] = total.astype(jnp.bfloat16)
        back = 4 - k
        return send(
            ici_snd.at[ph, k - 1], ici_in.at[ph, back - 1], ri_s.at[ph, k], ri_r.at[ph, back],
            chips[k],
        )

    def phase(buf, ph, work):
        got = spread(buf, ph)
        if ph == 0:
            for load in loads:
                load.wait()
        sums = {}
        for k in order:
            if k == 1:
                relay(buf, ph, got, 1)
                relay(buf, ph, got, 3)
            if k == 2:
                relay(buf, ph, got, 2)
            got[k].wait_recv()
            work(k)
            sums[k] = sum_out(ph, k)
        return sums

    def collect(ph, sums):
        total = sums[0]
        for k in (1, 3, 2):
            sums[k].wait_recv()
        for k in (1, 2, 3):
            total = total + ici_in[ph, k - 1].astype(jnp.float32)
        return total

    def forward(k):
        def one(t, carry):
            cols = pl.ds(pl.multiple_of(t * tile, tile), tile)
            block = seq[pair(k), :]
            gate = dot32(block, wg[cols, :], NT)
            up = dot32(block, wu[cols, :], NT)
            square = gate * gate
            th = jnp.tanh(GELU_C * gate * (1.0 + GELU_A * square))
            half = 0.5 * (1.0 + th)
            gelu = gate * half
            slope = half + (0.5 * GELU_C) * gate * (1.0 - th * th) * (1.0 + 3.0 * GELU_A * square)
            hid[pair(k), cols] = (gelu * up).astype(jnp.bfloat16)
            act_a[pair(k), cols] = up * slope
            act_b[pair(k), cols] = gelu
            return carry

        lax.fori_loop(0, units // tile, one, 0)
        part[...] = dot32(hid[pair(k), :], wd[...], NN)

    seq[mine(0), :] = normed_ref[...]
    sums = phase(seq, 0, forward)
    mlp = collect(0, sums)
    r = lax.rsqrt(jnp.mean(mlp * mlp, axis=-1, keepdims=True) + EPS)
    n = mlp * r
    gain = gain_ref[3:4, :]
    out_ref[...] = (mid_ref[...] + n * gain).astype(jnp.bfloat16)
    dy = cot_ref[...].astype(jnp.float32)
    ggain_ref[...] = jnp.sum(dy * n, axis=0, keepdims=True)
    dyg = dy * gain
    dv = r * (dyg - n * jnp.mean(dyg * n, axis=-1, keepdims=True))
    gseq[mine(0), :] = dv.astype(jnp.bfloat16)

    def backward(k):
        def one(t, carry):
            cols = pl.ds(pl.multiple_of(t * tile, tile), tile)
            gh = dot32(gseq[pair(k), :], wd[cols, :], NT)
            dgate[pair(k), cols] = (gh * act_a[pair(k), cols]).astype(jnp.bfloat16)
            dup[pair(k), cols] = (gh * act_b[pair(k), cols]).astype(jnp.bfloat16)
            return carry

        lax.fori_loop(0, units // tile, one, 0)
        part[...] = dot32(dgate[pair(k), :], wg[...], NN) + dot32(dup[pair(k), :], wu[...], NN)

    sums = phase(gseq, 1, backward)
    for i, (left, right) in enumerate(((dgate, seq), (dup, seq), (hid, gseq))):
        def one(t, carry, i=i, left=left, right=right):
            cols = pl.ds(pl.multiple_of(t * tile, tile), tile)
            group = tile // share
            dw[pl.ds(t * group, group), pl.ds(i * share, share), :] = (
                dot32(left[:, cols], right[...], TN).reshape(group, share, -1).astype(jnp.bfloat16)
            )
            return carry

        lax.fori_loop(0, units // tile, one, 0)
    store = pltpu.make_async_copy(dw, gff_hbm, o_sem)
    store.start()
    gn_ref[...] = collect(1, sums)
    for copy in started:
        copy.wait_send()
    store.wait()


def ffn(normed_two, mid, cot, gain, weights):
    rows = normed_two.shape[0]
    owners, lines = weights.shape[:2]
    units = owners * lines // 3
    seq_rows = rows * 8
    bf, f32 = jnp.bfloat16, jnp.float32
    vm = pl.BlockSpec(memory_space=pltpu.VMEM)
    hbm = pl.BlockSpec(memory_space=pl.ANY)
    dma = pltpu.SemaphoreType.DMA
    return pl.pallas_call(
        ffn_kernel,
        out_shape=(
            jax.ShapeDtypeStruct((rows, D), bf),
            jax.ShapeDtypeStruct((rows, D), f32),
            jax.ShapeDtypeStruct((1, D), f32),
            jax.ShapeDtypeStruct(weights.shape, bf),
        ),
        in_specs=[vm] * 4 + [hbm],
        out_specs=(vm, vm, vm, hbm),
        scratch_shapes=[
            pltpu.VMEM((units, D), bf),
            pltpu.VMEM((units, D), bf),
            pltpu.VMEM((units, D), bf),
            pltpu.VMEM((seq_rows, D), bf),
            pltpu.VMEM((seq_rows, D), bf),
            pltpu.VMEM((seq_rows, units), f32),
            pltpu.VMEM((seq_rows, units), f32),
            pltpu.VMEM((seq_rows, units), bf),
            pltpu.VMEM((seq_rows, units), bf),
            pltpu.VMEM((seq_rows, units), bf),
            pltpu.VMEM((2 * rows, D), f32),
            pltpu.VMEM((2, 4, rows, D), bf),
            pltpu.VMEM((2, 4, rows, D), bf),
            pltpu.VMEM((2, 3, rows, D), bf),
            pltpu.VMEM((2, 3, rows, D), bf),
            pltpu.VMEM(weights.shape, bf),
            dma((3, owners)), dma,
            dma((2, 8)), dma((2, 8)),
            dma((2, 4)), dma((2, 4)),
            dma((2, 4)), dma((2, 4)),
        ],
        compiler_params=pltpu.CompilerParams(
            collective_id=1, has_side_effects=True, vmem_limit_bytes=58 * 1024 * 1024
        ),
        cost_estimate=pl.CostEstimate(
            flops=18 * seq_rows * units * D, bytes_accessed=14 * units * D, transcendentals=0
        ),
    )(normed_two, mid, cot, gain, weights)


def place():
    fsdp = lax.axis_index("fsdp")
    ctx = lax.axis_index("ctx")
    y, z = fsdp // 4, lax.rem(fsdp, 4)
    chip, core = ctx // 2, lax.rem(ctx, 2)
    return y, z, chip, core


def shape_of(y, z, core):
    first = (1 - core) * y + core * z
    second = (1 - core) * z + core * y

    def block(i, j):
        return (1 - core) * (4 * i + j) + core * (4 * j + i)

    return first, second, block


def remote(src, dst, s_sem, r_sem, peer):
    return pltpu.make_async_remote_copy(
        src_ref=src, dst_ref=dst, send_sem=s_sem, recv_sem=r_sem,
        device_id=peer, device_id_type=MESH,
    )


def greet(peers):
    barrier = pltpu.get_barrier_semaphore()
    for peer in peers:
        pl.semaphore_signal(barrier, inc=1, device_id=peer, device_id_type=MESH)
    pl.semaphore_wait(barrier, len(peers))


def rms_back(values, grad, gain):
    r = lax.rsqrt(jnp.mean(values * values, axis=-1, keepdims=True) + EPS)
    n = values * r
    dyg = grad * gain
    return (
        r * (dyg - n * jnp.mean(dyg * n, axis=-1, keepdims=True)),
        jnp.sum(grad * n, axis=0, keepdims=True),
    )


def stack_heads(values):
    return jnp.concatenate([values[:, h * HD : (h + 1) * HD] for h in range(NH)], axis=0)


def turn_back(grad, cos_table, sin_table):
    left, right = grad[:, : HD // 2], grad[:, HD // 2 :]
    return jnp.concatenate(
        [left * cos_table + right * sin_table, right * cos_table - left * sin_table], axis=1
    )


def front_kernel(
    qkv_ref, wo_ref, ffn_ref, tok_ref, seg_ref, seg_col, table_ref,
    qkv_out, wo_all, ffn_all, gains_ref, qk_ref, normed_ref, proj_ref, q_ref, pair_ref, att_ref,
    attn_ref, mid_ref, low_ref, bias_ref, turn_ref,
    qkv_all, seg_in,
    l_sem, s1, r1, s2, r2, sd, rd, s1f, r1f, s2f, r2f, skv, rkv, ssg, rsg,
):
    f32, bf = jnp.float32, jnp.bfloat16
    y, z, chip, core = place()
    a, b, block = shape_of(y, z, core)
    _, _, block_there = shape_of(y, z, 1 - core)
    q_rows, width = qkv_ref.shape
    o_rows = wo_ref.shape[0]
    q_half, o_half = width // 2, o_rows // 2
    partner = {"ctx": chip * 2 + 1 - core}
    me = chip * 2 + core
    rows = tok_ref.shape[0]
    reach = pair_ref.shape[0] // rows - 1
    members = 2 * (lax.axis_size("ctx") // 2)

    def member(k):
        return {"ctx": lax.rem(me + k, members)}

    def views(f, half):
        return (
            qkv_all.at[
                pl.ds(pl.multiple_of(f * q_rows, 16), q_rows),
                pl.ds(pl.multiple_of(half * q_half, 128), q_half),
            ],
            wo_all.at[pl.ds(pl.multiple_of(f * o_rows + half * o_half, 16), o_half), :],
        )

    mine = (
        qkv_ref.at[:, pl.ds(pl.multiple_of(core * q_half, 128), q_half)],
        wo_ref.at[pl.ds(pl.multiple_of(core * o_half, 16), o_half), :],
    )
    here = block(a, b)
    locals_ = [
        pltpu.make_async_copy(
            qkv_ref, qkv_all.at[pl.ds(pl.multiple_of(here * q_rows, 16), q_rows), :], l_sem.at[0]
        ),
        pltpu.make_async_copy(
            wo_ref, wo_all.at[pl.ds(pl.multiple_of(here * o_rows, 16), o_rows), :], l_sem.at[1]
        ),
        pltpu.make_async_copy(ffn_ref, ffn_all.at[here], l_sem.at[2]),
        pltpu.make_async_copy(table_ref.at[me], turn_ref, l_sem.at[3]),
    ]
    for copy in locals_:
        copy.start()

    def first_peer(k):
        return {"fsdp": block(lax.rem(a + k, 4), b)}

    def second_peer(k):
        return {"fsdp": block(a, lax.rem(b + k, 4))}

    greet(
        [first_peer(k) for k in (1, 2, 3)]
        + [second_peer(k) for k in (1, 2, 3)]
        + [member(k) for k in range(1, members)]
    )

    def seg_send(d):
        return remote(
            seg_ref, seg_in.at[reach - d], ssg.at[d - 1], rsg.at[d - 1], member(d)
        )

    def ffn_one(k):
        return remote(ffn_ref, ffn_all.at[here], s1f.at[k], r1f.at[4 - k], first_peer(k))

    def ffn_block(j, m):
        return ffn_all.at[block(lax.rem(a + j, 4), lax.rem(b + m, 4))]

    def ffn_two(j, k):
        dst = ffn_block(j, 0)
        src = dst if j else ffn_ref
        return remote(src, dst, s2f.at[j, k], r2f.at[j, 4 - k], second_peer(k))

    def ffn_pass(j):
        dst, k = (ffn_block(j, 3), 1) if j < 2 else (ffn_block(j, 1), 3)
        return remote(dst, dst, s2f.at[j, 2], r2f.at[j, 2], second_peer(k))

    def ffn_got(j, m):
        dst = ffn_block(j, m)
        sems = (s1f.at[j], r1f.at[j]) if m == 0 else (s2f.at[j, m], r2f.at[j, m])
        return remote(dst, dst, *sems, partner)

    def hop_one(k, t):
        return remote(mine[t], views(here, core)[t], s1.at[k, t], r1.at[4 - k, t], first_peer(k))

    def hop_two(j, k, t):
        f = block(lax.rem(a + j, 4), b)
        dst = views(f, core)[t]
        src = dst if j else mine[t]
        return remote(src, dst, s2.at[j, k, t], r2.at[j, 4 - k, t], second_peer(k))

    def arrive_one(j, t):
        dst = views(block(lax.rem(a + j, 4), b), core)[t]
        return remote(dst, dst, s1.at[j, t], r1.at[j, t], partner)

    def arrive_two(j, m, t):
        dst = views(block(lax.rem(a + j, 4), lax.rem(b + m, 4)), core)[t]
        return remote(dst, dst, s2.at[j, m, t], r2.at[j, m, t], partner)

    def cross(j, m, t):
        dst = views(block(lax.rem(a + j, 4), lax.rem(b + m, 4)), core)[t]
        return remote(dst, dst, sd.at[j, m, t], rd.at[j, m, t], partner)

    def arrive_cross(j, m, t):
        dst = views(block_there(lax.rem(b + j, 4), lax.rem(a + m, 4)), 1 - core)[t]
        return remote(dst, dst, sd.at[j, m, t], rd.at[j, m, t], partner)

    both = (0, 1)
    for k in (1, 3, 2):
        for t in both:
            hop_one(k, t).start()
    for k in (1, 3, 2):
        for t in both:
            hop_two(0, k, t).start()
    for j in (1, 3, 2):
        for t in both:
            arrive_one(j, t).wait_recv()
            for k in (1, 3, 2):
                hop_two(j, k, t).start()
            cross(j, 0, t).start()

    for d in range(1, reach + 1):
        seg_send(d).start()
    for k in (1, 3, 2):
        ffn_one(k).start()
    for k in (1, 3):
        ffn_two(0, k).start()

    def pass_on(i, carry):
        m, j = i // 4 + 1, lax.rem(i, 4)
        for t in both:
            arrive_two(j, m, t).wait_recv()
            cross(j, m, t).start()
        return carry

    lax.fori_loop(0, 12, pass_on, 0)

    def land(i, carry):
        m, j = i // 4, lax.rem(i, 4)
        for t in both:
            arrive_cross(j, m, t).wait_recv()
            cross(j, m, t).wait_send()
        return carry

    lax.fori_loop(1, 16, land, 0)
    for copy in locals_:
        copy.wait()
    for k in (1, 2, 3):
        for t in both:
            hop_one(k, t).wait_send()
            for j in range(4):
                hop_two(j, k, t).wait_send()

    keep = qkv_out.shape[0] // 16
    extra = jnp.zeros((q_rows - keep, width), f32)
    for f in range(0, 16, 2):
        left = qkv_all[pl.ds(f * q_rows, q_rows), :].astype(f32)
        right = qkv_all[pl.ds((f + 1) * q_rows, q_rows), :].astype(f32)
        qkv_out[pl.ds(f * keep, 2 * keep), :] = jnp.concatenate(
            [left[:keep], right[:keep]], axis=0
        ).astype(bf)
        extra = extra + left[keep:] + right[keep:]
    gains = extra[:4, :D]
    gains_ref[...] = gains
    qk_ref[...] = extra[4:6, :HD]

    stream = tok_ref[...].astype(f32)
    normed_ref[...] = rms_norm(stream, gains[0:1]).astype(bf)
    proj_ref[...] = dot32(normed_ref[...], qkv_out[...], NN)
    cos_table, sin_table = turn_ref[:, : HD // 2], turn_ref[:, HD // 2 :]

    def turn(values, gain, cos_part, sin_part):
        values = rms_norm(values, gain)
        left, right = values[:, : HD // 2], values[:, HD // 2 :]
        return jnp.concatenate(
            [left * cos_part - right * sin_part, right * cos_part + left * sin_part], axis=1
        ).astype(bf)

    own = pl.ds(reach * rows, rows)
    pair_ref[own, :HD] = turn(
        proj_ref[:, NH * HD : NH * HD + HD], extra[5:6, :HD], cos_table, sin_table
    )
    pair_ref[own, HD:] = proj_ref[:, NH * HD + HD :].astype(bf)

    def kv_send(d):
        return remote(
            pair_ref.at[own],
            pair_ref.at[pl.ds((reach - d) * rows, rows)],
            skv.at[d - 1], rkv.at[d - 1], member(d),
        )

    for d in range(1, reach + 1):
        kv_send(d).start()
    for j in (1, 3, 2):
        ffn_got(j, 0).wait_recv()
        for k in (1, 3):
            ffn_two(j, k).start()
    queries = turn(
        stack_heads(proj_ref[:, : NH * HD]),
        extra[4:5, :HD],
        jnp.concatenate([cos_table] * NH, axis=0),
        jnp.concatenate([sin_table] * NH, axis=0),
    )
    for h in range(NH):
        q_ref[:, h * HD : (h + 1) * HD] = queries[h * rows : (h + 1) * rows]

    for d in range(1, reach + 1):
        seg_send(d).wait_recv()
    seg_in[reach] = seg_ref[...]
    key_seg = jnp.concatenate([seg_in[p][0:1, :] for p in range(reach + 1)], axis=1)
    shape = (rows, (reach + 1) * rows)
    spacing = (
        reach * rows + lax.broadcasted_iota(jnp.int32, shape, 0)
        - lax.broadcasted_iota(jnp.int32, shape, 1)
    )
    begun = lax.broadcasted_iota(jnp.int32, shape, 1) + (me - reach) * rows >= 0
    allowed = (spacing >= 0) & (spacing < WINDOW) & begun & (seg_col[...] == key_seg)
    bias_ref[...] = jnp.where(allowed, 0.0, NEG_FILL)
    for d in range(1, reach + 1):
        kv_send(d).wait_recv()
    scores = dot32(queries, pair_ref[:, :HD], NT) * (HD ** (-0.5)) + jnp.concatenate(
        [bias_ref[...]] * NH, axis=0
    )
    expo = jnp.exp(scores - jnp.max(scores, axis=-1, keepdims=True))
    probs = expo / jnp.sum(expo, axis=-1, keepdims=True)
    heads = dot32(probs.astype(bf), pair_ref[:, HD:], NN).astype(bf)
    for h in range(NH):
        att_ref[:, h * HD : (h + 1) * HD] = heads[h * rows : (h + 1) * rows]
    attn = dot32(att_ref[...], wo_all[...], NN)
    attn_ref[...] = attn
    mid = stream + rms_norm(attn, gains[1:2])
    mid_ref[...] = mid
    low_ref[...] = rms_norm(mid, gains[2:3]).astype(bf)

    for j in range(4):
        ffn_got(j, 3 if j < 2 else 1).wait_recv()
        ffn_pass(j).start()
    for j in range(4):
        ffn_got(j, 1 if j < 2 else 3).wait_recv()
        ffn_got(j, 2).wait_recv()
    for j in range(4):
        ffn_pass(j).wait_send()
        for k in (1, 3):
            ffn_two(j, k).wait_send()
    for k in (1, 2, 3):
        ffn_one(k).wait_send()
    for d in range(1, reach + 1):
        seg_send(d).wait_send()
        kv_send(d).wait_send()


def front(qkv_shard, wo_shard, ffn_shard, tokens, seg_rows, seg_col, table, keep):
    f32, bf = jnp.float32, jnp.bfloat16
    vm = pl.BlockSpec(memory_space=pltpu.VMEM)
    hbm = pl.BlockSpec(memory_space=pl.ANY)
    dma = pltpu.SemaphoreType.DMA
    q_rows, width = qkv_shard.shape
    o_rows, o_width = wo_shard.shape
    rows = tokens.shape[0]
    reach = min(-(-(WINDOW - 1) // rows), lax.axis_size("ctx") - 1)
    pairs = (reach + 1) * rows
    shapes = (
        ((16 * keep, width), bf),
        ((16 * o_rows, o_width), bf),
        ((16, *ffn_shard.shape), bf),
        ((4, D), f32),
        ((2, HD), f32),
        ((rows, D), bf),
        ((rows, width), f32),
        ((rows, NH * HD), bf),
        ((pairs, 2 * HD), bf),
        ((rows, NH * HD), bf),
        ((rows, D), f32),
        ((rows, D), f32),
        ((rows, D), bf),
        ((rows, pairs), f32),
        ((rows, HD), f32),
    )
    return pl.pallas_call(
        front_kernel,
        out_shape=tuple(jax.ShapeDtypeStruct(*s) for s in shapes),
        in_specs=[vm, vm, hbm, vm, vm, vm, hbm],
        out_specs=(vm, vm, hbm) + (vm,) * (len(shapes) - 3),
        scratch_shapes=[
            pltpu.VMEM((16 * q_rows, width), bf),
            pltpu.VMEM((reach + 1, 8, rows), jnp.int32),
            dma((4,)),
            dma((4, 2)), dma((4, 2)),
            dma((4, 4, 2)), dma((4, 4, 2)),
            dma((4, 4, 2)), dma((4, 4, 2)),
            dma((4,)), dma((4,)),
            dma((4, 4)), dma((4, 4)),
            dma((reach,)), dma((reach,)),
            dma((reach,)), dma((reach,)),
        ],
        compiler_params=pltpu.CompilerParams(
            collective_id=2, has_side_effects=True, vmem_limit_bytes=48 * 1024 * 1024
        ),
        cost_estimate=pl.CostEstimate(
            flops=6 * rows * width * D, bytes_accessed=64 * q_rows * width, transcendentals=0
        ),
    )(qkv_shard, wo_shard, ffn_shard, tokens, seg_rows, seg_col, table)


def back_kernel(
    gff, gn_ref, mid_ref, attn_ref, cot_ref, tok_ref, gains_ref, qk_ref, proj_ref, q_ref,
    pair_ref, att_ref, normed_ref, qkv_ref, wo_ref, turn_ref, bias_ref, g3_ref,
    gt_ref, oq_out, tail_out, oo_ref, og_ref, ou_ref, od_ref,
    oq_ref, own_ff, in1_ff, t_ff, in2_ff, all_ff, kv_snd, kv_in, gmid, gpair, gproj, tail,
    stage, go, dq, do, sq, so, iq1, io1, tq, to, iq2, io2, xq, xo,
    l_sem, s1f, r1f, s2f, r2f, sag, rag, skv, rkv,
    sd, rd, s1, r1, s2, r2, sx, rx, sf, rf,
):
    y, z, chip, core = place()
    a, b, block = shape_of(y, z, core)
    _, _, block_there = shape_of(y, z, 1 - core)
    me = chip * 2 + core
    rows = gn_ref.shape[0]
    q_rows, width = oq_ref.shape
    keep = normed_ref.shape[1] // 16
    o_rows = oo_ref.shape[0]
    q_half, o_half = width // 2, o_rows // 2
    chips = xq.shape[0]
    members = 2 * chips
    reach = kv_in.shape[0]
    scale = HD ** (-0.5)
    f32, bf = jnp.float32, jnp.bfloat16
    partner = {"ctx": chip * 2 + 1 - core}

    def first_peer(k):
        return {"fsdp": block(lax.rem(a + k, 4), b)}

    def second_peer(k):
        return {"fsdp": block(a, lax.rem(b + k, 4))}

    def chip_peer(k):
        return {"ctx": lax.rem(chip + k, chips) * 2 + core}

    def member(k):
        return {"ctx": lax.rem(me + k, members)}

    def q_cols(half):
        return pl.ds(pl.multiple_of(half * q_half, 128), q_half)

    def o_lines(half):
        return pl.ds(pl.multiple_of(half * o_half, 16), o_half)

    own_loads = [
        pltpu.make_async_copy(gff.at[block(a, j)], own_ff.at[j], l_sem.at[j]) for j in range(4)
    ]
    for copy in own_loads:
        copy.start()
    greet(
        [first_peer(k) for k in (1, 2, 3)]
        + [second_peer(k) for k in (1, 2, 3)]
        + [member(k) for k in range(1, members)]
    )

    def ff_one(k, j):
        return remote(
            gff.at[block(lax.rem(a + k, 4), j)], in1_ff.at[3 - k, j],
            s1f.at[k, j], r1f.at[4 - k, j], first_peer(k),
        )

    for i in (2, 1, 3, 0):
        for k in (1, 3, 2):
            ff_one(k, lax.rem(b + i, 4)).start()

    grad_final = cot_ref[...].astype(f32)
    part, gain_two = rms_back(mid_ref[...], gn_ref[...], gains_ref[2:3, :])
    grad_mid = grad_final + part
    gmid[...] = grad_mid
    grad_attn, gain_one = rms_back(attn_ref[...], grad_mid, gains_ref[1:2, :])
    grad_attn_low = grad_attn.astype(bf)
    grad_attended = dot32(grad_attn_low, wo_ref[...], NT).astype(bf)

    def out_tile(t, carry):
        cols = pl.ds(pl.multiple_of(t * 256, 256), 256)
        go[pl.ds(t * 4, 4)] = (
            dot32(att_ref[:, cols], grad_attn_low, TN).reshape(4, 64, D).astype(bf)
        )
        return carry

    lax.fori_loop(0, NH * HD // 256, out_tile, 0)

    def away(i, t):
        k, j = lax.rem(i // 4 + 1, 4), lax.rem(i, 4)
        line = lax.rem(b + k, 4)
        f = block_there(line, j)
        slot = line * 4 + j
        if t == 0:
            src, dst = stage.at[f, :, q_cols(1 - core)], dq.at[slot]
        else:
            src, dst = go.at[f, o_lines(1 - core), :], do.at[slot]
        return remote(src, dst, sd.at[i, t], rd.at[i, t], partner)

    def home(i, t):
        k, j = lax.rem(i // 4 + 1, 4), lax.rem(i, 4)
        slot = lax.rem(a + k, 4) * 4 + j
        dst = (dq, do)[t].at[slot]
        return remote(dst, dst, sd.at[i, t], rd.at[i, t], partner)

    def start_away(t):
        def one(i, carry):
            away(i, t).start()
            return carry

        lax.fori_loop(0, 16, one, 0)

    start_away(1)

    keys, vals = pair_ref[:, :HD], pair_ref[:, HD:]
    queries = stack_heads(q_ref[...])
    grad_heads = stack_heads(grad_attended)
    scores = dot32(queries, keys, NT) * scale + jnp.concatenate([bias_ref[...]] * NH, axis=0)
    expo = jnp.exp(scores - jnp.max(scores, axis=-1, keepdims=True))
    probs = expo / jnp.sum(expo, axis=-1, keepdims=True)
    grad_probs = dot32(grad_heads, vals, NT)
    row_total = jnp.sum(probs * grad_probs, axis=-1, keepdims=True)
    grad_scores = (probs * (grad_probs - row_total)).astype(bf)
    gpair[:, HD:] = dot32(probs.astype(bf), grad_heads, TN)
    gpair[:, :HD] = dot32(grad_scores, queries, TN) * scale

    def kv_send(d):
        return remote(
            kv_snd.at[d - 1], kv_in.at[d - 1], skv.at[d - 1], rkv.at[d - 1], member(members - d)
        )

    for d in range(1, reach + 1):
        kv_snd[d - 1] = gpair[pl.ds((reach - d) * rows, rows), :].astype(bf)
        kv_send(d).start()

    cos_table, sin_table = turn_ref[:, : HD // 2], turn_ref[:, HD // 2 :]
    cos_all = jnp.concatenate([cos_table] * NH, axis=0)
    sin_all = jnp.concatenate([sin_table] * NH, axis=0)
    grad_queries = dot32(grad_scores, keys, NN) * scale
    grad_q, qk_gain_q = rms_back(
        stack_heads(proj_ref[:, : NH * HD]),
        turn_back(grad_queries, cos_all, sin_all),
        qk_ref[0:1, :],
    )
    for h in range(NH):
        gproj[:, h * HD : (h + 1) * HD] = grad_q[h * rows : (h + 1) * rows].astype(bf)

    def hop_one(k, t):
        src, dst = ((sq, iq1), (so, io1))[t]
        line = pl.ds(lax.rem(a + k, 4) * 4, 4)
        return remote(
            src.at[line], dst.at[3 - k], s1.at[k, t], r1.at[4 - k, t], first_peer(k)
        )

    def fold_cores(t):
        for k in (1, 2, 3, 0):
            def add(j, carry, k=k):
                line = lax.rem(a + k, 4)
                slot = line * 4 + j
                f = block(line, j)
                home((k + 3) % 4 * 4 + j, t).wait_recv()
                if t == 0:
                    sq[slot] = (
                        stage[f, :, q_cols(core)].astype(f32) + dq[slot].astype(f32)
                    ).astype(bf)
                else:
                    so[slot] = (
                        go[f, o_lines(core), :].astype(f32) + do[slot].astype(f32)
                    ).astype(bf)
                return carry

            lax.fori_loop(0, 4, add, 0)
            if k:
                hop_one(k, t).start()

    fold_cores(1)

    total = gpair[pl.ds(reach * rows, rows), :]
    for d in range(1, reach + 1):
        kv_send(d).wait_recv()
        total = total + kv_in[d - 1].astype(f32)
    grad_k, qk_gain_k = rms_back(
        proj_ref[:, NH * HD : NH * HD + HD],
        turn_back(total[:, :HD], cos_table, sin_table),
        qk_ref[1:2, :],
    )
    gproj[:, NH * HD : NH * HD + HD] = grad_k.astype(bf)
    gproj[:, NH * HD + HD :] = total[:, HD:].astype(bf)
    stream = tok_ref[...].astype(f32)
    grad_in, gain_zero = rms_back(stream, dot32(gproj[...], qkv_ref[...], NT), gains_ref[0:1, :])
    gt_ref[...] = gmid[...] + grad_in
    tail[...] = jnp.zeros_like(tail)
    for i, line in enumerate((gain_zero, gain_one, gain_two, g3_ref[...])):
        tail[i : i + 1, :D] = line
    tail[4:5, :HD] = qk_gain_q
    tail[5:6, :HD] = qk_gain_k

    def qkv_tile(t, carry):
        cols = pl.ds(pl.multiple_of(t * 256, 256), 256)
        res = dot32(normed_ref[...], gproj[:, cols], TN)
        low = tail[:, cols]
        for f in range(16):
            stage[f, :, cols] = jnp.concatenate(
                [res[f * keep : (f + 1) * keep], low], axis=0
            ).astype(bf)
        return carry

    lax.fori_loop(0, width // 256, qkv_tile, 0)
    start_away(0)
    fold_cores(0)

    for copy in own_loads:
        copy.wait()

    def ff_two(k):
        return remote(
            t_ff.at[lax.rem(b + k, 4)], in2_ff.at[3 - k], s2f.at[k], r2f.at[4 - k], second_peer(k)
        )

    for k in (2, 1, 3, 0):
        j = lax.rem(b + k, 4)
        for m in (1, 2, 3):
            dst = in1_ff.at[m - 1, j]
            remote(dst, dst, s1f.at[m, j], r1f.at[m, j], partner).wait_recv()
        total = own_ff[j].astype(f32)
        for m in range(3):
            total = total + in1_ff[m, j].astype(f32)
        t_ff[j] = total.astype(bf)
        if k:
            ff_two(k).start()

    def hop_two(k, t):
        src, dst = ((tq, iq2), (to, io2))[t]
        return remote(
            src.at[lax.rem(b + k, 4)], dst.at[3 - k], s2.at[k, t], r2.at[4 - k, t], second_peer(k)
        )

    for t in (1, 0):
        own, got, dst = ((sq, iq1, tq), (so, io1, to))[t]
        for k in (1, 3, 2):
            hop_one(4 - k, t).wait_recv()
        for k in (2, 1, 3, 0):
            j = lax.rem(b + k, 4)
            total = own[a * 4 + j].astype(f32)
            for m in range(3):
                total = total + got[m, j].astype(f32)
            dst[j] = total.astype(bf)
            if k:
                hop_two(k, t).start()

    for k in (1, 3, 2):
        ff_two(4 - k).wait_recv()
    total = t_ff[b].astype(f32)
    for m in range(3):
        total = total + in2_ff[m].astype(f32)
    all_ff[me] = total.astype(bf)

    def ff_all(k):
        peer = chip_peer(k) if k else partner
        return remote(
            all_ff.at[me], all_ff.at[me], sag.at[k], rag.at[(chips - k) % chips], peer
        )

    def ff_from(k):
        dst = all_ff.at[lax.rem(chip + k, chips) * 2 + core]
        return remote(dst, dst, sag.at[chips + k], rag.at[k], partner)

    def ff_cross(k):
        dst = all_ff.at[lax.rem(chip + k, chips) * 2 + core]
        return remote(dst, dst, sag.at[chips + k], rag.at[chips + k], partner)

    def ff_crossed(k):
        dst = all_ff.at[lax.rem(chip + k, chips) * 2 + 1 - core]
        return remote(dst, dst, sag.at[k], rag.at[chips + k if k else 0], partner)

    for k in (*range(1, chips), 0):
        ff_all(k).start()

    def hop_chip(k, t):
        buf = (xq, xo)[t]
        return remote(
            buf.at[chip], buf.at[chip], sx.at[k, t], rx.at[chips - k, t], chip_peer(k)
        )

    for t in (1, 0):
        own, got, dst = ((tq, iq2, xq), (to, io2, xo))[t]
        for k in (1, 3, 2):
            hop_two(4 - k, t).wait_recv()
        total = own[b].astype(f32)
        for m in range(3):
            total = total + got[m].astype(f32)
        dst[chip] = total.astype(bf)
        for k in range(1, chips):
            hop_chip(k, t).start()

    def last(t, half):
        part = (oq_ref.at[:, q_cols(half)], oo_ref.at[o_lines(half), :])[t]
        return remote(part, part, sf.at[t], rf.at[t], partner)

    for k in range(1, chips):
        ff_from(k).wait_recv()
        ff_cross(k).start()

    for t in (1, 0):
        buf = (xq, xo)[t]
        for k in range(1, chips):
            dst = buf.at[lax.rem(chip + k, chips)]
            remote(dst, dst, sx.at[k, t], rx.at[k, t], partner).wait_recv()
        total = buf[0].astype(f32)
        for m in range(1, chips):
            total = total + buf[m].astype(f32)
        if t == 0:
            oq_ref[:, q_cols(core)] = total
        else:
            oo_ref[o_lines(core), :] = total
        last(t, core).start()

    for k in range(chips):
        ff_crossed(k).wait_recv()
    lines = og_ref.shape[0] // members
    share = all_ff.shape[1] // 3
    for i, dst in enumerate((og_ref, ou_ref, od_ref)):
        for m in range(members):
            dst[m * lines : (m + 1) * lines, :] = all_ff[
                m, i * share : (i + 1) * share, :
            ].astype(f32)[:lines]

    def end_away(i, carry):
        for t in (0, 1):
            away(i, t).wait_send()
        return carry

    lax.fori_loop(0, 16, end_away, 0)
    for k in (1, 2, 3):
        for j in range(4):
            ff_one(k, j).wait_send()
        ff_two(k).wait_send()
    for d in range(1, reach + 1):
        kv_send(d).wait_send()
    for k in range(chips):
        ff_all(k).wait_send()
        if k:
            ff_cross(k).wait_send()
    for t in (0, 1):
        for k in (1, 2, 3):
            hop_one(k, t).wait_send()
            hop_two(k, t).wait_send()
        for k in range(1, chips):
            hop_chip(k, t).wait_send()
        last(t, core).wait_send()
        last(t, 1 - core).wait_recv()
    oq_out[...] = oq_ref[:keep, :]
    tail_out[...] = oq_ref[keep:, :]


def backward_rest(gff, values, keep, lines):
    f32, bf = jnp.float32, jnp.bfloat16
    vm = pl.BlockSpec(memory_space=pltpu.VMEM)
    hbm = pl.BlockSpec(memory_space=pl.ANY)
    dma = pltpu.SemaphoreType.DMA
    rows = values[0].shape[0]
    owners, ff_rows = gff.shape[:2]
    q_rows, width = keep + 8, (NH + 2) * HD
    o_rows, o_width = NH * HD // owners, D
    q_half, o_half = width // 2, o_rows // 2
    chips = lax.axis_size("ctx") // 2
    pairs = values[9].shape[0]
    reach = pairs // rows - 1

    def two(*lead):
        return [pltpu.VMEM(lead + (q_rows, q_half), bf), pltpu.VMEM(lead + (o_half, o_width), bf)]

    def ff(*lead):
        return pltpu.VMEM(lead + (ff_rows, D), bf)

    weight = jax.ShapeDtypeStruct((lines, D), f32)
    return pl.pallas_call(
        back_kernel,
        out_shape=(
            jax.ShapeDtypeStruct((rows, D), f32),
            jax.ShapeDtypeStruct((keep, width), f32),
            jax.ShapeDtypeStruct((8, width), f32),
            jax.ShapeDtypeStruct((o_rows, o_width), f32),
            weight, weight, weight,
        ),
        in_specs=[hbm] + [vm] * len(values),
        out_specs=(vm,) * 7,
        scratch_shapes=[
            pltpu.VMEM((q_rows, width), f32),
            ff(4), ff(3, 4), ff(4), ff(3), ff(2 * chips),
            pltpu.VMEM((reach, rows, 2 * HD), bf),
            pltpu.VMEM((reach, rows, 2 * HD), bf),
            pltpu.VMEM((rows, D), f32),
            pltpu.VMEM((pairs, 2 * HD), f32),
            pltpu.VMEM((rows, width), bf),
            pltpu.VMEM((8, width), f32),
            pltpu.VMEM((16, q_rows, width), bf),
            pltpu.VMEM((16, o_rows, o_width), bf),
            *two(16), *two(16), *two(3, 4), *two(4), *two(3), *two(chips),
            dma((4,)),
            dma((4, 4)), dma((4, 4)),
            dma((4,)), dma((4,)),
            dma((2 * chips,)), dma((2 * chips,)),
            dma((reach,)), dma((reach,)),
            dma((16, 2)), dma((16, 2)),
            dma((4, 2)), dma((4, 2)),
            dma((4, 2)), dma((4, 2)),
            dma((4, 2)), dma((4, 2)),
            dma((2,)), dma((2,)),
        ],
        compiler_params=pltpu.CompilerParams(
            collective_id=3, has_side_effects=True, vmem_limit_bytes=62 * 1024 * 1024
        ),
        cost_estimate=pl.CostEstimate(
            flops=12 * rows * width * D, bytes_accessed=64 * ff_rows * D, transcendentals=0
        ),
    )(gff, *values)


def on_device(
    tokens,
    norm_gains,
    qk_gains,
    qkv_weight,
    out_weight,
    gate_weight,
    up_weight,
    down_weight,
    segments,
    cotangent,
):
    local_len = tokens.shape[1]
    ctx_index = lax.axis_index("ctx")
    owner = lax.axis_index("fsdp")
    ctx_size = lax.axis_size("ctx")
    own_rows = gate_weight.shape[0]
    slice_rows = own_rows // ctx_size
    padded = -(-slice_rows // 16) * 16
    keep, width = qkv_weight.shape
    gain_lines, qk_lines = norm_gains.shape, qk_gains.shape
    gain_rows = jnp.zeros((8, width), jnp.bfloat16)
    gain_rows = lax.dynamic_update_slice(gain_rows, norm_gains, (0, owner * gain_lines[1]))
    gain_rows = lax.dynamic_update_slice(gain_rows, qk_gains, (4, owner * qk_lines[1]))

    def my_slice(weight):
        part = lax.dynamic_index_in_dim(
            weight.reshape(ctx_size, slice_rows, D), ctx_index, 0, False
        )
        return jnp.pad(part, ((0, padded - slice_rows), (0, 0)))

    ffn_shard = jnp.concatenate(
        [my_slice(gate_weight), my_slice(up_weight), my_slice(down_weight)], axis=0
    )
    places = np.arange(ctx_size * local_len, dtype=np.float32)
    rates = (ROPE_BASE ** (-(2.0 * np.arange(HD // 2)) / HD)).astype(np.float32)
    angles = (places[:, None] * rates).astype(np.float64)
    table = jnp.asarray(
        np.concatenate([np.cos(angles), np.sin(angles)], axis=1)
        .astype(np.float32)
        .reshape(ctx_size, local_len, HD)
    )
    flat = tokens.reshape(local_len, D)
    cot = cotangent.reshape(local_len, D)
    (
        qkv_full, out_full, ffn_full, gains_all, qk_all, normed, projected, queries, pair_all,
        attended, attn, mid, normed_two, bias, turn_table,
    ) = front(
        jnp.concatenate([qkv_weight, gain_rows], axis=0),
        out_weight,
        ffn_shard,
        flat,
        jnp.broadcast_to(segments, (8, local_len)),
        segments.reshape(local_len, 1),
        table,
        keep,
    )
    output, grad_normed_two, grad_gain_three, ffn_grads = ffn(
        normed_two, mid, cot, gains_all, ffn_full
    )
    grad_tokens, total_qkv, tail, total_out, total_gate, total_up, total_down = backward_rest(
        ffn_grads,
        (
            grad_normed_two, mid, attn, cot, flat, gains_all, qk_all, projected, queries,
            pair_all, attended, normed, qkv_full, out_full, turn_table, bias, grad_gain_three,
        ),
        keep,
        own_rows,
    )
    total_gains = lax.dynamic_slice(tail[:4, :D], (0, owner * gain_lines[1]), gain_lines)
    total_qk = lax.dynamic_slice(tail[4:6, :HD], (0, owner * qk_lines[1]), qk_lines)
    return (
        output.reshape(tokens.shape),
        grad_tokens.reshape(tokens.shape),
        total_gains,
        total_qk,
        total_qkv,
        total_out,
        total_gate,
        total_up,
        total_down,
    )


def solution(mesh):
    in_specs = (
        P("fsdp", "ctx", None),
        P(None, "fsdp"),
        P(None, "fsdp"),
        P("fsdp", None),
        P("fsdp", None),
        P("fsdp", None),
        P("fsdp", None),
        P("fsdp", None),
        P("fsdp", "ctx"),
        P("fsdp", "ctx", None),
    )
    out_specs = (
        P("fsdp", "ctx", None),
        P("fsdp", "ctx", None),
        P(None, "fsdp"),
        P(None, "fsdp"),
        P("fsdp", None),
        P("fsdp", None),
        P("fsdp", None),
        P("fsdp", None),
        P("fsdp", None),
    )
    return jax.shard_map(
        on_device, mesh=mesh, in_specs=in_specs, out_specs=out_specs, check_vma=False
    )
```

```python
import jax
import numpy as np
import jax.numpy as jnp
from jax import lax
from jax.experimental import pallas as pl
from jax.experimental.pallas import tpu as pltpu
from jax.sharding import PartitionSpec as P

D = 1152
NH = 4
HD = 256
WINDOW = 512


EPS = 1e-06
ROPE_BASE = 10000.0
NEG_FILL = -1e30


def rms_norm(values, gain_vec):
    return values * lax.rsqrt(jnp.mean(values * values, axis=-1, keepdims=True) + EPS) * gain_vec


MESH = pl.DeviceIdType.MESH
NT = (((1,), (1,)), ((), ()))
NN = (((1,), (0,)), ((), ()))
TN = (((0,), (0,)), ((), ()))
GELU_C = 0.7978845608028654
GELU_A = 0.044715


def dot32(left, right, dims):
    return lax.dot_general(left, right, dims, preferred_element_type=jnp.float32)


def ffn_kernel(
    normed_ref, mid_ref, cot_ref, gain_ref, w_hbm,
    out_ref, gn_ref, ggain_ref, gff_hbm,
    wg, wu, wd, seq, gseq, act_a, act_b, hid, dgate, dup, part,
    d2d_snd, d2d_in, ici_snd, ici_in, dw,
    w_sem, o_sem, ag_s, ag_r, rd_s, rd_r, ri_s, ri_r,
):
    rows = normed_ref.shape[0]
    units = wg.shape[0]
    share = units // w_hbm.shape[0]
    tile = 256
    me = lax.axis_index("ctx")
    chip, core = me // 2, lax.rem(me, 2)
    partner = {"ctx": chip * 2 + 1 - core}
    chips = {k: {"ctx": lax.rem(chip + k, 4) * 2 + core} for k in (1, 2, 3)}
    order = (0, 1, 3, 2)

    loads = [
        pltpu.make_async_copy(
            w_hbm.at[f, pl.ds(i * share, share), :], dst.at[pl.ds(f * share, share), :], w_sem.at[i, f]
        )
        for i, dst in enumerate((wg, wu, wd))
        for f in range(w_hbm.shape[0])
    ]
    for load in loads:
        load.start()

    barrier = pltpu.get_barrier_semaphore()
    for peer in (partner, chips[1], chips[2], chips[3]):
        pl.semaphore_signal(barrier, inc=1, device_id=peer, device_id_type=MESH)
    pl.semaphore_wait(barrier, 4)

    started = []

    def send(src, dst, s_sem, r_sem, peer):
        copy = pltpu.make_async_remote_copy(
            src_ref=src, dst_ref=dst, send_sem=s_sem, recv_sem=r_sem,
            device_id=peer, device_id_type=MESH,
        )
        copy.start()
        started.append(copy)
        return copy

    def mine(k):
        return pl.ds(k * 2 * rows, rows)

    def other(k):
        return pl.ds(k * 2 * rows + rows, rows)

    def pair(k):
        return pl.ds(k * 2 * rows, 2 * rows)

    def spread(buf, ph):
        own = buf.at[mine(0)]
        got = {}
        for k in (1, 3):
            back = 4 - k
            got[back] = send(own, buf.at[mine(back)], ag_s.at[ph, k], ag_r.at[ph, back], chips[k])
        got[0] = send(own, buf.at[other(0)], ag_s.at[ph, 0], ag_r.at[ph, 0], partner)
        return got

    def half_of(k, h, offset=0):
        return pl.ds(k * 2 * rows + offset + h * (rows // 2), rows // 2)

    def relay(buf, ph, got, k):
        got[k].wait_recv()
        h = 0 if k == 3 else 1
        got[2, h] = send(
            buf.at[half_of(k, h)], buf.at[half_of(2, h)],
            ag_s.at[ph, 2 + 2 * h], ag_r.at[ph, 2 + 2 * h], chips[4 - k],
        )
        got[k] = send(
            buf.at[mine(k)], buf.at[other(k)], ag_s.at[ph, 4 + k], ag_r.at[ph, 4 + k], partner
        )

    def relay_far(buf, ph, got):
        for h in (0, 1):
            got[2, h].wait_recv()
            got[2, h] = send(
                buf.at[half_of(2, h)], buf.at[half_of(2, h, rows)],
                ag_s.at[ph, 6 + 2 * h], ag_r.at[ph, 6 + 2 * h], partner,
            )

    def sum_out(ph, k):
        d2d_snd[ph, k] = part[pl.ds(rows, rows), :].astype(jnp.bfloat16)
        copy = send(
            d2d_snd.at[ph, k], d2d_in.at[ph, k], rd_s.at[ph, k], rd_r.at[ph, k], partner
        )
        copy.wait_recv()
        total = part[pl.ds(0, rows), :] + d2d_in[ph, k].astype(jnp.float32)
        if k == 0:
            return total
        ici_snd[ph, k - 1] = total.astype(jnp.bfloat16)
        back = 4 - k
        return send(
            ici_snd.at[ph, k - 1], ici_in.at[ph, back - 1], ri_s.at[ph, k], ri_r.at[ph, back],
            chips[k],
        )

    def phase(buf, ph, work):
        got = spread(buf, ph)
        if ph == 0:
            for load in loads:
                load.wait()
        sums = {}
        for k in order:
            if k == 1:
                relay(buf, ph, got, 1)
                relay(buf, ph, got, 3)
            if k == 2:
                relay_far(buf, ph, got)
                got[2, 0].wait_recv()
                got[2, 1].wait_recv()
            else:
                got[k].wait_recv()
            work(k)
            sums[k] = sum_out(ph, k)
        return sums

    def collect(ph, sums):
        total = sums[0]
        for k in (1, 3, 2):
            sums[k].wait_recv()
        for k in (1, 2, 3):
            total = total + ici_in[ph, k - 1].astype(jnp.float32)
        return total

    def forward(k):
        def one(t, carry):
            cols = pl.ds(pl.multiple_of(t * tile, tile), tile)
            block = seq[pair(k), :]
            gate = dot32(block, wg[cols, :], NT)
            up = dot32(block, wu[cols, :], NT)
            square = gate * gate
            th = jnp.tanh(GELU_C * gate * (1.0 + GELU_A * square))
            half = 0.5 * (1.0 + th)
            gelu = gate * half
            slope = half + (0.5 * GELU_C) * gate * (1.0 - th * th) * (1.0 + 3.0 * GELU_A * square)
            hid[pair(k), cols] = (gelu * up).astype(jnp.bfloat16)
            act_a[pair(k), cols] = up * slope
            act_b[pair(k), cols] = gelu
            return carry

        lax.fori_loop(0, units // tile, one, 0)
        part[...] = dot32(hid[pair(k), :], wd[...], NN)

    seq[mine(0), :] = normed_ref[...]
    sums = phase(seq, 0, forward)
    mlp = collect(0, sums)
    r = lax.rsqrt(jnp.mean(mlp * mlp, axis=-1, keepdims=True) + EPS)
    n = mlp * r
    gain = gain_ref[3:4, :]
    out_ref[...] = (mid_ref[...] + n * gain).astype(jnp.bfloat16)
    dy = cot_ref[...].astype(jnp.float32)
    ggain_ref[...] = jnp.sum(dy * n, axis=0, keepdims=True)
    dyg = dy * gain
    dv = r * (dyg - n * jnp.mean(dyg * n, axis=-1, keepdims=True))
    gseq[mine(0), :] = dv.astype(jnp.bfloat16)

    def backward(k):
        def one(t, carry):
            cols = pl.ds(pl.multiple_of(t * tile, tile), tile)
            gh = dot32(gseq[pair(k), :], wd[cols, :], NT)
            dgate[pair(k), cols] = (gh * act_a[pair(k), cols]).astype(jnp.bfloat16)
            dup[pair(k), cols] = (gh * act_b[pair(k), cols]).astype(jnp.bfloat16)
            return carry

        lax.fori_loop(0, units // tile, one, 0)
        part[...] = dot32(dgate[pair(k), :], wg[...], NN) + dot32(dup[pair(k), :], wu[...], NN)

    sums = phase(gseq, 1, backward)
    for i, (left, right) in enumerate(((dgate, seq), (dup, seq), (hid, gseq))):
        def one(t, carry, i=i, left=left, right=right):
            cols = pl.ds(pl.multiple_of(t * tile, tile), tile)
            group = tile // share
            dw[pl.ds(t * group, group), pl.ds(i * share, share), :] = (
                dot32(left[:, cols], right[...], TN).reshape(group, share, -1).astype(jnp.bfloat16)
            )
            return carry

        lax.fori_loop(0, units // tile, one, 0)
    store = pltpu.make_async_copy(dw, gff_hbm, o_sem)
    store.start()
    gn_ref[...] = collect(1, sums)
    for copy in started:
        copy.wait_send()
    store.wait()


def ffn(normed_two, mid, cot, gain, weights):
    rows = normed_two.shape[0]
    owners, lines = weights.shape[:2]
    units = owners * lines // 3
    seq_rows = rows * 8
    bf, f32 = jnp.bfloat16, jnp.float32
    vm = pl.BlockSpec(memory_space=pltpu.VMEM)
    hbm = pl.BlockSpec(memory_space=pl.ANY)
    dma = pltpu.SemaphoreType.DMA
    return pl.pallas_call(
        ffn_kernel,
        out_shape=(
            jax.ShapeDtypeStruct((rows, D), bf),
            jax.ShapeDtypeStruct((rows, D), f32),
            jax.ShapeDtypeStruct((1, D), f32),
            jax.ShapeDtypeStruct(weights.shape, bf),
        ),
        in_specs=[vm] * 4 + [hbm],
        out_specs=(vm, vm, vm, hbm),
        scratch_shapes=[
            pltpu.VMEM((units, D), bf),
            pltpu.VMEM((units, D), bf),
            pltpu.VMEM((units, D), bf),
            pltpu.VMEM((seq_rows, D), bf),
            pltpu.VMEM((seq_rows, D), bf),
            pltpu.VMEM((seq_rows, units), f32),
            pltpu.VMEM((seq_rows, units), f32),
            pltpu.VMEM((seq_rows, units), bf),
            pltpu.VMEM((seq_rows, units), bf),
            pltpu.VMEM((seq_rows, units), bf),
            pltpu.VMEM((2 * rows, D), f32),
            pltpu.VMEM((2, 4, rows, D), bf),
            pltpu.VMEM((2, 4, rows, D), bf),
            pltpu.VMEM((2, 3, rows, D), bf),
            pltpu.VMEM((2, 3, rows, D), bf),
            pltpu.VMEM(weights.shape, bf),
            dma((3, owners)), dma,
            dma((2, 10)), dma((2, 10)),
            dma((2, 4)), dma((2, 4)),
            dma((2, 4)), dma((2, 4)),
        ],
        compiler_params=pltpu.CompilerParams(
            collective_id=1, has_side_effects=True, vmem_limit_bytes=62 * 1024 * 1024
        ),
        cost_estimate=pl.CostEstimate(
            flops=18 * seq_rows * units * D, bytes_accessed=14 * units * D, transcendentals=0
        ),
    )(normed_two, mid, cot, gain, weights)


def place():
    fsdp = lax.axis_index("fsdp")
    ctx = lax.axis_index("ctx")
    y, z = fsdp // 4, lax.rem(fsdp, 4)
    chip, core = ctx // 2, lax.rem(ctx, 2)
    return y, z, chip, core


def shape_of(y, z, core):
    first = (1 - core) * y + core * z
    second = (1 - core) * z + core * y

    def block(i, j):
        return (1 - core) * (4 * i + j) + core * (4 * j + i)

    return first, second, block


def remote(src, dst, s_sem, r_sem, peer):
    return pltpu.make_async_remote_copy(
        src_ref=src, dst_ref=dst, send_sem=s_sem, recv_sem=r_sem,
        device_id=peer, device_id_type=MESH,
    )


def greet(peers):
    barrier = pltpu.get_barrier_semaphore()
    for peer in peers:
        pl.semaphore_signal(barrier, inc=1, device_id=peer, device_id_type=MESH)
    pl.semaphore_wait(barrier, len(peers))


def rms_back(values, grad, gain):
    r = lax.rsqrt(jnp.mean(values * values, axis=-1, keepdims=True) + EPS)
    n = values * r
    dyg = grad * gain
    return (
        r * (dyg - n * jnp.mean(dyg * n, axis=-1, keepdims=True)),
        jnp.sum(grad * n, axis=0, keepdims=True),
    )


def stack_heads(values):
    return jnp.concatenate([values[:, h * HD : (h + 1) * HD] for h in range(NH)], axis=0)


def turn_back(grad, cos_table, sin_table):
    left, right = grad[:, : HD // 2], grad[:, HD // 2 :]
    return jnp.concatenate(
        [left * cos_table + right * sin_table, right * cos_table - left * sin_table], axis=1
    )


def front_kernel(
    qkv_ref, wo_ref, ffn_ref, tok_ref, seg_ref, seg_col, table_ref,
    qkv_out, wo_all, ffn_all, gains_ref, qk_ref, normed_ref, proj_ref, q_ref, pair_ref, att_ref,
    attn_ref, mid_ref, low_ref, bias_ref, turn_ref,
    qkv_all, seg_in,
    l_sem, s1, r1, s2, r2, sd, rd, s1f, r1f, s2f, r2f, skv, rkv, ssg, rsg,
):
    f32, bf = jnp.float32, jnp.bfloat16
    y, z, chip, core = place()
    a, b, block = shape_of(y, z, core)
    _, _, block_there = shape_of(y, z, 1 - core)
    q_rows, width = qkv_ref.shape
    o_rows = wo_ref.shape[0]
    q_half, o_half = width // 2, o_rows // 2
    partner = {"ctx": chip * 2 + 1 - core}
    me = chip * 2 + core
    rows = tok_ref.shape[0]
    reach = pair_ref.shape[0] // rows - 1
    members = 2 * (lax.axis_size("ctx") // 2)

    def member(k):
        return {"ctx": lax.rem(me + k, members)}

    def views(f, half):
        return (
            qkv_all.at[
                pl.ds(pl.multiple_of(f * q_rows, 16), q_rows),
                pl.ds(pl.multiple_of(half * q_half, 128), q_half),
            ],
            wo_all.at[pl.ds(pl.multiple_of(f * o_rows + half * o_half, 16), o_half), :],
        )

    mine = (
        qkv_ref.at[:, pl.ds(pl.multiple_of(core * q_half, 128), q_half)],
        wo_ref.at[pl.ds(pl.multiple_of(core * o_half, 16), o_half), :],
    )
    here = block(a, b)
    locals_ = [
        pltpu.make_async_copy(
            qkv_ref, qkv_all.at[pl.ds(pl.multiple_of(here * q_rows, 16), q_rows), :], l_sem.at[0]
        ),
        pltpu.make_async_copy(
            wo_ref, wo_all.at[pl.ds(pl.multiple_of(here * o_rows, 16), o_rows), :], l_sem.at[1]
        ),
        pltpu.make_async_copy(ffn_ref, ffn_all.at[here], l_sem.at[2]),
        pltpu.make_async_copy(table_ref.at[me], turn_ref, l_sem.at[3]),
    ]
    for copy in locals_:
        copy.start()

    def first_peer(k):
        return {"fsdp": block(lax.rem(a + k, 4), b)}

    def second_peer(k):
        return {"fsdp": block(a, lax.rem(b + k, 4))}

    greet(
        [first_peer(k) for k in (1, 2, 3)]
        + [second_peer(k) for k in (1, 2, 3)]
        + [member(k) for k in range(1, members)]
    )

    def seg_send(d):
        return remote(
            seg_ref, seg_in.at[reach - d], ssg.at[d - 1], rsg.at[d - 1], member(d)
        )

    def ffn_one(k):
        return remote(ffn_ref, ffn_all.at[here], s1f.at[k], r1f.at[4 - k], first_peer(k))

    def ffn_block(j, m):
        return ffn_all.at[block(lax.rem(a + j, 4), lax.rem(b + m, 4))]

    def ffn_two(j, k):
        dst = ffn_block(j, 0)
        src = dst if j else ffn_ref
        return remote(src, dst, s2f.at[j, k], r2f.at[j, 4 - k], second_peer(k))

    def ffn_pass(j):
        dst, k = (ffn_block(j, 3), 1) if j < 2 else (ffn_block(j, 1), 3)
        return remote(dst, dst, s2f.at[j, 2], r2f.at[j, 2], second_peer(k))

    def ffn_got(j, m):
        dst = ffn_block(j, m)
        sems = (s1f.at[j], r1f.at[j]) if m == 0 else (s2f.at[j, m], r2f.at[j, m])
        return remote(dst, dst, *sems, partner)

    def hop_one(k, t):
        return remote(mine[t], views(here, core)[t], s1.at[k, t], r1.at[4 - k, t], first_peer(k))

    def hop_two(j, k, t):
        f = block(lax.rem(a + j, 4), b)
        dst = views(f, core)[t]
        src = dst if j else mine[t]
        return remote(src, dst, s2.at[j, k, t], r2.at[j, 4 - k, t], second_peer(k))

    def arrive_one(j, t):
        dst = views(block(lax.rem(a + j, 4), b), core)[t]
        return remote(dst, dst, s1.at[j, t], r1.at[j, t], partner)

    def arrive_two(j, m, t):
        dst = views(block(lax.rem(a + j, 4), lax.rem(b + m, 4)), core)[t]
        return remote(dst, dst, s2.at[j, m, t], r2.at[j, m, t], partner)

    def cross(j, m, t):
        dst = views(block(lax.rem(a + j, 4), lax.rem(b + m, 4)), core)[t]
        return remote(dst, dst, sd.at[j, m, t], rd.at[j, m, t], partner)

    def arrive_cross(j, m, t):
        dst = views(block_there(lax.rem(b + j, 4), lax.rem(a + m, 4)), 1 - core)[t]
        return remote(dst, dst, sd.at[j, m, t], rd.at[j, m, t], partner)

    both = (0, 1)
    for k in (1, 3, 2):
        for t in both:
            hop_one(k, t).start()
    for k in (1, 3, 2):
        for t in both:
            hop_two(0, k, t).start()
    for j in (1, 3, 2):
        for t in both:
            arrive_one(j, t).wait_recv()
            for k in (1, 3, 2):
                hop_two(j, k, t).start()
            cross(j, 0, t).start()

    for d in range(1, reach + 1):
        seg_send(d).start()
    for k in (1, 3, 2):
        ffn_one(k).start()
    for k in (1, 3):
        ffn_two(0, k).start()

    def pass_on(i, carry):
        m, j = i // 4 + 1, lax.rem(i, 4)
        for t in both:
            arrive_two(j, m, t).wait_recv()
            cross(j, m, t).start()
        return carry

    lax.fori_loop(0, 12, pass_on, 0)

    def land(i, carry):
        m, j = i // 4, lax.rem(i, 4)
        for t in both:
            arrive_cross(j, m, t).wait_recv()
            cross(j, m, t).wait_send()
        return carry

    lax.fori_loop(1, 16, land, 0)
    for copy in locals_:
        copy.wait()
    for k in (1, 2, 3):
        for t in both:
            hop_one(k, t).wait_send()
            for j in range(4):
                hop_two(j, k, t).wait_send()

    keep = qkv_out.shape[0] // 16
    extra = jnp.zeros((q_rows - keep, width), f32)
    for f in range(0, 16, 2):
        left = qkv_all[pl.ds(f * q_rows, q_rows), :].astype(f32)
        right = qkv_all[pl.ds((f + 1) * q_rows, q_rows), :].astype(f32)
        qkv_out[pl.ds(f * keep, 2 * keep), :] = jnp.concatenate(
            [left[:keep], right[:keep]], axis=0
        ).astype(bf)
        extra = extra + left[keep:] + right[keep:]
    gains = extra[:4, :D]
    gains_ref[...] = gains
    qk_ref[...] = extra[4:6, :HD]

    stream = tok_ref[...].astype(f32)
    normed_ref[...] = rms_norm(stream, gains[0:1]).astype(bf)
    proj_ref[...] = dot32(normed_ref[...], qkv_out[...], NN)
    cos_table, sin_table = turn_ref[:, : HD // 2], turn_ref[:, HD // 2 :]

    def turn(values, gain, cos_part, sin_part):
        values = rms_norm(values, gain)
        left, right = values[:, : HD // 2], values[:, HD // 2 :]
        return jnp.concatenate(
            [left * cos_part - right * sin_part, right * cos_part + left * sin_part], axis=1
        ).astype(bf)

    own = pl.ds(reach * rows, rows)
    pair_ref[own, :HD] = turn(
        proj_ref[:, NH * HD : NH * HD + HD], extra[5:6, :HD], cos_table, sin_table
    )
    pair_ref[own, HD:] = proj_ref[:, NH * HD + HD :].astype(bf)

    def kv_send(d):
        return remote(
            pair_ref.at[own],
            pair_ref.at[pl.ds((reach - d) * rows, rows)],
            skv.at[d - 1], rkv.at[d - 1], member(d),
        )

    for d in range(1, reach + 1):
        kv_send(d).start()
    for j in (1, 3, 2):
        ffn_got(j, 0).wait_recv()
        for k in (1, 3):
            ffn_two(j, k).start()
    queries = turn(
        stack_heads(proj_ref[:, : NH * HD]),
        extra[4:5, :HD],
        jnp.concatenate([cos_table] * NH, axis=0),
        jnp.concatenate([sin_table] * NH, axis=0),
    )
    for h in range(NH):
        q_ref[:, h * HD : (h + 1) * HD] = queries[h * rows : (h + 1) * rows]

    for d in range(1, reach + 1):
        seg_send(d).wait_recv()
    seg_in[reach] = seg_ref[...]
    key_seg = jnp.concatenate([seg_in[p][0:1, :] for p in range(reach + 1)], axis=1)
    shape = (rows, (reach + 1) * rows)
    spacing = (
        reach * rows + lax.broadcasted_iota(jnp.int32, shape, 0)
        - lax.broadcasted_iota(jnp.int32, shape, 1)
    )
    begun = lax.broadcasted_iota(jnp.int32, shape, 1) + (me - reach) * rows >= 0
    allowed = (spacing >= 0) & (spacing < WINDOW) & begun & (seg_col[...] == key_seg)
    bias_ref[...] = jnp.where(allowed, 0.0, NEG_FILL)
    for d in range(1, reach + 1):
        kv_send(d).wait_recv()
    scores = dot32(queries, pair_ref[:, :HD], NT) * (HD ** (-0.5)) + jnp.concatenate(
        [bias_ref[...]] * NH, axis=0
    )
    expo = jnp.exp(scores - jnp.max(scores, axis=-1, keepdims=True))
    probs = expo / jnp.sum(expo, axis=-1, keepdims=True)
    heads = dot32(probs.astype(bf), pair_ref[:, HD:], NN).astype(bf)
    for h in range(NH):
        att_ref[:, h * HD : (h + 1) * HD] = heads[h * rows : (h + 1) * rows]
    attn = dot32(att_ref[...], wo_all[...], NN)
    attn_ref[...] = attn
    mid = stream + rms_norm(attn, gains[1:2])
    mid_ref[...] = mid
    low_ref[...] = rms_norm(mid, gains[2:3]).astype(bf)

    for j in range(4):
        ffn_got(j, 3 if j < 2 else 1).wait_recv()
        ffn_pass(j).start()
    for j in range(4):
        ffn_got(j, 1 if j < 2 else 3).wait_recv()
        ffn_got(j, 2).wait_recv()
    for j in range(4):
        ffn_pass(j).wait_send()
        for k in (1, 3):
            ffn_two(j, k).wait_send()
    for k in (1, 2, 3):
        ffn_one(k).wait_send()
    for d in range(1, reach + 1):
        seg_send(d).wait_send()
        kv_send(d).wait_send()


def front(qkv_shard, wo_shard, ffn_shard, tokens, seg_rows, seg_col, table, keep):
    f32, bf = jnp.float32, jnp.bfloat16
    vm = pl.BlockSpec(memory_space=pltpu.VMEM)
    hbm = pl.BlockSpec(memory_space=pl.ANY)
    dma = pltpu.SemaphoreType.DMA
    q_rows, width = qkv_shard.shape
    o_rows, o_width = wo_shard.shape
    rows = tokens.shape[0]
    reach = min(-(-(WINDOW - 1) // rows), lax.axis_size("ctx") - 1)
    pairs = (reach + 1) * rows
    shapes = (
        ((16 * keep, width), bf),
        ((16 * o_rows, o_width), bf),
        ((16, *ffn_shard.shape), bf),
        ((4, D), f32),
        ((2, HD), f32),
        ((rows, D), bf),
        ((rows, width), f32),
        ((rows, NH * HD), bf),
        ((pairs, 2 * HD), bf),
        ((rows, NH * HD), bf),
        ((rows, D), f32),
        ((rows, D), f32),
        ((rows, D), bf),
        ((rows, pairs), f32),
        ((rows, HD), f32),
    )
    return pl.pallas_call(
        front_kernel,
        out_shape=tuple(jax.ShapeDtypeStruct(*s) for s in shapes),
        in_specs=[vm, vm, hbm, vm, vm, vm, hbm],
        out_specs=(vm, vm, hbm) + (vm,) * (len(shapes) - 3),
        scratch_shapes=[
            pltpu.VMEM((16 * q_rows, width), bf),
            pltpu.VMEM((reach + 1, 8, rows), jnp.int32),
            dma((4,)),
            dma((4, 2)), dma((4, 2)),
            dma((4, 4, 2)), dma((4, 4, 2)),
            dma((4, 4, 2)), dma((4, 4, 2)),
            dma((4,)), dma((4,)),
            dma((4, 4)), dma((4, 4)),
            dma((reach,)), dma((reach,)),
            dma((reach,)), dma((reach,)),
        ],
        compiler_params=pltpu.CompilerParams(
            collective_id=2, has_side_effects=True, vmem_limit_bytes=62 * 1024 * 1024
        ),
        cost_estimate=pl.CostEstimate(
            flops=6 * rows * width * D, bytes_accessed=64 * q_rows * width, transcendentals=0
        ),
    )(qkv_shard, wo_shard, ffn_shard, tokens, seg_rows, seg_col, table)


def back_kernel(
    gff, gn_ref, mid_ref, attn_ref, cot_ref, tok_ref, gains_ref, qk_ref, proj_ref, q_ref,
    pair_ref, att_ref, normed_ref, turn_ref, bias_ref, g3_ref, qkv_hbm, wo_hbm,
    gt_ref, oq_out, tail_out, oo_ref, all_ff,
    qkv_ref, wo_ref, oq_ref, own_ff, far_own, far_in, in1_ff, t_ff, in2_ff, kv_snd, kv_in, gmid, gpair, gproj, tail,
    stage, go, dq, do, sq, so, iq1, io1, tq, to, iq2, io2, xq, xo,
    l_sem, sfar, rfar, s1f, r1f, s2f, r2f, sag, rag, skv, rkv,
    sd, rd, s1, r1, s2, r2, sx, rx, sf, rf,
):
    y, z, chip, core = place()
    a, b, block = shape_of(y, z, core)
    _, _, block_there = shape_of(y, z, 1 - core)
    me = chip * 2 + core
    rows = gn_ref.shape[0]
    q_rows, width = oq_ref.shape
    keep = normed_ref.shape[1] // 16
    o_rows = oo_ref.shape[0]
    q_half, o_half = width // 2, o_rows // 2
    chips = xq.shape[0]
    members = 2 * chips
    reach = kv_in.shape[0]
    scale = HD ** (-0.5)
    f32, bf = jnp.float32, jnp.bfloat16
    partner = {"ctx": chip * 2 + 1 - core}

    def first_peer(k):
        return {"fsdp": block(lax.rem(a + k, 4), b)}

    def second_peer(k):
        return {"fsdp": block(a, lax.rem(b + k, 4))}

    def chip_peer(k):
        return {"ctx": lax.rem(chip + k, chips) * 2 + core}

    def member(k):
        return {"ctx": lax.rem(me + k, members)}

    def q_cols(half):
        return pl.ds(pl.multiple_of(half * q_half, 128), q_half)

    def o_lines(half):
        return pl.ds(pl.multiple_of(half * o_half, 16), o_half)

    def line(k):
        return lax.rem(a + k, 4)

    own_loads = [
        pltpu.make_async_copy(gff.at[block(a, j)], own_ff.at[j], l_sem.at[j]) for j in range(4)
    ] + [
        pltpu.make_async_copy(
            gff.at[block(line(1 if j < 2 else 3), j)], far_own.at[j], l_sem.at[4 + j]
        )
        for j in range(4)
    ]
    weight_loads = [
        pltpu.make_async_copy(wo_hbm, wo_ref, l_sem.at[8]),
        pltpu.make_async_copy(qkv_hbm, qkv_ref, l_sem.at[9]),
    ]
    for copy in own_loads + weight_loads:
        copy.start()
    greet(
        [first_peer(k) for k in (1, 2, 3)]
        + [second_peer(k) for k in (1, 2, 3)]
        + [member(k) for k in range(1, members)]
    )

    def ff_far(j):
        k = 1 if j < 2 else 3
        return remote(
            gff.at[block(line(2), j)], far_in.at[j], sfar.at[j], rfar.at[j], first_peer(k)
        )

    def ff_near(k, j):
        side = 0 if k == 1 else 1
        direct = (j >= 2) == (k == 1)
        src = gff.at[block(line(k), j)] if direct else far_own.at[j]
        return remote(src, in1_ff.at[side, j], s1f.at[side, j], r1f.at[side, j], first_peer(k))

    for j in (0, 2, 1, 3):
        ff_far(j).start()
    for k, j in ((1, 2), (3, 0), (1, 3), (3, 1)):
        ff_near(k, j).start()

    def pass_far(js):
        for j in js:
            ff_far(j).wait_recv()
            own_loads[4 + j].wait()
            far_own[j] = (far_own[j].astype(f32) + far_in[j].astype(f32)).astype(bf)
            ff_near(1 if j < 2 else 3, j).start()

    for copy in weight_loads[:1]:
        copy.wait()

    grad_final = cot_ref[...].astype(f32)
    part, gain_two = rms_back(mid_ref[...], gn_ref[...], gains_ref[2:3, :])
    grad_mid = grad_final + part
    gmid[...] = grad_mid
    grad_attn, gain_one = rms_back(attn_ref[...], grad_mid, gains_ref[1:2, :])
    grad_attn_low = grad_attn.astype(bf)
    grad_attended = dot32(grad_attn_low, wo_ref[...], NT).astype(bf)

    def out_tile(t, carry):
        cols = pl.ds(pl.multiple_of(t * 256, 256), 256)
        go[pl.ds(t * 4, 4)] = (
            dot32(att_ref[:, cols], grad_attn_low, TN).reshape(4, 64, D).astype(bf)
        )
        return carry

    lax.fori_loop(0, NH * HD // 256, out_tile, 0)

    def away(i, t):
        k, j = lax.rem(i // 4 + 1, 4), lax.rem(i, 4)
        there = lax.rem(b + k, 4)
        f = block_there(there, j)
        slot = there * 4 + j
        if t == 0:
            src, dst = stage.at[f, :, q_cols(1 - core)], dq.at[slot]
        else:
            src, dst = go.at[f, o_lines(1 - core), :], do.at[slot]
        return remote(src, dst, sd.at[i, t], rd.at[i, t], partner)

    def home(i, t):
        k, j = lax.rem(i // 4 + 1, 4), lax.rem(i, 4)
        slot = lax.rem(a + k, 4) * 4 + j
        dst = (dq, do)[t].at[slot]
        return remote(dst, dst, sd.at[i, t], rd.at[i, t], partner)

    def start_away(t):
        def one(i, carry):
            away(i, t).start()
            return carry

        lax.fori_loop(0, 16, one, 0)

    start_away(1)

    keys, vals = pair_ref[:, :HD], pair_ref[:, HD:]
    queries = stack_heads(q_ref[...])
    grad_heads = stack_heads(grad_attended)
    scores = dot32(queries, keys, NT) * scale + jnp.concatenate([bias_ref[...]] * NH, axis=0)
    expo = jnp.exp(scores - jnp.max(scores, axis=-1, keepdims=True))
    probs = expo / jnp.sum(expo, axis=-1, keepdims=True)
    grad_probs = dot32(grad_heads, vals, NT)
    row_total = jnp.sum(probs * grad_probs, axis=-1, keepdims=True)
    grad_scores = (probs * (grad_probs - row_total)).astype(bf)
    gpair[:, HD:] = dot32(probs.astype(bf), grad_heads, TN)
    gpair[:, :HD] = dot32(grad_scores, queries, TN) * scale

    def kv_send(d):
        return remote(
            kv_snd.at[d - 1], kv_in.at[d - 1], skv.at[d - 1], rkv.at[d - 1], member(members - d)
        )

    for d in range(1, reach + 1):
        kv_snd[d - 1] = gpair[pl.ds((reach - d) * rows, rows), :].astype(bf)
        kv_send(d).start()

    pass_far((0, 2))
    cos_table, sin_table = turn_ref[:, : HD // 2], turn_ref[:, HD // 2 :]
    cos_all = jnp.concatenate([cos_table] * NH, axis=0)
    sin_all = jnp.concatenate([sin_table] * NH, axis=0)
    grad_queries = dot32(grad_scores, keys, NN) * scale
    grad_q, qk_gain_q = rms_back(
        stack_heads(proj_ref[:, : NH * HD]),
        turn_back(grad_queries, cos_all, sin_all),
        qk_ref[0:1, :],
    )
    for h in range(NH):
        gproj[:, h * HD : (h + 1) * HD] = grad_q[h * rows : (h + 1) * rows].astype(bf)

    def hop_one(k, t):
        src, dst = ((sq, iq1), (so, io1))[t]
        return remote(
            src.at[pl.ds(line(k) * 4, 4)], dst.at[3 - k], s1.at[k, t], r1.at[4 - k, t], first_peer(k)
        )

    def fold_cores(t):
        for k in (1, 2, 3, 0):
            def add(j, carry, k=k):
                slot = line(k) * 4 + j
                f = block(line(k), j)
                home((k + 3) % 4 * 4 + j, t).wait_recv()
                if t == 0:
                    sq[slot] = (
                        stage[f, :, q_cols(core)].astype(f32) + dq[slot].astype(f32)
                    ).astype(bf)
                else:
                    so[slot] = (
                        go[f, o_lines(core), :].astype(f32) + do[slot].astype(f32)
                    ).astype(bf)
                return carry

            lax.fori_loop(0, 4, add, 0)
            if k:
                hop_one(k, t).start()

    pass_far((1, 3))

    total = gpair[pl.ds(reach * rows, rows), :]
    for d in range(1, reach + 1):
        kv_send(d).wait_recv()
        total = total + kv_in[d - 1].astype(f32)
    grad_k, qk_gain_k = rms_back(
        proj_ref[:, NH * HD : NH * HD + HD],
        turn_back(total[:, :HD], cos_table, sin_table),
        qk_ref[1:2, :],
    )
    gproj[:, NH * HD : NH * HD + HD] = grad_k.astype(bf)
    gproj[:, NH * HD + HD :] = total[:, HD:].astype(bf)
    for copy in weight_loads[1:]:
        copy.wait()
    stream = tok_ref[...].astype(f32)
    grad_in, gain_zero = rms_back(stream, dot32(gproj[...], qkv_ref[...], NT), gains_ref[0:1, :])
    gt_ref[...] = gmid[...] + grad_in
    tail[...] = jnp.zeros_like(tail)
    for i, total_gain in enumerate((gain_zero, gain_one, gain_two, g3_ref[...])):
        tail[i : i + 1, :D] = total_gain
    tail[4:5, :HD] = qk_gain_q
    tail[5:6, :HD] = qk_gain_k

    def qkv_tile(t, carry):
        cols = pl.ds(pl.multiple_of(t * 256, 256), 256)
        res = dot32(normed_ref[...], gproj[:, cols], TN)
        low = tail[:, cols]
        for f in range(16):
            stage[f, :, cols] = jnp.concatenate(
                [res[f * keep : (f + 1) * keep], low], axis=0
            ).astype(bf)
        return carry

    lax.fori_loop(0, width // 256, qkv_tile, 0)
    start_away(0)

    for copy in own_loads[:4]:
        copy.wait()

    def ff_two(k):
        return remote(
            t_ff.at[lax.rem(b + k, 4)], in2_ff.at[3 - k], s2f.at[k], r2f.at[4 - k], second_peer(k)
        )

    for k in (2, 1, 3, 0):
        j = lax.rem(b + k, 4)
        for m in (0, 1):
            dst = in1_ff.at[m, j]
            remote(dst, dst, s1f.at[m, j], r1f.at[m, j], partner).wait_recv()
        total = own_ff[j].astype(f32)
        for m in (0, 1):
            total = total + in1_ff[m, j].astype(f32)
        t_ff[j] = total.astype(bf)
        if k:
            ff_two(k).start()

    fold_cores(1)
    fold_cores(0)

    def hop_two(k, t):
        src, dst = ((tq, iq2), (to, io2))[t]
        return remote(
            src.at[lax.rem(b + k, 4)], dst.at[3 - k], s2.at[k, t], r2.at[4 - k, t], second_peer(k)
        )

    for k in (1, 3, 2):
        ff_two(4 - k).wait_recv()
    total = t_ff[b].astype(f32)
    for m in range(3):
        total = total + in2_ff[m].astype(f32)
    all_ff[me] = total.astype(bf)

    half = all_ff.shape[1] // 2

    def ff_slot(k, there=0):
        return lax.rem(chip + k, chips) * 2 + (1 - core if there else core)

    def ff_all(k):
        peer = chip_peer(k) if k else partner
        return remote(
            all_ff.at[me], all_ff.at[me], sag.at[k], rag.at[(chips - k) % chips], peer
        )

    def ff_from(k):
        dst = all_ff.at[ff_slot(k)]
        return remote(dst, dst, sag.at[k], rag.at[k], partner)

    def ff_half(k, h, there=0):
        return all_ff.at[ff_slot(k, there), pl.ds(h * half, half), :]

    def ff_on(k):
        h = 0 if k == 3 else 1
        dst = ff_half(k, h)
        return remote(dst, dst, sag.at[8 + h], rag.at[8 + h], chip_peer(4 - k))

    def ff_far_got(h):
        dst = ff_half(2, h)
        return remote(dst, dst, sag.at[8 + h], rag.at[8 + h], partner)

    def ff_cross(k, h=None, there=0):
        if h is None:
            dst, i = all_ff.at[ff_slot(k, there)], 4 + k
        else:
            dst, i = ff_half(2, h, there), 10 + h
        return remote(dst, dst, sag.at[i], rag.at[i], partner)

    for k in (1, 3, 0):
        ff_all(k).start()

    for t in (1, 0):
        own, got, dst = ((sq, iq1, tq), (so, io1, to))[t]
        for k in (1, 3, 2):
            hop_one(4 - k, t).wait_recv()
        for k in (2, 1, 3, 0):
            j = lax.rem(b + k, 4)
            total = own[a * 4 + j].astype(f32)
            for m in range(3):
                total = total + got[m, j].astype(f32)
            dst[j] = total.astype(bf)
            if k:
                hop_two(k, t).start()

    for k in (1, 3):
        ff_from(k).wait_recv()
        ff_on(k).start()
        ff_cross(k).start()

    def hop_chip(k, t):
        buf = (xq, xo)[t]
        return remote(
            buf.at[chip], buf.at[chip], sx.at[k, t], rx.at[chips - k, t], chip_peer(k)
        )

    for t in (1, 0):
        own, got, dst = ((tq, iq2, xq), (to, io2, xo))[t]
        for k in (1, 3, 2):
            hop_two(4 - k, t).wait_recv()
        total = own[b].astype(f32)
        for m in range(3):
            total = total + got[m].astype(f32)
        dst[chip] = total.astype(bf)
        for k in range(1, chips):
            hop_chip(k, t).start()

    def last(t, half):
        part = (oq_ref.at[:, q_cols(half)], oo_ref.at[o_lines(half), :])[t]
        return remote(part, part, sf.at[t], rf.at[t], partner)

    for h in (0, 1):
        ff_far_got(h).wait_recv()
        ff_cross(2, h).start()

    for t in (1, 0):
        buf = (xq, xo)[t]
        for k in range(1, chips):
            dst = buf.at[lax.rem(chip + k, chips)]
            remote(dst, dst, sx.at[k, t], rx.at[k, t], partner).wait_recv()
        total = buf[0].astype(f32)
        for m in range(1, chips):
            total = total + buf[m].astype(f32)
        if t == 0:
            oq_ref[:, q_cols(core)] = total
        else:
            oo_ref[o_lines(core), :] = total
        last(t, core).start()

    everywhere = all_ff.at[ff_slot(0, 1)]
    remote(everywhere, everywhere, sag.at[0], rag.at[0], partner).wait_recv()
    for k in (1, 3):
        ff_cross(k, there=1).wait_recv()
    for h in (0, 1):
        ff_cross(2, h, there=1).wait_recv()

    def end_away(i, carry):
        for t in (0, 1):
            away(i, t).wait_send()
        return carry

    lax.fori_loop(0, 16, end_away, 0)
    for j in range(4):
        ff_far(j).wait_send()
        ff_near(1, j).wait_send()
        ff_near(3, j).wait_send()
    for k in (1, 2, 3):
        ff_two(k).wait_send()
    for d in range(1, reach + 1):
        kv_send(d).wait_send()
    for k in (1, 3, 0):
        ff_all(k).wait_send()
    for k in (1, 3):
        ff_on(k).wait_send()
        ff_cross(k).wait_send()
    for h in (0, 1):
        ff_cross(2, h).wait_send()
    for t in (0, 1):
        for k in (1, 2, 3):
            hop_one(k, t).wait_send()
            hop_two(k, t).wait_send()
        for k in range(1, chips):
            hop_chip(k, t).wait_send()
        last(t, core).wait_send()
        last(t, 1 - core).wait_recv()
    oq_out[...] = oq_ref[:keep, :]
    tail_out[...] = oq_ref[keep:, :]


def backward_rest(gff, values, weights, keep):
    f32, bf = jnp.float32, jnp.bfloat16
    vm = pl.BlockSpec(memory_space=pltpu.VMEM)
    hbm = pl.BlockSpec(memory_space=pl.ANY)
    dma = pltpu.SemaphoreType.DMA
    rows = values[0].shape[0]
    owners, ff_rows = gff.shape[:2]
    q_rows, width = keep + 8, (NH + 2) * HD
    o_rows, o_width = NH * HD // owners, D
    q_half, o_half = width // 2, o_rows // 2
    chips = lax.axis_size("ctx") // 2
    pairs = values[9].shape[0]
    reach = pairs // rows - 1

    def two(*lead):
        return [pltpu.VMEM(lead + (q_rows, q_half), bf), pltpu.VMEM(lead + (o_half, o_width), bf)]

    def ff(*lead):
        return pltpu.VMEM(lead + (ff_rows, D), bf)

    return pl.pallas_call(
        back_kernel,
        out_shape=(
            jax.ShapeDtypeStruct((rows, D), f32),
            jax.ShapeDtypeStruct((keep, width), f32),
            jax.ShapeDtypeStruct((8, width), f32),
            jax.ShapeDtypeStruct((o_rows, o_width), f32),
            jax.ShapeDtypeStruct((2 * chips, ff_rows, D), bf),
        ),
        in_specs=[hbm] + [vm] * len(values) + [hbm] * 2,
        out_specs=(vm,) * 5,
        scratch_shapes=[
            pltpu.VMEM((16 * keep, width), bf),
            pltpu.VMEM((16 * o_rows, o_width), bf),
            pltpu.VMEM((q_rows, width), f32),
            ff(4), ff(4), ff(4), ff(2, 4), ff(4), ff(3),
            pltpu.VMEM((reach, rows, 2 * HD), bf),
            pltpu.VMEM((reach, rows, 2 * HD), bf),
            pltpu.VMEM((rows, D), f32),
            pltpu.VMEM((pairs, 2 * HD), f32),
            pltpu.VMEM((rows, width), bf),
            pltpu.VMEM((8, width), f32),
            pltpu.VMEM((16, q_rows, width), bf),
            pltpu.VMEM((16, o_rows, o_width), bf),
            *two(16), *two(16), *two(3, 4), *two(4), *two(3), *two(chips),
            dma((10,)),
            dma((4,)), dma((4,)),
            dma((2, 4)), dma((2, 4)),
            dma((4,)), dma((4,)),
            dma((12,)), dma((12,)),
            dma((reach,)), dma((reach,)),
            dma((16, 2)), dma((16, 2)),
            dma((4, 2)), dma((4, 2)),
            dma((4, 2)), dma((4, 2)),
            dma((4, 2)), dma((4, 2)),
            dma((2,)), dma((2,)),
        ],
        compiler_params=pltpu.CompilerParams(
            collective_id=3, has_side_effects=True, vmem_limit_bytes=62 * 1024 * 1024
        ),
        cost_estimate=pl.CostEstimate(
            flops=12 * rows * width * D, bytes_accessed=64 * ff_rows * D, transcendentals=0
        ),
    )(gff, *values, *weights)


def finish_kernel(
    all_hbm, gt_hbm, oq_hbm, oo_hbm, out_hbm,
    og, ou, od, gt, oq, oo, out,
    buf, wide, i_sem, o_sem,
):
    through = [
        pltpu.make_async_copy(src, dst, o_sem.at[3 + i])
        for i, (src, dst) in enumerate(((gt_hbm, gt), (oq_hbm, oq), (oo_hbm, oo), (out_hbm, out)))
    ]
    members = buf.shape[0]
    share = buf.shape[1] // 3
    lines = wide.shape[1] // members
    loads = [
        pltpu.make_async_copy(
            all_hbm.at[:, pl.ds(i * share, share), :],
            buf.at[:, pl.ds(i * share, share), :],
            i_sem.at[i],
        )
        for i in range(3)
    ]
    for copy in loads + through:
        copy.start()
    stores = []
    for i, dst in enumerate((og, ou, od)):
        loads[i].wait()
        for m in range(members):
            wide[i, m * lines : (m + 1) * lines, :] = buf[
                m, i * share : (i + 1) * share, :
            ].astype(jnp.float32)[:lines]
        store = pltpu.make_async_copy(wide.at[i], dst, o_sem.at[i])
        store.start()
        stores.append(store)
    for copy in through + stores:
        copy.wait()


def finish(all_ff, lines, *rest):
    hbm = pl.BlockSpec(memory_space=pl.ANY)
    weight = jax.ShapeDtypeStruct((lines, D), jnp.float32)
    return pl.pallas_call(
        finish_kernel,
        out_shape=(weight,) * 3 + tuple(jax.ShapeDtypeStruct(r.shape, r.dtype) for r in rest),
        in_specs=[hbm] * (1 + len(rest)),
        out_specs=(hbm,) * (3 + len(rest)),
        scratch_shapes=[
            pltpu.VMEM(all_ff.shape, all_ff.dtype),
            pltpu.VMEM((3, lines, D), jnp.float32),
            pltpu.SemaphoreType.DMA((3,)),
            pltpu.SemaphoreType.DMA((3 + len(rest),)),
        ],
        compiler_params=pltpu.CompilerParams(vmem_limit_bytes=62 * 1024 * 1024),
    )(all_ff, *rest)


def on_device(
    tokens,
    norm_gains,
    qk_gains,
    qkv_weight,
    out_weight,
    gate_weight,
    up_weight,
    down_weight,
    segments,
    cotangent,
):
    local_len = tokens.shape[1]
    ctx_index = lax.axis_index("ctx")
    owner = lax.axis_index("fsdp")
    ctx_size = lax.axis_size("ctx")
    own_rows = gate_weight.shape[0]
    slice_rows = own_rows // ctx_size
    padded = -(-slice_rows // 16) * 16
    keep, width = qkv_weight.shape
    gain_lines, qk_lines = norm_gains.shape, qk_gains.shape
    def placed(lines):
        count, own = lines.shape
        room = (lax.axis_size("fsdp") - 1) * own
        padded_lines = jnp.pad(lines, ((0, 0), (room, room)))
        spread = lax.dynamic_slice(padded_lines, (0, room - owner * own), (count, room + own))
        return jnp.pad(spread, ((0, 0), (0, width - room - own)))

    gain_rows = jnp.concatenate(
        [placed(norm_gains), placed(qk_gains), jnp.zeros((2, width), jnp.bfloat16)], axis=0
    )

    def my_slice(weight):
        part = lax.dynamic_slice(weight, (ctx_index * slice_rows, 0), (slice_rows, D))
        return jnp.pad(part, ((0, padded - slice_rows), (0, 0)))

    ffn_shard = jnp.concatenate(
        [my_slice(gate_weight), my_slice(up_weight), my_slice(down_weight)], axis=0
    )
    places = np.arange(ctx_size * local_len, dtype=np.float32)
    rates = (ROPE_BASE ** (-(2.0 * np.arange(HD // 2)) / HD)).astype(np.float32)
    angles = (places[:, None] * rates).astype(np.float64)
    table = jnp.asarray(
        np.concatenate([np.cos(angles), np.sin(angles)], axis=1)
        .astype(np.float32)
        .reshape(ctx_size, local_len, HD)
    )
    flat = tokens.reshape(local_len, D)
    cot = cotangent.reshape(local_len, D)
    (
        qkv_full, out_full, ffn_full, gains_all, qk_all, normed, projected, queries, pair_all,
        attended, attn, mid, normed_two, bias, turn_table,
    ) = front(
        jnp.concatenate([qkv_weight, gain_rows], axis=0),
        out_weight,
        ffn_shard,
        flat,
        jnp.broadcast_to(segments, (8, local_len)),
        segments.reshape(local_len, 1),
        table,
        keep,
    )
    output, grad_normed_two, grad_gain_three, ffn_grads = ffn(
        normed_two, mid, cot, gains_all, ffn_full
    )
    grad_tokens, total_qkv, tail, total_out, all_ff = backward_rest(
        ffn_grads,
        (
            grad_normed_two, mid, attn, cot, flat, gains_all, qk_all, projected, queries,
            pair_all, attended, normed, turn_table, bias, grad_gain_three,
        ),
        (qkv_full, out_full),
        keep,
    )
    total_gate, total_up, total_down, grad_tokens, total_qkv, total_out, output = finish(
        all_ff, own_rows, grad_tokens, total_qkv, total_out, output
    )
    total_gains = lax.dynamic_slice(tail, (0, owner * gain_lines[1]), gain_lines)
    total_qk = lax.dynamic_slice(tail, (4, owner * qk_lines[1]), qk_lines)
    return (
        output.reshape(tokens.shape),
        grad_tokens.reshape(tokens.shape),
        total_gains,
        total_qk,
        total_qkv,
        total_out,
        total_gate,
        total_up,
        total_down,
    )


def solution(mesh):
    in_specs = (
        P("fsdp", "ctx", None),
        P(None, "fsdp"),
        P(None, "fsdp"),
        P("fsdp", None),
        P("fsdp", None),
        P("fsdp", None),
        P("fsdp", None),
        P("fsdp", None),
        P("fsdp", "ctx"),
        P("fsdp", "ctx", None),
    )
    out_specs = (
        P("fsdp", "ctx", None),
        P("fsdp", "ctx", None),
        P(None, "fsdp"),
        P(None, "fsdp"),
        P("fsdp", None),
        P("fsdp", None),
        P("fsdp", None),
        P("fsdp", None),
        P("fsdp", None),
    )
    return jax.shard_map(
        on_device, mesh=mesh, in_specs=in_specs, out_specs=out_specs, check_vma=False
    )
```

```python
import jax
import numpy as np
import jax.numpy as jnp
from jax import lax
from jax.experimental import pallas as pl
from jax.experimental.pallas import tpu as pltpu
from jax.sharding import PartitionSpec as P

D = 1152
NH = 4
HD = 256
WINDOW = 512


EPS = 1e-06
ROPE_BASE = 10000.0
NEG_FILL = -1e30


def rms_norm(values, gain_vec):
    return values * lax.rsqrt(jnp.mean(values * values, axis=-1, keepdims=True) + EPS) * gain_vec


MESH = pl.DeviceIdType.MESH
NT = (((1,), (1,)), ((), ()))
NN = (((1,), (0,)), ((), ()))
TN = (((0,), (0,)), ((), ()))
GELU_C = 0.7978845608028654
GELU_A = 0.044715


def dot32(left, right, dims):
    return lax.dot_general(left, right, dims, preferred_element_type=jnp.float32)


def ffn_kernel(
    normed_ref, mid_ref, cot_ref, gain_ref, w_hbm,
    out_ref, gn_ref, ggain_ref, gff_hbm,
    wg, wu, wd, seq, gseq, act_a, act_b, hid, dgate, dup, part, keep, base,
    d2d_snd, d2d_in, ici_snd, ici_in, dw,
    w_sem, o_sem, ag_s, ag_r, rd_s, rd_r, ri_s, ri_r,
):
    rows = normed_ref.shape[0]
    units = wg.shape[0]
    share = units // w_hbm.shape[0]
    tile = 256
    me = lax.axis_index("ctx")
    chip, core = me // 2, lax.rem(me, 2)
    partner = {"ctx": chip * 2 + 1 - core}
    chips = {k: {"ctx": lax.rem(chip + k, 4) * 2 + core} for k in (1, 2, 3)}
    order = (0, 1, 3, 2)

    loads = [
        pltpu.make_async_copy(
            w_hbm.at[f, pl.ds(i * share, share), :], dst.at[pl.ds(f * share, share), :], w_sem.at[i, f]
        )
        for i, dst in enumerate((wg, wu, wd))
        for f in range(w_hbm.shape[0])
    ]
    for load in loads:
        load.start()

    barrier = pltpu.get_barrier_semaphore()
    for peer in (partner, chips[1], chips[2], chips[3]):
        pl.semaphore_signal(barrier, inc=1, device_id=peer, device_id_type=MESH)
    pl.semaphore_wait(barrier, 4)

    started = []

    def send(src, dst, s_sem, r_sem, peer):
        copy = pltpu.make_async_remote_copy(
            src_ref=src, dst_ref=dst, send_sem=s_sem, recv_sem=r_sem,
            device_id=peer, device_id_type=MESH,
        )
        copy.start()
        started.append(copy)
        return copy

    def mine(k):
        return pl.ds(k * 2 * rows, rows)

    def other(k):
        return pl.ds(k * 2 * rows + rows, rows)

    def pair(k):
        return pl.ds(k * 2 * rows, 2 * rows)

    def spread(buf, ph):
        own = buf.at[mine(0)]
        got = {}
        for k in (1, 3):
            back = 4 - k
            got[back] = send(own, buf.at[mine(back)], ag_s.at[ph, k], ag_r.at[ph, back], chips[k])
        got[0] = send(own, buf.at[other(0)], ag_s.at[ph, 0], ag_r.at[ph, 0], partner)
        return got

    def half_of(k, h, offset=0):
        return pl.ds(k * 2 * rows + offset + h * (rows // 2), rows // 2)

    def relay(buf, ph, got, k):
        got[k].wait_recv()
        h = 0 if k == 3 else 1
        got[2, h] = send(
            buf.at[half_of(k, h)], buf.at[half_of(2, h)],
            ag_s.at[ph, 2 + 2 * h], ag_r.at[ph, 2 + 2 * h], chips[4 - k],
        )
        got[k] = send(
            buf.at[mine(k)], buf.at[other(k)], ag_s.at[ph, 4 + k], ag_r.at[ph, 4 + k], partner
        )

    def relay_far(buf, ph, got):
        for h in (0, 1):
            got[2, h].wait_recv()
            got[2, h] = send(
                buf.at[half_of(2, h)], buf.at[half_of(2, h, rows)],
                ag_s.at[ph, 6 + 2 * h], ag_r.at[ph, 6 + 2 * h], partner,
            )

    def swap(ph, k):
        d2d_snd[ph, k] = part[pl.ds(rows, rows), :].astype(jnp.bfloat16)
        keep[order.index(k) % 2] = part[pl.ds(0, rows), :]
        return send(d2d_snd.at[ph, k], d2d_in.at[ph, k], rd_s.at[ph, k], rd_r.at[ph, k], partner)

    def sum_out(ph, k, copy):
        copy.wait_recv()
        total = keep[order.index(k) % 2] + d2d_in[ph, k].astype(jnp.float32)
        if k == 0:
            base[...] = total
            return None
        ici_snd[ph, k - 1] = total.astype(jnp.bfloat16)
        back = 4 - k
        return send(
            ici_snd.at[ph, k - 1], ici_in.at[ph, back - 1], ri_s.at[ph, k], ri_r.at[ph, back],
            chips[k],
        )

    def phase(buf, ph, work):
        got = spread(buf, ph)
        if ph == 0:
            for load in loads:
                load.wait()
        sums = {}
        copy = waiting = None
        for k in order:
            if k == 1:
                relay(buf, ph, got, 1)
                relay(buf, ph, got, 3)
            if k == 2:
                relay_far(buf, ph, got)
                got[2, 0].wait_recv()
                got[2, 1].wait_recv()
            else:
                got[k].wait_recv()
            if waiting is not None and k == 2:
                sums[waiting] = sum_out(ph, waiting, copy)
                waiting = None
            work(k)
            if waiting is not None:
                sums[waiting] = sum_out(ph, waiting, copy)
            copy, waiting = swap(ph, k), k
        sums[waiting] = sum_out(ph, waiting, copy)
        return sums

    def collect(ph, sums):
        total = base[...]
        for k in (1, 3, 2):
            sums[k].wait_recv()
        for k in (1, 2, 3):
            total = total + ici_in[ph, k - 1].astype(jnp.float32)
        return total

    def forward(k):
        def one(t, carry):
            cols = pl.ds(pl.multiple_of(t * tile, tile), tile)
            block = seq[pair(k), :]
            gate = dot32(block, wg[cols, :], NT)
            up = dot32(block, wu[cols, :], NT)
            square = gate * gate
            th = jnp.tanh(GELU_C * gate * (1.0 + GELU_A * square))
            half = 0.5 * (1.0 + th)
            gelu = gate * half
            slope = half + (0.5 * GELU_C) * gate * (1.0 - th * th) * (1.0 + 3.0 * GELU_A * square)
            hid[pair(k), cols] = (gelu * up).astype(jnp.bfloat16)
            act_a[pair(k), cols] = up * slope
            act_b[pair(k), cols] = gelu
            return carry

        lax.fori_loop(0, units // tile, one, 0)
        part[...] = dot32(hid[pair(k), :], wd[...], NN)

    seq[mine(0), :] = normed_ref[...]
    sums = phase(seq, 0, forward)
    mlp = collect(0, sums)
    r = lax.rsqrt(jnp.mean(mlp * mlp, axis=-1, keepdims=True) + EPS)
    n = mlp * r
    gain = gain_ref[3:4, :]
    out_ref[...] = (mid_ref[...] + n * gain).astype(jnp.bfloat16)
    dy = cot_ref[...].astype(jnp.float32)
    ggain_ref[...] = jnp.sum(dy * n, axis=0, keepdims=True)
    dyg = dy * gain
    dv = r * (dyg - n * jnp.mean(dyg * n, axis=-1, keepdims=True))
    gseq[mine(0), :] = dv.astype(jnp.bfloat16)

    def backward(k):
        def one(t, carry):
            cols = pl.ds(pl.multiple_of(t * tile, tile), tile)
            gh = dot32(gseq[pair(k), :], wd[cols, :], NT)
            dgate[pair(k), cols] = (gh * act_a[pair(k), cols]).astype(jnp.bfloat16)
            dup[pair(k), cols] = (gh * act_b[pair(k), cols]).astype(jnp.bfloat16)
            return carry

        lax.fori_loop(0, units // tile, one, 0)
        part[...] = dot32(dgate[pair(k), :], wg[...], NN) + dot32(dup[pair(k), :], wu[...], NN)

    sums = phase(gseq, 1, backward)
    for i, (left, right) in enumerate(((dgate, seq), (dup, seq), (hid, gseq))):
        def one(t, carry, i=i, left=left, right=right):
            cols = pl.ds(pl.multiple_of(t * tile, tile), tile)
            group = tile // share
            dw[pl.ds(t * group, group), pl.ds(i * share, share), :] = (
                dot32(left[:, cols], right[...], TN).reshape(group, share, -1).astype(jnp.bfloat16)
            )
            return carry

        lax.fori_loop(0, units // tile, one, 0)
    store = pltpu.make_async_copy(dw, gff_hbm, o_sem)
    store.start()
    gn_ref[...] = collect(1, sums)
    for copy in started:
        copy.wait_send()
    store.wait()


def ffn(normed_two, mid, cot, gain, weights):
    rows = normed_two.shape[0]
    owners, lines = weights.shape[:2]
    units = owners * lines // 3
    seq_rows = rows * 8
    bf, f32 = jnp.bfloat16, jnp.float32
    vm = pl.BlockSpec(memory_space=pltpu.VMEM)
    hbm = pl.BlockSpec(memory_space=pl.ANY)
    dma = pltpu.SemaphoreType.DMA
    return pl.pallas_call(
        ffn_kernel,
        out_shape=(
            jax.ShapeDtypeStruct((rows, D), bf),
            jax.ShapeDtypeStruct((rows, D), f32),
            jax.ShapeDtypeStruct((1, D), f32),
            jax.ShapeDtypeStruct(weights.shape, bf),
        ),
        in_specs=[vm] * 4 + [hbm],
        out_specs=(vm, vm, vm, hbm),
        scratch_shapes=[
            pltpu.VMEM((units, D), bf),
            pltpu.VMEM((units, D), bf),
            pltpu.VMEM((units, D), bf),
            pltpu.VMEM((seq_rows, D), bf),
            pltpu.VMEM((seq_rows, D), bf),
            pltpu.VMEM((seq_rows, units), f32),
            pltpu.VMEM((seq_rows, units), f32),
            pltpu.VMEM((seq_rows, units), bf),
            pltpu.VMEM((seq_rows, units), bf),
            pltpu.VMEM((seq_rows, units), bf),
            pltpu.VMEM((2 * rows, D), f32),
            pltpu.VMEM((2, rows, D), f32),
            pltpu.VMEM((rows, D), f32),
            pltpu.VMEM((2, 4, rows, D), bf),
            pltpu.VMEM((2, 4, rows, D), bf),
            pltpu.VMEM((2, 3, rows, D), bf),
            pltpu.VMEM((2, 3, rows, D), bf),
            pltpu.VMEM(weights.shape, bf),
            dma((3, owners)), dma,
            dma((2, 10)), dma((2, 10)),
            dma((2, 4)), dma((2, 4)),
            dma((2, 4)), dma((2, 4)),
        ],
        compiler_params=pltpu.CompilerParams(
            collective_id=1, has_side_effects=True, vmem_limit_bytes=62 * 1024 * 1024
        ),
        cost_estimate=pl.CostEstimate(
            flops=18 * seq_rows * units * D, bytes_accessed=14 * units * D, transcendentals=0
        ),
    )(normed_two, mid, cot, gain, weights)


def place():
    fsdp = lax.axis_index("fsdp")
    ctx = lax.axis_index("ctx")
    y, z = fsdp // 4, lax.rem(fsdp, 4)
    chip, core = ctx // 2, lax.rem(ctx, 2)
    return y, z, chip, core


def shape_of(y, z, core):
    first = (1 - core) * y + core * z
    second = (1 - core) * z + core * y

    def block(i, j):
        return (1 - core) * (4 * i + j) + core * (4 * j + i)

    return first, second, block


def remote(src, dst, s_sem, r_sem, peer):
    return pltpu.make_async_remote_copy(
        src_ref=src, dst_ref=dst, send_sem=s_sem, recv_sem=r_sem,
        device_id=peer, device_id_type=MESH,
    )


def greet(peers):
    barrier = pltpu.get_barrier_semaphore()
    for peer in peers:
        pl.semaphore_signal(barrier, inc=1, device_id=peer, device_id_type=MESH)
    pl.semaphore_wait(barrier, len(peers))


def rms_back(values, grad, gain):
    r = lax.rsqrt(jnp.mean(values * values, axis=-1, keepdims=True) + EPS)
    n = values * r
    dyg = grad * gain
    return (
        r * (dyg - n * jnp.mean(dyg * n, axis=-1, keepdims=True)),
        jnp.sum(grad * n, axis=0, keepdims=True),
    )


def stack_heads(values):
    return jnp.concatenate([values[:, h * HD : (h + 1) * HD] for h in range(NH)], axis=0)


def turn_back(grad, cos_table, sin_table):
    left, right = grad[:, : HD // 2], grad[:, HD // 2 :]
    return jnp.concatenate(
        [left * cos_table + right * sin_table, right * cos_table - left * sin_table], axis=1
    )


def front_kernel(
    qkv_ref, wo_ref, ffn_ref, tok_ref, seg_ref, seg_col, table_ref,
    qkv_out, wo_all, ffn_all, gains_ref, qk_ref, normed_ref, proj_ref, q_ref, pair_ref, att_ref,
    attn_ref, mid_ref, low_ref, bias_ref, turn_ref,
    qkv_all, seg_in,
    l_sem, s1, r1, s2, r2, sd, rd, s1f, r1f, s2f, r2f, skv, rkv, ssg, rsg,
):
    f32, bf = jnp.float32, jnp.bfloat16
    y, z, chip, core = place()
    a, b, block = shape_of(y, z, core)
    _, _, block_there = shape_of(y, z, 1 - core)
    q_rows, width = qkv_ref.shape
    o_rows = wo_ref.shape[0]
    q_half, o_half = width // 2, o_rows // 2
    partner = {"ctx": chip * 2 + 1 - core}
    me = chip * 2 + core
    rows = tok_ref.shape[0]
    reach = pair_ref.shape[0] // rows - 1
    members = 2 * (lax.axis_size("ctx") // 2)

    def member(k):
        return {"ctx": lax.rem(me + k, members)}

    def views(f, half):
        return (
            qkv_all.at[
                pl.ds(pl.multiple_of(f * q_rows, 16), q_rows),
                pl.ds(pl.multiple_of(half * q_half, 128), q_half),
            ],
            wo_all.at[pl.ds(pl.multiple_of(f * o_rows + half * o_half, 16), o_half), :],
        )

    mine = (
        qkv_ref.at[:, pl.ds(pl.multiple_of(core * q_half, 128), q_half)],
        wo_ref.at[pl.ds(pl.multiple_of(core * o_half, 16), o_half), :],
    )
    here = block(a, b)
    locals_ = [
        pltpu.make_async_copy(
            qkv_ref, qkv_all.at[pl.ds(pl.multiple_of(here * q_rows, 16), q_rows), :], l_sem.at[0]
        ),
        pltpu.make_async_copy(
            wo_ref, wo_all.at[pl.ds(pl.multiple_of(here * o_rows, 16), o_rows), :], l_sem.at[1]
        ),
        pltpu.make_async_copy(ffn_ref, ffn_all.at[here], l_sem.at[2]),
        pltpu.make_async_copy(table_ref.at[me], turn_ref, l_sem.at[3]),
    ]
    for copy in locals_:
        copy.start()

    def first_peer(k):
        return {"fsdp": block(lax.rem(a + k, 4), b)}

    def second_peer(k):
        return {"fsdp": block(a, lax.rem(b + k, 4))}

    greet(
        [first_peer(k) for k in (1, 2, 3)]
        + [second_peer(k) for k in (1, 2, 3)]
        + [member(k) for k in range(1, members)]
    )

    def seg_send(d):
        return remote(
            seg_ref, seg_in.at[reach - d], ssg.at[d - 1], rsg.at[d - 1], member(d)
        )

    def ffn_one(k):
        return remote(ffn_ref, ffn_all.at[here], s1f.at[k], r1f.at[4 - k], first_peer(k))

    def ffn_block(j, m):
        return ffn_all.at[block(lax.rem(a + j, 4), lax.rem(b + m, 4))]

    def ffn_two(j, k):
        dst = ffn_block(j, 0)
        src = dst if j else ffn_ref
        return remote(src, dst, s2f.at[j, k], r2f.at[j, 4 - k], second_peer(k))

    def ffn_pass(j):
        dst, k = (ffn_block(j, 3), 1) if j < 2 else (ffn_block(j, 1), 3)
        return remote(dst, dst, s2f.at[j, 2], r2f.at[j, 2], second_peer(k))

    def ffn_got(j, m):
        dst = ffn_block(j, m)
        sems = (s1f.at[j], r1f.at[j]) if m == 0 else (s2f.at[j, m], r2f.at[j, m])
        return remote(dst, dst, *sems, partner)

    def hop_one(k, t):
        return remote(mine[t], views(here, core)[t], s1.at[k, t], r1.at[4 - k, t], first_peer(k))

    def hop_two(j, k, t):
        f = block(lax.rem(a + j, 4), b)
        dst = views(f, core)[t]
        src = dst if j else mine[t]
        return remote(src, dst, s2.at[j, k, t], r2.at[j, 4 - k, t], second_peer(k))

    def arrive_one(j, t):
        dst = views(block(lax.rem(a + j, 4), b), core)[t]
        return remote(dst, dst, s1.at[j, t], r1.at[j, t], partner)

    def arrive_two(j, m, t):
        dst = views(block(lax.rem(a + j, 4), lax.rem(b + m, 4)), core)[t]
        return remote(dst, dst, s2.at[j, m, t], r2.at[j, m, t], partner)

    def cross(j, m, t):
        dst = views(block(lax.rem(a + j, 4), lax.rem(b + m, 4)), core)[t]
        return remote(dst, dst, sd.at[j, m, t], rd.at[j, m, t], partner)

    def arrive_cross(j, m, t):
        dst = views(block_there(lax.rem(b + j, 4), lax.rem(a + m, 4)), 1 - core)[t]
        return remote(dst, dst, sd.at[j, m, t], rd.at[j, m, t], partner)

    both = (0, 1)
    for k in (1, 3, 2):
        for t in both:
            hop_one(k, t).start()
    for k in (1, 3, 2):
        for t in both:
            hop_two(0, k, t).start()
    for j in (1, 3, 2):
        for t in both:
            arrive_one(j, t).wait_recv()
            for k in (1, 3, 2):
                hop_two(j, k, t).start()
            cross(j, 0, t).start()

    for d in range(1, reach + 1):
        seg_send(d).start()
    for k in (1, 3, 2):
        ffn_one(k).start()
    for k in (1, 3):
        ffn_two(0, k).start()

    def pass_on(i, carry):
        m, j = i // 4 + 1, lax.rem(i, 4)
        for t in both:
            arrive_two(j, m, t).wait_recv()
            cross(j, m, t).start()
        return carry

    lax.fori_loop(0, 12, pass_on, 0)

    def land(i, carry):
        m, j = i // 4, lax.rem(i, 4)
        for t in both:
            arrive_cross(j, m, t).wait_recv()
            cross(j, m, t).wait_send()
        return carry

    lax.fori_loop(1, 16, land, 0)
    for copy in locals_:
        copy.wait()
    for k in (1, 2, 3):
        for t in both:
            hop_one(k, t).wait_send()
            for j in range(4):
                hop_two(j, k, t).wait_send()

    keep = qkv_out.shape[0] // 16
    extra = jnp.zeros((q_rows - keep, width), f32)
    for f in range(0, 16, 2):
        left = qkv_all[pl.ds(f * q_rows, q_rows), :].astype(f32)
        right = qkv_all[pl.ds((f + 1) * q_rows, q_rows), :].astype(f32)
        qkv_out[pl.ds(f * keep, 2 * keep), :] = jnp.concatenate(
            [left[:keep], right[:keep]], axis=0
        ).astype(bf)
        extra = extra + left[keep:] + right[keep:]
    gains = extra[:4, :D]
    gains_ref[...] = gains
    qk_ref[...] = extra[4:6, :HD]

    stream = tok_ref[...].astype(f32)
    normed_ref[...] = rms_norm(stream, gains[0:1]).astype(bf)
    proj_ref[...] = dot32(normed_ref[...], qkv_out[...], NN)
    cos_table, sin_table = turn_ref[:, : HD // 2], turn_ref[:, HD // 2 :]

    def turn(values, gain, cos_part, sin_part):
        values = rms_norm(values, gain)
        left, right = values[:, : HD // 2], values[:, HD // 2 :]
        return jnp.concatenate(
            [left * cos_part - right * sin_part, right * cos_part + left * sin_part], axis=1
        ).astype(bf)

    own = pl.ds(reach * rows, rows)
    pair_ref[own, :HD] = turn(
        proj_ref[:, NH * HD : NH * HD + HD], extra[5:6, :HD], cos_table, sin_table
    )
    pair_ref[own, HD:] = proj_ref[:, NH * HD + HD :].astype(bf)

    def kv_send(d):
        return remote(
            pair_ref.at[own],
            pair_ref.at[pl.ds((reach - d) * rows, rows)],
            skv.at[d - 1], rkv.at[d - 1], member(d),
        )

    for d in range(1, reach + 1):
        kv_send(d).start()
    for j in (1, 3, 2):
        ffn_got(j, 0).wait_recv()
        for k in (1, 3):
            ffn_two(j, k).start()
    queries = turn(
        stack_heads(proj_ref[:, : NH * HD]),
        extra[4:5, :HD],
        jnp.concatenate([cos_table] * NH, axis=0),
        jnp.concatenate([sin_table] * NH, axis=0),
    )
    for h in range(NH):
        q_ref[:, h * HD : (h + 1) * HD] = queries[h * rows : (h + 1) * rows]

    for d in range(1, reach + 1):
        seg_send(d).wait_recv()
    seg_in[reach] = seg_ref[...]
    key_seg = jnp.concatenate([seg_in[p][0:1, :] for p in range(reach + 1)], axis=1)
    shape = (rows, (reach + 1) * rows)
    spacing = (
        reach * rows + lax.broadcasted_iota(jnp.int32, shape, 0)
        - lax.broadcasted_iota(jnp.int32, shape, 1)
    )
    begun = lax.broadcasted_iota(jnp.int32, shape, 1) + (me - reach) * rows >= 0
    allowed = (spacing >= 0) & (spacing < WINDOW) & begun & (seg_col[...] == key_seg)
    bias_ref[...] = jnp.where(allowed, 0.0, NEG_FILL)
    for d in range(1, reach + 1):
        kv_send(d).wait_recv()
    scores = dot32(queries, pair_ref[:, :HD], NT) * (HD ** (-0.5)) + jnp.concatenate(
        [bias_ref[...]] * NH, axis=0
    )
    expo = jnp.exp(scores - jnp.max(scores, axis=-1, keepdims=True))
    probs = expo / jnp.sum(expo, axis=-1, keepdims=True)
    heads = dot32(probs.astype(bf), pair_ref[:, HD:], NN).astype(bf)
    for h in range(NH):
        att_ref[:, h * HD : (h + 1) * HD] = heads[h * rows : (h + 1) * rows]
    attn = dot32(att_ref[...], wo_all[...], NN)
    attn_ref[...] = attn
    mid = stream + rms_norm(attn, gains[1:2])
    mid_ref[...] = mid
    low_ref[...] = rms_norm(mid, gains[2:3]).astype(bf)

    for j in range(4):
        ffn_got(j, 3 if j < 2 else 1).wait_recv()
        ffn_pass(j).start()
    for j in range(4):
        ffn_got(j, 1 if j < 2 else 3).wait_recv()
        ffn_got(j, 2).wait_recv()
    for j in range(4):
        ffn_pass(j).wait_send()
        for k in (1, 3):
            ffn_two(j, k).wait_send()
    for k in (1, 2, 3):
        ffn_one(k).wait_send()
    for d in range(1, reach + 1):
        seg_send(d).wait_send()
        kv_send(d).wait_send()


def front(qkv_shard, wo_shard, ffn_shard, tokens, seg_rows, seg_col, table, keep):
    f32, bf = jnp.float32, jnp.bfloat16
    vm = pl.BlockSpec(memory_space=pltpu.VMEM)
    hbm = pl.BlockSpec(memory_space=pl.ANY)
    dma = pltpu.SemaphoreType.DMA
    q_rows, width = qkv_shard.shape
    o_rows, o_width = wo_shard.shape
    rows = tokens.shape[0]
    reach = min(-(-(WINDOW - 1) // rows), lax.axis_size("ctx") - 1)
    pairs = (reach + 1) * rows
    shapes = (
        ((16 * keep, width), bf),
        ((16 * o_rows, o_width), bf),
        ((16, *ffn_shard.shape), bf),
        ((4, D), f32),
        ((2, HD), f32),
        ((rows, D), bf),
        ((rows, width), f32),
        ((rows, NH * HD), bf),
        ((pairs, 2 * HD), bf),
        ((rows, NH * HD), bf),
        ((rows, D), f32),
        ((rows, D), f32),
        ((rows, D), bf),
        ((rows, pairs), f32),
        ((rows, HD), f32),
    )
    return pl.pallas_call(
        front_kernel,
        out_shape=tuple(jax.ShapeDtypeStruct(*s) for s in shapes),
        in_specs=[vm, vm, hbm, vm, vm, vm, hbm],
        out_specs=(vm, vm, hbm) + (vm,) * (len(shapes) - 3),
        scratch_shapes=[
            pltpu.VMEM((16 * q_rows, width), bf),
            pltpu.VMEM((reach + 1, 8, rows), jnp.int32),
            dma((4,)),
            dma((4, 2)), dma((4, 2)),
            dma((4, 4, 2)), dma((4, 4, 2)),
            dma((4, 4, 2)), dma((4, 4, 2)),
            dma((4,)), dma((4,)),
            dma((4, 4)), dma((4, 4)),
            dma((reach,)), dma((reach,)),
            dma((reach,)), dma((reach,)),
        ],
        compiler_params=pltpu.CompilerParams(
            collective_id=2, has_side_effects=True, vmem_limit_bytes=62 * 1024 * 1024
        ),
        cost_estimate=pl.CostEstimate(
            flops=6 * rows * width * D, bytes_accessed=64 * q_rows * width, transcendentals=0
        ),
    )(qkv_shard, wo_shard, ffn_shard, tokens, seg_rows, seg_col, table)


def back_kernel(
    gff, gn_ref, mid_ref, attn_ref, cot_ref, tok_ref, gains_ref, qk_ref, proj_ref, q_ref,
    pair_ref, att_ref, normed_ref, turn_ref, bias_ref, g3_ref, qkv_hbm, wo_hbm,
    gt_ref, oq_out, tail_out, oo_ref, all_ff,
    qkv_ref, wo_ref, oq_ref, own_ff, far_own, far_in, in1_ff, t_ff, in2_ff, kv_snd, kv_in, gmid, gpair, gproj, tail,
    stage, go, dq, do, sq, so, iq1, io1, tq, to, iq2, io2, xq, xo,
    l_sem, sfar, rfar, s1f, r1f, s2f, r2f, sag, rag, skv, rkv,
    sd, rd, s1, r1, s2, r2, sx, rx, sf, rf,
):
    y, z, chip, core = place()
    a, b, block = shape_of(y, z, core)
    _, _, block_there = shape_of(y, z, 1 - core)
    me = chip * 2 + core
    rows = gn_ref.shape[0]
    q_rows, width = oq_ref.shape
    keep = normed_ref.shape[1] // 16
    o_rows = oo_ref.shape[0]
    q_half, o_half = width // 2, o_rows // 2
    chips = xq.shape[0]
    members = 2 * chips
    reach = kv_in.shape[0]
    scale = HD ** (-0.5)
    f32, bf = jnp.float32, jnp.bfloat16
    partner = {"ctx": chip * 2 + 1 - core}

    def first_peer(k):
        return {"fsdp": block(lax.rem(a + k, 4), b)}

    def second_peer(k):
        return {"fsdp": block(a, lax.rem(b + k, 4))}

    def chip_peer(k):
        return {"ctx": lax.rem(chip + k, chips) * 2 + core}

    def member(k):
        return {"ctx": lax.rem(me + k, members)}

    def q_cols(half):
        return pl.ds(pl.multiple_of(half * q_half, 128), q_half)

    def o_lines(half):
        return pl.ds(pl.multiple_of(half * o_half, 16), o_half)

    def line(k):
        return lax.rem(a + k, 4)

    own_loads = [
        pltpu.make_async_copy(gff.at[block(a, j)], own_ff.at[j], l_sem.at[j]) for j in range(4)
    ] + [
        pltpu.make_async_copy(
            gff.at[block(line(1 if j < 2 else 3), j)], far_own.at[j], l_sem.at[4 + j]
        )
        for j in range(4)
    ]
    weight_loads = [
        pltpu.make_async_copy(wo_hbm, wo_ref, l_sem.at[8]),
        pltpu.make_async_copy(qkv_hbm, qkv_ref, l_sem.at[9]),
    ]
    for copy in own_loads + weight_loads:
        copy.start()
    greet(
        [first_peer(k) for k in (1, 2, 3)]
        + [second_peer(k) for k in (1, 2, 3)]
        + [member(k) for k in range(1, members)]
    )

    def ff_far(j):
        k = 1 if j < 2 else 3
        return remote(
            gff.at[block(line(2), j)], far_in.at[j], sfar.at[j], rfar.at[j], first_peer(k)
        )

    def ff_near(k, j):
        side = 0 if k == 1 else 1
        direct = (j >= 2) == (k == 1)
        src = gff.at[block(line(k), j)] if direct else far_own.at[j]
        return remote(src, in1_ff.at[side, j], s1f.at[side, j], r1f.at[side, j], first_peer(k))

    for j in (0, 2, 1, 3):
        ff_far(j).start()
    for k, j in ((1, 2), (3, 0), (1, 3), (3, 1)):
        ff_near(k, j).start()

    def pass_far(js):
        for j in js:
            ff_far(j).wait_recv()
            own_loads[4 + j].wait()
            far_own[j] = (far_own[j].astype(f32) + far_in[j].astype(f32)).astype(bf)
            ff_near(1 if j < 2 else 3, j).start()

    for copy in weight_loads[:1]:
        copy.wait()

    grad_final = cot_ref[...].astype(f32)
    part, gain_two = rms_back(mid_ref[...], gn_ref[...], gains_ref[2:3, :])
    grad_mid = grad_final + part
    gmid[...] = grad_mid
    grad_attn, gain_one = rms_back(attn_ref[...], grad_mid, gains_ref[1:2, :])
    grad_attn_low = grad_attn.astype(bf)
    grad_attended = dot32(grad_attn_low, wo_ref[...], NT).astype(bf)

    def out_tile(t, carry):
        cols = pl.ds(pl.multiple_of(t * 256, 256), 256)
        go[pl.ds(t * 4, 4)] = (
            dot32(att_ref[:, cols], grad_attn_low, TN).reshape(4, 64, D).astype(bf)
        )
        return carry

    lax.fori_loop(0, NH * HD // 256, out_tile, 0)

    def away(i, t):
        k, j = lax.rem(i // 4 + 1, 4), lax.rem(i, 4)
        there = lax.rem(b + k, 4)
        f = block_there(there, j)
        slot = there * 4 + j
        if t == 0:
            src, dst = stage.at[f, :, q_cols(1 - core)], dq.at[slot]
        else:
            src, dst = go.at[f, o_lines(1 - core), :], do.at[slot]
        return remote(src, dst, sd.at[i, t], rd.at[i, t], partner)

    def home(i, t):
        k, j = lax.rem(i // 4 + 1, 4), lax.rem(i, 4)
        slot = lax.rem(a + k, 4) * 4 + j
        dst = (dq, do)[t].at[slot]
        return remote(dst, dst, sd.at[i, t], rd.at[i, t], partner)

    def start_away(t):
        def one(i, carry):
            away(i, t).start()
            return carry

        lax.fori_loop(0, 16, one, 0)

    start_away(1)

    keys, vals = pair_ref[:, :HD], pair_ref[:, HD:]
    queries = stack_heads(q_ref[...])
    grad_heads = stack_heads(grad_attended)
    scores = dot32(queries, keys, NT) * scale + jnp.concatenate([bias_ref[...]] * NH, axis=0)
    expo = jnp.exp(scores - jnp.max(scores, axis=-1, keepdims=True))
    probs = expo / jnp.sum(expo, axis=-1, keepdims=True)
    grad_probs = dot32(grad_heads, vals, NT)
    row_total = jnp.sum(probs * grad_probs, axis=-1, keepdims=True)
    grad_scores = (probs * (grad_probs - row_total)).astype(bf)
    gpair[:, HD:] = dot32(probs.astype(bf), grad_heads, TN)
    gpair[:, :HD] = dot32(grad_scores, queries, TN) * scale

    def kv_send(d):
        return remote(
            kv_snd.at[d - 1], kv_in.at[d - 1], skv.at[d - 1], rkv.at[d - 1], member(members - d)
        )

    for d in range(1, reach + 1):
        kv_snd[d - 1] = gpair[pl.ds((reach - d) * rows, rows), :].astype(bf)
        kv_send(d).start()

    pass_far((0, 2))
    cos_table, sin_table = turn_ref[:, : HD // 2], turn_ref[:, HD // 2 :]
    cos_all = jnp.concatenate([cos_table] * NH, axis=0)
    sin_all = jnp.concatenate([sin_table] * NH, axis=0)
    grad_queries = dot32(grad_scores, keys, NN) * scale
    grad_q, qk_gain_q = rms_back(
        stack_heads(proj_ref[:, : NH * HD]),
        turn_back(grad_queries, cos_all, sin_all),
        qk_ref[0:1, :],
    )
    for h in range(NH):
        gproj[:, h * HD : (h + 1) * HD] = grad_q[h * rows : (h + 1) * rows].astype(bf)

    def hop_one(k, t):
        src, dst = ((sq, iq1), (so, io1))[t]
        return remote(
            src.at[pl.ds(line(k) * 4, 4)], dst.at[3 - k], s1.at[k, t], r1.at[4 - k, t], first_peer(k)
        )

    def fold_cores(t):
        for k in (1, 2, 3, 0):
            def add(j, carry, k=k):
                slot = line(k) * 4 + j
                f = block(line(k), j)
                home((k + 3) % 4 * 4 + j, t).wait_recv()
                if t == 0:
                    sq[slot] = (
                        stage[f, :, q_cols(core)].astype(f32) + dq[slot].astype(f32)
                    ).astype(bf)
                else:
                    so[slot] = (
                        go[f, o_lines(core), :].astype(f32) + do[slot].astype(f32)
                    ).astype(bf)
                return carry

            lax.fori_loop(0, 4, add, 0)
            if k:
                hop_one(k, t).start()

    pass_far((1, 3))

    total = gpair[pl.ds(reach * rows, rows), :]
    for d in range(1, reach + 1):
        kv_send(d).wait_recv()
        total = total + kv_in[d - 1].astype(f32)
    grad_k, qk_gain_k = rms_back(
        proj_ref[:, NH * HD : NH * HD + HD],
        turn_back(total[:, :HD], cos_table, sin_table),
        qk_ref[1:2, :],
    )
    gproj[:, NH * HD : NH * HD + HD] = grad_k.astype(bf)
    gproj[:, NH * HD + HD :] = total[:, HD:].astype(bf)
    for copy in weight_loads[1:]:
        copy.wait()
    stream = tok_ref[...].astype(f32)
    grad_in, gain_zero = rms_back(stream, dot32(gproj[...], qkv_ref[...], NT), gains_ref[0:1, :])
    gt_ref[...] = gmid[...] + grad_in
    tail[...] = jnp.zeros_like(tail)
    for i, total_gain in enumerate((gain_zero, gain_one, gain_two, g3_ref[...])):
        tail[i : i + 1, :D] = total_gain
    tail[4:5, :HD] = qk_gain_q
    tail[5:6, :HD] = qk_gain_k

    def qkv_tile(t, carry):
        cols = pl.ds(pl.multiple_of(t * 256, 256), 256)
        res = dot32(normed_ref[...], gproj[:, cols], TN)
        low = tail[:, cols]
        for f in range(16):
            stage[f, :, cols] = jnp.concatenate(
                [res[f * keep : (f + 1) * keep], low], axis=0
            ).astype(bf)
        return carry

    lax.fori_loop(0, width // 256, qkv_tile, 0)
    start_away(0)

    for copy in own_loads[:4]:
        copy.wait()

    def ff_two(k):
        return remote(
            t_ff.at[lax.rem(b + k, 4)], in2_ff.at[3 - k], s2f.at[k], r2f.at[4 - k], second_peer(k)
        )

    for k in (2, 1, 3, 0):
        j = lax.rem(b + k, 4)
        for m in (0, 1):
            dst = in1_ff.at[m, j]
            remote(dst, dst, s1f.at[m, j], r1f.at[m, j], partner).wait_recv()
        total = own_ff[j].astype(f32)
        for m in (0, 1):
            total = total + in1_ff[m, j].astype(f32)
        t_ff[j] = total.astype(bf)
        if k:
            ff_two(k).start()

    fold_cores(1)
    fold_cores(0)

    def hop_two(k, t):
        src, dst = ((tq, iq2), (to, io2))[t]
        return remote(
            src.at[lax.rem(b + k, 4)], dst.at[3 - k], s2.at[k, t], r2.at[4 - k, t], second_peer(k)
        )

    for k in (1, 3, 2):
        ff_two(4 - k).wait_recv()
    total = t_ff[b].astype(f32)
    for m in range(3):
        total = total + in2_ff[m].astype(f32)
    all_ff[me] = total.astype(bf)

    half = all_ff.shape[1] // 2

    def ff_slot(k, there=0):
        return lax.rem(chip + k, chips) * 2 + (1 - core if there else core)

    def ff_all(k):
        peer = chip_peer(k) if k else partner
        return remote(
            all_ff.at[me], all_ff.at[me], sag.at[k], rag.at[(chips - k) % chips], peer
        )

    def ff_from(k):
        dst = all_ff.at[ff_slot(k)]
        return remote(dst, dst, sag.at[k], rag.at[k], partner)

    def ff_half(k, h, there=0):
        return all_ff.at[ff_slot(k, there), pl.ds(h * half, half), :]

    def ff_on(k):
        h = 0 if k == 3 else 1
        dst = ff_half(k, h)
        return remote(dst, dst, sag.at[8 + h], rag.at[8 + h], chip_peer(4 - k))

    def ff_far_got(h):
        dst = ff_half(2, h)
        return remote(dst, dst, sag.at[8 + h], rag.at[8 + h], partner)

    def ff_cross(k, h=None, there=0):
        if h is None:
            dst, i = all_ff.at[ff_slot(k, there)], 4 + k
        else:
            dst, i = ff_half(2, h, there), 10 + h
        return remote(dst, dst, sag.at[i], rag.at[i], partner)

    for k in (1, 3, 0):
        ff_all(k).start()

    for t in (1, 0):
        own, got, dst = ((sq, iq1, tq), (so, io1, to))[t]
        for k in (1, 3, 2):
            hop_one(4 - k, t).wait_recv()
        for k in (2, 1, 3, 0):
            j = lax.rem(b + k, 4)
            total = own[a * 4 + j].astype(f32)
            for m in range(3):
                total = total + got[m, j].astype(f32)
            dst[j] = total.astype(bf)
            if k:
                hop_two(k, t).start()

    for k in (1, 3):
        ff_from(k).wait_recv()
        ff_on(k).start()
        ff_cross(k).start()

    def hop_chip(k, t):
        buf = (xq, xo)[t]
        return remote(
            buf.at[chip], buf.at[chip], sx.at[k, t], rx.at[chips - k, t], chip_peer(k)
        )

    for t in (1, 0):
        own, got, dst = ((tq, iq2, xq), (to, io2, xo))[t]
        for k in (1, 3, 2):
            hop_two(4 - k, t).wait_recv()
        total = own[b].astype(f32)
        for m in range(3):
            total = total + got[m].astype(f32)
        dst[chip] = total.astype(bf)
        for k in range(1, chips):
            hop_chip(k, t).start()

    def last(t, half):
        part = (oq_ref.at[:, q_cols(half)], oo_ref.at[o_lines(half), :])[t]
        return remote(part, part, sf.at[t], rf.at[t], partner)

    for h in (0, 1):
        ff_far_got(h).wait_recv()
        ff_cross(2, h).start()

    for t in (1, 0):
        buf = (xq, xo)[t]
        for k in range(1, chips):
            dst = buf.at[lax.rem(chip + k, chips)]
            remote(dst, dst, sx.at[k, t], rx.at[k, t], partner).wait_recv()
        total = buf[0].astype(f32)
        for m in range(1, chips):
            total = total + buf[m].astype(f32)
        if t == 0:
            oq_ref[:, q_cols(core)] = total
        else:
            oo_ref[o_lines(core), :] = total
        last(t, core).start()

    everywhere = all_ff.at[ff_slot(0, 1)]
    remote(everywhere, everywhere, sag.at[0], rag.at[0], partner).wait_recv()
    for k in (1, 3):
        ff_cross(k, there=1).wait_recv()
    for h in (0, 1):
        ff_cross(2, h, there=1).wait_recv()

    def end_away(i, carry):
        for t in (0, 1):
            away(i, t).wait_send()
        return carry

    lax.fori_loop(0, 16, end_away, 0)
    for j in range(4):
        ff_far(j).wait_send()
        ff_near(1, j).wait_send()
        ff_near(3, j).wait_send()
    for k in (1, 2, 3):
        ff_two(k).wait_send()
    for d in range(1, reach + 1):
        kv_send(d).wait_send()
    for k in (1, 3, 0):
        ff_all(k).wait_send()
    for k in (1, 3):
        ff_on(k).wait_send()
        ff_cross(k).wait_send()
    for h in (0, 1):
        ff_cross(2, h).wait_send()
    for t in (0, 1):
        for k in (1, 2, 3):
            hop_one(k, t).wait_send()
            hop_two(k, t).wait_send()
        for k in range(1, chips):
            hop_chip(k, t).wait_send()
        last(t, core).wait_send()
        last(t, 1 - core).wait_recv()
    oq_out[...] = oq_ref[:keep, :]
    tail_out[...] = oq_ref[keep:, :]


def backward_rest(gff, values, weights, keep):
    f32, bf = jnp.float32, jnp.bfloat16
    vm = pl.BlockSpec(memory_space=pltpu.VMEM)
    hbm = pl.BlockSpec(memory_space=pl.ANY)
    dma = pltpu.SemaphoreType.DMA
    rows = values[0].shape[0]
    owners, ff_rows = gff.shape[:2]
    q_rows, width = keep + 8, (NH + 2) * HD
    o_rows, o_width = NH * HD // owners, D
    q_half, o_half = width // 2, o_rows // 2
    chips = lax.axis_size("ctx") // 2
    pairs = values[9].shape[0]
    reach = pairs // rows - 1

    def two(*lead):
        return [pltpu.VMEM(lead + (q_rows, q_half), bf), pltpu.VMEM(lead + (o_half, o_width), bf)]

    def ff(*lead):
        return pltpu.VMEM(lead + (ff_rows, D), bf)

    return pl.pallas_call(
        back_kernel,
        out_shape=(
            jax.ShapeDtypeStruct((rows, D), f32),
            jax.ShapeDtypeStruct((keep, width), f32),
            jax.ShapeDtypeStruct((8, width), f32),
            jax.ShapeDtypeStruct((o_rows, o_width), f32),
            jax.ShapeDtypeStruct((2 * chips, ff_rows, D), bf),
        ),
        in_specs=[hbm] + [vm] * len(values) + [hbm] * 2,
        out_specs=(vm,) * 5,
        scratch_shapes=[
            pltpu.VMEM((16 * keep, width), bf),
            pltpu.VMEM((16 * o_rows, o_width), bf),
            pltpu.VMEM((q_rows, width), f32),
            ff(4), ff(4), ff(4), ff(2, 4), ff(4), ff(3),
            pltpu.VMEM((reach, rows, 2 * HD), bf),
            pltpu.VMEM((reach, rows, 2 * HD), bf),
            pltpu.VMEM((rows, D), f32),
            pltpu.VMEM((pairs, 2 * HD), f32),
            pltpu.VMEM((rows, width), bf),
            pltpu.VMEM((8, width), f32),
            pltpu.VMEM((16, q_rows, width), bf),
            pltpu.VMEM((16, o_rows, o_width), bf),
            *two(16), *two(16), *two(3, 4), *two(4), *two(3), *two(chips),
            dma((10,)),
            dma((4,)), dma((4,)),
            dma((2, 4)), dma((2, 4)),
            dma((4,)), dma((4,)),
            dma((12,)), dma((12,)),
            dma((reach,)), dma((reach,)),
            dma((16, 2)), dma((16, 2)),
            dma((4, 2)), dma((4, 2)),
            dma((4, 2)), dma((4, 2)),
            dma((4, 2)), dma((4, 2)),
            dma((2,)), dma((2,)),
        ],
        compiler_params=pltpu.CompilerParams(
            collective_id=3, has_side_effects=True, vmem_limit_bytes=62 * 1024 * 1024
        ),
        cost_estimate=pl.CostEstimate(
            flops=12 * rows * width * D, bytes_accessed=64 * ff_rows * D, transcendentals=0
        ),
    )(gff, *values, *weights)


def finish_kernel(*refs):
    count = (len(refs) - 3 - 1) // 2
    all_ref, sources = refs[0], refs[1 : 1 + count]
    weights, results = refs[1 + count : 4 + count], refs[4 + count :]
    for src, dst in zip(sources, results):
        dst[...] = src[...]
    members = all_ref.shape[0]
    share = all_ref.shape[1] // 3
    lines = weights[0].shape[0] // members
    for i, dst in enumerate(weights):
        for m in range(members):
            dst[m * lines : (m + 1) * lines, :] = all_ref[
                m, i * share : (i + 1) * share, :
            ].astype(jnp.float32)[:lines]


def finish(all_ff, lines, *rest):
    vm = pl.BlockSpec(memory_space=pltpu.VMEM)
    weight = jax.ShapeDtypeStruct((lines, D), jnp.float32)
    return pl.pallas_call(
        finish_kernel,
        out_shape=(weight,) * 3 + tuple(jax.ShapeDtypeStruct(r.shape, r.dtype) for r in rest),
        in_specs=[vm] * (1 + len(rest)),
        out_specs=(vm,) * (3 + len(rest)),
        compiler_params=pltpu.CompilerParams(vmem_limit_bytes=62 * 1024 * 1024),
    )(all_ff, *rest)


def on_device(
    tokens,
    norm_gains,
    qk_gains,
    qkv_weight,
    out_weight,
    gate_weight,
    up_weight,
    down_weight,
    segments,
    cotangent,
):
    local_len = tokens.shape[1]
    ctx_index = lax.axis_index("ctx")
    owner = lax.axis_index("fsdp")
    ctx_size = lax.axis_size("ctx")
    own_rows = gate_weight.shape[0]
    slice_rows = own_rows // ctx_size
    padded = -(-slice_rows // 16) * 16
    keep, width = qkv_weight.shape
    gain_lines, qk_lines = norm_gains.shape, qk_gains.shape
    def placed(lines):
        count, own = lines.shape
        room = (lax.axis_size("fsdp") - 1) * own
        padded_lines = jnp.pad(lines, ((0, 0), (room, room)))
        spread = lax.dynamic_slice(padded_lines, (0, room - owner * own), (count, room + own))
        return jnp.pad(spread, ((0, 0), (0, width - room - own)))

    gain_rows = jnp.concatenate(
        [placed(norm_gains), placed(qk_gains), jnp.zeros((2, width), jnp.bfloat16)], axis=0
    )

    def my_slice(weight):
        part = lax.dynamic_slice(weight, (ctx_index * slice_rows, 0), (slice_rows, D))
        return jnp.pad(part, ((0, padded - slice_rows), (0, 0)))

    ffn_shard = jnp.concatenate(
        [my_slice(gate_weight), my_slice(up_weight), my_slice(down_weight)], axis=0
    )
    places = np.arange(ctx_size * local_len, dtype=np.float32)
    rates = (ROPE_BASE ** (-(2.0 * np.arange(HD // 2)) / HD)).astype(np.float32)
    angles = (places[:, None] * rates).astype(np.float64)
    table = jnp.asarray(
        np.concatenate([np.cos(angles), np.sin(angles)], axis=1)
        .astype(np.float32)
        .reshape(ctx_size, local_len, HD)
    )
    flat = tokens.reshape(local_len, D)
    cot = cotangent.reshape(local_len, D)
    (
        qkv_full, out_full, ffn_full, gains_all, qk_all, normed, projected, queries, pair_all,
        attended, attn, mid, normed_two, bias, turn_table,
    ) = front(
        jnp.concatenate([qkv_weight, gain_rows], axis=0),
        out_weight,
        ffn_shard,
        flat,
        jnp.broadcast_to(segments, (8, local_len)),
        segments.reshape(local_len, 1),
        table,
        keep,
    )
    output, grad_normed_two, grad_gain_three, ffn_grads = ffn(
        normed_two, mid, cot, gains_all, ffn_full
    )
    grad_tokens, total_qkv, tail, total_out, all_ff = backward_rest(
        ffn_grads,
        (
            grad_normed_two, mid, attn, cot, flat, gains_all, qk_all, projected, queries,
            pair_all, attended, normed, turn_table, bias, grad_gain_three,
        ),
        (qkv_full, out_full),
        keep,
    )
    total_gate, total_up, total_down, grad_tokens, total_qkv, total_out, output = finish(
        all_ff, own_rows, grad_tokens, total_qkv, total_out, output
    )
    total_gains = lax.dynamic_slice(tail, (0, owner * gain_lines[1]), gain_lines)
    total_qk = lax.dynamic_slice(tail, (4, owner * qk_lines[1]), qk_lines)
    return (
        output.reshape(tokens.shape),
        grad_tokens.reshape(tokens.shape),
        total_gains,
        total_qk,
        total_qkv,
        total_out,
        total_gate,
        total_up,
        total_down,
    )


def solution(mesh):
    in_specs = (
        P("fsdp", "ctx", None),
        P(None, "fsdp"),
        P(None, "fsdp"),
        P("fsdp", None),
        P("fsdp", None),
        P("fsdp", None),
        P("fsdp", None),
        P("fsdp", None),
        P("fsdp", "ctx"),
        P("fsdp", "ctx", None),
    )
    out_specs = (
        P("fsdp", "ctx", None),
        P("fsdp", "ctx", None),
        P(None, "fsdp"),
        P(None, "fsdp"),
        P("fsdp", None),
        P("fsdp", None),
        P("fsdp", None),
        P("fsdp", None),
        P("fsdp", None),
    )
    return jax.shard_map(
        on_device, mesh=mesh, in_specs=in_specs, out_specs=out_specs, check_vma=False
    )
```

```python
import jax
import numpy as np
import jax.numpy as jnp
from jax import lax
from jax.experimental import pallas as pl
from jax.experimental.pallas import tpu as pltpu
from jax.sharding import PartitionSpec as P

D = 1152
NH = 4
HD = 256
WINDOW = 512


EPS = 1e-06
ROPE_BASE = 10000.0
NEG_FILL = -1e30


def rms_norm(values, gain_vec):
    return values * lax.rsqrt(jnp.mean(values * values, axis=-1, keepdims=True) + EPS) * gain_vec


MESH = pl.DeviceIdType.MESH
NT = (((1,), (1,)), ((), ()))
NN = (((1,), (0,)), ((), ()))
TN = (((0,), (0,)), ((), ()))
GELU_C = 0.7978845608028654
GELU_A = 0.044715


def dot32(left, right, dims):
    return lax.dot_general(left, right, dims, preferred_element_type=jnp.float32)


def ffn_kernel(
    normed_ref, mid_ref, cot_ref, gain_ref, w_hbm,
    out_ref, gn_ref, ggain_ref, gff_hbm,
    wg, wu, wd, seq, gseq, act_a, act_b, hid, dgate, dup, part, keep, base,
    d2d_snd, d2d_in, ici_snd, ici_in, dw,
    w_sem, o_sem, ag_s, ag_r, rd_s, rd_r, ri_s, ri_r,
):
    rows = normed_ref.shape[0]
    units = wg.shape[0]
    share = units // w_hbm.shape[0]
    tile = 256
    me = lax.axis_index("ctx")
    chip, core = me // 2, lax.rem(me, 2)
    partner = {"ctx": chip * 2 + 1 - core}
    chips = {k: {"ctx": lax.rem(chip + k, 4) * 2 + core} for k in (1, 2, 3)}
    order = (0, 1, 3, 2)

    loads = [
        pltpu.make_async_copy(
            w_hbm.at[f, pl.ds(i * share, share), :], dst.at[pl.ds(f * share, share), :], w_sem.at[i, f]
        )
        for i, dst in enumerate((wg, wu, wd))
        for f in range(w_hbm.shape[0])
    ]
    for load in loads:
        load.start()

    barrier = pltpu.get_barrier_semaphore()
    for peer in (partner, chips[1], chips[2], chips[3]):
        pl.semaphore_signal(barrier, inc=1, device_id=peer, device_id_type=MESH)
    pl.semaphore_wait(barrier, 4)

    started = []

    def send(src, dst, s_sem, r_sem, peer):
        copy = pltpu.make_async_remote_copy(
            src_ref=src, dst_ref=dst, send_sem=s_sem, recv_sem=r_sem,
            device_id=peer, device_id_type=MESH,
        )
        copy.start()
        started.append(copy)
        return copy

    def mine(k):
        return pl.ds(k * 2 * rows, rows)

    def other(k):
        return pl.ds(k * 2 * rows + rows, rows)

    def pair(k):
        return pl.ds(k * 2 * rows, 2 * rows)

    def spread(buf, ph):
        own = buf.at[mine(0)]
        got = {}
        for k in (1, 3):
            back = 4 - k
            got[back] = send(own, buf.at[mine(back)], ag_s.at[ph, k], ag_r.at[ph, back], chips[k])
        got[0] = send(own, buf.at[other(0)], ag_s.at[ph, 0], ag_r.at[ph, 0], partner)
        return got

    def half_of(k, h, offset=0):
        return pl.ds(k * 2 * rows + offset + h * (rows // 2), rows // 2)

    def relay(buf, ph, got, k):
        got[k].wait_recv()
        h = 0 if k == 3 else 1
        got[2, h] = send(
            buf.at[half_of(k, h)], buf.at[half_of(2, h)],
            ag_s.at[ph, 2 + 2 * h], ag_r.at[ph, 2 + 2 * h], chips[4 - k],
        )
        got[k] = send(
            buf.at[mine(k)], buf.at[other(k)], ag_s.at[ph, 4 + k], ag_r.at[ph, 4 + k], partner
        )

    def relay_far(buf, ph, got):
        for h in (0, 1):
            got[2, h].wait_recv()
            got[2, h] = send(
                buf.at[half_of(2, h)], buf.at[half_of(2, h, rows)],
                ag_s.at[ph, 6 + 2 * h], ag_r.at[ph, 6 + 2 * h], partner,
            )

    def swap(ph, k):
        d2d_snd[ph, k] = part[pl.ds(rows, rows), :].astype(jnp.bfloat16)
        keep[order.index(k) % 2] = part[pl.ds(0, rows), :]
        return send(d2d_snd.at[ph, k], d2d_in.at[ph, k], rd_s.at[ph, k], rd_r.at[ph, k], partner)

    def sum_out(ph, k, copy):
        copy.wait_recv()
        total = keep[order.index(k) % 2] + d2d_in[ph, k].astype(jnp.float32)
        if k == 0:
            base[...] = total
            return None
        ici_snd[ph, k - 1] = total.astype(jnp.bfloat16)
        back = 4 - k
        return send(
            ici_snd.at[ph, k - 1], ici_in.at[ph, back - 1], ri_s.at[ph, k], ri_r.at[ph, back],
            chips[k],
        )

    def phase(buf, ph, work):
        got = spread(buf, ph)
        if ph == 0:
            for load in loads:
                load.wait()
        sums = {}
        copy = waiting = None
        for k in order:
            if k == 1:
                relay(buf, ph, got, 1)
                relay(buf, ph, got, 3)
            if k == 2:
                relay_far(buf, ph, got)
                got[2, 0].wait_recv()
                got[2, 1].wait_recv()
            else:
                got[k].wait_recv()
            if waiting is not None and k == 2:
                sums[waiting] = sum_out(ph, waiting, copy)
                waiting = None
            work(k)
            if waiting is not None:
                sums[waiting] = sum_out(ph, waiting, copy)
            copy, waiting = swap(ph, k), k
        sums[waiting] = sum_out(ph, waiting, copy)
        return sums

    def collect(ph, sums):
        total = base[...]
        for k in (1, 3, 2):
            sums[k].wait_recv()
        for k in (1, 2, 3):
            total = total + ici_in[ph, k - 1].astype(jnp.float32)
        return total

    def forward(k):
        def one(t, carry):
            cols = pl.ds(pl.multiple_of(t * tile, tile), tile)
            block = seq[pair(k), :]
            gate = dot32(block, wg[cols, :], NT)
            up = dot32(block, wu[cols, :], NT)
            square = gate * gate
            th = jnp.tanh(GELU_C * gate * (1.0 + GELU_A * square))
            half = 0.5 * (1.0 + th)
            gelu = gate * half
            slope = half + (0.5 * GELU_C) * gate * (1.0 - th * th) * (1.0 + 3.0 * GELU_A * square)
            hid[pair(k), cols] = (gelu * up).astype(jnp.bfloat16)
            act_a[pair(k), cols] = up * slope
            act_b[pair(k), cols] = gelu
            return carry

        lax.fori_loop(0, units // tile, one, 0)
        part[...] = dot32(hid[pair(k), :], wd[...], NN)

    seq[mine(0), :] = normed_ref[...]
    sums = phase(seq, 0, forward)
    mlp = collect(0, sums)
    r = lax.rsqrt(jnp.mean(mlp * mlp, axis=-1, keepdims=True) + EPS)
    n = mlp * r
    gain = gain_ref[3:4, :]
    out_ref[...] = (mid_ref[...] + n * gain).astype(jnp.bfloat16)
    dy = cot_ref[...].astype(jnp.float32)
    ggain_ref[...] = jnp.sum(dy * n, axis=0, keepdims=True)
    dyg = dy * gain
    dv = r * (dyg - n * jnp.mean(dyg * n, axis=-1, keepdims=True))
    gseq[mine(0), :] = dv.astype(jnp.bfloat16)

    def backward(k):
        def one(t, carry):
            cols = pl.ds(pl.multiple_of(t * tile, tile), tile)
            gh = dot32(gseq[pair(k), :], wd[cols, :], NT)
            dgate[pair(k), cols] = (gh * act_a[pair(k), cols]).astype(jnp.bfloat16)
            dup[pair(k), cols] = (gh * act_b[pair(k), cols]).astype(jnp.bfloat16)
            return carry

        lax.fori_loop(0, units // tile, one, 0)
        part[...] = dot32(dgate[pair(k), :], wg[...], NN) + dot32(dup[pair(k), :], wu[...], NN)

    sums = phase(gseq, 1, backward)
    stores = []
    for i, (left, right) in enumerate(((dgate, seq), (dup, seq), (hid, gseq))):
        def one(t, carry, i=i, left=left, right=right):
            cols = pl.ds(pl.multiple_of(t * tile, tile), tile)
            group = tile // share
            dw[pl.ds(t * group, group), pl.ds(i * share, share), :] = (
                dot32(left[:, cols], right[...], TN).reshape(group, share, -1).astype(jnp.bfloat16)
            )
            return carry

        lax.fori_loop(0, units // tile, one, 0)
        third = pl.ds(i * share, share)
        stores.append(
            pltpu.make_async_copy(dw.at[:, third, :], gff_hbm.at[:, third, :], o_sem.at[i])
        )
        stores[-1].start()
    gn_ref[...] = collect(1, sums)
    for copy in started:
        copy.wait_send()
    for store in stores:
        store.wait()


def ffn(normed_two, mid, cot, gain, weights):
    rows = normed_two.shape[0]
    owners, lines = weights.shape[:2]
    units = owners * lines // 3
    seq_rows = rows * 8
    bf, f32 = jnp.bfloat16, jnp.float32
    vm = pl.BlockSpec(memory_space=pltpu.VMEM)
    hbm = pl.BlockSpec(memory_space=pl.ANY)
    dma = pltpu.SemaphoreType.DMA
    return pl.pallas_call(
        ffn_kernel,
        out_shape=(
            jax.ShapeDtypeStruct((rows, D), bf),
            jax.ShapeDtypeStruct((rows, D), f32),
            jax.ShapeDtypeStruct((1, D), f32),
            jax.ShapeDtypeStruct(weights.shape, bf),
        ),
        in_specs=[vm] * 4 + [hbm],
        out_specs=(vm, vm, vm, hbm),
        scratch_shapes=[
            pltpu.VMEM((units, D), bf),
            pltpu.VMEM((units, D), bf),
            pltpu.VMEM((units, D), bf),
            pltpu.VMEM((seq_rows, D), bf),
            pltpu.VMEM((seq_rows, D), bf),
            pltpu.VMEM((seq_rows, units), f32),
            pltpu.VMEM((seq_rows, units), f32),
            pltpu.VMEM((seq_rows, units), bf),
            pltpu.VMEM((seq_rows, units), bf),
            pltpu.VMEM((seq_rows, units), bf),
            pltpu.VMEM((2 * rows, D), f32),
            pltpu.VMEM((2, rows, D), f32),
            pltpu.VMEM((rows, D), f32),
            pltpu.VMEM((2, 4, rows, D), bf),
            pltpu.VMEM((2, 4, rows, D), bf),
            pltpu.VMEM((2, 3, rows, D), bf),
            pltpu.VMEM((2, 3, rows, D), bf),
            pltpu.VMEM(weights.shape, bf),
            dma((3, owners)), dma((3,)),
            dma((2, 10)), dma((2, 10)),
            dma((2, 4)), dma((2, 4)),
            dma((2, 4)), dma((2, 4)),
        ],
        compiler_params=pltpu.CompilerParams(
            collective_id=1, has_side_effects=True, vmem_limit_bytes=62 * 1024 * 1024
        ),
        cost_estimate=pl.CostEstimate(
            flops=18 * seq_rows * units * D, bytes_accessed=14 * units * D, transcendentals=0
        ),
    )(normed_two, mid, cot, gain, weights)


def place():
    fsdp = lax.axis_index("fsdp")
    ctx = lax.axis_index("ctx")
    y, z = fsdp // 4, lax.rem(fsdp, 4)
    chip, core = ctx // 2, lax.rem(ctx, 2)
    return y, z, chip, core


def shape_of(y, z, core):
    first = (1 - core) * y + core * z
    second = (1 - core) * z + core * y

    def block(i, j):
        return (1 - core) * (4 * i + j) + core * (4 * j + i)

    return first, second, block


def remote(src, dst, s_sem, r_sem, peer):
    return pltpu.make_async_remote_copy(
        src_ref=src, dst_ref=dst, send_sem=s_sem, recv_sem=r_sem,
        device_id=peer, device_id_type=MESH,
    )


def greet(peers):
    barrier = pltpu.get_barrier_semaphore()
    for peer in peers:
        pl.semaphore_signal(barrier, inc=1, device_id=peer, device_id_type=MESH)
    pl.semaphore_wait(barrier, len(peers))


def rms_back(values, grad, gain):
    r = lax.rsqrt(jnp.mean(values * values, axis=-1, keepdims=True) + EPS)
    n = values * r
    dyg = grad * gain
    return (
        r * (dyg - n * jnp.mean(dyg * n, axis=-1, keepdims=True)),
        jnp.sum(grad * n, axis=0, keepdims=True),
    )


def stack_heads(values):
    return jnp.concatenate([values[:, h * HD : (h + 1) * HD] for h in range(NH)], axis=0)


def turn_back(grad, cos_table, sin_table):
    left, right = grad[:, : HD // 2], grad[:, HD // 2 :]
    return jnp.concatenate(
        [left * cos_table + right * sin_table, right * cos_table - left * sin_table], axis=1
    )


def front_kernel(
    qkv_ref, wo_ref, ffn_ref, tok_ref, seg_line, table_ref,
    qkv_hbm, wo_hbm, ffn_all, gains_ref, qk_ref, normed_ref, proj_ref, q_ref, pair_ref, att_ref,
    attn_ref, mid_ref, low_ref, bias_ref, turn_ref,
    qkv_all, qkv_out, wo_all, seg_ref, seg_in,
    l_sem, s1, r1, s2, r2, sd, rd, s1f, r1f, s2f, r2f, skv, rkv, ssg, rsg,
):
    f32, bf = jnp.float32, jnp.bfloat16
    y, z, chip, core = place()
    a, b, block = shape_of(y, z, core)
    _, _, block_there = shape_of(y, z, 1 - core)
    q_rows, width = qkv_ref.shape
    o_rows = wo_ref.shape[0]
    q_half, o_half = width // 2, o_rows // 2
    partner = {"ctx": chip * 2 + 1 - core}
    me = chip * 2 + core
    rows = tok_ref.shape[0]
    reach = pair_ref.shape[0] // rows - 1
    members = 2 * (lax.axis_size("ctx") // 2)

    def member(k):
        return {"ctx": lax.rem(me + k, members)}

    seg_ref[...] = jnp.broadcast_to(seg_line[...], seg_ref.shape)

    def views(f, half):
        return (
            qkv_all.at[
                pl.ds(pl.multiple_of(f * q_rows, 16), q_rows),
                pl.ds(pl.multiple_of(half * q_half, 128), q_half),
            ],
            wo_all.at[pl.ds(pl.multiple_of(f * o_rows + half * o_half, 16), o_half), :],
        )

    mine = (
        qkv_ref.at[:, pl.ds(pl.multiple_of(core * q_half, 128), q_half)],
        wo_ref.at[pl.ds(pl.multiple_of(core * o_half, 16), o_half), :],
    )
    here = block(a, b)
    locals_ = [
        pltpu.make_async_copy(
            qkv_ref, qkv_all.at[pl.ds(pl.multiple_of(here * q_rows, 16), q_rows), :], l_sem.at[0]
        ),
        pltpu.make_async_copy(
            wo_ref, wo_all.at[pl.ds(pl.multiple_of(here * o_rows, 16), o_rows), :], l_sem.at[1]
        ),
        pltpu.make_async_copy(ffn_ref, ffn_all.at[here], l_sem.at[2]),
        pltpu.make_async_copy(table_ref.at[me], turn_ref, l_sem.at[3]),
    ]
    for copy in locals_:
        copy.start()

    def first_peer(k):
        return {"fsdp": block(lax.rem(a + k, 4), b)}

    def second_peer(k):
        return {"fsdp": block(a, lax.rem(b + k, 4))}

    greet(
        [first_peer(k) for k in (1, 2, 3)]
        + [second_peer(k) for k in (1, 2, 3)]
        + [member(k) for k in range(1, members)]
    )

    def seg_send(d):
        return remote(
            seg_ref, seg_in.at[reach - d], ssg.at[d - 1], rsg.at[d - 1], member(d)
        )

    def ffn_one(k):
        return remote(ffn_ref, ffn_all.at[here], s1f.at[k], r1f.at[4 - k], first_peer(k))

    def ffn_block(j, m):
        return ffn_all.at[block(lax.rem(a + j, 4), lax.rem(b + m, 4))]

    def ffn_two(j, k):
        dst = ffn_block(j, 0)
        src = dst if j else ffn_ref
        return remote(src, dst, s2f.at[j, k], r2f.at[j, 4 - k], second_peer(k))

    def ffn_pass(j):
        dst, k = (ffn_block(j, 3), 1) if j < 2 else (ffn_block(j, 1), 3)
        return remote(dst, dst, s2f.at[j, 2], r2f.at[j, 2], second_peer(k))

    def ffn_got(j, m):
        dst = ffn_block(j, m)
        sems = (s1f.at[j], r1f.at[j]) if m == 0 else (s2f.at[j, m], r2f.at[j, m])
        return remote(dst, dst, *sems, partner)

    def hop_one(k, t):
        return remote(mine[t], views(here, core)[t], s1.at[k, t], r1.at[4 - k, t], first_peer(k))

    def hop_two(j, k, t):
        f = block(lax.rem(a + j, 4), b)
        dst = views(f, core)[t]
        src = dst if j else mine[t]
        return remote(src, dst, s2.at[j, k, t], r2.at[j, 4 - k, t], second_peer(k))

    def arrive_one(j, t):
        dst = views(block(lax.rem(a + j, 4), b), core)[t]
        return remote(dst, dst, s1.at[j, t], r1.at[j, t], partner)

    def arrive_two(j, m, t):
        dst = views(block(lax.rem(a + j, 4), lax.rem(b + m, 4)), core)[t]
        return remote(dst, dst, s2.at[j, m, t], r2.at[j, m, t], partner)

    def cross(j, m, t):
        dst = views(block(lax.rem(a + j, 4), lax.rem(b + m, 4)), core)[t]
        return remote(dst, dst, sd.at[j, m, t], rd.at[j, m, t], partner)

    def arrive_cross(j, m, t):
        dst = views(block_there(lax.rem(b + j, 4), lax.rem(a + m, 4)), 1 - core)[t]
        return remote(dst, dst, sd.at[j, m, t], rd.at[j, m, t], partner)

    both = (0, 1)
    for k in (1, 3, 2):
        for t in both:
            hop_one(k, t).start()
    def hop_pass(j, t):
        m, k = (3, 1) if j < 2 else (1, 3)
        dst = views(block(lax.rem(a + j, 4), lax.rem(b + m, 4)), core)[t]
        return remote(dst, dst, s2.at[j, 2, t], r2.at[j, 2, t], second_peer(k))

    for k in (1, 3):
        for t in both:
            hop_two(0, k, t).start()
    for j in (1, 3, 2):
        for t in both:
            arrive_one(j, t).wait_recv()
            for k in (1, 3):
                hop_two(j, k, t).start()
            cross(j, 0, t).start()

    for d in range(1, reach + 1):
        seg_send(d).start()
    for k in (1, 3, 2):
        ffn_one(k).start()
    for k in (1, 3):
        ffn_two(0, k).start()

    for j in (0, 1, 3, 2):
        for m in (3, 1) if j < 2 else (1, 3):
            for t in both:
                arrive_two(j, m, t).wait_recv()
                if m == (3 if j < 2 else 1):
                    hop_pass(j, t).start()
                cross(j, m, t).start()
    for j in (0, 1, 3, 2):
        for t in both:
            arrive_two(j, 2, t).wait_recv()
            cross(j, 2, t).start()

    def land(i, carry):
        m, j = i // 4, lax.rem(i, 4)
        for t in both:
            arrive_cross(j, m, t).wait_recv()
            cross(j, m, t).wait_send()
        return carry

    lax.fori_loop(1, 16, land, 0)
    for copy in locals_[:2]:
        copy.wait()
    for t in both:
        for k in (1, 2, 3):
            hop_one(k, t).wait_send()
        for j in range(4):
            hop_pass(j, t).wait_send()
            for k in (1, 3):
                hop_two(j, k, t).wait_send()
    saves = [
        pltpu.make_async_copy(qkv_out, qkv_hbm, l_sem.at[4]),
        pltpu.make_async_copy(wo_all, wo_hbm, l_sem.at[5]),
    ]
    saves[1].start()

    keep = qkv_out.shape[0] // 16
    extra = jnp.zeros((q_rows - keep, width), f32)
    for f in range(0, 16, 2):
        left = qkv_all[pl.ds(f * q_rows, q_rows), :].astype(f32)
        right = qkv_all[pl.ds((f + 1) * q_rows, q_rows), :].astype(f32)
        qkv_out[pl.ds(f * keep, 2 * keep), :] = jnp.concatenate(
            [left[:keep], right[:keep]], axis=0
        ).astype(bf)
        extra = extra + left[keep:] + right[keep:]
    saves[0].start()
    gains = extra[:4, :D]
    gains_ref[...] = gains
    qk_ref[...] = extra[4:6, :HD]

    stream = tok_ref[...].astype(f32)
    normed_ref[...] = rms_norm(stream, gains[0:1]).astype(bf)
    proj_ref[...] = dot32(normed_ref[...], qkv_out[...], NN)
    locals_[3].wait()
    cos_table, sin_table = turn_ref[:, : HD // 2], turn_ref[:, HD // 2 :]

    def turn(values, gain, cos_part, sin_part):
        values = rms_norm(values, gain)
        left, right = values[:, : HD // 2], values[:, HD // 2 :]
        return jnp.concatenate(
            [left * cos_part - right * sin_part, right * cos_part + left * sin_part], axis=1
        ).astype(bf)

    own = pl.ds(reach * rows, rows)
    pair_ref[own, :HD] = turn(
        proj_ref[:, NH * HD : NH * HD + HD], extra[5:6, :HD], cos_table, sin_table
    )
    pair_ref[own, HD:] = proj_ref[:, NH * HD + HD :].astype(bf)

    def kv_send(d):
        return remote(
            pair_ref.at[own],
            pair_ref.at[pl.ds((reach - d) * rows, rows)],
            skv.at[d - 1], rkv.at[d - 1], member(d),
        )

    for d in range(1, reach + 1):
        kv_send(d).start()
    for j in (1, 3, 2):
        ffn_got(j, 0).wait_recv()
        for k in (1, 3):
            ffn_two(j, k).start()
    queries = turn(
        stack_heads(proj_ref[:, : NH * HD]),
        extra[4:5, :HD],
        jnp.concatenate([cos_table] * NH, axis=0),
        jnp.concatenate([sin_table] * NH, axis=0),
    )
    for h in range(NH):
        q_ref[:, h * HD : (h + 1) * HD] = queries[h * rows : (h + 1) * rows]

    for d in range(1, reach + 1):
        seg_send(d).wait_recv()
    seg_in[reach] = seg_ref[...]
    key_seg = jnp.concatenate([seg_in[p][0:1, :] for p in range(reach + 1)], axis=1)
    shape = (rows, (reach + 1) * rows)
    spacing = (
        reach * rows + lax.broadcasted_iota(jnp.int32, shape, 0)
        - lax.broadcasted_iota(jnp.int32, shape, 1)
    )
    begun = lax.broadcasted_iota(jnp.int32, shape, 1) + (me - reach) * rows >= 0
    wide = jnp.broadcast_to(seg_line[...], (rows, rows)).astype(f32)
    query_seg = jnp.concatenate([wide.T] * (reach + 1), axis=1)
    allowed = (
        (spacing >= 0) & (spacing < WINDOW) & begun & (query_seg == key_seg.astype(f32))
    )
    bias_ref[...] = jnp.where(allowed, 0.0, NEG_FILL)
    def ffn_onward(j):
        ffn_got(j, 3 if j < 2 else 1).wait_recv()
        ffn_pass(j).start()

    ffn_onward(0)
    for d in range(1, reach + 1):
        kv_send(d).wait_recv()
    scores = dot32(queries, pair_ref[:, :HD], NT) * (HD ** (-0.5)) + jnp.concatenate(
        [bias_ref[...]] * NH, axis=0
    )
    expo = jnp.exp(scores - jnp.max(scores, axis=-1, keepdims=True))
    probs = expo / jnp.sum(expo, axis=-1, keepdims=True)
    heads = dot32(probs.astype(bf), pair_ref[:, HD:], NN).astype(bf)
    for h in range(NH):
        att_ref[:, h * HD : (h + 1) * HD] = heads[h * rows : (h + 1) * rows]
    ffn_onward(1)
    ffn_onward(3)
    attn = dot32(att_ref[...], wo_all[...], NN)
    attn_ref[...] = attn
    mid = stream + rms_norm(attn, gains[1:2])
    mid_ref[...] = mid
    low_ref[...] = rms_norm(mid, gains[2:3]).astype(bf)

    ffn_onward(2)
    for copy in saves + locals_[2:3]:
        copy.wait()
    for j in range(4):
        ffn_got(j, 1 if j < 2 else 3).wait_recv()
        ffn_got(j, 2).wait_recv()
    for j in range(4):
        ffn_pass(j).wait_send()
        for k in (1, 3):
            ffn_two(j, k).wait_send()
    for k in (1, 2, 3):
        ffn_one(k).wait_send()
    for d in range(1, reach + 1):
        seg_send(d).wait_send()
        kv_send(d).wait_send()


def front(qkv_shard, wo_shard, ffn_shard, tokens, seg_line, table, keep):
    f32, bf = jnp.float32, jnp.bfloat16
    vm = pl.BlockSpec(memory_space=pltpu.VMEM)
    hbm = pl.BlockSpec(memory_space=pl.ANY)
    dma = pltpu.SemaphoreType.DMA
    q_rows, width = qkv_shard.shape
    o_rows, o_width = wo_shard.shape
    rows = tokens.shape[0]
    reach = min(-(-(WINDOW - 1) // rows), lax.axis_size("ctx") - 1)
    pairs = (reach + 1) * rows
    shapes = (
        ((16 * keep, width), bf),
        ((16 * o_rows, o_width), bf),
        ((16, *ffn_shard.shape), bf),
        ((4, D), f32),
        ((2, HD), f32),
        ((rows, D), bf),
        ((rows, width), f32),
        ((rows, NH * HD), bf),
        ((pairs, 2 * HD), bf),
        ((rows, NH * HD), bf),
        ((rows, D), f32),
        ((rows, D), f32),
        ((rows, D), bf),
        ((rows, pairs), f32),
        ((rows, HD), f32),
    )
    return pl.pallas_call(
        front_kernel,
        out_shape=tuple(jax.ShapeDtypeStruct(*s) for s in shapes),
        in_specs=[vm, vm, hbm, vm, vm, hbm],
        out_specs=(hbm,) * 3 + (vm,) * (len(shapes) - 3),
        scratch_shapes=[
            pltpu.VMEM((16 * q_rows, width), bf),
            pltpu.VMEM((16 * keep, width), bf),
            pltpu.VMEM((16 * o_rows, o_width), bf),
            pltpu.VMEM((8, rows), jnp.int32),
            pltpu.VMEM((reach + 1, 8, rows), jnp.int32),
            dma((6,)),
            dma((4, 2)), dma((4, 2)),
            dma((4, 4, 2)), dma((4, 4, 2)),
            dma((4, 4, 2)), dma((4, 4, 2)),
            dma((4,)), dma((4,)),
            dma((4, 4)), dma((4, 4)),
            dma((reach,)), dma((reach,)),
            dma((reach,)), dma((reach,)),
        ],
        compiler_params=pltpu.CompilerParams(
            collective_id=2, has_side_effects=True, vmem_limit_bytes=62 * 1024 * 1024
        ),
        cost_estimate=pl.CostEstimate(
            flops=6 * rows * width * D, bytes_accessed=64 * q_rows * width, transcendentals=0
        ),
    )(qkv_shard, wo_shard, ffn_shard, tokens, seg_line, table)


def back_kernel(
    gff, gn_ref, mid_ref, attn_ref, cot_ref, tok_ref, gains_ref, qk_ref, proj_ref, q_ref,
    pair_ref, att_ref, normed_ref, turn_ref, bias_ref, g3_ref, qkv_hbm, wo_hbm,
    gt_ref, oq_out, tail_out, oo_ref, all_ff,
    qkv_ref, wo_ref, oq_ref, own_ff, far_own, far_in, in1_ff, t_ff, in2_ff, kv_snd, kv_in, gmid, gpair, gproj, tail,
    stage, go, dq, do, sq, so, fq, fo, iq1, io1, tq, to, iq2, io2, xq, xo,
    l_sem, sfar, rfar, s1f, r1f, s2f, r2f, sag, rag, skv, rkv,
    sd, rd, sfa, rfa, s1, r1, s2, r2, sx, rx, sf, rf,
):
    y, z, chip, core = place()
    a, b, block = shape_of(y, z, core)
    _, _, block_there = shape_of(y, z, 1 - core)
    me = chip * 2 + core
    rows = gn_ref.shape[0]
    q_rows, width = oq_ref.shape
    keep = normed_ref.shape[1] // 16
    o_rows = oo_ref.shape[0]
    q_half, o_half = width // 2, o_rows // 2
    chips = xq.shape[0]
    members = 2 * chips
    reach = kv_in.shape[0]
    scale = HD ** (-0.5)
    f32, bf = jnp.float32, jnp.bfloat16
    partner = {"ctx": chip * 2 + 1 - core}

    def first_peer(k):
        return {"fsdp": block(lax.rem(a + k, 4), b)}

    def second_peer(k):
        return {"fsdp": block(a, lax.rem(b + k, 4))}

    def chip_peer(k):
        return {"ctx": lax.rem(chip + k, chips) * 2 + core}

    def member(k):
        return {"ctx": lax.rem(me + k, members)}

    def q_cols(half):
        return pl.ds(pl.multiple_of(half * q_half, 128), q_half)

    def o_lines(half):
        return pl.ds(pl.multiple_of(half * o_half, 16), o_half)

    def line(k):
        return lax.rem(a + k, 4)

    own_loads = [
        pltpu.make_async_copy(gff.at[block(a, j)], own_ff.at[j], l_sem.at[j]) for j in range(4)
    ] + [
        pltpu.make_async_copy(
            gff.at[block(line(1 if j < 2 else 3), j)], far_own.at[j], l_sem.at[4 + j]
        )
        for j in range(4)
    ]
    weight_loads = [
        pltpu.make_async_copy(wo_hbm, wo_ref, l_sem.at[8]),
        pltpu.make_async_copy(qkv_hbm, qkv_ref, l_sem.at[9]),
    ]
    for copy in own_loads + weight_loads:
        copy.start()
    greet(
        [first_peer(k) for k in (1, 2, 3)]
        + [second_peer(k) for k in (1, 2, 3)]
        + [member(k) for k in range(1, members)]
    )

    def ff_far(j):
        k = 1 if j < 2 else 3
        return remote(
            gff.at[block(line(2), j)], far_in.at[j], sfar.at[j], rfar.at[j], first_peer(k)
        )

    def ff_near(k, j):
        side = 0 if k == 1 else 1
        direct = (j >= 2) == (k == 1)
        src = gff.at[block(line(k), j)] if direct else far_own.at[j]
        return remote(src, in1_ff.at[side, j], s1f.at[side, j], r1f.at[side, j], first_peer(k))

    for j in (0, 2, 1, 3):
        ff_far(j).start()
    for k, j in ((1, 2), (3, 0), (1, 3), (3, 1)):
        ff_near(k, j).start()

    def pass_far(js):
        for j in js:
            ff_far(j).wait_recv()
            own_loads[4 + j].wait()
            far_own[j] = (far_own[j].astype(f32) + far_in[j].astype(f32)).astype(bf)
            ff_near(1 if j < 2 else 3, j).start()

    for copy in weight_loads[:1]:
        copy.wait()

    grad_final = cot_ref[...].astype(f32)
    part, gain_two = rms_back(mid_ref[...], gn_ref[...], gains_ref[2:3, :])
    grad_mid = grad_final + part
    gmid[...] = grad_mid
    grad_attn, gain_one = rms_back(attn_ref[...], grad_mid, gains_ref[1:2, :])
    grad_attn_low = grad_attn.astype(bf)
    grad_attended = dot32(grad_attn_low, wo_ref[...], NT).astype(bf)

    def out_tile(t, carry):
        cols = pl.ds(pl.multiple_of(t * 256, 256), 256)
        go[pl.ds(t * 4, 4)] = (
            dot32(att_ref[:, cols], grad_attn_low, TN).reshape(4, 64, D).astype(bf)
        )
        return carry

    lax.fori_loop(0, NH * HD // 256, out_tile, 0)

    def away(i, t):
        k, j = lax.rem(i // 4 + 2, 4), lax.rem(i, 4)
        there = lax.rem(b + k, 4)
        f = block_there(there, j)
        slot = there * 4 + j
        if t == 0:
            src, dst = stage.at[f, :, q_cols(1 - core)], dq.at[slot]
        else:
            src, dst = go.at[f, o_lines(1 - core), :], do.at[slot]
        return remote(src, dst, sd.at[i, t], rd.at[i, t], partner)

    def home(i, t):
        k, j = lax.rem(i // 4 + 2, 4), lax.rem(i, 4)
        slot = lax.rem(a + k, 4) * 4 + j
        dst = (dq, do)[t].at[slot]
        return remote(dst, dst, sd.at[i, t], rd.at[i, t], partner)

    def start_away(t):
        def one(i, carry):
            away(i, t).start()
            return carry

        lax.fori_loop(0, 16, one, 0)

    start_away(1)

    keys, vals = pair_ref[:, :HD], pair_ref[:, HD:]
    queries = stack_heads(q_ref[...])
    grad_heads = stack_heads(grad_attended)
    scores = dot32(queries, keys, NT) * scale + jnp.concatenate([bias_ref[...]] * NH, axis=0)
    expo = jnp.exp(scores - jnp.max(scores, axis=-1, keepdims=True))
    probs = expo / jnp.sum(expo, axis=-1, keepdims=True)
    grad_probs = dot32(grad_heads, vals, NT)
    row_total = jnp.sum(probs * grad_probs, axis=-1, keepdims=True)
    grad_scores = (probs * (grad_probs - row_total)).astype(bf)
    gpair[:, HD:] = dot32(probs.astype(bf), grad_heads, TN)
    gpair[:, :HD] = dot32(grad_scores, queries, TN) * scale

    def kv_send(d):
        return remote(
            kv_snd.at[d - 1], kv_in.at[d - 1], skv.at[d - 1], rkv.at[d - 1], member(members - d)
        )

    for d in range(1, reach + 1):
        kv_snd[d - 1] = gpair[pl.ds((reach - d) * rows, rows), :].astype(bf)
        kv_send(d).start()

    pass_far((0, 2))
    cos_table, sin_table = turn_ref[:, : HD // 2], turn_ref[:, HD // 2 :]
    cos_all = jnp.concatenate([cos_table] * NH, axis=0)
    sin_all = jnp.concatenate([sin_table] * NH, axis=0)
    grad_queries = dot32(grad_scores, keys, NN) * scale
    grad_q, qk_gain_q = rms_back(
        stack_heads(proj_ref[:, : NH * HD]),
        turn_back(grad_queries, cos_all, sin_all),
        qk_ref[0:1, :],
    )
    for h in range(NH):
        gproj[:, h * HD : (h + 1) * HD] = grad_q[h * rows : (h + 1) * rows].astype(bf)

    def pair_of(k, h):
        return pl.ds(line(k) * 4 + 2 * h, 2)

    def sum_far(h, t):
        src, dst = ((sq, fq), (so, fo))[t]
        return remote(
            src.at[pair_of(2, h)], dst.at[pl.ds(2 * h, 2)],
            sfa.at[h, t], rfa.at[h, t], first_peer(3 if h else 1),
        )

    def sum_near(k, h, t):
        src, dst = ((sq, iq1), (so, io1))[t]
        side = 0 if k == 1 else 1
        return remote(
            src.at[pair_of(k, h)], dst.at[side, pl.ds(2 * h, 2)],
            s1.at[side, h, t], r1.at[side, h, t], first_peer(k),
        )

    def fold_cores(t):
        for k in (2, 3, 1, 0):
            def add(j, carry, k=k):
                slot = line(k) * 4 + j
                f = block(line(k), j)
                home((k + 2) % 4 * 4 + j, t).wait_recv()
                if t == 0:
                    sq[slot] = (
                        stage[f, :, q_cols(core)].astype(f32) + dq[slot].astype(f32)
                    ).astype(bf)
                else:
                    so[slot] = (
                        go[f, o_lines(core), :].astype(f32) + do[slot].astype(f32)
                    ).astype(bf)
                return carry

            lax.fori_loop(0, 4, add, 0)
            if k == 2:
                sum_far(0, t).start()
                sum_far(1, t).start()
            elif k:
                sum_near(k, 0 if k == 3 else 1, t).start()

    def fold_far(t):
        acc, far = ((sq, fq), (so, fo))[t]
        for h, k in ((0, 1), (1, 3)):
            sum_far(h, t).wait_recv()
            acc[pair_of(k, h)] = (
                acc[pair_of(k, h)].astype(f32) + far[2 * h : 2 * h + 2].astype(f32)
            ).astype(bf)
            sum_near(k, h, t).start()

    pass_far((1, 3))

    total = gpair[pl.ds(reach * rows, rows), :]
    for d in range(1, reach + 1):
        kv_send(d).wait_recv()
        total = total + kv_in[d - 1].astype(f32)
    grad_k, qk_gain_k = rms_back(
        proj_ref[:, NH * HD : NH * HD + HD],
        turn_back(total[:, :HD], cos_table, sin_table),
        qk_ref[1:2, :],
    )
    gproj[:, NH * HD : NH * HD + HD] = grad_k.astype(bf)
    gproj[:, NH * HD + HD :] = total[:, HD:].astype(bf)
    for copy in weight_loads[1:]:
        copy.wait()
    stream = tok_ref[...].astype(f32)
    grad_in, gain_zero = rms_back(stream, dot32(gproj[...], qkv_ref[...], NT), gains_ref[0:1, :])
    gt_ref[...] = gmid[...] + grad_in
    tail[...] = jnp.zeros_like(tail)
    for i, total_gain in enumerate((gain_zero, gain_one, gain_two, g3_ref[...])):
        tail[i : i + 1, :D] = total_gain
    tail[4:5, :HD] = qk_gain_q
    tail[5:6, :HD] = qk_gain_k

    def qkv_tile(t, carry):
        cols = pl.ds(pl.multiple_of(t * 256, 256), 256)
        res = dot32(normed_ref[...], gproj[:, cols], TN)
        low = tail[:, cols]
        for f in range(16):
            stage[f, :, cols] = jnp.concatenate(
                [res[f * keep : (f + 1) * keep], low], axis=0
            ).astype(bf)
        return carry

    lax.fori_loop(0, width // 256, qkv_tile, 0)
    start_away(0)

    for copy in own_loads[:4]:
        copy.wait()

    def ff_two(k):
        return remote(
            t_ff.at[lax.rem(b + k, 4)], in2_ff.at[3 - k], s2f.at[k], r2f.at[4 - k], second_peer(k)
        )

    for k in (2, 1, 3, 0):
        j = lax.rem(b + k, 4)
        for m in (0, 1):
            dst = in1_ff.at[m, j]
            remote(dst, dst, s1f.at[m, j], r1f.at[m, j], partner).wait_recv()
        total = own_ff[j].astype(f32)
        for m in (0, 1):
            total = total + in1_ff[m, j].astype(f32)
        t_ff[j] = total.astype(bf)
        if k:
            ff_two(k).start()

    fold_cores(1)
    fold_cores(0)
    fold_far(1)
    fold_far(0)

    def hop_two(k, t):
        src, dst = ((tq, iq2), (to, io2))[t]
        return remote(
            src.at[lax.rem(b + k, 4)], dst.at[3 - k], s2.at[k, t], r2.at[4 - k, t], second_peer(k)
        )

    for k in (1, 3, 2):
        ff_two(4 - k).wait_recv()
    total = t_ff[b].astype(f32)
    for m in range(3):
        total = total + in2_ff[m].astype(f32)
    all_ff[me] = total.astype(bf)

    half = all_ff.shape[1] // 2

    def ff_slot(k, there=0):
        return lax.rem(chip + k, chips) * 2 + (1 - core if there else core)

    def ff_all(k):
        peer = chip_peer(k) if k else partner
        return remote(
            all_ff.at[me], all_ff.at[me], sag.at[k], rag.at[(chips - k) % chips], peer
        )

    def ff_from(k):
        dst = all_ff.at[ff_slot(k)]
        return remote(dst, dst, sag.at[k], rag.at[k], partner)

    def ff_half(k, h, there=0):
        return all_ff.at[ff_slot(k, there), pl.ds(h * half, half), :]

    def ff_on(k):
        h = 0 if k == 3 else 1
        dst = ff_half(k, h)
        return remote(dst, dst, sag.at[8 + h], rag.at[8 + h], chip_peer(4 - k))

    def ff_far_got(h):
        dst = ff_half(2, h)
        return remote(dst, dst, sag.at[8 + h], rag.at[8 + h], partner)

    def ff_cross(k, h=None, there=0):
        if h is None:
            dst, i = all_ff.at[ff_slot(k, there)], 4 + k
        else:
            dst, i = ff_half(2, h, there), 10 + h
        return remote(dst, dst, sag.at[i], rag.at[i], partner)

    for k in (1, 3, 0):
        ff_all(k).start()

    for t in (1, 0):
        own, got, dst = ((sq, iq1, tq), (so, io1, to))[t]
        for k in (1, 3):
            for h in (0, 1):
                sum_near(k, h, t).wait_recv()
        for k in (2, 1, 3, 0):
            j = lax.rem(b + k, 4)
            total = own[a * 4 + j].astype(f32)
            for m in (0, 1):
                total = total + got[m, j].astype(f32)
            dst[j] = total.astype(bf)
            if k:
                hop_two(k, t).start()

    for k in (1, 3):
        ff_from(k).wait_recv()
        ff_on(k).start()
        ff_cross(k).start()

    def hop_chip(k, t):
        buf = (xq, xo)[t]
        return remote(
            buf.at[chip], buf.at[chip], sx.at[k, t], rx.at[chips - k, t], chip_peer(k)
        )

    for t in (1, 0):
        own, got, dst = ((tq, iq2, xq), (to, io2, xo))[t]
        for k in (1, 3, 2):
            hop_two(4 - k, t).wait_recv()
        total = own[b].astype(f32)
        for m in range(3):
            total = total + got[m].astype(f32)
        dst[chip] = total.astype(bf)
        for k in range(1, chips):
            hop_chip(k, t).start()

    def last(t, half):
        part = (oq_ref.at[:, q_cols(half)], oo_ref.at[o_lines(half), :])[t]
        return remote(part, part, sf.at[t], rf.at[t], partner)

    for h in (0, 1):
        ff_far_got(h).wait_recv()
        ff_cross(2, h).start()

    for t in (1, 0):
        buf = (xq, xo)[t]
        for k in range(1, chips):
            dst = buf.at[lax.rem(chip + k, chips)]
            remote(dst, dst, sx.at[k, t], rx.at[k, t], partner).wait_recv()
        total = buf[0].astype(f32)
        for m in range(1, chips):
            total = total + buf[m].astype(f32)
        if t == 0:
            oq_ref[:, q_cols(core)] = total
        else:
            oo_ref[o_lines(core), :] = total
        last(t, core).start()

    everywhere = all_ff.at[ff_slot(0, 1)]
    remote(everywhere, everywhere, sag.at[0], rag.at[0], partner).wait_recv()
    for k in (1, 3):
        ff_cross(k, there=1).wait_recv()
    for h in (0, 1):
        ff_cross(2, h, there=1).wait_recv()

    def end_away(i, carry):
        for t in (0, 1):
            away(i, t).wait_send()
        return carry

    lax.fori_loop(0, 16, end_away, 0)
    for j in range(4):
        ff_far(j).wait_send()
        ff_near(1, j).wait_send()
        ff_near(3, j).wait_send()
    for k in (1, 2, 3):
        ff_two(k).wait_send()
    for d in range(1, reach + 1):
        kv_send(d).wait_send()
    for k in (1, 3, 0):
        ff_all(k).wait_send()
    for k in (1, 3):
        ff_on(k).wait_send()
        ff_cross(k).wait_send()
    for h in (0, 1):
        ff_cross(2, h).wait_send()
    for t in (0, 1):
        for h in (0, 1):
            sum_far(h, t).wait_send()
            sum_near(1, h, t).wait_send()
            sum_near(3, h, t).wait_send()
        for k in (1, 2, 3):
            hop_two(k, t).wait_send()
        for k in range(1, chips):
            hop_chip(k, t).wait_send()
        last(t, core).wait_send()
        last(t, 1 - core).wait_recv()
    oq_out[...] = oq_ref[:keep, :]
    tail_out[...] = oq_ref[keep:, :]


def backward_rest(gff, values, weights, keep):
    f32, bf = jnp.float32, jnp.bfloat16
    vm = pl.BlockSpec(memory_space=pltpu.VMEM)
    hbm = pl.BlockSpec(memory_space=pl.ANY)
    dma = pltpu.SemaphoreType.DMA
    rows = values[0].shape[0]
    owners, ff_rows = gff.shape[:2]
    q_rows, width = keep + 8, (NH + 2) * HD
    o_rows, o_width = NH * HD // owners, D
    q_half, o_half = width // 2, o_rows // 2
    chips = lax.axis_size("ctx") // 2
    pairs = values[9].shape[0]
    reach = pairs // rows - 1

    def two(*lead):
        return [pltpu.VMEM(lead + (q_rows, q_half), bf), pltpu.VMEM(lead + (o_half, o_width), bf)]

    def ff(*lead):
        return pltpu.VMEM(lead + (ff_rows, D), bf)

    return pl.pallas_call(
        back_kernel,
        out_shape=(
            jax.ShapeDtypeStruct((rows, D), f32),
            jax.ShapeDtypeStruct((keep, width), f32),
            jax.ShapeDtypeStruct((8, width), f32),
            jax.ShapeDtypeStruct((o_rows, o_width), f32),
            jax.ShapeDtypeStruct((2 * chips, ff_rows, D), bf),
        ),
        in_specs=[hbm] + [vm] * len(values) + [hbm] * 2,
        out_specs=(vm,) * 5,
        scratch_shapes=[
            pltpu.VMEM((16 * keep, width), bf),
            pltpu.VMEM((16 * o_rows, o_width), bf),
            pltpu.VMEM((q_rows, width), f32),
            ff(4), ff(4), ff(4), ff(2, 4), ff(4), ff(3),
            pltpu.VMEM((reach, rows, 2 * HD), bf),
            pltpu.VMEM((reach, rows, 2 * HD), bf),
            pltpu.VMEM((rows, D), f32),
            pltpu.VMEM((pairs, 2 * HD), f32),
            pltpu.VMEM((rows, width), bf),
            pltpu.VMEM((8, width), f32),
            pltpu.VMEM((16, q_rows, width), bf),
            pltpu.VMEM((16, o_rows, o_width), bf),
            *two(16), *two(16), *two(4), *two(2, 4), *two(4), *two(3), *two(chips),
            dma((10,)),
            dma((4,)), dma((4,)),
            dma((2, 4)), dma((2, 4)),
            dma((4,)), dma((4,)),
            dma((12,)), dma((12,)),
            dma((reach,)), dma((reach,)),
            dma((16, 2)), dma((16, 2)),
            dma((2, 2)), dma((2, 2)),
            dma((2, 2, 2)), dma((2, 2, 2)),
            dma((4, 2)), dma((4, 2)),
            dma((4, 2)), dma((4, 2)),
            dma((2,)), dma((2,)),
        ],
        compiler_params=pltpu.CompilerParams(
            collective_id=3, has_side_effects=True, vmem_limit_bytes=62 * 1024 * 1024
        ),
        cost_estimate=pl.CostEstimate(
            flops=12 * rows * width * D, bytes_accessed=64 * ff_rows * D, transcendentals=0
        ),
    )(gff, *values, *weights)


def finish_kernel(*refs):
    count = (len(refs) - 7) // 2
    all_ref, tail_ref, sources = refs[0], refs[1], refs[2 : 2 + count]
    weights, gains, qk = refs[2 + count : 5 + count], refs[5 + count], refs[6 + count]
    for src, dst in zip(sources, refs[7 + count :]):
        dst[...] = src[...]
    owner = lax.axis_index("fsdp")
    width = tail_ref.shape[1]
    for first, dst in ((0, gains), (4, qk)):
        lines, own = dst.shape
        shift = lax.rem(width - owner * own, width)
        dst[...] = pltpu.roll(tail_ref[...], shift, 1)[first : first + lines, :own]
    members = all_ref.shape[0]
    share = all_ref.shape[1] // 3
    lines = weights[0].shape[0] // members
    for i, dst in enumerate(weights):
        for m in range(members):
            dst[m * lines : (m + 1) * lines, :] = all_ref[
                m, i * share : (i + 1) * share, :
            ].astype(jnp.float32)[:lines]


def finish(all_ff, tail, lines, gain_lines, qk_lines, *rest):
    vm = pl.BlockSpec(memory_space=pltpu.VMEM)
    f32 = jnp.float32
    results = ((lines, D),) * 3 + (gain_lines, qk_lines)
    return pl.pallas_call(
        finish_kernel,
        out_shape=tuple(jax.ShapeDtypeStruct(s, f32) for s in results)
        + tuple(jax.ShapeDtypeStruct(r.shape, r.dtype) for r in rest),
        in_specs=[vm] * (2 + len(rest)),
        out_specs=(vm,) * (5 + len(rest)),
        compiler_params=pltpu.CompilerParams(vmem_limit_bytes=62 * 1024 * 1024),
    )(all_ff, tail, *rest)


def on_device(
    tokens,
    norm_gains,
    qk_gains,
    qkv_weight,
    out_weight,
    gate_weight,
    up_weight,
    down_weight,
    segments,
    cotangent,
):
    local_len = tokens.shape[1]
    ctx_index = lax.axis_index("ctx")
    owner = lax.axis_index("fsdp")
    ctx_size = lax.axis_size("ctx")
    own_rows = gate_weight.shape[0]
    slice_rows = own_rows // ctx_size
    padded = -(-slice_rows // 16) * 16
    keep, width = qkv_weight.shape
    gain_lines, qk_lines = norm_gains.shape, qk_gains.shape
    def placed(lines):
        count, own = lines.shape
        room = (lax.axis_size("fsdp") - 1) * own
        padded_lines = jnp.pad(lines, ((0, 0), (room, room)))
        spread = lax.dynamic_slice(padded_lines, (0, room - owner * own), (count, room + own))
        return jnp.pad(spread, ((0, 0), (0, width - room - own)))

    gain_rows = jnp.concatenate(
        [placed(norm_gains), placed(qk_gains), jnp.zeros((2, width), jnp.bfloat16)], axis=0
    )

    def my_slice(weight):
        part = lax.dynamic_slice(weight, (ctx_index * slice_rows, 0), (slice_rows, D))
        return jnp.pad(part, ((0, padded - slice_rows), (0, 0)))

    ffn_shard = jnp.concatenate(
        [my_slice(gate_weight), my_slice(up_weight), my_slice(down_weight)], axis=0
    )
    places = np.arange(ctx_size * local_len, dtype=np.float32)
    rates = (ROPE_BASE ** (-(2.0 * np.arange(HD // 2)) / HD)).astype(np.float32)
    angles = (places[:, None] * rates).astype(np.float64)
    table = jnp.asarray(
        np.concatenate([np.cos(angles), np.sin(angles)], axis=1)
        .astype(np.float32)
        .reshape(ctx_size, local_len, HD)
    )
    flat = tokens.reshape(local_len, D)
    cot = cotangent.reshape(local_len, D)
    (
        qkv_full, out_full, ffn_full, gains_all, qk_all, normed, projected, queries, pair_all,
        attended, attn, mid, normed_two, bias, turn_table,
    ) = front(
        jnp.concatenate([qkv_weight, gain_rows], axis=0),
        out_weight,
        ffn_shard,
        flat,
        segments,
        table,
        keep,
    )
    output, grad_normed_two, grad_gain_three, ffn_grads = ffn(
        normed_two, mid, cot, gains_all, ffn_full
    )
    grad_tokens, total_qkv, tail, total_out, all_ff = backward_rest(
        ffn_grads,
        (
            grad_normed_two, mid, attn, cot, flat, gains_all, qk_all, projected, queries,
            pair_all, attended, normed, turn_table, bias, grad_gain_three,
        ),
        (qkv_full, out_full),
        keep,
    )
    (
        total_gate, total_up, total_down, total_gains, total_qk,
        grad_tokens, total_qkv, total_out, output,
    ) = finish(
        all_ff, tail, own_rows, gain_lines, qk_lines, grad_tokens, total_qkv, total_out, output
    )
    return (
        output.reshape(tokens.shape),
        grad_tokens.reshape(tokens.shape),
        total_gains,
        total_qk,
        total_qkv,
        total_out,
        total_gate,
        total_up,
        total_down,
    )


def solution(mesh):
    in_specs = (
        P("fsdp", "ctx", None),
        P(None, "fsdp"),
        P(None, "fsdp"),
        P("fsdp", None),
        P("fsdp", None),
        P("fsdp", None),
        P("fsdp", None),
        P("fsdp", None),
        P("fsdp", "ctx"),
        P("fsdp", "ctx", None),
    )
    out_specs = (
        P("fsdp", "ctx", None),
        P("fsdp", "ctx", None),
        P(None, "fsdp"),
        P(None, "fsdp"),
        P("fsdp", None),
        P("fsdp", None),
        P("fsdp", None),
        P("fsdp", None),
        P("fsdp", None),
    )
    return jax.shard_map(
        on_device, mesh=mesh, in_specs=in_specs, out_specs=out_specs, check_vma=False
    )
```

```python
import jax
import numpy as np
import jax.numpy as jnp
from jax import lax
from jax.experimental import pallas as pl
from jax.experimental.pallas import tpu as pltpu
from jax.sharding import PartitionSpec as P

D = 1152
NH = 4
HD = 256
WINDOW = 512


EPS = 1e-06
ROPE_BASE = 10000.0
NEG_FILL = -1e30


def rms_norm(values, gain_vec):
    return values * lax.rsqrt(jnp.mean(values * values, axis=-1, keepdims=True) + EPS) * gain_vec


MESH = pl.DeviceIdType.MESH
NT = (((1,), (1,)), ((), ()))
NN = (((1,), (0,)), ((), ()))
TN = (((0,), (0,)), ((), ()))
GELU_C = 0.7978845608028654
GELU_A = 0.044715


def dot32(left, right, dims):
    return lax.dot_general(left, right, dims, preferred_element_type=jnp.float32)


def place():
    fsdp = lax.axis_index("fsdp")
    ctx = lax.axis_index("ctx")
    y, z = fsdp // 4, lax.rem(fsdp, 4)
    chip, core = ctx // 2, lax.rem(ctx, 2)
    return y, z, chip, core


def shape_of(y, z, core):
    first = (1 - core) * y + core * z
    second = (1 - core) * z + core * y

    def block(i, j):
        return (1 - core) * (4 * i + j) + core * (4 * j + i)

    return first, second, block


def remote(src, dst, s_sem, r_sem, peer):
    return pltpu.make_async_remote_copy(
        src_ref=src, dst_ref=dst, send_sem=s_sem, recv_sem=r_sem,
        device_id=peer, device_id_type=MESH,
    )


def greet(peers):
    barrier = pltpu.get_barrier_semaphore()
    for peer in peers:
        pl.semaphore_signal(barrier, inc=1, device_id=peer, device_id_type=MESH)
    pl.semaphore_wait(barrier, len(peers))


def ring_gather(buf, rows, partner, chips, s_sem, r_sem):
    started, got = [], {}

    def send(src, dst, i, back, peer):
        copy = remote(src, dst, s_sem.at[i], r_sem.at[back], peer)
        copy.start()
        started.append(copy)
        return copy

    def mine(k):
        return buf.at[pl.ds(k * 2 * rows, rows)]

    def other(k):
        return buf.at[pl.ds(k * 2 * rows + rows, rows)]

    def half_of(k, h, offset=0):
        return buf.at[pl.ds(k * 2 * rows + offset + h * (rows // 2), rows // 2)]

    def spread():
        for k in (1, 3):
            got[4 - k] = send(mine(0), mine(4 - k), k, 4 - k, chips[k])
        got[0] = send(mine(0), other(0), 0, 0, partner)

    def relay(k):
        got[k].wait_recv()
        h = 0 if k == 3 else 1
        got[2, h] = send(half_of(k, h), half_of(2, h), 2 + 2 * h, 2 + 2 * h, chips[4 - k])
        got[k] = send(mine(k), other(k), 4 + k, 4 + k, partner)

    def relay_far():
        for h in (0, 1):
            got[2, h].wait_recv()
            got[2, h] = send(half_of(2, h), half_of(2, h, rows), 6 + 2 * h, 6 + 2 * h, partner)

    return spread, relay, relay_far, got, started


def ffn_kernel(
    seq, mid_ref, cot_ref, gain_ref, w_hbm,
    out_ref, gn_ref, ggain_ref, gff_hbm,
    wg, wu, wd, gseq, act_a, act_b, hid, dgate, dup, part, keep, base,
    d2d_snd, d2d_in, ici_snd, ici_in, dw,
    w_sem, o_sem, ag_s, ag_r, rd_s, rd_r, ri_s, ri_r,
):
    rows = mid_ref.shape[0]
    units = wg.shape[0]
    owners = w_hbm.shape[0]
    share = units // owners
    tile = 256
    me = lax.axis_index("ctx")
    chip, core = me // 2, lax.rem(me, 2)
    partner = {"ctx": chip * 2 + 1 - core}
    chips = {k: {"ctx": lax.rem(chip + k, 4) * 2 + core} for k in (1, 2, 3)}
    order = (0, 1, 3, 2)

    loads = [
        pltpu.make_async_copy(
            w_hbm.at[f, pl.ds(i * share, share), :], dst.at[pl.ds(f * share, share), :], w_sem.at[i, f]
        )
        for i, dst in enumerate((wg, wu, wd))
        for f in range(owners)
    ]
    for load in loads:
        load.start()

    barrier = pltpu.get_barrier_semaphore()
    for peer in (partner, chips[1], chips[2], chips[3]):
        pl.semaphore_signal(barrier, inc=1, device_id=peer, device_id_type=MESH)
    pl.semaphore_wait(barrier, 4)

    started = []

    def send(src, dst, s_sem, r_sem, peer):
        copy = pltpu.make_async_remote_copy(
            src_ref=src, dst_ref=dst, send_sem=s_sem, recv_sem=r_sem,
            device_id=peer, device_id_type=MESH,
        )
        copy.start()
        started.append(copy)
        return copy

    spread, relay, relay_far, got, gathers = ring_gather(gseq, rows, partner, chips, ag_s, ag_r)

    def pair(k):
        return pl.ds(k * 2 * rows, 2 * rows)

    def swap(ph, k):
        d2d_snd[ph, k] = part[pl.ds(rows, rows), :].astype(jnp.bfloat16)
        keep[order.index(k) % 2] = part[pl.ds(0, rows), :]
        return send(d2d_snd.at[ph, k], d2d_in.at[ph, k], rd_s.at[ph, k], rd_r.at[ph, k], partner)

    def sum_out(ph, k, copy):
        copy.wait_recv()
        total = keep[order.index(k) % 2] + d2d_in[ph, k].astype(jnp.float32)
        if k == 0:
            base[...] = total
            return None
        ici_snd[ph, k - 1] = total.astype(jnp.bfloat16)
        back = 4 - k
        return send(
            ici_snd.at[ph, k - 1], ici_in.at[ph, back - 1], ri_s.at[ph, k], ri_r.at[ph, back],
            chips[k],
        )

    def phase(ph, work):
        sums = {}
        copy = waiting = None
        for k in order:
            if ph == 1:
                if k == 1:
                    relay(1)
                    relay(3)
                if k == 2:
                    relay_far()
                    got[2, 0].wait_recv()
                    got[2, 1].wait_recv()
                else:
                    got[k].wait_recv()
            if waiting is not None and k == 2:
                sums[waiting] = sum_out(ph, waiting, copy)
                waiting = None
            work(k)
            if waiting is not None:
                sums[waiting] = sum_out(ph, waiting, copy)
            copy, waiting = swap(ph, k), k
        sums[waiting] = sum_out(ph, waiting, copy)
        return sums

    def collect(ph, sums):
        total = base[...]
        for k in (1, 3, 2):
            sums[k].wait_recv()
        for k in (1, 2, 3):
            total = total + ici_in[ph, k - 1].astype(jnp.float32)
        return total

    def forward(k):
        def one(t, carry):
            cols = pl.ds(pl.multiple_of(t * tile, tile), tile)
            block = seq[pair(k), :]
            gate = dot32(block, wg[cols, :], NT)
            up = dot32(block, wu[cols, :], NT)
            square = gate * gate
            th = jnp.tanh(GELU_C * gate * (1.0 + GELU_A * square))
            half = 0.5 * (1.0 + th)
            gelu = gate * half
            slope = half + (0.5 * GELU_C) * gate * (1.0 - th * th) * (1.0 + 3.0 * GELU_A * square)
            hid[pair(k), cols] = (gelu * up).astype(jnp.bfloat16)
            act_a[pair(k), cols] = up * slope
            act_b[pair(k), cols] = gelu
            return carry

        lax.fori_loop(0, units // tile, one, 0)
        if k == 0:
            for load in loads[2 * owners :]:
                load.wait()
        part[...] = dot32(hid[pair(k), :], wd[...], NN)

    for load in loads[: 2 * owners]:
        load.wait()
    sums = phase(0, forward)
    mlp = collect(0, sums)
    r = lax.rsqrt(jnp.mean(mlp * mlp, axis=-1, keepdims=True) + EPS)
    n = mlp * r
    gain = gain_ref[3:4, :]
    out_ref[...] = (mid_ref[...] + n * gain).astype(jnp.bfloat16)
    dy = cot_ref[...].astype(jnp.float32)
    ggain_ref[...] = jnp.sum(dy * n, axis=0, keepdims=True)
    dyg = dy * gain
    dv = r * (dyg - n * jnp.mean(dyg * n, axis=-1, keepdims=True))
    gseq[pl.ds(0, rows), :] = dv.astype(jnp.bfloat16)
    spread()

    def backward(k):
        def one(t, carry):
            cols = pl.ds(pl.multiple_of(t * tile, tile), tile)
            gh = dot32(gseq[pair(k), :], wd[cols, :], NT)
            dgate[pair(k), cols] = (gh * act_a[pair(k), cols]).astype(jnp.bfloat16)
            dup[pair(k), cols] = (gh * act_b[pair(k), cols]).astype(jnp.bfloat16)
            return carry

        lax.fori_loop(0, units // tile, one, 0)
        part[...] = dot32(dgate[pair(k), :], wg[...], NN) + dot32(dup[pair(k), :], wu[...], NN)

    sums = phase(1, backward)
    stores = []
    for i, (left, right) in enumerate(((dgate, seq), (dup, seq), (hid, gseq))):
        def one(t, carry, i=i, left=left, right=right):
            cols = pl.ds(pl.multiple_of(t * tile, tile), tile)
            group = tile // share
            dw[pl.ds(t * group, group), pl.ds(i * share, share), :] = (
                dot32(left[:, cols], right[...], TN).reshape(group, share, -1).astype(jnp.bfloat16)
            )
            return carry

        lax.fori_loop(0, units // tile, one, 0)
        third = pl.ds(i * share, share)
        stores.append(
            pltpu.make_async_copy(dw.at[:, third, :], gff_hbm.at[:, third, :], o_sem.at[i])
        )
        stores[-1].start()
    gn_ref[...] = collect(1, sums)
    for copy in started + gathers:
        copy.wait_send()
    for store in stores:
        store.wait()


def ffn(normed_seq, mid, cot, gain, weights):
    rows = mid.shape[0]
    owners, lines = weights.shape[:2]
    units = owners * lines // 3
    seq_rows = rows * 8
    bf, f32 = jnp.bfloat16, jnp.float32
    vm = pl.BlockSpec(memory_space=pltpu.VMEM)
    hbm = pl.BlockSpec(memory_space=pl.ANY)
    dma = pltpu.SemaphoreType.DMA
    return pl.pallas_call(
        ffn_kernel,
        out_shape=(
            jax.ShapeDtypeStruct((rows, D), bf),
            jax.ShapeDtypeStruct((rows, D), f32),
            jax.ShapeDtypeStruct((1, D), f32),
            jax.ShapeDtypeStruct(weights.shape, bf),
        ),
        in_specs=[vm] * 4 + [hbm],
        out_specs=(vm, vm, vm, hbm),
        scratch_shapes=[
            pltpu.VMEM((units, D), bf),
            pltpu.VMEM((units, D), bf),
            pltpu.VMEM((units, D), bf),
            pltpu.VMEM((seq_rows, D), bf),
            pltpu.VMEM((seq_rows, units), f32),
            pltpu.VMEM((seq_rows, units), f32),
            pltpu.VMEM((seq_rows, units), bf),
            pltpu.VMEM((seq_rows, units), bf),
            pltpu.VMEM((seq_rows, units), bf),
            pltpu.VMEM((2 * rows, D), f32),
            pltpu.VMEM((2, rows, D), f32),
            pltpu.VMEM((rows, D), f32),
            pltpu.VMEM((2, 4, rows, D), bf),
            pltpu.VMEM((2, 4, rows, D), bf),
            pltpu.VMEM((2, 3, rows, D), bf),
            pltpu.VMEM((2, 3, rows, D), bf),
            pltpu.VMEM(weights.shape, bf),
            dma((3, owners)), dma((3,)),
            dma((10,)), dma((10,)),
            dma((2, 4)), dma((2, 4)),
            dma((2, 4)), dma((2, 4)),
        ],
        compiler_params=pltpu.CompilerParams(
            collective_id=1, has_side_effects=True, vmem_limit_bytes=62 * 1024 * 1024
        ),
        cost_estimate=pl.CostEstimate(
            flops=18 * seq_rows * units * D, bytes_accessed=14 * units * D, transcendentals=0
        ),
    )(normed_seq, mid, cot, gain, weights)


def rms_back(values, grad, gain):
    r = lax.rsqrt(jnp.mean(values * values, axis=-1, keepdims=True) + EPS)
    n = values * r
    dyg = grad * gain
    return (
        r * (dyg - n * jnp.mean(dyg * n, axis=-1, keepdims=True)),
        jnp.sum(grad * n, axis=0, keepdims=True),
    )


def stack_heads(values):
    return jnp.concatenate([values[:, h * HD : (h + 1) * HD] for h in range(NH)], axis=0)


def turn_back(grad, cos_table, sin_table):
    left, right = grad[:, : HD // 2], grad[:, HD // 2 :]
    return jnp.concatenate(
        [left * cos_table + right * sin_table, right * cos_table - left * sin_table], axis=1
    )


def front_kernel(
    qkv_ref, wo_ref, ffn_ref, tok_ref, seg_line, table_ref,
    qkv_hbm, wo_hbm, ffn_all, gains_ref, qk_ref, normed_ref, proj_ref, q_ref, pair_ref, att_ref,
    attn_ref, mid_ref, seq, bias_ref, turn_ref,
    qkv_all, qkv_out, wo_all, seg_ref, seg_in,
    l_sem, s1, r1, s2, r2, sd, rd, s1f, r1f, s2f, r2f, skv, rkv, ssg, rsg, ag_s, ag_r,
):
    f32, bf = jnp.float32, jnp.bfloat16
    y, z, chip, core = place()
    a, b, block = shape_of(y, z, core)
    _, _, block_there = shape_of(y, z, 1 - core)
    q_rows, width = qkv_ref.shape
    o_rows = wo_ref.shape[0]
    q_half, o_half = width // 2, o_rows // 2
    partner = {"ctx": chip * 2 + 1 - core}
    me = chip * 2 + core
    rows = tok_ref.shape[0]
    reach = pair_ref.shape[0] // rows - 1
    members = 2 * (lax.axis_size("ctx") // 2)

    def member(k):
        return {"ctx": lax.rem(me + k, members)}

    seg_ref[...] = jnp.broadcast_to(seg_line[...], seg_ref.shape)

    def views(f, half):
        return (
            qkv_all.at[
                pl.ds(pl.multiple_of(f * q_rows, 16), q_rows),
                pl.ds(pl.multiple_of(half * q_half, 128), q_half),
            ],
            wo_all.at[pl.ds(pl.multiple_of(f * o_rows + half * o_half, 16), o_half), :],
        )

    mine = (
        qkv_ref.at[:, pl.ds(pl.multiple_of(core * q_half, 128), q_half)],
        wo_ref.at[pl.ds(pl.multiple_of(core * o_half, 16), o_half), :],
    )
    here = block(a, b)
    locals_ = [
        pltpu.make_async_copy(
            qkv_ref, qkv_all.at[pl.ds(pl.multiple_of(here * q_rows, 16), q_rows), :], l_sem.at[0]
        ),
        pltpu.make_async_copy(
            wo_ref, wo_all.at[pl.ds(pl.multiple_of(here * o_rows, 16), o_rows), :], l_sem.at[1]
        ),
        pltpu.make_async_copy(ffn_ref, ffn_all.at[here], l_sem.at[2]),
        pltpu.make_async_copy(table_ref.at[me], turn_ref, l_sem.at[3]),
    ]
    for copy in locals_:
        copy.start()

    def first_peer(k):
        return {"fsdp": block(lax.rem(a + k, 4), b)}

    def second_peer(k):
        return {"fsdp": block(a, lax.rem(b + k, 4))}

    greet(
        [first_peer(k) for k in (1, 2, 3)]
        + [second_peer(k) for k in (1, 2, 3)]
        + [member(k) for k in range(1, members)]
    )

    def seg_send(d):
        return remote(
            seg_ref, seg_in.at[reach - d], ssg.at[d - 1], rsg.at[d - 1], member(d)
        )

    def ffn_one(k):
        return remote(ffn_ref, ffn_all.at[here], s1f.at[k], r1f.at[4 - k], first_peer(k))

    def ffn_block(j, m):
        return ffn_all.at[block(lax.rem(a + j, 4), lax.rem(b + m, 4))]

    def ffn_two(j, k):
        dst = ffn_block(j, 0)
        src = dst if j else ffn_ref
        return remote(src, dst, s2f.at[j, k], r2f.at[j, 4 - k], second_peer(k))

    def ffn_pass(j):
        dst, k = (ffn_block(j, 3), 1) if j < 2 else (ffn_block(j, 1), 3)
        return remote(dst, dst, s2f.at[j, 2], r2f.at[j, 2], second_peer(k))

    def ffn_got(j, m):
        dst = ffn_block(j, m)
        sems = (s1f.at[j], r1f.at[j]) if m == 0 else (s2f.at[j, m], r2f.at[j, m])
        return remote(dst, dst, *sems, partner)

    def hop_one(k, t):
        return remote(mine[t], views(here, core)[t], s1.at[k, t], r1.at[4 - k, t], first_peer(k))

    def hop_two(j, k, t):
        f = block(lax.rem(a + j, 4), b)
        dst = views(f, core)[t]
        src = dst if j else mine[t]
        return remote(src, dst, s2.at[j, k, t], r2.at[j, 4 - k, t], second_peer(k))

    def arrive_one(j, t):
        dst = views(block(lax.rem(a + j, 4), b), core)[t]
        return remote(dst, dst, s1.at[j, t], r1.at[j, t], partner)

    def arrive_two(j, m, t):
        dst = views(block(lax.rem(a + j, 4), lax.rem(b + m, 4)), core)[t]
        return remote(dst, dst, s2.at[j, m, t], r2.at[j, m, t], partner)

    def cross(j, m, t):
        dst = views(block(lax.rem(a + j, 4), lax.rem(b + m, 4)), core)[t]
        return remote(dst, dst, sd.at[j, m, t], rd.at[j, m, t], partner)

    def arrive_cross(j, m, t):
        dst = views(block_there(lax.rem(b + j, 4), lax.rem(a + m, 4)), 1 - core)[t]
        return remote(dst, dst, sd.at[j, m, t], rd.at[j, m, t], partner)

    both = (0, 1)
    for k in (1, 3, 2):
        for t in both:
            hop_one(k, t).start()
    def hop_pass(j, t):
        m, k = (3, 1) if j < 2 else (1, 3)
        dst = views(block(lax.rem(a + j, 4), lax.rem(b + m, 4)), core)[t]
        return remote(dst, dst, s2.at[j, 2, t], r2.at[j, 2, t], second_peer(k))

    for k in (1, 3):
        for t in both:
            hop_two(0, k, t).start()
    for j in (1, 3, 2):
        for t in both:
            arrive_one(j, t).wait_recv()
            for k in (1, 3):
                hop_two(j, k, t).start()
            cross(j, 0, t).start()

    for d in range(1, reach + 1):
        seg_send(d).start()
    for k in (1, 3, 2):
        ffn_one(k).start()
    for k in (1, 3):
        ffn_two(0, k).start()

    for j in (0, 1, 3, 2):
        for m in (3, 1) if j < 2 else (1, 3):
            for t in both:
                arrive_two(j, m, t).wait_recv()
                if m == (3 if j < 2 else 1):
                    hop_pass(j, t).start()
                cross(j, m, t).start()
    for j in (0, 1, 3, 2):
        for t in both:
            arrive_two(j, 2, t).wait_recv()
            cross(j, 2, t).start()

    def land(i, carry):
        m, j = i // 4, lax.rem(i, 4)
        for t in both:
            arrive_cross(j, m, t).wait_recv()
            cross(j, m, t).wait_send()
        return carry

    lax.fori_loop(1, 16, land, 0)
    for copy in locals_[:2]:
        copy.wait()
    for t in both:
        for k in (1, 2, 3):
            hop_one(k, t).wait_send()
        for j in range(4):
            hop_pass(j, t).wait_send()
            for k in (1, 3):
                hop_two(j, k, t).wait_send()
    saves = [
        pltpu.make_async_copy(qkv_out, qkv_hbm, l_sem.at[4]),
        pltpu.make_async_copy(wo_all, wo_hbm, l_sem.at[5]),
    ]
    saves[1].start()

    keep = qkv_out.shape[0] // 16
    extra = jnp.zeros((q_rows - keep, width), f32)
    for f in range(0, 16, 2):
        left = qkv_all[pl.ds(f * q_rows, q_rows), :].astype(f32)
        right = qkv_all[pl.ds((f + 1) * q_rows, q_rows), :].astype(f32)
        qkv_out[pl.ds(f * keep, 2 * keep), :] = jnp.concatenate(
            [left[:keep], right[:keep]], axis=0
        ).astype(bf)
        extra = extra + left[keep:] + right[keep:]
    saves[0].start()
    gains = extra[:4, :D]
    gains_ref[...] = gains
    qk_ref[...] = extra[4:6, :HD]

    stream = tok_ref[...].astype(f32)
    normed_ref[...] = rms_norm(stream, gains[0:1]).astype(bf)
    proj_ref[...] = dot32(normed_ref[...], qkv_out[...], NN)
    locals_[3].wait()
    cos_table, sin_table = turn_ref[:, : HD // 2], turn_ref[:, HD // 2 :]

    def turn(values, gain, cos_part, sin_part):
        values = rms_norm(values, gain)
        left, right = values[:, : HD // 2], values[:, HD // 2 :]
        return jnp.concatenate(
            [left * cos_part - right * sin_part, right * cos_part + left * sin_part], axis=1
        ).astype(bf)

    own = pl.ds(reach * rows, rows)
    pair_ref[own, :HD] = turn(
        proj_ref[:, NH * HD : NH * HD + HD], extra[5:6, :HD], cos_table, sin_table
    )
    pair_ref[own, HD:] = proj_ref[:, NH * HD + HD :].astype(bf)

    def kv_send(d):
        return remote(
            pair_ref.at[own],
            pair_ref.at[pl.ds((reach - d) * rows, rows)],
            skv.at[d - 1], rkv.at[d - 1], member(d),
        )

    for d in range(1, reach + 1):
        kv_send(d).start()
    for j in (1, 3, 2):
        ffn_got(j, 0).wait_recv()
        for k in (1, 3):
            ffn_two(j, k).start()
    queries = turn(
        stack_heads(proj_ref[:, : NH * HD]),
        extra[4:5, :HD],
        jnp.concatenate([cos_table] * NH, axis=0),
        jnp.concatenate([sin_table] * NH, axis=0),
    )
    for h in range(NH):
        q_ref[:, h * HD : (h + 1) * HD] = queries[h * rows : (h + 1) * rows]

    for d in range(1, reach + 1):
        seg_send(d).wait_recv()
    seg_in[reach] = seg_ref[...]
    key_seg = jnp.concatenate([seg_in[p][0:1, :] for p in range(reach + 1)], axis=1)
    shape = (rows, (reach + 1) * rows)
    spacing = (
        reach * rows + lax.broadcasted_iota(jnp.int32, shape, 0)
        - lax.broadcasted_iota(jnp.int32, shape, 1)
    )
    begun = lax.broadcasted_iota(jnp.int32, shape, 1) + (me - reach) * rows >= 0
    wide = jnp.broadcast_to(seg_line[...], (rows, rows)).astype(f32)
    query_seg = jnp.concatenate([wide.T] * (reach + 1), axis=1)
    allowed = (
        (spacing >= 0) & (spacing < WINDOW) & begun & (query_seg == key_seg.astype(f32))
    )
    bias_ref[...] = jnp.where(allowed, 0.0, NEG_FILL)
    def ffn_onward(j):
        ffn_got(j, 3 if j < 2 else 1).wait_recv()
        ffn_pass(j).start()

    ffn_onward(0)
    for d in range(1, reach + 1):
        kv_send(d).wait_recv()
    scores = dot32(queries, pair_ref[:, :HD], NT) * (HD ** (-0.5)) + jnp.concatenate(
        [bias_ref[...]] * NH, axis=0
    )
    expo = jnp.exp(scores - jnp.max(scores, axis=-1, keepdims=True))
    probs = expo * (1.0 / jnp.sum(expo, axis=-1, keepdims=True))
    heads = dot32(probs.astype(bf), pair_ref[:, HD:], NN).astype(bf)
    for h in range(NH):
        att_ref[:, h * HD : (h + 1) * HD] = heads[h * rows : (h + 1) * rows]
    ffn_onward(1)
    ffn_onward(3)
    attn = dot32(att_ref[...], wo_all[...], NN)
    attn_ref[...] = attn
    mid = stream + rms_norm(attn, gains[1:2])
    mid_ref[...] = mid
    seq[pl.ds(0, rows), :] = rms_norm(mid, gains[2:3]).astype(bf)
    ring = {k: {"ctx": lax.rem(chip + k, members // 2) * 2 + core} for k in (1, 2, 3)}
    spread, relay, relay_far, got, gathers = ring_gather(seq, rows, partner, ring, ag_s, ag_r)
    spread()

    ffn_onward(2)
    relay(1)
    relay(3)
    for copy in saves + locals_[2:3]:
        copy.wait()
    for j in range(4):
        ffn_got(j, 1 if j < 2 else 3).wait_recv()
        ffn_got(j, 2).wait_recv()
    relay_far()
    for copy in got.values():
        copy.wait_recv()
    for copy in gathers:
        copy.wait_send()
    for j in range(4):
        ffn_pass(j).wait_send()
        for k in (1, 3):
            ffn_two(j, k).wait_send()
    for k in (1, 2, 3):
        ffn_one(k).wait_send()
    for d in range(1, reach + 1):
        seg_send(d).wait_send()
        kv_send(d).wait_send()


def front(qkv_shard, wo_shard, ffn_shard, tokens, seg_line, table, keep):
    f32, bf = jnp.float32, jnp.bfloat16
    vm = pl.BlockSpec(memory_space=pltpu.VMEM)
    hbm = pl.BlockSpec(memory_space=pl.ANY)
    dma = pltpu.SemaphoreType.DMA
    q_rows, width = qkv_shard.shape
    o_rows, o_width = wo_shard.shape
    rows = tokens.shape[0]
    reach = min(-(-(WINDOW - 1) // rows), lax.axis_size("ctx") - 1)
    pairs = (reach + 1) * rows
    shapes = (
        ((16 * keep, width), bf),
        ((16 * o_rows, o_width), bf),
        ((16, *ffn_shard.shape), bf),
        ((4, D), f32),
        ((2, HD), f32),
        ((rows, D), bf),
        ((rows, width), f32),
        ((rows, NH * HD), bf),
        ((pairs, 2 * HD), bf),
        ((rows, NH * HD), bf),
        ((rows, D), f32),
        ((rows, D), f32),
        ((rows * lax.axis_size("ctx"), D), bf),
        ((rows, pairs), f32),
        ((rows, HD), f32),
    )
    return pl.pallas_call(
        front_kernel,
        out_shape=tuple(jax.ShapeDtypeStruct(*s) for s in shapes),
        in_specs=[vm, vm, hbm, vm, vm, hbm],
        out_specs=(hbm,) * 3 + (vm,) * (len(shapes) - 3),
        scratch_shapes=[
            pltpu.VMEM((16 * q_rows, width), bf),
            pltpu.VMEM((16 * keep, width), bf),
            pltpu.VMEM((16 * o_rows, o_width), bf),
            pltpu.VMEM((8, rows), jnp.int32),
            pltpu.VMEM((reach + 1, 8, rows), jnp.int32),
            dma((6,)),
            dma((4, 2)), dma((4, 2)),
            dma((4, 4, 2)), dma((4, 4, 2)),
            dma((4, 4, 2)), dma((4, 4, 2)),
            dma((4,)), dma((4,)),
            dma((4, 4)), dma((4, 4)),
            dma((reach,)), dma((reach,)),
            dma((reach,)), dma((reach,)),
            dma((10,)), dma((10,)),
        ],
        compiler_params=pltpu.CompilerParams(
            collective_id=2, has_side_effects=True, vmem_limit_bytes=62 * 1024 * 1024
        ),
        cost_estimate=pl.CostEstimate(
            flops=6 * rows * width * D, bytes_accessed=64 * q_rows * width, transcendentals=0
        ),
    )(qkv_shard, wo_shard, ffn_shard, tokens, seg_line, table)


def back_kernel(
    gff, gn_ref, mid_ref, attn_ref, cot_ref, tok_ref, gains_ref, qk_ref, proj_ref, q_ref,
    pair_ref, att_ref, normed_ref, turn_ref, bias_ref, g3_ref, qkv_hbm, wo_hbm,
    gt_ref, oq_out, tail_out, oo_ref, all_ff,
    qkv_ref, wo_ref, oq_ref, own_ff, far_own, far_in, in1_ff, t_ff, in2_ff, kv_snd, kv_in, gmid, gpair, gproj, tail,
    stage, go, dq, do, sq, so, fq, fo, iq1, io1, tq, to, iq2, io2, xq, xo,
    l_sem, sfar, rfar, s1f, r1f, s2f, r2f, sag, rag, skv, rkv,
    sd, rd, sfa, rfa, s1, r1, s2, r2, sx, rx, sf, rf,
):
    y, z, chip, core = place()
    a, b, block = shape_of(y, z, core)
    _, _, block_there = shape_of(y, z, 1 - core)
    me = chip * 2 + core
    rows = gn_ref.shape[0]
    q_rows, width = oq_ref.shape
    keep = normed_ref.shape[1] // 16
    o_rows = oo_ref.shape[0]
    q_half, o_half = width // 2, o_rows // 2
    chips = xq.shape[0]
    members = 2 * chips
    reach = kv_in.shape[0]
    scale = HD ** (-0.5)
    f32, bf = jnp.float32, jnp.bfloat16
    partner = {"ctx": chip * 2 + 1 - core}

    def first_peer(k):
        return {"fsdp": block(lax.rem(a + k, 4), b)}

    def second_peer(k):
        return {"fsdp": block(a, lax.rem(b + k, 4))}

    def chip_peer(k):
        return {"ctx": lax.rem(chip + k, chips) * 2 + core}

    def member(k):
        return {"ctx": lax.rem(me + k, members)}

    def q_cols(half):
        return pl.ds(pl.multiple_of(half * q_half, 128), q_half)

    def o_lines(half):
        return pl.ds(pl.multiple_of(half * o_half, 16), o_half)

    def line(k):
        return lax.rem(a + k, 4)

    own_loads = [
        pltpu.make_async_copy(gff.at[block(a, j)], own_ff.at[j], l_sem.at[j]) for j in range(4)
    ] + [
        pltpu.make_async_copy(
            gff.at[block(line(1 if j < 2 else 3), j)], far_own.at[j], l_sem.at[4 + j]
        )
        for j in range(4)
    ]
    weight_loads = [
        pltpu.make_async_copy(wo_hbm, wo_ref, l_sem.at[8]),
        pltpu.make_async_copy(qkv_hbm, qkv_ref, l_sem.at[9]),
    ]
    for copy in own_loads + weight_loads:
        copy.start()
    greet(
        [first_peer(k) for k in (1, 2, 3)]
        + [second_peer(k) for k in (1, 2, 3)]
        + [member(k) for k in range(1, members)]
    )

    def ff_far(j):
        k = 1 if j < 2 else 3
        return remote(
            gff.at[block(line(2), j)], far_in.at[j], sfar.at[j], rfar.at[j], first_peer(k)
        )

    def ff_near(k, j):
        side = 0 if k == 1 else 1
        direct = (j >= 2) == (k == 1)
        src = gff.at[block(line(k), j)] if direct else far_own.at[j]
        return remote(src, in1_ff.at[side, j], s1f.at[side, j], r1f.at[side, j], first_peer(k))

    for j in (0, 2, 1, 3):
        ff_far(j).start()
    for k, j in ((1, 2), (3, 0), (1, 3), (3, 1)):
        ff_near(k, j).start()

    def pass_far(js):
        for j in js:
            ff_far(j).wait_recv()
            own_loads[4 + j].wait()
            far_own[j] = (far_own[j].astype(f32) + far_in[j].astype(f32)).astype(bf)
            ff_near(1 if j < 2 else 3, j).start()

    for copy in weight_loads[:1]:
        copy.wait()

    grad_final = cot_ref[...].astype(f32)
    part, gain_two = rms_back(mid_ref[...], gn_ref[...], gains_ref[2:3, :])
    grad_mid = grad_final + part
    gmid[...] = grad_mid
    grad_attn, gain_one = rms_back(attn_ref[...], grad_mid, gains_ref[1:2, :])
    grad_attn_low = grad_attn.astype(bf)
    grad_attended = dot32(grad_attn_low, wo_ref[...], NT).astype(bf)

    def out_tile(t, carry):
        cols = pl.ds(pl.multiple_of(t * 256, 256), 256)
        go[pl.ds(t * 4, 4)] = (
            dot32(att_ref[:, cols], grad_attn_low, TN).reshape(4, 64, D).astype(bf)
        )
        return carry

    lax.fori_loop(0, NH * HD // 256, out_tile, 0)

    def away(i, t):
        k, j = lax.rem(i // 4 + 2, 4), lax.rem(i, 4)
        there = lax.rem(b + k, 4)
        f = block_there(there, j)
        slot = there * 4 + j
        if t == 0:
            src, dst = stage.at[f, :, q_cols(1 - core)], dq.at[slot]
        else:
            src, dst = go.at[f, o_lines(1 - core), :], do.at[slot]
        return remote(src, dst, sd.at[i, t], rd.at[i, t], partner)

    def home(i, t):
        k, j = lax.rem(i // 4 + 2, 4), lax.rem(i, 4)
        slot = lax.rem(a + k, 4) * 4 + j
        dst = (dq, do)[t].at[slot]
        return remote(dst, dst, sd.at[i, t], rd.at[i, t], partner)

    def start_away(t):
        def one(i, carry):
            away(i, t).start()
            return carry

        lax.fori_loop(0, 16, one, 0)

    start_away(1)

    keys, vals = pair_ref[:, :HD], pair_ref[:, HD:]
    queries = stack_heads(q_ref[...])
    grad_heads = stack_heads(grad_attended)
    scores = dot32(queries, keys, NT) * scale + jnp.concatenate([bias_ref[...]] * NH, axis=0)
    expo = jnp.exp(scores - jnp.max(scores, axis=-1, keepdims=True))
    probs = expo * (1.0 / jnp.sum(expo, axis=-1, keepdims=True))
    grad_probs = dot32(grad_heads, vals, NT)
    row_total = jnp.sum(probs * grad_probs, axis=-1, keepdims=True)
    grad_scores = (probs * (grad_probs - row_total)).astype(bf)
    gpair[:, HD:] = dot32(probs.astype(bf), grad_heads, TN)
    gpair[:, :HD] = dot32(grad_scores, queries, TN) * scale

    def kv_send(d):
        return remote(
            kv_snd.at[d - 1], kv_in.at[d - 1], skv.at[d - 1], rkv.at[d - 1], member(members - d)
        )

    for d in range(1, reach + 1):
        kv_snd[d - 1] = gpair[pl.ds((reach - d) * rows, rows), :].astype(bf)
        kv_send(d).start()

    pass_far((0, 2))
    cos_table, sin_table = turn_ref[:, : HD // 2], turn_ref[:, HD // 2 :]
    cos_all = jnp.concatenate([cos_table] * NH, axis=0)
    sin_all = jnp.concatenate([sin_table] * NH, axis=0)
    grad_queries = dot32(grad_scores, keys, NN) * scale
    grad_q, qk_gain_q = rms_back(
        stack_heads(proj_ref[:, : NH * HD]),
        turn_back(grad_queries, cos_all, sin_all),
        qk_ref[0:1, :],
    )
    for h in range(NH):
        gproj[:, h * HD : (h + 1) * HD] = grad_q[h * rows : (h + 1) * rows].astype(bf)

    def pair_of(k, h):
        return pl.ds(line(k) * 4 + 2 * h, 2)

    def sum_far(h, t):
        src, dst = ((sq, fq), (so, fo))[t]
        return remote(
            src.at[pair_of(2, h)], dst.at[pl.ds(2 * h, 2)],
            sfa.at[h, t], rfa.at[h, t], first_peer(3 if h else 1),
        )

    def sum_near(k, h, t):
        src, dst = ((sq, iq1), (so, io1))[t]
        side = 0 if k == 1 else 1
        return remote(
            src.at[pair_of(k, h)], dst.at[side, pl.ds(2 * h, 2)],
            s1.at[side, h, t], r1.at[side, h, t], first_peer(k),
        )

    def fold_cores(t):
        for k in (2, 3, 1, 0):
            def add(j, carry, k=k):
                slot = line(k) * 4 + j
                f = block(line(k), j)
                home((k + 2) % 4 * 4 + j, t).wait_recv()
                if t == 0:
                    sq[slot] = (
                        stage[f, :, q_cols(core)].astype(f32) + dq[slot].astype(f32)
                    ).astype(bf)
                else:
                    so[slot] = (
                        go[f, o_lines(core), :].astype(f32) + do[slot].astype(f32)
                    ).astype(bf)
                return carry

            lax.fori_loop(0, 4, add, 0)

    def send_cores(t):
        sum_far(0, t).start()
        sum_far(1, t).start()
        sum_near(3, 0, t).start()
        sum_near(1, 1, t).start()

    def fold_far(t):
        acc, far = ((sq, fq), (so, fo))[t]
        for h, k in ((0, 1), (1, 3)):
            sum_far(h, t).wait_recv()
            acc[pair_of(k, h)] = (
                acc[pair_of(k, h)].astype(f32) + far[2 * h : 2 * h + 2].astype(f32)
            ).astype(bf)
            sum_near(k, h, t).start()

    fold_cores(1)
    send_cores(1)
    pass_far((1, 3))

    total = gpair[pl.ds(reach * rows, rows), :]
    for d in range(1, reach + 1):
        kv_send(d).wait_recv()
        total = total + kv_in[d - 1].astype(f32)
    grad_k, qk_gain_k = rms_back(
        proj_ref[:, NH * HD : NH * HD + HD],
        turn_back(total[:, :HD], cos_table, sin_table),
        qk_ref[1:2, :],
    )
    gproj[:, NH * HD : NH * HD + HD] = grad_k.astype(bf)
    gproj[:, NH * HD + HD :] = total[:, HD:].astype(bf)
    for copy in weight_loads[1:]:
        copy.wait()
    stream = tok_ref[...].astype(f32)
    grad_in, gain_zero = rms_back(stream, dot32(gproj[...], qkv_ref[...], NT), gains_ref[0:1, :])
    gt_ref[...] = gmid[...] + grad_in
    tail[...] = jnp.zeros_like(tail)
    for i, total_gain in enumerate((gain_zero, gain_one, gain_two, g3_ref[...])):
        tail[i : i + 1, :D] = total_gain
    tail[4:5, :HD] = qk_gain_q
    tail[5:6, :HD] = qk_gain_k

    def qkv_tile(t, carry):
        cols = pl.ds(pl.multiple_of(t * 256, 256), 256)
        res = dot32(normed_ref[...], gproj[:, cols], TN)
        low = tail[:, cols]
        for f in range(16):
            stage[f, :, cols] = jnp.concatenate(
                [res[f * keep : (f + 1) * keep], low], axis=0
            ).astype(bf)
        return carry

    lax.fori_loop(0, width // 256, qkv_tile, 0)
    start_away(0)
    fold_cores(0)

    for copy in own_loads[:4]:
        copy.wait()

    def ff_two(k):
        return remote(
            t_ff.at[lax.rem(b + k, 4)], in2_ff.at[3 - k], s2f.at[k], r2f.at[4 - k], second_peer(k)
        )

    for k in (2, 1, 3, 0):
        j = lax.rem(b + k, 4)
        for m in (0, 1):
            dst = in1_ff.at[m, j]
            remote(dst, dst, s1f.at[m, j], r1f.at[m, j], partner).wait_recv()
        total = own_ff[j].astype(f32)
        for m in (0, 1):
            total = total + in1_ff[m, j].astype(f32)
        t_ff[j] = total.astype(bf)
        if k:
            ff_two(k).start()

    send_cores(0)
    fold_far(1)
    fold_far(0)

    def hop_two(k, t):
        src, dst = ((tq, iq2), (to, io2))[t]
        return remote(
            src.at[lax.rem(b + k, 4)], dst.at[3 - k], s2.at[k, t], r2.at[4 - k, t], second_peer(k)
        )

    for k in (1, 3, 2):
        ff_two(4 - k).wait_recv()
    total = t_ff[b].astype(f32)
    for m in range(3):
        total = total + in2_ff[m].astype(f32)
    all_ff[me] = total.astype(bf)

    half = all_ff.shape[1] // 2

    def ff_slot(k, there=0):
        return lax.rem(chip + k, chips) * 2 + (1 - core if there else core)

    def ff_all(k):
        peer = chip_peer(k) if k else partner
        return remote(
            all_ff.at[me], all_ff.at[me], sag.at[k], rag.at[(chips - k) % chips], peer
        )

    def ff_from(k):
        dst = all_ff.at[ff_slot(k)]
        return remote(dst, dst, sag.at[k], rag.at[k], partner)

    def ff_half(k, h, there=0):
        return all_ff.at[ff_slot(k, there), pl.ds(h * half, half), :]

    def ff_on(k):
        h = 0 if k == 3 else 1
        dst = ff_half(k, h)
        return remote(dst, dst, sag.at[8 + h], rag.at[8 + h], chip_peer(4 - k))

    def ff_far_got(h):
        dst = ff_half(2, h)
        return remote(dst, dst, sag.at[8 + h], rag.at[8 + h], partner)

    def ff_cross(k, h=None, there=0):
        if h is None:
            dst, i = all_ff.at[ff_slot(k, there)], 4 + k
        else:
            dst, i = ff_half(2, h, there), 10 + h
        return remote(dst, dst, sag.at[i], rag.at[i], partner)

    for k in (1, 3, 0):
        ff_all(k).start()

    for t in (1, 0):
        own, got, dst = ((sq, iq1, tq), (so, io1, to))[t]
        for k in (1, 3):
            for h in (0, 1):
                sum_near(k, h, t).wait_recv()
        for k in (2, 1, 3, 0):
            j = lax.rem(b + k, 4)
            total = own[a * 4 + j].astype(f32)
            for m in (0, 1):
                total = total + got[m, j].astype(f32)
            dst[j] = total.astype(bf)
            if k:
                hop_two(k, t).start()

    for k in (1, 3):
        ff_from(k).wait_recv()
        ff_on(k).start()
        ff_cross(k).start()

    def hop_chip(k, t):
        buf = (xq, xo)[t]
        return remote(
            buf.at[chip], buf.at[chip], sx.at[k, t], rx.at[chips - k, t], chip_peer(k)
        )

    for t in (1, 0):
        own, got, dst = ((tq, iq2, xq), (to, io2, xo))[t]
        for k in (1, 3, 2):
            hop_two(4 - k, t).wait_recv()
        total = own[b].astype(f32)
        for m in range(3):
            total = total + got[m].astype(f32)
        dst[chip] = total.astype(bf)
        for k in range(1, chips):
            hop_chip(k, t).start()

    def last(t, half):
        part = (oq_ref.at[:, q_cols(half)], oo_ref.at[o_lines(half), :])[t]
        return remote(part, part, sf.at[t], rf.at[t], partner)

    for h in (0, 1):
        ff_far_got(h).wait_recv()
        ff_cross(2, h).start()

    for t in (1, 0):
        buf = (xq, xo)[t]
        for k in range(1, chips):
            dst = buf.at[lax.rem(chip + k, chips)]
            remote(dst, dst, sx.at[k, t], rx.at[k, t], partner).wait_recv()
        total = buf[0].astype(f32)
        for m in range(1, chips):
            total = total + buf[m].astype(f32)
        if t == 0:
            oq_ref[:, q_cols(core)] = total
        else:
            oo_ref[o_lines(core), :] = total
        last(t, core).start()

    everywhere = all_ff.at[ff_slot(0, 1)]
    remote(everywhere, everywhere, sag.at[0], rag.at[0], partner).wait_recv()
    for k in (1, 3):
        ff_cross(k, there=1).wait_recv()
    for h in (0, 1):
        ff_cross(2, h, there=1).wait_recv()

    def end_away(i, carry):
        for t in (0, 1):
            away(i, t).wait_send()
        return carry

    lax.fori_loop(0, 16, end_away, 0)
    for j in range(4):
        ff_far(j).wait_send()
        ff_near(1, j).wait_send()
        ff_near(3, j).wait_send()
    for k in (1, 2, 3):
        ff_two(k).wait_send()
    for d in range(1, reach + 1):
        kv_send(d).wait_send()
    for k in (1, 3, 0):
        ff_all(k).wait_send()
    for k in (1, 3):
        ff_on(k).wait_send()
        ff_cross(k).wait_send()
    for h in (0, 1):
        ff_cross(2, h).wait_send()
    for t in (0, 1):
        for h in (0, 1):
            sum_far(h, t).wait_send()
            sum_near(1, h, t).wait_send()
            sum_near(3, h, t).wait_send()
        for k in (1, 2, 3):
            hop_two(k, t).wait_send()
        for k in range(1, chips):
            hop_chip(k, t).wait_send()
        last(t, core).wait_send()
        last(t, 1 - core).wait_recv()
    oq_out[...] = oq_ref[:keep, :]
    tail_out[...] = oq_ref[keep:, :]


def backward_rest(gff, values, weights, keep):
    f32, bf = jnp.float32, jnp.bfloat16
    vm = pl.BlockSpec(memory_space=pltpu.VMEM)
    hbm = pl.BlockSpec(memory_space=pl.ANY)
    dma = pltpu.SemaphoreType.DMA
    rows = values[0].shape[0]
    owners, ff_rows = gff.shape[:2]
    q_rows, width = keep + 8, (NH + 2) * HD
    o_rows, o_width = NH * HD // owners, D
    q_half, o_half = width // 2, o_rows // 2
    chips = lax.axis_size("ctx") // 2
    pairs = values[9].shape[0]
    reach = pairs // rows - 1

    def two(*lead):
        return [pltpu.VMEM(lead + (q_rows, q_half), bf), pltpu.VMEM(lead + (o_half, o_width), bf)]

    def ff(*lead):
        return pltpu.VMEM(lead + (ff_rows, D), bf)

    return pl.pallas_call(
        back_kernel,
        out_shape=(
            jax.ShapeDtypeStruct((rows, D), f32),
            jax.ShapeDtypeStruct((keep, width), f32),
            jax.ShapeDtypeStruct((8, width), f32),
            jax.ShapeDtypeStruct((o_rows, o_width), f32),
            jax.ShapeDtypeStruct((2 * chips, ff_rows, D), bf),
        ),
        in_specs=[hbm] + [vm] * len(values) + [hbm] * 2,
        out_specs=(vm,) * 5,
        scratch_shapes=[
            pltpu.VMEM((16 * keep, width), bf),
            pltpu.VMEM((16 * o_rows, o_width), bf),
            pltpu.VMEM((q_rows, width), f32),
            ff(4), ff(4), ff(4), ff(2, 4), ff(4), ff(3),
            pltpu.VMEM((reach, rows, 2 * HD), bf),
            pltpu.VMEM((reach, rows, 2 * HD), bf),
            pltpu.VMEM((rows, D), f32),
            pltpu.VMEM((pairs, 2 * HD), f32),
            pltpu.VMEM((rows, width), bf),
            pltpu.VMEM((8, width), f32),
            pltpu.VMEM((16, q_rows, width), bf),
            pltpu.VMEM((16, o_rows, o_width), bf),
            *two(16), *two(16), *two(4), *two(2, 4), *two(4), *two(3), *two(chips),
            dma((10,)),
            dma((4,)), dma((4,)),
            dma((2, 4)), dma((2, 4)),
            dma((4,)), dma((4,)),
            dma((12,)), dma((12,)),
            dma((reach,)), dma((reach,)),
            dma((16, 2)), dma((16, 2)),
            dma((2, 2)), dma((2, 2)),
            dma((2, 2, 2)), dma((2, 2, 2)),
            dma((4, 2)), dma((4, 2)),
            dma((4, 2)), dma((4, 2)),
            dma((2,)), dma((2,)),
        ],
        compiler_params=pltpu.CompilerParams(
            collective_id=3, has_side_effects=True, vmem_limit_bytes=62 * 1024 * 1024
        ),
        cost_estimate=pl.CostEstimate(
            flops=12 * rows * width * D, bytes_accessed=64 * ff_rows * D, transcendentals=0
        ),
    )(gff, *values, *weights)


def finish_kernel(*refs):
    refs, (buf, wide, i_sem, o_sem) = refs[:-4], refs[-4:]
    count = (len(refs) - 7) // 2
    all_hbm, tail_ref, sources = refs[0], refs[1], refs[2 : 2 + count]
    weights, gains, qk = refs[2 + count : 5 + count], refs[5 + count], refs[6 + count]
    members = buf.shape[0]
    share = buf.shape[1] // 3
    lines = wide.shape[1] // members
    loads, stores = [], []
    for i in range(3):
        third = pl.ds(i * share, share)
        loads.append(
            pltpu.make_async_copy(all_hbm.at[:, third, :], buf.at[:, third, :], i_sem.at[i])
        )
        loads[i].start()
    for src, dst in zip(sources, refs[7 + count :]):
        dst[...] = src[...]
    owner = lax.axis_index("fsdp")
    width = tail_ref.shape[1]
    for first, dst in ((0, gains), (4, qk)):
        count, own = dst.shape
        shift = lax.rem(width - owner * own, width)
        dst[...] = pltpu.roll(tail_ref[...], shift, 1)[first : first + count, :own]
    for i, dst in enumerate(weights):
        loads[i].wait()
        for m in range(members):
            wide[i, m * lines : (m + 1) * lines, :] = buf[
                m, i * share : (i + 1) * share, :
            ].astype(jnp.float32)[:lines]
        stores.append(pltpu.make_async_copy(wide.at[i], dst, o_sem.at[i]))
        stores[i].start()
    for copy in stores:
        copy.wait()


def finish(all_ff, tail, lines, gain_lines, qk_lines, *rest):
    vm = pl.BlockSpec(memory_space=pltpu.VMEM)
    hbm = pl.BlockSpec(memory_space=pl.ANY)
    f32 = jnp.float32
    results = ((lines, D),) * 3 + (gain_lines, qk_lines)
    return pl.pallas_call(
        finish_kernel,
        out_shape=tuple(jax.ShapeDtypeStruct(s, f32) for s in results)
        + tuple(jax.ShapeDtypeStruct(r.shape, r.dtype) for r in rest),
        in_specs=[hbm] + [vm] * (1 + len(rest)),
        out_specs=(hbm,) * 3 + (vm,) * (2 + len(rest)),
        scratch_shapes=[
            pltpu.VMEM(all_ff.shape, all_ff.dtype),
            pltpu.VMEM((3, lines, D), f32),
            pltpu.SemaphoreType.DMA((3,)),
            pltpu.SemaphoreType.DMA((3,)),
        ],
        compiler_params=pltpu.CompilerParams(vmem_limit_bytes=62 * 1024 * 1024),
    )(all_ff, tail, *rest)


def on_device(
    tokens,
    norm_gains,
    qk_gains,
    qkv_weight,
    out_weight,
    gate_weight,
    up_weight,
    down_weight,
    segments,
    cotangent,
):
    local_len = tokens.shape[1]
    ctx_index = lax.axis_index("ctx")
    owner = lax.axis_index("fsdp")
    ctx_size = lax.axis_size("ctx")
    own_rows = gate_weight.shape[0]
    slice_rows = own_rows // ctx_size
    padded = -(-slice_rows // 16) * 16
    keep, width = qkv_weight.shape
    gain_lines, qk_lines = norm_gains.shape, qk_gains.shape
    def placed(lines):
        count, own = lines.shape
        room = (lax.axis_size("fsdp") - 1) * own
        padded_lines = jnp.pad(lines, ((0, 0), (room, room)))
        spread = lax.dynamic_slice(padded_lines, (0, room - owner * own), (count, room + own))
        return jnp.pad(spread, ((0, 0), (0, width - room - own)))

    gain_rows = jnp.concatenate(
        [placed(norm_gains), placed(qk_gains), jnp.zeros((2, width), jnp.bfloat16)], axis=0
    )

    def my_slice(weight):
        part = lax.dynamic_slice(weight, (ctx_index * slice_rows, 0), (slice_rows, D))
        return jnp.pad(part, ((0, padded - slice_rows), (0, 0)))

    ffn_shard = jnp.concatenate(
        [my_slice(gate_weight), my_slice(up_weight), my_slice(down_weight)], axis=0
    )
    places = np.arange(ctx_size * local_len, dtype=np.float32)
    rates = (ROPE_BASE ** (-(2.0 * np.arange(HD // 2)) / HD)).astype(np.float32)
    angles = (places[:, None] * rates).astype(np.float64)
    table = jnp.asarray(
        np.concatenate([np.cos(angles), np.sin(angles)], axis=1)
        .astype(np.float32)
        .reshape(ctx_size, local_len, HD)
    )
    flat = tokens.reshape(local_len, D)
    cot = cotangent.reshape(local_len, D)
    (
        qkv_full, out_full, ffn_full, gains_all, qk_all, normed, projected, queries, pair_all,
        attended, attn, mid, normed_seq, bias, turn_table,
    ) = front(
        jnp.concatenate([qkv_weight, gain_rows], axis=0),
        out_weight,
        ffn_shard,
        flat,
        segments,
        table,
        keep,
    )
    output, grad_normed_two, grad_gain_three, ffn_grads = ffn(
        normed_seq, mid, cot, gains_all, ffn_full
    )
    grad_tokens, total_qkv, tail, total_out, all_ff = backward_rest(
        ffn_grads,
        (
            grad_normed_two, mid, attn, cot, flat, gains_all, qk_all, projected, queries,
            pair_all, attended, normed, turn_table, bias, grad_gain_three,
        ),
        (qkv_full, out_full),
        keep,
    )
    (
        total_gate, total_up, total_down, total_gains, total_qk,
        grad_tokens, total_qkv, total_out, output,
    ) = finish(
        all_ff, tail, own_rows, gain_lines, qk_lines, grad_tokens, total_qkv, total_out, output
    )
    return (
        output.reshape(tokens.shape),
        grad_tokens.reshape(tokens.shape),
        total_gains,
        total_qk,
        total_qkv,
        total_out,
        total_gate,
        total_up,
        total_down,
    )


def solution(mesh):
    in_specs = (
        P("fsdp", "ctx", None),
        P(None, "fsdp"),
        P(None, "fsdp"),
        P("fsdp", None),
        P("fsdp", None),
        P("fsdp", None),
        P("fsdp", None),
        P("fsdp", None),
        P("fsdp", "ctx"),
        P("fsdp", "ctx", None),
    )
    out_specs = (
        P("fsdp", "ctx", None),
        P("fsdp", "ctx", None),
        P(None, "fsdp"),
        P(None, "fsdp"),
        P("fsdp", None),
        P("fsdp", None),
        P("fsdp", None),
        P("fsdp", None),
        P("fsdp", None),
    )
    return jax.shard_map(
        on_device, mesh=mesh, in_specs=in_specs, out_specs=out_specs, check_vma=False
    )
```

```python
import jax
import numpy as np
import jax.numpy as jnp
from jax import lax
from jax.experimental import pallas as pl
from jax.experimental.pallas import tpu as pltpu
from jax.sharding import PartitionSpec as P

D = 1152
NH = 4
HD = 256
WINDOW = 512


EPS = 1e-06
ROPE_BASE = 10000.0
NEG_FILL = -1e30


def rms_norm(values, gain_vec):
    return values * lax.rsqrt(jnp.mean(values * values, axis=-1, keepdims=True) + EPS) * gain_vec


MESH = pl.DeviceIdType.MESH
NT = (((1,), (1,)), ((), ()))
NN = (((1,), (0,)), ((), ()))
TN = (((0,), (0,)), ((), ()))
GELU_C = 0.7978845608028654
GELU_A = 0.044715


def dot32(left, right, dims):
    return lax.dot_general(left, right, dims, preferred_element_type=jnp.float32)


def place():
    fsdp = lax.axis_index("fsdp")
    ctx = lax.axis_index("ctx")
    y, z = fsdp // 4, lax.rem(fsdp, 4)
    chip, core = ctx // 2, lax.rem(ctx, 2)
    return y, z, chip, core


def shape_of(y, z, core):
    first = (1 - core) * y + core * z
    second = (1 - core) * z + core * y

    def block(i, j):
        return (1 - core) * (4 * i + j) + core * (4 * j + i)

    return first, second, block


def remote(src, dst, s_sem, r_sem, peer):
    return pltpu.make_async_remote_copy(
        src_ref=src, dst_ref=dst, send_sem=s_sem, recv_sem=r_sem,
        device_id=peer, device_id_type=MESH,
    )


def greet(peers):
    barrier = pltpu.get_barrier_semaphore()
    for peer in peers:
        pl.semaphore_signal(barrier, inc=1, device_id=peer, device_id_type=MESH)
    pl.semaphore_wait(barrier, len(peers))


def ring_gather(buf, rows, partner, chips, s_sem, r_sem):
    started, got = [], {}

    def send(src, dst, i, back, peer):
        copy = remote(src, dst, s_sem.at[i], r_sem.at[back], peer)
        copy.start()
        started.append(copy)
        return copy

    def mine(k):
        return buf.at[pl.ds(k * 2 * rows, rows)]

    def other(k):
        return buf.at[pl.ds(k * 2 * rows + rows, rows)]

    def half_of(k, h, offset=0):
        return buf.at[pl.ds(k * 2 * rows + offset + h * (rows // 2), rows // 2)]

    def spread():
        for k in (1, 3):
            got[4 - k] = send(mine(0), mine(4 - k), k, 4 - k, chips[k])
        got[0] = send(mine(0), other(0), 0, 0, partner)

    def relay(k):
        got[k].wait_recv()
        h = 0 if k == 3 else 1
        got[2, h] = send(half_of(k, h), half_of(2, h), 2 + 2 * h, 2 + 2 * h, chips[4 - k])
        got[k] = send(mine(k), other(k), 4 + k, 4 + k, partner)

    def relay_far():
        for h in (0, 1):
            got[2, h].wait_recv()
            got[2, h] = send(half_of(2, h), half_of(2, h, rows), 6 + 2 * h, 6 + 2 * h, partner)

    return spread, relay, relay_far, got, started


def plane_gather(src, dst, a, b, block, partner, s1, r1, s2, r2):
    here = block(a, b)

    def first_peer(k):
        return {"fsdp": block(lax.rem(a + k, 4), b)}

    def second_peer(k):
        return {"fsdp": block(a, lax.rem(b + k, 4))}

    def part(j, m):
        return dst(block(lax.rem(a + j, 4), lax.rem(b + m, 4)))

    def one(k):
        return remote(src, dst(here), s1.at[k], r1.at[4 - k], first_peer(k))

    def two(j, k):
        return remote(
            part(j, 0) if j else src, part(j, 0), s2.at[j, k], r2.at[j, 4 - k], second_peer(k)
        )

    def far(j):
        m, k = (3, 1) if j < 2 else (1, 3)
        return remote(part(j, m), part(j, m), s2.at[j, 2], r2.at[j, 2], second_peer(k))

    def got(j, m):
        sems = (s1.at[j], r1.at[j]) if m == 0 else (s2.at[j, m], r2.at[j, m])
        return remote(part(j, m), part(j, m), *sems, partner)

    def start():
        for k in (1, 3, 2):
            one(k).start()
        for k in (1, 3):
            two(0, k).start()

    def turn_axis():
        for j in (1, 3, 2):
            got(j, 0).wait_recv()
            for k in (1, 3):
                two(j, k).start()

    def onward(j):
        got(j, 3 if j < 2 else 1).wait_recv()
        far(j).start()

    def end():
        for j in range(4):
            got(j, 1 if j < 2 else 3).wait_recv()
            got(j, 2).wait_recv()

    def sent():
        for j in range(4):
            far(j).wait_send()
            for k in (1, 3):
                two(j, k).wait_send()
        for k in (1, 2, 3):
            one(k).wait_send()

    return start, turn_axis, onward, end, sent


def ffn_kernel(
    seq, mid_ref, cot_ref, gain_ref, down_ref, w_hbm,
    out_ref, gn_ref, ggain_ref, gff_hbm,
    wg, wu, wd, gseq, act_a, act_b, hid, dgate, dup, part, keep, base,
    d2d_snd, d2d_in, ici_snd, ici_in, dw,
    w_sem, o_sem, l_sem, s1f, r1f, s2f, r2f, ag_s, ag_r, rd_s, rd_r, ri_s, ri_r,
):
    rows = mid_ref.shape[0]
    units = wg.shape[0]
    owners = w_hbm.shape[0]
    share = down_ref.shape[0]
    tile = 256
    y, z, chip, core = place()
    a, b, block = shape_of(y, z, core)
    partner = {"ctx": chip * 2 + 1 - core}
    chips = {k: {"ctx": lax.rem(chip + k, 4) * 2 + core} for k in (1, 2, 3)}
    order = (0, 1, 3, 2)

    loads = [
        pltpu.make_async_copy(
            w_hbm.at[f, pl.ds(i * share, share), :], dst.at[pl.ds(f * share, share), :], w_sem.at[i, f]
        )
        for i, dst in enumerate((wg, wu))
        for f in range(owners)
    ]
    def down_lines(f):
        return wd.at[pl.ds(pl.multiple_of(f * share, 16), share), :]

    own_down = pltpu.make_async_copy(down_ref, down_lines(block(a, b)), l_sem)
    own_down.start()
    for load in loads:
        load.start()
    down_start, down_turn, down_onward, down_end, down_sent = plane_gather(
        down_ref, down_lines, a, b, block, partner, s1f, r1f, s2f, r2f
    )
    greet(
        [partner, chips[1], chips[2], chips[3]]
        + [{"fsdp": block(lax.rem(a + k, 4), b)} for k in (1, 2, 3)]
        + [{"fsdp": block(a, lax.rem(b + k, 4))} for k in (1, 2, 3)]
    )
    down_start()

    started = []

    def send(src, dst, s_sem, r_sem, peer):
        copy = pltpu.make_async_remote_copy(
            src_ref=src, dst_ref=dst, send_sem=s_sem, recv_sem=r_sem,
            device_id=peer, device_id_type=MESH,
        )
        copy.start()
        started.append(copy)
        return copy

    spread, relay, relay_far, got, gathers = ring_gather(gseq, rows, partner, chips, ag_s, ag_r)

    def pair(k):
        return pl.ds(k * 2 * rows, 2 * rows)

    def swap(ph, k):
        d2d_snd[ph, k] = part[pl.ds(rows, rows), :].astype(jnp.bfloat16)
        keep[k // 2] = part[pl.ds(0, rows), :]
        return send(d2d_snd.at[ph, k], d2d_in.at[ph, k], rd_s.at[ph, k], rd_r.at[ph, k], partner)

    def sum_out(ph, k, copy):
        copy.wait_recv()
        total = keep[k // 2] + d2d_in[ph, k].astype(jnp.float32)
        if k == 0:
            base[...] = total
            return None
        ici_snd[ph, k - 1] = total.astype(jnp.bfloat16)
        back = 4 - k
        return send(
            ici_snd.at[ph, k - 1], ici_in.at[ph, back - 1], ri_s.at[ph, k], ri_r.at[ph, back],
            chips[k],
        )

    def phase(ph, work, ready, order):
        sums = {}
        copy = waiting = None
        for k in order:
            ready(k)
            if waiting is not None and k == order[-1]:
                sums[waiting] = sum_out(ph, waiting, copy)
                waiting = None
            work(k)
            if waiting is not None:
                sums[waiting] = sum_out(ph, waiting, copy)
            copy, waiting = swap(ph, k), k
        sums[waiting] = sum_out(ph, waiting, copy)
        return sums

    def gathered(k):
        if k == 1:
            relay(1)
            relay(3)
        if k == 2:
            relay_far()
            got[2, 0].wait_recv()
            got[2, 1].wait_recv()
        else:
            got[k].wait_recv()

    def collect(ph, sums):
        total = base[...]
        for k in (1, 3, 2):
            sums[k].wait_recv()
        for k in (1, 2, 3):
            total = total + ici_in[ph, k - 1].astype(jnp.float32)
        return total

    def forward(k):
        def one(t, carry):
            cols = pl.ds(pl.multiple_of(t * tile, tile), tile)
            block = seq[pair(k), :]
            gate = dot32(block, wg[cols, :], NT)
            up = dot32(block, wu[cols, :], NT)
            square = gate * gate
            th = jnp.tanh(GELU_C * gate * (1.0 + GELU_A * square))
            half = 0.5 * (1.0 + th)
            gelu = gate * half
            slope = half + (0.5 * GELU_C) * gate * (1.0 - th * th) * (1.0 + 3.0 * GELU_A * square)
            hid[pair(k), cols] = (gelu * up).astype(jnp.bfloat16)
            act_a[pair(k), cols] = up * slope
            act_b[pair(k), cols] = gelu
            return carry

        lax.fori_loop(0, units // tile, one, 0)

    def project(k):
        part[...] = dot32(hid[pair(k), :], wd[...], NN)

    for load in loads:
        load.wait()
    forward(0)
    down_turn()
    forward(1)
    down_onward(0)
    down_onward(1)
    forward(3)
    down_onward(3)
    down_onward(2)
    forward(2)
    down_end()
    own_down.wait()
    sums = phase(0, project, lambda k: None, (2, 1, 3, 0))
    mlp = collect(0, sums)
    r = lax.rsqrt(jnp.mean(mlp * mlp, axis=-1, keepdims=True) + EPS)
    n = mlp * r
    gain = gain_ref[3:4, :]
    out_ref[...] = (mid_ref[...] + n * gain).astype(jnp.bfloat16)
    dy = cot_ref[...].astype(jnp.float32)
    ggain_ref[...] = jnp.sum(dy * n, axis=0, keepdims=True)
    dyg = dy * gain
    dv = r * (dyg - n * jnp.mean(dyg * n, axis=-1, keepdims=True))
    gseq[pl.ds(0, rows), :] = dv.astype(jnp.bfloat16)
    spread()

    def backward(k):
        def one(t, carry):
            cols = pl.ds(pl.multiple_of(t * tile, tile), tile)
            gh = dot32(gseq[pair(k), :], wd[cols, :], NT)
            dgate[pair(k), cols] = (gh * act_a[pair(k), cols]).astype(jnp.bfloat16)
            dup[pair(k), cols] = (gh * act_b[pair(k), cols]).astype(jnp.bfloat16)
            return carry

        lax.fori_loop(0, units // tile, one, 0)
        part[...] = dot32(dgate[pair(k), :], wg[...], NN) + dot32(dup[pair(k), :], wu[...], NN)

    sums = phase(1, backward, gathered, order)
    stores = []
    for i, (left, right) in enumerate(((dgate, seq), (dup, seq), (hid, gseq))):
        def one(t, carry, i=i, left=left, right=right):
            cols = pl.ds(pl.multiple_of(t * tile, tile), tile)
            group = tile // share
            dw[pl.ds(t * group, group), pl.ds(i * share, share), :] = (
                dot32(left[:, cols], right[...], TN).reshape(group, share, -1).astype(jnp.bfloat16)
            )
            return carry

        lax.fori_loop(0, units // tile, one, 0)
        third = pl.ds(i * share, share)
        stores.append(
            pltpu.make_async_copy(dw.at[:, third, :], gff_hbm.at[:, third, :], o_sem.at[i])
        )
        stores[-1].start()
    gn_ref[...] = collect(1, sums)
    for copy in started + gathers:
        copy.wait_send()
    down_sent()
    for store in stores:
        store.wait()


def ffn(normed_seq, mid, cot, gain, down, weights):
    rows = mid.shape[0]
    owners, share = weights.shape[0], down.shape[0]
    units = owners * share
    seq_rows = rows * 8
    bf, f32 = jnp.bfloat16, jnp.float32
    vm = pl.BlockSpec(memory_space=pltpu.VMEM)
    hbm = pl.BlockSpec(memory_space=pl.ANY)
    dma = pltpu.SemaphoreType.DMA
    return pl.pallas_call(
        ffn_kernel,
        out_shape=(
            jax.ShapeDtypeStruct((rows, D), bf),
            jax.ShapeDtypeStruct((rows, D), f32),
            jax.ShapeDtypeStruct((1, D), f32),
            jax.ShapeDtypeStruct((owners, 3 * share, D), bf),
        ),
        in_specs=[vm] * 5 + [hbm],
        out_specs=(vm, vm, vm, hbm),
        scratch_shapes=[
            pltpu.VMEM((units, D), bf),
            pltpu.VMEM((units, D), bf),
            pltpu.VMEM((units, D), bf),
            pltpu.VMEM((seq_rows, D), bf),
            pltpu.VMEM((seq_rows, units), f32),
            pltpu.VMEM((seq_rows, units), f32),
            pltpu.VMEM((seq_rows, units), bf),
            pltpu.VMEM((seq_rows, units), bf),
            pltpu.VMEM((seq_rows, units), bf),
            pltpu.VMEM((2 * rows, D), f32),
            pltpu.VMEM((2, rows, D), f32),
            pltpu.VMEM((rows, D), f32),
            pltpu.VMEM((2, 4, rows, D), bf),
            pltpu.VMEM((2, 4, rows, D), bf),
            pltpu.VMEM((2, 3, rows, D), bf),
            pltpu.VMEM((2, 3, rows, D), bf),
            pltpu.VMEM((owners, 3 * share, D), bf),
            dma((2, owners)), dma((3,)), dma,
            dma((4,)), dma((4,)), dma((4, 4)), dma((4, 4)),
            dma((10,)), dma((10,)),
            dma((2, 4)), dma((2, 4)),
            dma((2, 4)), dma((2, 4)),
        ],
        compiler_params=pltpu.CompilerParams(
            collective_id=1, has_side_effects=True, vmem_limit_bytes=62 * 1024 * 1024
        ),
        cost_estimate=pl.CostEstimate(
            flops=18 * seq_rows * units * D, bytes_accessed=14 * units * D, transcendentals=0
        ),
    )(normed_seq, mid, cot, gain, down, weights)


def rms_back(values, grad, gain):
    r = lax.rsqrt(jnp.mean(values * values, axis=-1, keepdims=True) + EPS)
    n = values * r
    dyg = grad * gain
    return (
        r * (dyg - n * jnp.mean(dyg * n, axis=-1, keepdims=True)),
        jnp.sum(grad * n, axis=0, keepdims=True),
    )


def stack_heads(values):
    return jnp.concatenate([values[:, h * HD : (h + 1) * HD] for h in range(NH)], axis=0)


def turn_back(grad, cos_table, sin_table):
    left, right = grad[:, : HD // 2], grad[:, HD // 2 :]
    return jnp.concatenate(
        [left * cos_table + right * sin_table, right * cos_table - left * sin_table], axis=1
    )


def front_kernel(
    qkv_ref, wo_ref, ffn_ref, tok_ref, seg_line, table_ref,
    qkv_hbm, wo_hbm, ffn_all, gains_ref, qk_ref, normed_ref, proj_ref, q_ref, pair_ref, att_ref,
    attn_ref, mid_ref, seq, bias_ref, turn_ref,
    qkv_all, qkv_out, wo_all, seg_ref, seg_in,
    l_sem, s1, r1, s2, r2, sd, rd, s1f, r1f, s2f, r2f, skv, rkv, ssg, rsg, ag_s, ag_r,
):
    f32, bf = jnp.float32, jnp.bfloat16
    y, z, chip, core = place()
    a, b, block = shape_of(y, z, core)
    _, _, block_there = shape_of(y, z, 1 - core)
    q_rows, width = qkv_ref.shape
    o_rows = wo_ref.shape[0]
    q_half, o_half = width // 2, o_rows // 2
    partner = {"ctx": chip * 2 + 1 - core}
    me = chip * 2 + core
    rows = tok_ref.shape[0]
    reach = pair_ref.shape[0] // rows - 1
    members = 2 * (lax.axis_size("ctx") // 2)

    def member(k):
        return {"ctx": lax.rem(me + k, members)}

    seg_ref[...] = jnp.broadcast_to(seg_line[...], seg_ref.shape)

    def views(f, half):
        return (
            qkv_all.at[
                pl.ds(pl.multiple_of(f * q_rows, 16), q_rows),
                pl.ds(pl.multiple_of(half * q_half, 128), q_half),
            ],
            wo_all.at[pl.ds(pl.multiple_of(f * o_rows + half * o_half, 16), o_half), :],
        )

    mine = (
        qkv_ref.at[:, pl.ds(pl.multiple_of(core * q_half, 128), q_half)],
        wo_ref.at[pl.ds(pl.multiple_of(core * o_half, 16), o_half), :],
    )
    here = block(a, b)
    locals_ = [
        pltpu.make_async_copy(
            qkv_ref, qkv_all.at[pl.ds(pl.multiple_of(here * q_rows, 16), q_rows), :], l_sem.at[0]
        ),
        pltpu.make_async_copy(
            wo_ref, wo_all.at[pl.ds(pl.multiple_of(here * o_rows, 16), o_rows), :], l_sem.at[1]
        ),
        pltpu.make_async_copy(ffn_ref, ffn_all.at[here], l_sem.at[2]),
        pltpu.make_async_copy(table_ref.at[me], turn_ref, l_sem.at[3]),
    ]
    for copy in locals_:
        copy.start()

    def first_peer(k):
        return {"fsdp": block(lax.rem(a + k, 4), b)}

    def second_peer(k):
        return {"fsdp": block(a, lax.rem(b + k, 4))}

    greet(
        [first_peer(k) for k in (1, 2, 3)]
        + [second_peer(k) for k in (1, 2, 3)]
        + [member(k) for k in range(1, members)]
    )

    def seg_send(d):
        return remote(
            seg_ref, seg_in.at[reach - d], ssg.at[d - 1], rsg.at[d - 1], member(d)
        )

    ffn_start, ffn_turn, ffn_onward, ffn_end, ffn_sent = plane_gather(
        ffn_ref, lambda f: ffn_all.at[f], a, b, block, partner, s1f, r1f, s2f, r2f
    )

    def hop_one(k, t):
        return remote(mine[t], views(here, core)[t], s1.at[k, t], r1.at[4 - k, t], first_peer(k))

    def hop_two(j, k, t):
        f = block(lax.rem(a + j, 4), b)
        dst = views(f, core)[t]
        src = dst if j else mine[t]
        return remote(src, dst, s2.at[j, k, t], r2.at[j, 4 - k, t], second_peer(k))

    def arrive_one(j, t):
        dst = views(block(lax.rem(a + j, 4), b), core)[t]
        return remote(dst, dst, s1.at[j, t], r1.at[j, t], partner)

    def arrive_two(j, m, t):
        dst = views(block(lax.rem(a + j, 4), lax.rem(b + m, 4)), core)[t]
        return remote(dst, dst, s2.at[j, m, t], r2.at[j, m, t], partner)

    def cross(j, m, t):
        dst = views(block(lax.rem(a + j, 4), lax.rem(b + m, 4)), core)[t]
        return remote(dst, dst, sd.at[j, m, t], rd.at[j, m, t], partner)

    def arrive_cross(j, m, t):
        dst = views(block_there(lax.rem(b + j, 4), lax.rem(a + m, 4)), 1 - core)[t]
        return remote(dst, dst, sd.at[j, m, t], rd.at[j, m, t], partner)

    both = (0, 1)
    for k in (1, 3, 2):
        for t in both:
            hop_one(k, t).start()
    def hop_pass(j, t):
        m, k = (3, 1) if j < 2 else (1, 3)
        dst = views(block(lax.rem(a + j, 4), lax.rem(b + m, 4)), core)[t]
        return remote(dst, dst, s2.at[j, 2, t], r2.at[j, 2, t], second_peer(k))

    for k in (1, 3):
        for t in both:
            hop_two(0, k, t).start()
    for j in (1, 3, 2):
        for t in both:
            arrive_one(j, t).wait_recv()
            for k in (1, 3):
                hop_two(j, k, t).start()
            cross(j, 0, t).start()

    for d in range(1, reach + 1):
        seg_send(d).start()
    ffn_start()

    for j in (0, 1, 3, 2):
        for m in (3, 1) if j < 2 else (1, 3):
            for t in both:
                arrive_two(j, m, t).wait_recv()
                if m == (3 if j < 2 else 1):
                    hop_pass(j, t).start()
                cross(j, m, t).start()
    for j in (0, 1, 3, 2):
        for t in both:
            arrive_two(j, 2, t).wait_recv()
            cross(j, 2, t).start()

    def land(i, carry):
        m, j = i // 4, lax.rem(i, 4)
        for t in both:
            arrive_cross(j, m, t).wait_recv()
            cross(j, m, t).wait_send()
        return carry

    lax.fori_loop(1, 16, land, 0)
    for copy in locals_[:2]:
        copy.wait()
    for t in both:
        for k in (1, 2, 3):
            hop_one(k, t).wait_send()
        for j in range(4):
            hop_pass(j, t).wait_send()
            for k in (1, 3):
                hop_two(j, k, t).wait_send()
    saves = [
        pltpu.make_async_copy(qkv_out, qkv_hbm, l_sem.at[4]),
        pltpu.make_async_copy(wo_all, wo_hbm, l_sem.at[5]),
    ]
    saves[1].start()

    keep = qkv_out.shape[0] // 16
    extra = jnp.zeros((q_rows - keep, width), f32)
    for f in range(0, 16, 2):
        left = qkv_all[pl.ds(f * q_rows, q_rows), :].astype(f32)
        right = qkv_all[pl.ds((f + 1) * q_rows, q_rows), :].astype(f32)
        qkv_out[pl.ds(f * keep, 2 * keep), :] = jnp.concatenate(
            [left[:keep], right[:keep]], axis=0
        ).astype(bf)
        extra = extra + left[keep:] + right[keep:]
    saves[0].start()
    gains = extra[:4, :D]
    gains_ref[...] = gains
    qk_ref[...] = extra[4:6, :HD]

    stream = tok_ref[...].astype(f32)
    normed_ref[...] = rms_norm(stream, gains[0:1]).astype(bf)
    proj_ref[...] = dot32(normed_ref[...], qkv_out[...], NN)
    locals_[3].wait()
    cos_table, sin_table = turn_ref[:, : HD // 2], turn_ref[:, HD // 2 :]

    def turn(values, gain, cos_part, sin_part):
        values = rms_norm(values, gain)
        left, right = values[:, : HD // 2], values[:, HD // 2 :]
        return jnp.concatenate(
            [left * cos_part - right * sin_part, right * cos_part + left * sin_part], axis=1
        ).astype(bf)

    own = pl.ds(reach * rows, rows)
    pair_ref[own, :HD] = turn(
        proj_ref[:, NH * HD : NH * HD + HD], extra[5:6, :HD], cos_table, sin_table
    )
    pair_ref[own, HD:] = proj_ref[:, NH * HD + HD :].astype(bf)

    def kv_send(d):
        return remote(
            pair_ref.at[own],
            pair_ref.at[pl.ds((reach - d) * rows, rows)],
            skv.at[d - 1], rkv.at[d - 1], member(d),
        )

    for d in range(1, reach + 1):
        kv_send(d).start()
    ffn_turn()
    queries = turn(
        stack_heads(proj_ref[:, : NH * HD]),
        extra[4:5, :HD],
        jnp.concatenate([cos_table] * NH, axis=0),
        jnp.concatenate([sin_table] * NH, axis=0),
    )
    for h in range(NH):
        q_ref[:, h * HD : (h + 1) * HD] = queries[h * rows : (h + 1) * rows]

    for d in range(1, reach + 1):
        seg_send(d).wait_recv()
    seg_in[reach] = seg_ref[...]
    key_seg = jnp.concatenate([seg_in[p][0:1, :] for p in range(reach + 1)], axis=1)
    shape = (rows, (reach + 1) * rows)
    spacing = (
        reach * rows + lax.broadcasted_iota(jnp.int32, shape, 0)
        - lax.broadcasted_iota(jnp.int32, shape, 1)
    )
    begun = lax.broadcasted_iota(jnp.int32, shape, 1) + (me - reach) * rows >= 0
    wide = jnp.broadcast_to(seg_line[...], (rows, rows)).astype(f32)
    query_seg = jnp.concatenate([wide.T] * (reach + 1), axis=1)
    allowed = (
        (spacing >= 0) & (spacing < WINDOW) & begun & (query_seg == key_seg.astype(f32))
    )
    bias_ref[...] = jnp.where(allowed, 0.0, NEG_FILL)
    ffn_onward(0)
    for d in range(1, reach + 1):
        kv_send(d).wait_recv()
    scores = dot32(queries, pair_ref[:, :HD], NT) * (HD ** (-0.5)) + jnp.concatenate(
        [bias_ref[...]] * NH, axis=0
    )
    expo = jnp.exp(scores - jnp.max(scores, axis=-1, keepdims=True))
    probs = expo * (1.0 / jnp.sum(expo, axis=-1, keepdims=True))
    heads = dot32(probs.astype(bf), pair_ref[:, HD:], NN).astype(bf)
    for h in range(NH):
        att_ref[:, h * HD : (h + 1) * HD] = heads[h * rows : (h + 1) * rows]
    ffn_onward(1)
    ffn_onward(3)
    attn = dot32(att_ref[...], wo_all[...], NN)
    attn_ref[...] = attn
    mid = stream + rms_norm(attn, gains[1:2])
    mid_ref[...] = mid
    seq[pl.ds(0, rows), :] = rms_norm(mid, gains[2:3]).astype(bf)
    ring = {k: {"ctx": lax.rem(chip + k, members // 2) * 2 + core} for k in (1, 2, 3)}
    spread, relay, relay_far, got, gathers = ring_gather(seq, rows, partner, ring, ag_s, ag_r)
    spread()

    ffn_onward(2)
    relay(1)
    relay(3)
    for copy in saves + locals_[2:3]:
        copy.wait()
    ffn_end()
    relay_far()
    for copy in got.values():
        copy.wait_recv()
    for copy in gathers:
        copy.wait_send()
    ffn_sent()
    for d in range(1, reach + 1):
        seg_send(d).wait_send()
        kv_send(d).wait_send()


def front(qkv_shard, wo_shard, ffn_shard, tokens, seg_line, table, keep):
    f32, bf = jnp.float32, jnp.bfloat16
    vm = pl.BlockSpec(memory_space=pltpu.VMEM)
    hbm = pl.BlockSpec(memory_space=pl.ANY)
    dma = pltpu.SemaphoreType.DMA
    q_rows, width = qkv_shard.shape
    o_rows, o_width = wo_shard.shape
    rows = tokens.shape[0]
    reach = min(-(-(WINDOW - 1) // rows), lax.axis_size("ctx") - 1)
    pairs = (reach + 1) * rows
    shapes = (
        ((16 * keep, width), bf),
        ((16 * o_rows, o_width), bf),
        ((16, *ffn_shard.shape), bf),
        ((4, D), f32),
        ((2, HD), f32),
        ((rows, D), bf),
        ((rows, width), f32),
        ((rows, NH * HD), bf),
        ((pairs, 2 * HD), bf),
        ((rows, NH * HD), bf),
        ((rows, D), f32),
        ((rows, D), f32),
        ((rows * lax.axis_size("ctx"), D), bf),
        ((rows, pairs), f32),
        ((rows, HD), f32),
    )
    return pl.pallas_call(
        front_kernel,
        out_shape=tuple(jax.ShapeDtypeStruct(*s) for s in shapes),
        in_specs=[vm, vm, hbm, vm, vm, hbm],
        out_specs=(hbm,) * 3 + (vm,) * (len(shapes) - 3),
        scratch_shapes=[
            pltpu.VMEM((16 * q_rows, width), bf),
            pltpu.VMEM((16 * keep, width), bf),
            pltpu.VMEM((16 * o_rows, o_width), bf),
            pltpu.VMEM((8, rows), jnp.int32),
            pltpu.VMEM((reach + 1, 8, rows), jnp.int32),
            dma((6,)),
            dma((4, 2)), dma((4, 2)),
            dma((4, 4, 2)), dma((4, 4, 2)),
            dma((4, 4, 2)), dma((4, 4, 2)),
            dma((4,)), dma((4,)),
            dma((4, 4)), dma((4, 4)),
            dma((reach,)), dma((reach,)),
            dma((reach,)), dma((reach,)),
            dma((10,)), dma((10,)),
        ],
        compiler_params=pltpu.CompilerParams(
            collective_id=2, has_side_effects=True, vmem_limit_bytes=62 * 1024 * 1024
        ),
        cost_estimate=pl.CostEstimate(
            flops=6 * rows * width * D, bytes_accessed=64 * q_rows * width, transcendentals=0
        ),
    )(qkv_shard, wo_shard, ffn_shard, tokens, seg_line, table)


def back_kernel(
    gff, gn_ref, mid_ref, attn_ref, cot_ref, tok_ref, gains_ref, qk_ref, proj_ref, q_ref,
    pair_ref, att_ref, normed_ref, turn_ref, bias_ref, g3_ref, qkv_hbm, wo_hbm,
    gt_ref, oq_out, tail_out, oo_ref, all_ff,
    qkv_ref, wo_ref, oq_ref, own_ff, far_own, far_in, in1_ff, t_ff, in2_ff, kv_snd, kv_in, gmid, gpair, gproj, tail,
    stage, go, dq, do, sq, so, fq, fo, iq1, io1, tq, to, iq2, io2, xq, xo,
    l_sem, sfar, rfar, s1f, r1f, s2f, r2f, sag, rag, skv, rkv,
    sd, rd, sfa, rfa, s1, r1, s2, r2, sx, rx, sf, rf,
):
    y, z, chip, core = place()
    a, b, block = shape_of(y, z, core)
    _, _, block_there = shape_of(y, z, 1 - core)
    me = chip * 2 + core
    rows = gn_ref.shape[0]
    q_rows, width = oq_ref.shape
    keep = normed_ref.shape[1] // 16
    o_rows = oo_ref.shape[0]
    q_half, o_half = width // 2, o_rows // 2
    chips = xq.shape[0]
    members = 2 * chips
    reach = kv_in.shape[0]
    scale = HD ** (-0.5)
    f32, bf = jnp.float32, jnp.bfloat16
    partner = {"ctx": chip * 2 + 1 - core}

    def first_peer(k):
        return {"fsdp": block(lax.rem(a + k, 4), b)}

    def second_peer(k):
        return {"fsdp": block(a, lax.rem(b + k, 4))}

    def chip_peer(k):
        return {"ctx": lax.rem(chip + k, chips) * 2 + core}

    def member(k):
        return {"ctx": lax.rem(me + k, members)}

    def q_cols(half):
        return pl.ds(pl.multiple_of(half * q_half, 128), q_half)

    def o_lines(half):
        return pl.ds(pl.multiple_of(half * o_half, 16), o_half)

    def line(k):
        return lax.rem(a + k, 4)

    own_loads = [
        pltpu.make_async_copy(gff.at[block(a, j)], own_ff.at[j], l_sem.at[j]) for j in range(4)
    ] + [
        pltpu.make_async_copy(
            gff.at[block(line(1 if j < 2 else 3), j)], far_own.at[j], l_sem.at[4 + j]
        )
        for j in range(4)
    ]
    weight_loads = [
        pltpu.make_async_copy(wo_hbm, wo_ref, l_sem.at[8]),
        pltpu.make_async_copy(qkv_hbm, qkv_ref, l_sem.at[9]),
    ]
    for copy in own_loads + weight_loads:
        copy.start()
    greet(
        [first_peer(k) for k in (1, 2, 3)]
        + [second_peer(k) for k in (1, 2, 3)]
        + [member(k) for k in range(1, members)]
    )

    def ff_far(j):
        k = 1 if j < 2 else 3
        return remote(
            gff.at[block(line(2), j)], far_in.at[j], sfar.at[j], rfar.at[j], first_peer(k)
        )

    def ff_near(k, j):
        side = 0 if k == 1 else 1
        direct = (j >= 2) == (k == 1)
        src = gff.at[block(line(k), j)] if direct else far_own.at[j]
        return remote(src, in1_ff.at[side, j], s1f.at[side, j], r1f.at[side, j], first_peer(k))

    for j in (0, 2, 1, 3):
        ff_far(j).start()
    for k, j in ((1, 2), (3, 0), (1, 3), (3, 1)):
        ff_near(k, j).start()

    def pass_far(js):
        for j in js:
            ff_far(j).wait_recv()
            own_loads[4 + j].wait()
            far_own[j] = (far_own[j].astype(f32) + far_in[j].astype(f32)).astype(bf)
            ff_near(1 if j < 2 else 3, j).start()

    for copy in weight_loads[:1]:
        copy.wait()

    grad_final = cot_ref[...].astype(f32)
    part, gain_two = rms_back(mid_ref[...], gn_ref[...], gains_ref[2:3, :])
    grad_mid = grad_final + part
    gmid[...] = grad_mid
    grad_attn, gain_one = rms_back(attn_ref[...], grad_mid, gains_ref[1:2, :])
    grad_attn_low = grad_attn.astype(bf)
    grad_attended = dot32(grad_attn_low, wo_ref[...], NT).astype(bf)

    def out_tile(t, carry):
        cols = pl.ds(pl.multiple_of(t * 256, 256), 256)
        go[pl.ds(t * 4, 4)] = (
            dot32(att_ref[:, cols], grad_attn_low, TN).reshape(4, 64, D).astype(bf)
        )
        return carry

    lax.fori_loop(0, NH * HD // 256, out_tile, 0)

    def away(i, t):
        k, j = lax.rem(i // 4 + 2, 4), lax.rem(i, 4)
        there = lax.rem(b + k, 4)
        f = block_there(there, j)
        slot = there * 4 + j
        if t == 0:
            src, dst = stage.at[f, :, q_cols(1 - core)], dq.at[slot]
        else:
            src, dst = go.at[f, o_lines(1 - core), :], do.at[slot]
        return remote(src, dst, sd.at[i, t], rd.at[i, t], partner)

    def home(i, t):
        k, j = lax.rem(i // 4 + 2, 4), lax.rem(i, 4)
        slot = lax.rem(a + k, 4) * 4 + j
        dst = (dq, do)[t].at[slot]
        return remote(dst, dst, sd.at[i, t], rd.at[i, t], partner)

    def start_away(t):
        def one(i, carry):
            away(i, t).start()
            return carry

        lax.fori_loop(0, 16, one, 0)

    start_away(1)

    keys, vals = pair_ref[:, :HD], pair_ref[:, HD:]
    queries = stack_heads(q_ref[...])
    grad_heads = stack_heads(grad_attended)
    scores = dot32(queries, keys, NT) * scale + jnp.concatenate([bias_ref[...]] * NH, axis=0)
    expo = jnp.exp(scores - jnp.max(scores, axis=-1, keepdims=True))
    probs = expo * (1.0 / jnp.sum(expo, axis=-1, keepdims=True))
    grad_probs = dot32(grad_heads, vals, NT)
    row_total = jnp.sum(probs * grad_probs, axis=-1, keepdims=True)
    grad_scores = (probs * (grad_probs - row_total)).astype(bf)
    gpair[:, HD:] = dot32(probs.astype(bf), grad_heads, TN)
    gpair[:, :HD] = dot32(grad_scores, queries, TN) * scale

    def kv_send(d):
        return remote(
            kv_snd.at[d - 1], kv_in.at[d - 1], skv.at[d - 1], rkv.at[d - 1], member(members - d)
        )

    for d in range(1, reach + 1):
        kv_snd[d - 1] = gpair[pl.ds((reach - d) * rows, rows), :].astype(bf)
        kv_send(d).start()

    pass_far((0, 2))
    cos_table, sin_table = turn_ref[:, : HD // 2], turn_ref[:, HD // 2 :]
    cos_all = jnp.concatenate([cos_table] * NH, axis=0)
    sin_all = jnp.concatenate([sin_table] * NH, axis=0)
    grad_queries = dot32(grad_scores, keys, NN) * scale
    grad_q, qk_gain_q = rms_back(
        stack_heads(proj_ref[:, : NH * HD]),
        turn_back(grad_queries, cos_all, sin_all),
        qk_ref[0:1, :],
    )
    for h in range(NH):
        gproj[:, h * HD : (h + 1) * HD] = grad_q[h * rows : (h + 1) * rows].astype(bf)

    def pair_of(k, h):
        return pl.ds(line(k) * 4 + 2 * h, 2)

    def sum_far(h, t):
        src, dst = ((sq, fq), (so, fo))[t]
        return remote(
            src.at[pair_of(2, h)], dst.at[pl.ds(2 * h, 2)],
            sfa.at[h, t], rfa.at[h, t], first_peer(3 if h else 1),
        )

    def sum_near(k, h, t):
        src, dst = ((sq, iq1), (so, io1))[t]
        side = 0 if k == 1 else 1
        return remote(
            src.at[pair_of(k, h)], dst.at[side, pl.ds(2 * h, 2)],
            s1.at[side, h, t], r1.at[side, h, t], first_peer(k),
        )

    def fold_cores(t):
        for k in (2, 3, 1, 0):
            def add(j, carry, k=k):
                slot = line(k) * 4 + j
                f = block(line(k), j)
                home((k + 2) % 4 * 4 + j, t).wait_recv()
                if t == 0:
                    sq[slot] = (
                        stage[f, :, q_cols(core)].astype(f32) + dq[slot].astype(f32)
                    ).astype(bf)
                else:
                    so[slot] = (
                        go[f, o_lines(core), :].astype(f32) + do[slot].astype(f32)
                    ).astype(bf)
                return carry

            lax.fori_loop(0, 4, add, 0)
            if k == 2:
                sum_far(0, t).start()
                sum_far(1, t).start()
            elif k:
                sum_near(k, 0 if k == 3 else 1, t).start()

    def fold_far(t):
        acc, far = ((sq, fq), (so, fo))[t]
        for h, k in ((0, 1), (1, 3)):
            sum_far(h, t).wait_recv()
            acc[pair_of(k, h)] = (
                acc[pair_of(k, h)].astype(f32) + far[2 * h : 2 * h + 2].astype(f32)
            ).astype(bf)
            sum_near(k, h, t).start()

    pass_far((1, 3))

    total = gpair[pl.ds(reach * rows, rows), :]
    for d in range(1, reach + 1):
        kv_send(d).wait_recv()
        total = total + kv_in[d - 1].astype(f32)
    grad_k, qk_gain_k = rms_back(
        proj_ref[:, NH * HD : NH * HD + HD],
        turn_back(total[:, :HD], cos_table, sin_table),
        qk_ref[1:2, :],
    )
    gproj[:, NH * HD : NH * HD + HD] = grad_k.astype(bf)
    gproj[:, NH * HD + HD :] = total[:, HD:].astype(bf)
    for copy in weight_loads[1:]:
        copy.wait()
    stream = tok_ref[...].astype(f32)
    grad_in, gain_zero = rms_back(stream, dot32(gproj[...], qkv_ref[...], NT), gains_ref[0:1, :])
    gt_ref[...] = gmid[...] + grad_in
    tail[...] = jnp.zeros_like(tail)
    for i, total_gain in enumerate((gain_zero, gain_one, gain_two, g3_ref[...])):
        tail[i : i + 1, :D] = total_gain
    tail[4:5, :HD] = qk_gain_q
    tail[5:6, :HD] = qk_gain_k

    def qkv_tile(t, carry):
        cols = pl.ds(pl.multiple_of(t * 256, 256), 256)
        res = dot32(normed_ref[...], gproj[:, cols], TN)
        low = tail[:, cols]
        for f in range(16):
            stage[f, :, cols] = jnp.concatenate(
                [res[f * keep : (f + 1) * keep], low], axis=0
            ).astype(bf)
        return carry

    lax.fori_loop(0, width // 256, qkv_tile, 0)
    start_away(0)

    for copy in own_loads[:4]:
        copy.wait()

    def ff_two(k):
        return remote(
            t_ff.at[lax.rem(b + k, 4)], in2_ff.at[3 - k], s2f.at[k], r2f.at[4 - k], second_peer(k)
        )

    for k in (2, 1, 3, 0):
        j = lax.rem(b + k, 4)
        for m in (0, 1):
            dst = in1_ff.at[m, j]
            remote(dst, dst, s1f.at[m, j], r1f.at[m, j], partner).wait_recv()
        total = own_ff[j].astype(f32)
        for m in (0, 1):
            total = total + in1_ff[m, j].astype(f32)
        t_ff[j] = total.astype(bf)
        if k:
            ff_two(k).start()

    fold_cores(1)
    fold_cores(0)
    fold_far(1)
    fold_far(0)

    def hop_two(k, t):
        src, dst = ((tq, iq2), (to, io2))[t]
        return remote(
            src.at[lax.rem(b + k, 4)], dst.at[3 - k], s2.at[k, t], r2.at[4 - k, t], second_peer(k)
        )

    for k in (1, 3, 2):
        ff_two(4 - k).wait_recv()
    total = t_ff[b].astype(f32)
    for m in range(3):
        total = total + in2_ff[m].astype(f32)
    all_ff[me] = total.astype(bf)

    half = all_ff.shape[1] // 2

    def ff_slot(k, there=0):
        return lax.rem(chip + k, chips) * 2 + (1 - core if there else core)

    def ff_all(k):
        peer = chip_peer(k) if k else partner
        return remote(
            all_ff.at[me], all_ff.at[me], sag.at[k], rag.at[(chips - k) % chips], peer
        )

    def ff_from(k):
        dst = all_ff.at[ff_slot(k)]
        return remote(dst, dst, sag.at[k], rag.at[k], partner)

    def ff_half(k, h, there=0):
        return all_ff.at[ff_slot(k, there), pl.ds(h * half, half), :]

    def ff_on(k):
        h = 0 if k == 3 else 1
        dst = ff_half(k, h)
        return remote(dst, dst, sag.at[8 + h], rag.at[8 + h], chip_peer(4 - k))

    def ff_far_got(h):
        dst = ff_half(2, h)
        return remote(dst, dst, sag.at[8 + h], rag.at[8 + h], partner)

    def ff_cross(k, h=None, there=0):
        if h is None:
            dst, i = all_ff.at[ff_slot(k, there)], 4 + k
        else:
            dst, i = ff_half(2, h, there), 10 + h
        return remote(dst, dst, sag.at[i], rag.at[i], partner)

    for k in (1, 3, 0):
        ff_all(k).start()

    for t in (1, 0):
        own, got, dst = ((sq, iq1, tq), (so, io1, to))[t]
        for k in (1, 3):
            for h in (0, 1):
                sum_near(k, h, t).wait_recv()
        for k in (2, 1, 3, 0):
            j = lax.rem(b + k, 4)
            total = own[a * 4 + j].astype(f32)
            for m in (0, 1):
                total = total + got[m, j].astype(f32)
            dst[j] = total.astype(bf)
            if k:
                hop_two(k, t).start()

    for k in (1, 3):
        ff_from(k).wait_recv()
        ff_on(k).start()
        ff_cross(k).start()

    def hop_chip(k, t):
        buf = (xq, xo)[t]
        return remote(
            buf.at[chip], buf.at[chip], sx.at[k, t], rx.at[chips - k, t], chip_peer(k)
        )

    for t in (1, 0):
        own, got, dst = ((tq, iq2, xq), (to, io2, xo))[t]
        for k in (1, 3, 2):
            hop_two(4 - k, t).wait_recv()
        total = own[b].astype(f32)
        for m in range(3):
            total = total + got[m].astype(f32)
        dst[chip] = total.astype(bf)
        for k in range(1, chips):
            hop_chip(k, t).start()

    def last(t, half):
        part = (oq_ref.at[:, q_cols(half)], oo_ref.at[o_lines(half), :])[t]
        return remote(part, part, sf.at[t], rf.at[t], partner)

    for h in (0, 1):
        ff_far_got(h).wait_recv()
        ff_cross(2, h).start()

    for t in (1, 0):
        buf = (xq, xo)[t]
        for k in range(1, chips):
            dst = buf.at[lax.rem(chip + k, chips)]
            remote(dst, dst, sx.at[k, t], rx.at[k, t], partner).wait_recv()
        total = buf[0].astype(f32)
        for m in range(1, chips):
            total = total + buf[m].astype(f32)
        if t == 0:
            oq_ref[:, q_cols(core)] = total
        else:
            oo_ref[o_lines(core), :] = total
        last(t, core).start()

    everywhere = all_ff.at[ff_slot(0, 1)]
    remote(everywhere, everywhere, sag.at[0], rag.at[0], partner).wait_recv()
    for k in (1, 3):
        ff_cross(k, there=1).wait_recv()
    for h in (0, 1):
        ff_cross(2, h, there=1).wait_recv()

    def end_away(i, carry):
        for t in (0, 1):
            away(i, t).wait_send()
        return carry

    lax.fori_loop(0, 16, end_away, 0)
    for j in range(4):
        ff_far(j).wait_send()
        ff_near(1, j).wait_send()
        ff_near(3, j).wait_send()
    for k in (1, 2, 3):
        ff_two(k).wait_send()
    for d in range(1, reach + 1):
        kv_send(d).wait_send()
    for k in (1, 3, 0):
        ff_all(k).wait_send()
    for k in (1, 3):
        ff_on(k).wait_send()
        ff_cross(k).wait_send()
    for h in (0, 1):
        ff_cross(2, h).wait_send()
    for t in (0, 1):
        for h in (0, 1):
            sum_far(h, t).wait_send()
            sum_near(1, h, t).wait_send()
            sum_near(3, h, t).wait_send()
        for k in (1, 2, 3):
            hop_two(k, t).wait_send()
        for k in range(1, chips):
            hop_chip(k, t).wait_send()
        last(t, core).wait_send()
        last(t, 1 - core).wait_recv()
    oq_out[...] = oq_ref[:keep, :]
    tail_out[...] = oq_ref[keep:, :]


def backward_rest(gff, values, weights, keep):
    f32, bf = jnp.float32, jnp.bfloat16
    vm = pl.BlockSpec(memory_space=pltpu.VMEM)
    hbm = pl.BlockSpec(memory_space=pl.ANY)
    dma = pltpu.SemaphoreType.DMA
    rows = values[0].shape[0]
    owners, ff_rows = gff.shape[:2]
    q_rows, width = keep + 8, (NH + 2) * HD
    o_rows, o_width = NH * HD // owners, D
    q_half, o_half = width // 2, o_rows // 2
    chips = lax.axis_size("ctx") // 2
    pairs = values[9].shape[0]
    reach = pairs // rows - 1

    def two(*lead):
        return [pltpu.VMEM(lead + (q_rows, q_half), bf), pltpu.VMEM(lead + (o_half, o_width), bf)]

    def ff(*lead):
        return pltpu.VMEM(lead + (ff_rows, D), bf)

    return pl.pallas_call(
        back_kernel,
        out_shape=(
            jax.ShapeDtypeStruct((rows, D), f32),
            jax.ShapeDtypeStruct((keep, width), f32),
            jax.ShapeDtypeStruct((8, width), f32),
            jax.ShapeDtypeStruct((o_rows, o_width), f32),
            jax.ShapeDtypeStruct((2 * chips, ff_rows, D), bf),
        ),
        in_specs=[hbm] + [vm] * len(values) + [hbm] * 2,
        out_specs=(vm,) * 5,
        scratch_shapes=[
            pltpu.VMEM((16 * keep, width), bf),
            pltpu.VMEM((16 * o_rows, o_width), bf),
            pltpu.VMEM((q_rows, width), f32),
            ff(4), ff(4), ff(4), ff(2, 4), ff(4), ff(3),
            pltpu.VMEM((reach, rows, 2 * HD), bf),
            pltpu.VMEM((reach, rows, 2 * HD), bf),
            pltpu.VMEM((rows, D), f32),
            pltpu.VMEM((pairs, 2 * HD), f32),
            pltpu.VMEM((rows, width), bf),
            pltpu.VMEM((8, width), f32),
            pltpu.VMEM((16, q_rows, width), bf),
            pltpu.VMEM((16, o_rows, o_width), bf),
            *two(16), *two(16), *two(4), *two(2, 4), *two(4), *two(3), *two(chips),
            dma((10,)),
            dma((4,)), dma((4,)),
            dma((2, 4)), dma((2, 4)),
            dma((4,)), dma((4,)),
            dma((12,)), dma((12,)),
            dma((reach,)), dma((reach,)),
            dma((16, 2)), dma((16, 2)),
            dma((2, 2)), dma((2, 2)),
            dma((2, 2, 2)), dma((2, 2, 2)),
            dma((4, 2)), dma((4, 2)),
            dma((4, 2)), dma((4, 2)),
            dma((2,)), dma((2,)),
        ],
        compiler_params=pltpu.CompilerParams(
            collective_id=3, has_side_effects=True, vmem_limit_bytes=62 * 1024 * 1024
        ),
        cost_estimate=pl.CostEstimate(
            flops=12 * rows * width * D, bytes_accessed=64 * ff_rows * D, transcendentals=0
        ),
    )(gff, *values, *weights)


def finish_kernel(*refs):
    count = (len(refs) - 7) // 2
    all_ref, tail_ref, sources = refs[0], refs[1], refs[2 : 2 + count]
    weights, gains, qk = refs[2 + count : 5 + count], refs[5 + count], refs[6 + count]
    for src, dst in zip(sources, refs[7 + count :]):
        dst[...] = src[...]
    owner = lax.axis_index("fsdp")
    width = tail_ref.shape[1]
    for first, dst in ((0, gains), (4, qk)):
        lines, own = dst.shape
        shift = lax.rem(width - owner * own, width)
        dst[...] = pltpu.roll(tail_ref[...], shift, 1)[first : first + lines, :own]
    members = all_ref.shape[0]
    share = all_ref.shape[1] // 3
    lines = weights[0].shape[0] // members
    for i, dst in enumerate(weights):
        for m in range(members):
            dst[m * lines : (m + 1) * lines, :] = all_ref[
                m, i * share : (i + 1) * share, :
            ].astype(jnp.float32)[:lines]


def finish(all_ff, tail, lines, gain_lines, qk_lines, *rest):
    vm = pl.BlockSpec(memory_space=pltpu.VMEM)
    f32 = jnp.float32
    results = ((lines, D),) * 3 + (gain_lines, qk_lines)
    return pl.pallas_call(
        finish_kernel,
        out_shape=tuple(jax.ShapeDtypeStruct(s, f32) for s in results)
        + tuple(jax.ShapeDtypeStruct(r.shape, r.dtype) for r in rest),
        in_specs=[vm] * (2 + len(rest)),
        out_specs=(vm,) * (5 + len(rest)),
        compiler_params=pltpu.CompilerParams(vmem_limit_bytes=62 * 1024 * 1024),
    )(all_ff, tail, *rest)


def on_device(
    tokens,
    norm_gains,
    qk_gains,
    qkv_weight,
    out_weight,
    gate_weight,
    up_weight,
    down_weight,
    segments,
    cotangent,
):
    local_len = tokens.shape[1]
    ctx_index = lax.axis_index("ctx")
    owner = lax.axis_index("fsdp")
    ctx_size = lax.axis_size("ctx")
    own_rows = gate_weight.shape[0]
    slice_rows = own_rows // ctx_size
    padded = -(-slice_rows // 16) * 16
    keep, width = qkv_weight.shape
    gain_lines, qk_lines = norm_gains.shape, qk_gains.shape
    def placed(lines):
        count, own = lines.shape
        room = (lax.axis_size("fsdp") - 1) * own
        padded_lines = jnp.pad(lines, ((0, 0), (room, room)))
        spread = lax.dynamic_slice(padded_lines, (0, room - owner * own), (count, room + own))
        return jnp.pad(spread, ((0, 0), (0, width - room - own)))

    gain_rows = jnp.concatenate(
        [placed(norm_gains), placed(qk_gains), jnp.zeros((2, width), jnp.bfloat16)], axis=0
    )

    def my_slice(weight):
        part = lax.dynamic_slice(weight, (ctx_index * slice_rows, 0), (slice_rows, D))
        return jnp.pad(part, ((0, padded - slice_rows), (0, 0)))

    ffn_shard = jnp.concatenate(
        [my_slice(gate_weight), my_slice(up_weight)], axis=0
    )
    places = np.arange(ctx_size * local_len, dtype=np.float32)
    rates = (ROPE_BASE ** (-(2.0 * np.arange(HD // 2)) / HD)).astype(np.float32)
    angles = (places[:, None] * rates).astype(np.float64)
    table = jnp.asarray(
        np.concatenate([np.cos(angles), np.sin(angles)], axis=1)
        .astype(np.float32)
        .reshape(ctx_size, local_len, HD)
    )
    flat = tokens.reshape(local_len, D)
    cot = cotangent.reshape(local_len, D)
    (
        qkv_full, out_full, ffn_full, gains_all, qk_all, normed, projected, queries, pair_all,
        attended, attn, mid, normed_seq, bias, turn_table,
    ) = front(
        jnp.concatenate([qkv_weight, gain_rows], axis=0),
        out_weight,
        ffn_shard,
        flat,
        segments,
        table,
        keep,
    )
    output, grad_normed_two, grad_gain_three, ffn_grads = ffn(
        normed_seq, mid, cot, gains_all, my_slice(down_weight), ffn_full
    )
    grad_tokens, total_qkv, tail, total_out, all_ff = backward_rest(
        ffn_grads,
        (
            grad_normed_two, mid, attn, cot, flat, gains_all, qk_all, projected, queries,
            pair_all, attended, normed, turn_table, bias, grad_gain_three,
        ),
        (qkv_full, out_full),
        keep,
    )
    (
        total_gate, total_up, total_down, total_gains, total_qk,
        grad_tokens, total_qkv, total_out, output,
    ) = finish(
        all_ff, tail, own_rows, gain_lines, qk_lines, grad_tokens, total_qkv, total_out, output
    )
    return (
        output.reshape(tokens.shape),
        grad_tokens.reshape(tokens.shape),
        total_gains,
        total_qk,
        total_qkv,
        total_out,
        total_gate,
        total_up,
        total_down,
    )


def solution(mesh):
    in_specs = (
        P("fsdp", "ctx", None),
        P(None, "fsdp"),
        P(None, "fsdp"),
        P("fsdp", None),
        P("fsdp", None),
        P("fsdp", None),
        P("fsdp", None),
        P("fsdp", None),
        P("fsdp", "ctx"),
        P("fsdp", "ctx", None),
    )
    out_specs = (
        P("fsdp", "ctx", None),
        P("fsdp", "ctx", None),
        P(None, "fsdp"),
        P(None, "fsdp"),
        P("fsdp", None),
        P("fsdp", None),
        P("fsdp", None),
        P("fsdp", None),
        P("fsdp", None),
    )
    return jax.shard_map(
        on_device, mesh=mesh, in_specs=in_specs, out_specs=out_specs, check_vma=False
    )
```

```python
import functools

import jax
import numpy as np
import jax.numpy as jnp
from jax import lax
from jax.experimental import pallas as pl
from jax.experimental.pallas import tpu as pltpu
from jax.sharding import PartitionSpec as P

D = 1152
NH = 4
HD = 256
WINDOW = 512


EPS = 1e-06
ROPE_BASE = 10000.0
NEG_FILL = -1e30


def rms_norm(values, gain_vec):
    return values * lax.rsqrt(jnp.mean(values * values, axis=-1, keepdims=True) + EPS) * gain_vec


MESH = pl.DeviceIdType.MESH
NT = (((1,), (1,)), ((), ()))
NN = (((1,), (0,)), ((), ()))
TN = (((0,), (0,)), ((), ()))
GELU_C = 0.7978845608028654
GELU_A = 0.044715


def dot32(left, right, dims):
    return lax.dot_general(left, right, dims, preferred_element_type=jnp.float32)


def ffn_kernel(
    normed_ref, mid_ref, cot_ref, gain_ref, w_hbm,
    out_ref, gn_ref, ggain_ref, gff_hbm,
    wg, wu, wd, seq, gseq, act_a, act_b, hid, dgate, dup, part, keep, base,
    d2d_snd, d2d_in, ici_snd, ici_in, dw,
    w_sem, o_sem, ag_s, ag_r, rd_s, rd_r, ri_s, ri_r,
):
    rows = normed_ref.shape[0]
    units = wg.shape[0]
    share = units // w_hbm.shape[0]
    tile = 256
    me = lax.axis_index("ctx")
    chip, core = me // 2, lax.rem(me, 2)
    partner = {"ctx": chip * 2 + 1 - core}
    chips = {k: {"ctx": lax.rem(chip + k, 4) * 2 + core} for k in (1, 2, 3)}
    order = (0, 1, 3, 2)

    loads = [
        pltpu.make_async_copy(
            w_hbm.at[f, pl.ds(i * share, share), :], dst.at[pl.ds(f * share, share), :], w_sem.at[i, f]
        )
        for i, dst in enumerate((wg, wu, wd))
        for f in range(w_hbm.shape[0])
    ]
    for load in loads:
        load.start()

    barrier = pltpu.get_barrier_semaphore()
    for peer in (partner, chips[1], chips[2], chips[3]):
        pl.semaphore_signal(barrier, inc=1, device_id=peer, device_id_type=MESH)
    pl.semaphore_wait(barrier, 4)

    started = []

    def send(src, dst, s_sem, r_sem, peer):
        copy = pltpu.make_async_remote_copy(
            src_ref=src, dst_ref=dst, send_sem=s_sem, recv_sem=r_sem,
            device_id=peer, device_id_type=MESH,
        )
        copy.start()
        started.append(copy)
        return copy

    def mine(k):
        return pl.ds(k * 2 * rows, rows)

    def other(k):
        return pl.ds(k * 2 * rows + rows, rows)

    def pair(k):
        return pl.ds(k * 2 * rows, 2 * rows)

    def spread(buf, ph):
        own = buf.at[mine(0)]
        got = {}
        for k in (1, 3):
            back = 4 - k
            got[back] = send(own, buf.at[mine(back)], ag_s.at[ph, k], ag_r.at[ph, back], chips[k])
        got[0] = send(own, buf.at[other(0)], ag_s.at[ph, 0], ag_r.at[ph, 0], partner)
        return got

    def half_of(k, h, offset=0):
        return pl.ds(k * 2 * rows + offset + h * (rows // 2), rows // 2)

    def relay(buf, ph, got, k):
        got[k].wait_recv()
        h = 0 if k == 3 else 1
        got[2, h] = send(
            buf.at[half_of(k, h)], buf.at[half_of(2, h)],
            ag_s.at[ph, 2 + 2 * h], ag_r.at[ph, 2 + 2 * h], chips[4 - k],
        )
        got[k] = send(
            buf.at[mine(k)], buf.at[other(k)], ag_s.at[ph, 4 + k], ag_r.at[ph, 4 + k], partner
        )

    def relay_far(buf, ph, got):
        for h in (0, 1):
            got[2, h].wait_recv()
            got[2, h] = send(
                buf.at[half_of(2, h)], buf.at[half_of(2, h, rows)],
                ag_s.at[ph, 6 + 2 * h], ag_r.at[ph, 6 + 2 * h], partner,
            )

    def swap(ph, k):
        d2d_snd[ph, k] = part[pl.ds(rows, rows), :].astype(jnp.bfloat16)
        keep[order.index(k) % 2] = part[pl.ds(0, rows), :]
        return send(d2d_snd.at[ph, k], d2d_in.at[ph, k], rd_s.at[ph, k], rd_r.at[ph, k], partner)

    def sum_out(ph, k, copy):
        copy.wait_recv()
        total = keep[order.index(k) % 2] + d2d_in[ph, k].astype(jnp.float32)
        if k == 0:
            base[...] = total
            return None
        ici_snd[ph, k - 1] = total.astype(jnp.bfloat16)
        back = 4 - k
        return send(
            ici_snd.at[ph, k - 1], ici_in.at[ph, back - 1], ri_s.at[ph, k], ri_r.at[ph, back],
            chips[k],
        )

    def phase(buf, ph, work):
        got = spread(buf, ph)
        if ph == 0:
            for load in loads:
                load.wait()
        sums = {}
        copy = waiting = None
        for k in order:
            if k == 1:
                relay(buf, ph, got, 1)
                relay(buf, ph, got, 3)
            if k == 2:
                relay_far(buf, ph, got)
                got[2, 0].wait_recv()
                got[2, 1].wait_recv()
            else:
                got[k].wait_recv()
            if waiting is not None and k == 2:
                sums[waiting] = sum_out(ph, waiting, copy)
                waiting = None
            work(k)
            if waiting is not None:
                sums[waiting] = sum_out(ph, waiting, copy)
            copy, waiting = swap(ph, k), k
        sums[waiting] = sum_out(ph, waiting, copy)
        return sums

    def collect(ph, sums):
        total = base[...]
        for k in (1, 3, 2):
            sums[k].wait_recv()
        for k in (1, 2, 3):
            total = total + ici_in[ph, k - 1].astype(jnp.float32)
        return total

    def forward(k):
        def one(t, carry):
            cols = pl.ds(pl.multiple_of(t * tile, tile), tile)
            block = seq[pair(k), :]
            gate = dot32(block, wg[cols, :], NT)
            up = dot32(block, wu[cols, :], NT)
            square = gate * gate
            th = jnp.tanh(GELU_C * gate * (1.0 + GELU_A * square))
            half = 0.5 * (1.0 + th)
            gelu = gate * half
            slope = half + (0.5 * GELU_C) * gate * (1.0 - th * th) * (1.0 + 3.0 * GELU_A * square)
            hid[pair(k), cols] = (gelu * up).astype(jnp.bfloat16)
            act_a[pair(k), cols] = up * slope
            act_b[pair(k), cols] = gelu
            return carry

        lax.fori_loop(0, units // tile, one, 0)
        part[...] = dot32(hid[pair(k), :], wd[...], NN)

    seq[mine(0), :] = normed_ref[...]
    sums = phase(seq, 0, forward)
    mlp = collect(0, sums)
    r = lax.rsqrt(jnp.mean(mlp * mlp, axis=-1, keepdims=True) + EPS)
    n = mlp * r
    gain = gain_ref[3:4, :]
    out_ref[...] = (mid_ref[...] + n * gain).astype(jnp.bfloat16)
    dy = cot_ref[...].astype(jnp.float32)
    ggain_ref[...] = jnp.sum(dy * n, axis=0, keepdims=True)
    dyg = dy * gain
    dv = r * (dyg - n * jnp.mean(dyg * n, axis=-1, keepdims=True))
    gseq[mine(0), :] = dv.astype(jnp.bfloat16)

    def backward(k):
        def one(t, carry):
            cols = pl.ds(pl.multiple_of(t * tile, tile), tile)
            gh = dot32(gseq[pair(k), :], wd[cols, :], NT)
            dgate[pair(k), cols] = (gh * act_a[pair(k), cols]).astype(jnp.bfloat16)
            dup[pair(k), cols] = (gh * act_b[pair(k), cols]).astype(jnp.bfloat16)
            return carry

        lax.fori_loop(0, units // tile, one, 0)
        part[...] = dot32(dgate[pair(k), :], wg[...], NN) + dot32(dup[pair(k), :], wu[...], NN)

    sums = phase(gseq, 1, backward)
    stores = []
    for i, (left, right) in enumerate(((dgate, seq), (dup, seq), (hid, gseq))):
        def one(t, carry, i=i, left=left, right=right):
            cols = pl.ds(pl.multiple_of(t * tile, tile), tile)
            group = tile // share
            dw[pl.ds(t * group, group), pl.ds(i * share, share), :] = (
                dot32(left[:, cols], right[...], TN).reshape(group, share, -1).astype(jnp.bfloat16)
            )
            return carry

        lax.fori_loop(0, units // tile, one, 0)
        third = pl.ds(i * share, share)
        stores.append(
            pltpu.make_async_copy(dw.at[:, third, :], gff_hbm.at[:, third, :], o_sem.at[i])
        )
        stores[-1].start()
    gn_ref[...] = collect(1, sums)
    for copy in started:
        copy.wait_send()
    for store in stores:
        store.wait()


def ffn(normed_two, mid, cot, gain, weights):
    rows = normed_two.shape[0]
    owners, lines = weights.shape[:2]
    units = owners * lines // 3
    seq_rows = rows * 8
    bf, f32 = jnp.bfloat16, jnp.float32
    vm = pl.BlockSpec(memory_space=pltpu.VMEM)
    hbm = pl.BlockSpec(memory_space=pl.ANY)
    dma = pltpu.SemaphoreType.DMA
    return pl.pallas_call(
        ffn_kernel,
        out_shape=(
            jax.ShapeDtypeStruct((rows, D), bf),
            jax.ShapeDtypeStruct((rows, D), f32),
            jax.ShapeDtypeStruct((1, D), f32),
            jax.ShapeDtypeStruct(weights.shape, bf),
        ),
        in_specs=[vm] * 4 + [hbm],
        out_specs=(vm, vm, vm, hbm),
        scratch_shapes=[
            pltpu.VMEM((units, D), bf),
            pltpu.VMEM((units, D), bf),
            pltpu.VMEM((units, D), bf),
            pltpu.VMEM((seq_rows, D), bf),
            pltpu.VMEM((seq_rows, D), bf),
            pltpu.VMEM((seq_rows, units), f32),
            pltpu.VMEM((seq_rows, units), f32),
            pltpu.VMEM((seq_rows, units), bf),
            pltpu.VMEM((seq_rows, units), bf),
            pltpu.VMEM((seq_rows, units), bf),
            pltpu.VMEM((2 * rows, D), f32),
            pltpu.VMEM((2, rows, D), f32),
            pltpu.VMEM((rows, D), f32),
            pltpu.VMEM((2, 4, rows, D), bf),
            pltpu.VMEM((2, 4, rows, D), bf),
            pltpu.VMEM((2, 3, rows, D), bf),
            pltpu.VMEM((2, 3, rows, D), bf),
            pltpu.VMEM(weights.shape, bf),
            dma((3, owners)), dma((3,)),
            dma((2, 10)), dma((2, 10)),
            dma((2, 4)), dma((2, 4)),
            dma((2, 4)), dma((2, 4)),
        ],
        compiler_params=pltpu.CompilerParams(
            collective_id=1, has_side_effects=True, vmem_limit_bytes=62 * 1024 * 1024
        ),
        cost_estimate=pl.CostEstimate(
            flops=18 * seq_rows * units * D, bytes_accessed=14 * units * D, transcendentals=0
        ),
    )(normed_two, mid, cot, gain, weights)


def place():
    fsdp = lax.axis_index("fsdp")
    ctx = lax.axis_index("ctx")
    y, z = fsdp // 4, lax.rem(fsdp, 4)
    chip, core = ctx // 2, lax.rem(ctx, 2)
    return y, z, chip, core


def shape_of(y, z, core):
    first = (1 - core) * y + core * z
    second = (1 - core) * z + core * y

    def block(i, j):
        return (1 - core) * (4 * i + j) + core * (4 * j + i)

    return first, second, block


def remote(src, dst, s_sem, r_sem, peer):
    return pltpu.make_async_remote_copy(
        src_ref=src, dst_ref=dst, send_sem=s_sem, recv_sem=r_sem,
        device_id=peer, device_id_type=MESH,
    )


def greet(peers, meanwhile=None):
    barrier = pltpu.get_barrier_semaphore()
    for peer in peers:
        pl.semaphore_signal(barrier, inc=1, device_id=peer, device_id_type=MESH)
    if meanwhile is not None:
        meanwhile()
    pl.semaphore_wait(barrier, len(peers))


def rms_back(values, grad, gain):
    r = lax.rsqrt(jnp.mean(values * values, axis=-1, keepdims=True) + EPS)
    n = values * r
    dyg = grad * gain
    return (
        r * (dyg - n * jnp.mean(dyg * n, axis=-1, keepdims=True)),
        jnp.sum(grad * n, axis=0, keepdims=True),
    )


def stack_heads(values):
    return jnp.concatenate([values[:, h * HD : (h + 1) * HD] for h in range(NH)], axis=0)


def turn_back(grad, cos_table, sin_table):
    left, right = grad[:, : HD // 2], grad[:, HD // 2 :]
    return jnp.concatenate(
        [left * cos_table + right * sin_table, right * cos_table - left * sin_table], axis=1
    )


def front_kernel(
    qkv_own, gain_own, qk_own, wo_ref, ffn_ref, tok_ref, seg_line, table_ref,
    qkv_hbm, wo_hbm, ffn_all, gains_ref, qk_ref, normed_ref, proj_ref, q_ref, pair_ref, att_ref,
    attn_ref, mid_ref, low_ref, bias_ref, turn_ref,
    qkv_ref, placing, qkv_all, qkv_out, wo_all, seg_ref, seg_in,
    l_sem, s1, r1, s2, r2, sd, rd, s1f, r1f, s2f, r2f, skv, rkv, ssg, rsg,
):
    f32, bf = jnp.float32, jnp.bfloat16
    y, z, chip, core = place()
    a, b, block = shape_of(y, z, core)
    _, _, block_there = shape_of(y, z, 1 - core)
    q_rows, width = qkv_ref.shape
    o_rows = wo_ref.shape[0]
    q_half, o_half = width // 2, o_rows // 2
    partner = {"ctx": chip * 2 + 1 - core}
    me = chip * 2 + core
    rows = tok_ref.shape[0]
    reach = pair_ref.shape[0] // rows - 1
    members = 2 * (lax.axis_size("ctx") // 2)

    def member(k):
        return {"ctx": lax.rem(me + k, members)}

    seg_ref[...] = jnp.broadcast_to(seg_line[...], seg_ref.shape)

    def views(f, half):
        return (
            qkv_all.at[
                pl.ds(pl.multiple_of(f * q_rows, 16), q_rows),
                pl.ds(pl.multiple_of(half * q_half, 128), q_half),
            ],
            wo_all.at[pl.ds(pl.multiple_of(f * o_rows + half * o_half, 16), o_half), :],
        )

    mine = (
        qkv_ref.at[:, pl.ds(pl.multiple_of(core * q_half, 128), q_half)],
        wo_ref.at[pl.ds(pl.multiple_of(core * o_half, 16), o_half), :],
    )
    here = block(a, b)
    def stage_shard():
        owner = lax.axis_index("fsdp")
        placing[...] = jnp.zeros_like(placing)
        lines, own = gain_own.shape
        placing[:lines, :own] = gain_own[...].astype(f32)
        placed = pltpu.roll(placing[...], owner * own, 1)
        placing[...] = jnp.zeros_like(placing)
        more, own = qk_own.shape
        placing[lines : lines + more, :own] = qk_own[...].astype(f32)
        placed = placed + pltpu.roll(placing[...], owner * own, 1)
        qkv_ref[...] = jnp.concatenate([qkv_own[...].astype(f32), placed], axis=0).astype(bf)

    locals_ = [
        pltpu.make_async_copy(
            qkv_ref, qkv_all.at[pl.ds(pl.multiple_of(here * q_rows, 16), q_rows), :], l_sem.at[0]
        ),
        pltpu.make_async_copy(
            wo_ref, wo_all.at[pl.ds(pl.multiple_of(here * o_rows, 16), o_rows), :], l_sem.at[1]
        ),
        pltpu.make_async_copy(ffn_ref, ffn_all.at[here], l_sem.at[2]),
        pltpu.make_async_copy(table_ref.at[me], turn_ref, l_sem.at[3]),
    ]
    for copy in locals_[1:]:
        copy.start()

    def first_peer(k):
        return {"fsdp": block(lax.rem(a + k, 4), b)}

    def second_peer(k):
        return {"fsdp": block(a, lax.rem(b + k, 4))}

    greet(
        [first_peer(k) for k in (1, 2, 3)]
        + [second_peer(k) for k in (1, 2, 3)]
        + [member(k) for k in range(1, members)],
        stage_shard,
    )
    locals_[0].start()

    def seg_send(d):
        return remote(
            seg_ref, seg_in.at[reach - d], ssg.at[d - 1], rsg.at[d - 1], member(d)
        )

    def ffn_one(k):
        return remote(ffn_ref, ffn_all.at[here], s1f.at[k], r1f.at[4 - k], first_peer(k))

    def ffn_block(j, m):
        return ffn_all.at[block(lax.rem(a + j, 4), lax.rem(b + m, 4))]

    def ffn_two(j, k):
        dst = ffn_block(j, 0)
        src = dst if j else ffn_ref
        return remote(src, dst, s2f.at[j, k], r2f.at[j, 4 - k], second_peer(k))

    def ffn_pass(j):
        dst, k = (ffn_block(j, 3), 1) if j < 2 else (ffn_block(j, 1), 3)
        return remote(dst, dst, s2f.at[j, 2], r2f.at[j, 2], second_peer(k))

    def ffn_got(j, m):
        dst = ffn_block(j, m)
        sems = (s1f.at[j], r1f.at[j]) if m == 0 else (s2f.at[j, m], r2f.at[j, m])
        return remote(dst, dst, *sems, partner)

    def hop_one(k, t):
        return remote(mine[t], views(here, core)[t], s1.at[k, t], r1.at[4 - k, t], first_peer(k))

    def hop_two(j, k, t):
        f = block(lax.rem(a + j, 4), b)
        dst = views(f, core)[t]
        src = dst if j else mine[t]
        return remote(src, dst, s2.at[j, k, t], r2.at[j, 4 - k, t], second_peer(k))

    def arrive_one(j, t):
        dst = views(block(lax.rem(a + j, 4), b), core)[t]
        return remote(dst, dst, s1.at[j, t], r1.at[j, t], partner)

    def arrive_two(j, m, t):
        dst = views(block(lax.rem(a + j, 4), lax.rem(b + m, 4)), core)[t]
        return remote(dst, dst, s2.at[j, m, t], r2.at[j, m, t], partner)

    def cross(j, m, t):
        dst = views(block(lax.rem(a + j, 4), lax.rem(b + m, 4)), core)[t]
        return remote(dst, dst, sd.at[j, m, t], rd.at[j, m, t], partner)

    def arrive_cross(j, m, t):
        dst = views(block_there(lax.rem(b + j, 4), lax.rem(a + m, 4)), 1 - core)[t]
        return remote(dst, dst, sd.at[j, m, t], rd.at[j, m, t], partner)

    both = (0, 1)
    for k in (1, 3, 2):
        for t in both:
            hop_one(k, t).start()
    def hop_pass(j, t):
        m, k = (3, 1) if j < 2 else (1, 3)
        dst = views(block(lax.rem(a + j, 4), lax.rem(b + m, 4)), core)[t]
        return remote(dst, dst, s2.at[j, 2, t], r2.at[j, 2, t], second_peer(k))

    for k in (1, 3):
        for t in both:
            hop_two(0, k, t).start()
    for j in (1, 3, 2):
        for t in both:
            arrive_one(j, t).wait_recv()
            for k in (1, 3):
                hop_two(j, k, t).start()
            cross(j, 0, t).start()

    for d in range(1, reach + 1):
        seg_send(d).start()
    for k in (1, 3, 2):
        ffn_one(k).start()
    for k in (1, 3):
        ffn_two(0, k).start()

    for j in (0, 1, 3, 2):
        for m in (3, 1) if j < 2 else (1, 3):
            for t in both:
                arrive_two(j, m, t).wait_recv()
                if m == (3 if j < 2 else 1):
                    hop_pass(j, t).start()
                cross(j, m, t).start()
    for j in (0, 1, 3, 2):
        for t in both:
            arrive_two(j, 2, t).wait_recv()
            cross(j, 2, t).start()

    def land(i, carry):
        m, j = i // 4, lax.rem(i, 4)
        for t in both:
            arrive_cross(j, m, t).wait_recv()
            cross(j, m, t).wait_send()
        return carry

    lax.fori_loop(1, 16, land, 0)
    for copy in locals_[:2]:
        copy.wait()
    for t in both:
        for k in (1, 2, 3):
            hop_one(k, t).wait_send()
        for j in range(4):
            hop_pass(j, t).wait_send()
            for k in (1, 3):
                hop_two(j, k, t).wait_send()
    saves = [
        pltpu.make_async_copy(qkv_out, qkv_hbm, l_sem.at[4]),
        pltpu.make_async_copy(wo_all, wo_hbm, l_sem.at[5]),
    ]
    saves[1].start()

    keep = qkv_out.shape[0] // 16
    extra = jnp.zeros((q_rows - keep, width), f32)
    for f in range(0, 16, 2):
        left = qkv_all[pl.ds(f * q_rows, q_rows), :].astype(f32)
        right = qkv_all[pl.ds((f + 1) * q_rows, q_rows), :].astype(f32)
        qkv_out[pl.ds(f * keep, 2 * keep), :] = jnp.concatenate(
            [left[:keep], right[:keep]], axis=0
        ).astype(bf)
        extra = extra + left[keep:] + right[keep:]
    saves[0].start()
    gains = extra[:4, :D]
    gains_ref[...] = gains
    qk_ref[...] = extra[4:6, :HD]

    stream = tok_ref[...].astype(f32)
    normed_ref[...] = rms_norm(stream, gains[0:1]).astype(bf)
    proj_ref[...] = dot32(normed_ref[...], qkv_out[...], NN)
    locals_[3].wait()
    cos_table, sin_table = turn_ref[:, : HD // 2], turn_ref[:, HD // 2 :]

    def turn(values, gain, cos_part, sin_part):
        values = rms_norm(values, gain)
        left, right = values[:, : HD // 2], values[:, HD // 2 :]
        return jnp.concatenate(
            [left * cos_part - right * sin_part, right * cos_part + left * sin_part], axis=1
        ).astype(bf)

    own = pl.ds(reach * rows, rows)
    pair_ref[own, :HD] = turn(
        proj_ref[:, NH * HD : NH * HD + HD], extra[5:6, :HD], cos_table, sin_table
    )
    pair_ref[own, HD:] = proj_ref[:, NH * HD + HD :].astype(bf)

    def kv_send(d):
        return remote(
            pair_ref.at[own],
            pair_ref.at[pl.ds((reach - d) * rows, rows)],
            skv.at[d - 1], rkv.at[d - 1], member(d),
        )

    for d in range(1, reach + 1):
        kv_send(d).start()
    for j in (1, 3, 2):
        ffn_got(j, 0).wait_recv()
        for k in (1, 3):
            ffn_two(j, k).start()
    queries = turn(
        stack_heads(proj_ref[:, : NH * HD]),
        extra[4:5, :HD],
        jnp.concatenate([cos_table] * NH, axis=0),
        jnp.concatenate([sin_table] * NH, axis=0),
    )
    for h in range(NH):
        q_ref[:, h * HD : (h + 1) * HD] = queries[h * rows : (h + 1) * rows]

    for d in range(1, reach + 1):
        seg_send(d).wait_recv()
    seg_in[reach] = seg_ref[...]
    key_seg = jnp.concatenate([seg_in[p][0:1, :] for p in range(reach + 1)], axis=1)
    shape = (rows, (reach + 1) * rows)
    spacing = (
        reach * rows + lax.broadcasted_iota(jnp.int32, shape, 0)
        - lax.broadcasted_iota(jnp.int32, shape, 1)
    )
    begun = lax.broadcasted_iota(jnp.int32, shape, 1) + (me - reach) * rows >= 0
    wide = jnp.broadcast_to(seg_line[...], (rows, rows)).astype(f32)
    query_seg = jnp.concatenate([wide.T] * (reach + 1), axis=1)
    allowed = (
        (spacing >= 0) & (spacing < WINDOW) & begun & (query_seg == key_seg.astype(f32))
    )
    bias_ref[...] = jnp.where(allowed, 0.0, NEG_FILL)
    def ffn_onward(j):
        ffn_got(j, 3 if j < 2 else 1).wait_recv()
        ffn_pass(j).start()

    ffn_onward(0)
    for d in range(1, reach + 1):
        kv_send(d).wait_recv()
    scores = dot32(queries, pair_ref[:, :HD], NT) * (HD ** (-0.5)) + jnp.concatenate(
        [bias_ref[...]] * NH, axis=0
    )
    expo = jnp.exp(scores - jnp.max(scores, axis=-1, keepdims=True))
    probs = expo * (1.0 / jnp.sum(expo, axis=-1, keepdims=True))
    heads = dot32(probs.astype(bf), pair_ref[:, HD:], NN).astype(bf)
    for h in range(NH):
        att_ref[:, h * HD : (h + 1) * HD] = heads[h * rows : (h + 1) * rows]
    ffn_onward(1)
    ffn_onward(3)
    attn = dot32(att_ref[...], wo_all[...], NN)
    attn_ref[...] = attn
    mid = stream + rms_norm(attn, gains[1:2])
    mid_ref[...] = mid
    low_ref[...] = rms_norm(mid, gains[2:3]).astype(bf)

    ffn_onward(2)
    for copy in saves + locals_[2:3]:
        copy.wait()
    for j in range(4):
        ffn_got(j, 1 if j < 2 else 3).wait_recv()
        ffn_got(j, 2).wait_recv()
    for j in range(4):
        ffn_pass(j).wait_send()
        for k in (1, 3):
            ffn_two(j, k).wait_send()
    for k in (1, 2, 3):
        ffn_one(k).wait_send()
    for d in range(1, reach + 1):
        seg_send(d).wait_send()
        kv_send(d).wait_send()


def front(qkv_own, gain_own, qk_own, wo_shard, ffn_shard, tokens, seg_line, table):
    f32, bf = jnp.float32, jnp.bfloat16
    vm = pl.BlockSpec(memory_space=pltpu.VMEM)
    hbm = pl.BlockSpec(memory_space=pl.ANY)
    dma = pltpu.SemaphoreType.DMA
    keep, width = qkv_own.shape
    q_rows = keep + 8
    o_rows, o_width = wo_shard.shape
    rows = tokens.shape[0]
    reach = min(-(-(WINDOW - 1) // rows), lax.axis_size("ctx") - 1)
    pairs = (reach + 1) * rows
    shapes = (
        ((16 * keep, width), bf),
        ((16 * o_rows, o_width), bf),
        ((16, *ffn_shard.shape), bf),
        ((4, D), f32),
        ((2, HD), f32),
        ((rows, D), bf),
        ((rows, width), f32),
        ((rows, NH * HD), bf),
        ((pairs, 2 * HD), bf),
        ((rows, NH * HD), bf),
        ((rows, D), f32),
        ((rows, D), f32),
        ((rows, D), bf),
        ((rows, pairs), f32),
        ((rows, HD), f32),
    )
    return pl.pallas_call(
        front_kernel,
        out_shape=tuple(jax.ShapeDtypeStruct(*s) for s in shapes),
        in_specs=[vm, vm, vm, vm, hbm, vm, vm, hbm],
        out_specs=(hbm,) * 3 + (vm,) * (len(shapes) - 3),
        scratch_shapes=[
            pltpu.VMEM((q_rows, width), bf),
            pltpu.VMEM((8, width), f32),
            pltpu.VMEM((16 * q_rows, width), bf),
            pltpu.VMEM((16 * keep, width), bf),
            pltpu.VMEM((16 * o_rows, o_width), bf),
            pltpu.VMEM((8, rows), jnp.int32),
            pltpu.VMEM((reach + 1, 8, rows), jnp.int32),
            dma((6,)),
            dma((4, 2)), dma((4, 2)),
            dma((4, 4, 2)), dma((4, 4, 2)),
            dma((4, 4, 2)), dma((4, 4, 2)),
            dma((4,)), dma((4,)),
            dma((4, 4)), dma((4, 4)),
            dma((reach,)), dma((reach,)),
            dma((reach,)), dma((reach,)),
        ],
        compiler_params=pltpu.CompilerParams(
            collective_id=2, has_side_effects=True, vmem_limit_bytes=62 * 1024 * 1024
        ),
        cost_estimate=pl.CostEstimate(
            flops=6 * rows * width * D, bytes_accessed=64 * q_rows * width, transcendentals=0
        ),
    )(qkv_own, gain_own, qk_own, wo_shard, ffn_shard, tokens, seg_line, table)


def back_entry(count, gff, *refs):
    sources, refs = refs[:count], refs[count:]
    hbm_and_out, refs = refs[:7], refs[7:]
    held, v_sem, rest = refs[:count], refs[count], refs[count + 1 :]
    loads = [
        pltpu.make_async_copy(src, dst, v_sem.at[i]) for i, (src, dst) in enumerate(zip(sources, held))
    ]
    for load in loads:
        load.start()
    back_kernel(loads, gff, *held, *hbm_and_out, *rest)


def back_kernel(
    loads, gff, gn_ref, mid_ref, attn_ref, cot_ref, tok_ref, gains_ref, qk_ref, proj_ref, q_ref,
    pair_ref, att_ref, normed_ref, turn_ref, bias_ref, g3_ref, qkv_hbm, wo_hbm,
    gt_ref, oq_out, tail_out, oo_ref, all_ff,
    qkv_ref, wo_ref, oq_ref, own_ff, far_own, far_in, in1_ff, t_ff, in2_ff, kv_snd, kv_in, gmid, gpair, gproj, tail,
    stage, go, dq, do, sq, so, fq, fo, iq1, io1, tq, to, iq2, io2, xq, xo,
    l_sem, sfar, rfar, s1f, r1f, s2f, r2f, sag, rag, skv, rkv,
    sd, rd, sfa, rfa, s1, r1, s2, r2, sx, rx, sf, rf,
):
    y, z, chip, core = place()
    a, b, block = shape_of(y, z, core)
    _, _, block_there = shape_of(y, z, 1 - core)
    me = chip * 2 + core
    rows = gn_ref.shape[0]
    q_rows, width = oq_ref.shape
    keep = normed_ref.shape[1] // 16
    o_rows = oo_ref.shape[0]
    q_half, o_half = width // 2, o_rows // 2
    chips = xq.shape[0]
    members = 2 * chips
    reach = kv_in.shape[0]
    scale = HD ** (-0.5)
    f32, bf = jnp.float32, jnp.bfloat16
    partner = {"ctx": chip * 2 + 1 - core}

    def first_peer(k):
        return {"fsdp": block(lax.rem(a + k, 4), b)}

    def second_peer(k):
        return {"fsdp": block(a, lax.rem(b + k, 4))}

    def chip_peer(k):
        return {"ctx": lax.rem(chip + k, chips) * 2 + core}

    def member(k):
        return {"ctx": lax.rem(me + k, members)}

    def q_cols(half):
        return pl.ds(pl.multiple_of(half * q_half, 128), q_half)

    def o_lines(half):
        return pl.ds(pl.multiple_of(half * o_half, 16), o_half)

    def line(k):
        return lax.rem(a + k, 4)

    own_loads = [
        pltpu.make_async_copy(gff.at[block(a, j)], own_ff.at[j], l_sem.at[j]) for j in range(4)
    ] + [
        pltpu.make_async_copy(
            gff.at[block(line(1 if j < 2 else 3), j)], far_own.at[j], l_sem.at[4 + j]
        )
        for j in range(4)
    ]
    weight_loads = [
        pltpu.make_async_copy(wo_hbm, wo_ref, l_sem.at[8]),
        pltpu.make_async_copy(qkv_hbm, qkv_ref, l_sem.at[9]),
    ]
    for copy in own_loads + weight_loads:
        copy.start()
    greet(
        [first_peer(k) for k in (1, 2, 3)]
        + [second_peer(k) for k in (1, 2, 3)]
        + [member(k) for k in range(1, members)]
    )

    def ff_far(j):
        k = 1 if j < 2 else 3
        return remote(
            gff.at[block(line(2), j)], far_in.at[j], sfar.at[j], rfar.at[j], first_peer(k)
        )

    def ff_near(k, j):
        side = 0 if k == 1 else 1
        direct = (j >= 2) == (k == 1)
        src = gff.at[block(line(k), j)] if direct else far_own.at[j]
        return remote(src, in1_ff.at[side, j], s1f.at[side, j], r1f.at[side, j], first_peer(k))

    for j in (0, 2, 1, 3):
        ff_far(j).start()
    for k, j in ((1, 2), (3, 0), (1, 3), (3, 1)):
        ff_near(k, j).start()

    def pass_far(js):
        for j in js:
            ff_far(j).wait_recv()
            own_loads[4 + j].wait()
            far_own[j] = (far_own[j].astype(f32) + far_in[j].astype(f32)).astype(bf)
            ff_near(1 if j < 2 else 3, j).start()

    for copy in loads + weight_loads[:1]:
        copy.wait()

    grad_final = cot_ref[...].astype(f32)
    part, gain_two = rms_back(mid_ref[...], gn_ref[...], gains_ref[2:3, :])
    grad_mid = grad_final + part
    gmid[...] = grad_mid
    grad_attn, gain_one = rms_back(attn_ref[...], grad_mid, gains_ref[1:2, :])
    grad_attn_low = grad_attn.astype(bf)
    grad_attended = dot32(grad_attn_low, wo_ref[...], NT).astype(bf)

    def out_tile(t, carry):
        cols = pl.ds(pl.multiple_of(t * 256, 256), 256)
        go[pl.ds(t * 4, 4)] = (
            dot32(att_ref[:, cols], grad_attn_low, TN).reshape(4, 64, D).astype(bf)
        )
        return carry

    lax.fori_loop(0, NH * HD // 256, out_tile, 0)

    def away(i, t):
        k, j = lax.rem(i // 4 + 2, 4), lax.rem(i, 4)
        there = lax.rem(b + k, 4)
        f = block_there(there, j)
        slot = there * 4 + j
        if t == 0:
            src, dst = stage.at[f, :, q_cols(1 - core)], dq.at[slot]
        else:
            src, dst = go.at[f, o_lines(1 - core), :], do.at[slot]
        return remote(src, dst, sd.at[i, t], rd.at[i, t], partner)

    def home(i, t):
        k, j = lax.rem(i // 4 + 2, 4), lax.rem(i, 4)
        slot = lax.rem(a + k, 4) * 4 + j
        dst = (dq, do)[t].at[slot]
        return remote(dst, dst, sd.at[i, t], rd.at[i, t], partner)

    def start_away(t):
        def one(i, carry):
            away(i, t).start()
            return carry

        lax.fori_loop(0, 16, one, 0)

    start_away(1)

    keys, vals = pair_ref[:, :HD], pair_ref[:, HD:]
    queries = stack_heads(q_ref[...])
    grad_heads = stack_heads(grad_attended)
    scores = dot32(queries, keys, NT) * scale + jnp.concatenate([bias_ref[...]] * NH, axis=0)
    expo = jnp.exp(scores - jnp.max(scores, axis=-1, keepdims=True))
    probs = expo * (1.0 / jnp.sum(expo, axis=-1, keepdims=True))
    grad_probs = dot32(grad_heads, vals, NT)
    row_total = jnp.sum(probs * grad_probs, axis=-1, keepdims=True)
    grad_scores = (probs * (grad_probs - row_total)).astype(bf)
    gpair[:, HD:] = dot32(probs.astype(bf), grad_heads, TN)
    gpair[:, :HD] = dot32(grad_scores, queries, TN) * scale

    def kv_send(d):
        return remote(
            kv_snd.at[d - 1], kv_in.at[d - 1], skv.at[d - 1], rkv.at[d - 1], member(members - d)
        )

    for d in range(1, reach + 1):
        kv_snd[d - 1] = gpair[pl.ds((reach - d) * rows, rows), :].astype(bf)
        kv_send(d).start()

    pass_far((0, 2))
    cos_table, sin_table = turn_ref[:, : HD // 2], turn_ref[:, HD // 2 :]
    cos_all = jnp.concatenate([cos_table] * NH, axis=0)
    sin_all = jnp.concatenate([sin_table] * NH, axis=0)
    grad_queries = dot32(grad_scores, keys, NN) * scale
    grad_q, qk_gain_q = rms_back(
        stack_heads(proj_ref[:, : NH * HD]),
        turn_back(grad_queries, cos_all, sin_all),
        qk_ref[0:1, :],
    )
    for h in range(NH):
        gproj[:, h * HD : (h + 1) * HD] = grad_q[h * rows : (h + 1) * rows].astype(bf)

    def pair_of(k, h):
        return pl.ds(line(k) * 4 + 2 * h, 2)

    def sum_far(h, t):
        src, dst = ((sq, fq), (so, fo))[t]
        return remote(
            src.at[pair_of(2, h)], dst.at[pl.ds(2 * h, 2)],
            sfa.at[h, t], rfa.at[h, t], first_peer(3 if h else 1),
        )

    def sum_near(k, h, t):
        src, dst = ((sq, iq1), (so, io1))[t]
        side = 0 if k == 1 else 1
        return remote(
            src.at[pair_of(k, h)], dst.at[side, pl.ds(2 * h, 2)],
            s1.at[side, h, t], r1.at[side, h, t], first_peer(k),
        )

    def fold_cores(t):
        for k in (2, 3, 1, 0):
            def add(j, carry, k=k):
                slot = line(k) * 4 + j
                f = block(line(k), j)
                home((k + 2) % 4 * 4 + j, t).wait_recv()
                if t == 0:
                    sq[slot] = (
                        stage[f, :, q_cols(core)].astype(f32) + dq[slot].astype(f32)
                    ).astype(bf)
                else:
                    so[slot] = (
                        go[f, o_lines(core), :].astype(f32) + do[slot].astype(f32)
                    ).astype(bf)
                return carry

            lax.fori_loop(0, 4, add, 0)
            if k == 2:
                sum_far(0, t).start()
                sum_far(1, t).start()
            elif k:
                sum_near(k, 0 if k == 3 else 1, t).start()

    def fold_far(t):
        acc, far = ((sq, fq), (so, fo))[t]
        for h, k in ((0, 1), (1, 3)):
            sum_far(h, t).wait_recv()
            acc[pair_of(k, h)] = (
                acc[pair_of(k, h)].astype(f32) + far[2 * h : 2 * h + 2].astype(f32)
            ).astype(bf)
            sum_near(k, h, t).start()

    pass_far((1, 3))

    total = gpair[pl.ds(reach * rows, rows), :]
    for d in range(1, reach + 1):
        kv_send(d).wait_recv()
        total = total + kv_in[d - 1].astype(f32)
    grad_k, qk_gain_k = rms_back(
        proj_ref[:, NH * HD : NH * HD + HD],
        turn_back(total[:, :HD], cos_table, sin_table),
        qk_ref[1:2, :],
    )
    gproj[:, NH * HD : NH * HD + HD] = grad_k.astype(bf)
    gproj[:, NH * HD + HD :] = total[:, HD:].astype(bf)
    for copy in weight_loads[1:]:
        copy.wait()
    stream = tok_ref[...].astype(f32)
    grad_in, gain_zero = rms_back(stream, dot32(gproj[...], qkv_ref[...], NT), gains_ref[0:1, :])
    gt_ref[...] = gmid[...] + grad_in
    tail[...] = jnp.zeros_like(tail)
    for i, total_gain in enumerate((gain_zero, gain_one, gain_two, g3_ref[...])):
        tail[i : i + 1, :D] = total_gain
    tail[4:5, :HD] = qk_gain_q
    tail[5:6, :HD] = qk_gain_k

    def qkv_tile(t, carry):
        cols = pl.ds(pl.multiple_of(t * 256, 256), 256)
        res = dot32(normed_ref[...], gproj[:, cols], TN)
        low = tail[:, cols]
        for f in range(16):
            stage[f, :, cols] = jnp.concatenate(
                [res[f * keep : (f + 1) * keep], low], axis=0
            ).astype(bf)
        return carry

    lax.fori_loop(0, width // 256, qkv_tile, 0)
    start_away(0)

    for copy in own_loads[:4]:
        copy.wait()

    def ff_two(k):
        return remote(
            t_ff.at[lax.rem(b + k, 4)], in2_ff.at[3 - k], s2f.at[k], r2f.at[4 - k], second_peer(k)
        )

    for k in (2, 1, 3, 0):
        j = lax.rem(b + k, 4)
        for m in (0, 1):
            dst = in1_ff.at[m, j]
            remote(dst, dst, s1f.at[m, j], r1f.at[m, j], partner).wait_recv()
        total = own_ff[j].astype(f32)
        for m in (0, 1):
            total = total + in1_ff[m, j].astype(f32)
        t_ff[j] = total.astype(bf)
        if k:
            ff_two(k).start()

    fold_cores(1)
    fold_cores(0)
    fold_far(1)
    fold_far(0)

    def hop_two(k, t):
        src, dst = ((tq, iq2), (to, io2))[t]
        return remote(
            src.at[lax.rem(b + k, 4)], dst.at[3 - k], s2.at[k, t], r2.at[4 - k, t], second_peer(k)
        )

    for k in (1, 3, 2):
        ff_two(4 - k).wait_recv()
    total = t_ff[b].astype(f32)
    for m in range(3):
        total = total + in2_ff[m].astype(f32)
    all_ff[me] = total.astype(bf)

    half = all_ff.shape[1] // 2

    def ff_slot(k, there=0):
        return lax.rem(chip + k, chips) * 2 + (1 - core if there else core)

    def ff_all(k):
        peer = chip_peer(k) if k else partner
        return remote(
            all_ff.at[me], all_ff.at[me], sag.at[k], rag.at[(chips - k) % chips], peer
        )

    def ff_from(k):
        dst = all_ff.at[ff_slot(k)]
        return remote(dst, dst, sag.at[k], rag.at[k], partner)

    def ff_half(k, h, there=0):
        return all_ff.at[ff_slot(k, there), pl.ds(h * half, half), :]

    def ff_on(k):
        h = 0 if k == 3 else 1
        dst = ff_half(k, h)
        return remote(dst, dst, sag.at[8 + h], rag.at[8 + h], chip_peer(4 - k))

    def ff_far_got(h):
        dst = ff_half(2, h)
        return remote(dst, dst, sag.at[8 + h], rag.at[8 + h], partner)

    def ff_cross(k, h=None, there=0):
        if h is None:
            dst, i = all_ff.at[ff_slot(k, there)], 4 + k
        else:
            dst, i = ff_half(2, h, there), 10 + h
        return remote(dst, dst, sag.at[i], rag.at[i], partner)

    for k in (1, 3, 0):
        ff_all(k).start()

    for t in (1, 0):
        own, got, dst = ((sq, iq1, tq), (so, io1, to))[t]
        for k in (1, 3):
            for h in (0, 1):
                sum_near(k, h, t).wait_recv()
        for k in (2, 1, 3, 0):
            j = lax.rem(b + k, 4)
            total = own[a * 4 + j].astype(f32)
            for m in (0, 1):
                total = total + got[m, j].astype(f32)
            dst[j] = total.astype(bf)
            if k:
                hop_two(k, t).start()

    for k in (1, 3):
        ff_from(k).wait_recv()
        ff_on(k).start()
        ff_cross(k).start()

    def hop_chip(k, t):
        buf = (xq, xo)[t]
        return remote(
            buf.at[chip], buf.at[chip], sx.at[k, t], rx.at[chips - k, t], chip_peer(k)
        )

    for t in (1, 0):
        own, got, dst = ((tq, iq2, xq), (to, io2, xo))[t]
        for k in (1, 3, 2):
            hop_two(4 - k, t).wait_recv()
        total = own[b].astype(f32)
        for m in range(3):
            total = total + got[m].astype(f32)
        dst[chip] = total.astype(bf)
        for k in range(1, chips):
            hop_chip(k, t).start()

    def last(t, half):
        part = (oq_ref.at[:, q_cols(half)], oo_ref.at[o_lines(half), :])[t]
        return remote(part, part, sf.at[t], rf.at[t], partner)

    for h in (0, 1):
        ff_far_got(h).wait_recv()
        ff_cross(2, h).start()

    for t in (1, 0):
        buf = (xq, xo)[t]
        for k in range(1, chips):
            dst = buf.at[lax.rem(chip + k, chips)]
            remote(dst, dst, sx.at[k, t], rx.at[k, t], partner).wait_recv()
        total = buf[0].astype(f32)
        for m in range(1, chips):
            total = total + buf[m].astype(f32)
        if t == 0:
            oq_ref[:, q_cols(core)] = total
        else:
            oo_ref[o_lines(core), :] = total
        last(t, core).start()

    everywhere = all_ff.at[ff_slot(0, 1)]
    remote(everywhere, everywhere, sag.at[0], rag.at[0], partner).wait_recv()
    for k in (1, 3):
        ff_cross(k, there=1).wait_recv()
    for h in (0, 1):
        ff_cross(2, h, there=1).wait_recv()

    def end_away(i, carry):
        for t in (0, 1):
            away(i, t).wait_send()
        return carry

    lax.fori_loop(0, 16, end_away, 0)
    for j in range(4):
        ff_far(j).wait_send()
        ff_near(1, j).wait_send()
        ff_near(3, j).wait_send()
    for k in (1, 2, 3):
        ff_two(k).wait_send()
    for d in range(1, reach + 1):
        kv_send(d).wait_send()
    for k in (1, 3, 0):
        ff_all(k).wait_send()
    for k in (1, 3):
        ff_on(k).wait_send()
        ff_cross(k).wait_send()
    for h in (0, 1):
        ff_cross(2, h).wait_send()
    for t in (0, 1):
        for h in (0, 1):
            sum_far(h, t).wait_send()
            sum_near(1, h, t).wait_send()
            sum_near(3, h, t).wait_send()
        for k in (1, 2, 3):
            hop_two(k, t).wait_send()
        for k in range(1, chips):
            hop_chip(k, t).wait_send()
        last(t, core).wait_send()
        last(t, 1 - core).wait_recv()
    oq_out[...] = oq_ref[:keep, :]
    tail_out[...] = oq_ref[keep:, :]


def backward_rest(gff, values, weights, keep):
    f32, bf = jnp.float32, jnp.bfloat16
    vm = pl.BlockSpec(memory_space=pltpu.VMEM)
    hbm = pl.BlockSpec(memory_space=pl.ANY)
    dma = pltpu.SemaphoreType.DMA
    rows = values[0].shape[0]
    owners, ff_rows = gff.shape[:2]
    q_rows, width = keep + 8, (NH + 2) * HD
    o_rows, o_width = NH * HD // owners, D
    q_half, o_half = width // 2, o_rows // 2
    chips = lax.axis_size("ctx") // 2
    pairs = values[9].shape[0]
    reach = pairs // rows - 1

    def two(*lead):
        return [pltpu.VMEM(lead + (q_rows, q_half), bf), pltpu.VMEM(lead + (o_half, o_width), bf)]

    def ff(*lead):
        return pltpu.VMEM(lead + (ff_rows, D), bf)

    return pl.pallas_call(
        functools.partial(back_entry, len(values)),
        out_shape=(
            jax.ShapeDtypeStruct((rows, D), f32),
            jax.ShapeDtypeStruct((keep, width), f32),
            jax.ShapeDtypeStruct((8, width), f32),
            jax.ShapeDtypeStruct((o_rows, o_width), f32),
            jax.ShapeDtypeStruct((2 * chips, ff_rows, D), bf),
        ),
        in_specs=[hbm] * (3 + len(values)),
        out_specs=(vm,) * 5,
        scratch_shapes=[
            *(pltpu.VMEM(v.shape, v.dtype) for v in values),
            dma((len(values),)),
            pltpu.VMEM((16 * keep, width), bf),
            pltpu.VMEM((16 * o_rows, o_width), bf),
            pltpu.VMEM((q_rows, width), f32),
            ff(4), ff(4), ff(4), ff(2, 4), ff(4), ff(3),
            pltpu.VMEM((reach, rows, 2 * HD), bf),
            pltpu.VMEM((reach, rows, 2 * HD), bf),
            pltpu.VMEM((rows, D), f32),
            pltpu.VMEM((pairs, 2 * HD), f32),
            pltpu.VMEM((rows, width), bf),
            pltpu.VMEM((8, width), f32),
            pltpu.VMEM((16, q_rows, width), bf),
            pltpu.VMEM((16, o_rows, o_width), bf),
            *two(16), *two(16), *two(4), *two(2, 4), *two(4), *two(3), *two(chips),
            dma((10,)),
            dma((4,)), dma((4,)),
            dma((2, 4)), dma((2, 4)),
            dma((4,)), dma((4,)),
            dma((12,)), dma((12,)),
            dma((reach,)), dma((reach,)),
            dma((16, 2)), dma((16, 2)),
            dma((2, 2)), dma((2, 2)),
            dma((2, 2, 2)), dma((2, 2, 2)),
            dma((4, 2)), dma((4, 2)),
            dma((4, 2)), dma((4, 2)),
            dma((2,)), dma((2,)),
        ],
        compiler_params=pltpu.CompilerParams(
            collective_id=3, has_side_effects=True, vmem_limit_bytes=62 * 1024 * 1024
        ),
        cost_estimate=pl.CostEstimate(
            flops=12 * rows * width * D, bytes_accessed=64 * ff_rows * D, transcendentals=0
        ),
    )(gff, *values, *weights)


def finish_kernel(*refs):
    count = (len(refs) - 7) // 2
    all_ref, tail_ref, sources = refs[0], refs[1], refs[2 : 2 + count]
    weights, gains, qk = refs[2 + count : 5 + count], refs[5 + count], refs[6 + count]
    for src, dst in zip(sources, refs[7 + count :]):
        dst[...] = src[...]
    owner = lax.axis_index("fsdp")
    width = tail_ref.shape[1]
    for first, dst in ((0, gains), (4, qk)):
        lines, own = dst.shape
        shift = lax.rem(width - owner * own, width)
        dst[...] = pltpu.roll(tail_ref[...], shift, 1)[first : first + lines, :own]
    members = all_ref.shape[0]
    share = all_ref.shape[1] // 3
    lines = weights[0].shape[0] // members
    for i, dst in enumerate(weights):
        for m in range(members):
            dst[m * lines : (m + 1) * lines, :] = all_ref[
                m, i * share : (i + 1) * share, :
            ].astype(jnp.float32)[:lines]


def finish(all_ff, tail, lines, gain_lines, qk_lines, *rest):
    vm = pl.BlockSpec(memory_space=pltpu.VMEM)
    f32 = jnp.float32
    results = ((lines, D),) * 3 + (gain_lines, qk_lines)
    return pl.pallas_call(
        finish_kernel,
        out_shape=tuple(jax.ShapeDtypeStruct(s, f32) for s in results)
        + tuple(jax.ShapeDtypeStruct(r.shape, r.dtype) for r in rest),
        in_specs=[vm] * (2 + len(rest)),
        out_specs=(vm,) * (5 + len(rest)),
        compiler_params=pltpu.CompilerParams(vmem_limit_bytes=62 * 1024 * 1024),
    )(all_ff, tail, *rest)


def on_device(
    tokens,
    norm_gains,
    qk_gains,
    qkv_weight,
    out_weight,
    gate_weight,
    up_weight,
    down_weight,
    segments,
    cotangent,
):
    local_len = tokens.shape[1]
    ctx_index = lax.axis_index("ctx")
    ctx_size = lax.axis_size("ctx")
    own_rows = gate_weight.shape[0]
    slice_rows = own_rows // ctx_size
    padded = -(-slice_rows // 16) * 16
    keep = qkv_weight.shape[0]
    gain_lines, qk_lines = norm_gains.shape, qk_gains.shape
    def my_slice(weight):
        part = lax.dynamic_slice(weight, (ctx_index * slice_rows, 0), (slice_rows, D))
        return jnp.pad(part, ((0, padded - slice_rows), (0, 0)))

    ffn_shard = jnp.concatenate(
        [my_slice(gate_weight), my_slice(up_weight), my_slice(down_weight)], axis=0
    )
    places = np.arange(ctx_size * local_len, dtype=np.float32)
    rates = (ROPE_BASE ** (-(2.0 * np.arange(HD // 2)) / HD)).astype(np.float32)
    angles = (places[:, None] * rates).astype(np.float64)
    table = jnp.asarray(
        np.concatenate([np.cos(angles), np.sin(angles)], axis=1)
        .astype(np.float32)
        .reshape(ctx_size, local_len, HD)
    )
    flat = tokens.reshape(local_len, D)
    cot = cotangent.reshape(local_len, D)
    (
        qkv_full, out_full, ffn_full, gains_all, qk_all, normed, projected, queries, pair_all,
        attended, attn, mid, normed_two, bias, turn_table,
    ) = front(
        qkv_weight,
        norm_gains,
        qk_gains,
        out_weight,
        ffn_shard,
        flat,
        segments,
        table,
    )
    output, grad_normed_two, grad_gain_three, ffn_grads = ffn(
        normed_two, mid, cot, gains_all, ffn_full
    )
    grad_tokens, total_qkv, tail, total_out, all_ff = backward_rest(
        ffn_grads,
        (
            grad_normed_two, mid, attn, cot, flat, gains_all, qk_all, projected, queries,
            pair_all, attended, normed, turn_table, bias, grad_gain_three,
        ),
        (qkv_full, out_full),
        keep,
    )
    (
        total_gate, total_up, total_down, total_gains, total_qk,
        grad_tokens, total_qkv, total_out, output,
    ) = finish(
        all_ff, tail, own_rows, gain_lines, qk_lines, grad_tokens, total_qkv, total_out, output
    )
    return (
        output.reshape(tokens.shape),
        grad_tokens.reshape(tokens.shape),
        total_gains,
        total_qk,
        total_qkv,
        total_out,
        total_gate,
        total_up,
        total_down,
    )


def solution(mesh):
    in_specs = (
        P("fsdp", "ctx", None),
        P(None, "fsdp"),
        P(None, "fsdp"),
        P("fsdp", None),
        P("fsdp", None),
        P("fsdp", None),
        P("fsdp", None),
        P("fsdp", None),
        P("fsdp", "ctx"),
        P("fsdp", "ctx", None),
    )
    out_specs = (
        P("fsdp", "ctx", None),
        P("fsdp", "ctx", None),
        P(None, "fsdp"),
        P(None, "fsdp"),
        P("fsdp", None),
        P("fsdp", None),
        P("fsdp", None),
        P("fsdp", None),
        P("fsdp", None),
    )
    return jax.shard_map(
        on_device, mesh=mesh, in_specs=in_specs, out_specs=out_specs, check_vma=False
    )
```

```python
import functools

import jax
import numpy as np
import jax.numpy as jnp
from jax import lax
from jax.experimental import pallas as pl
from jax.experimental.pallas import tpu as pltpu
from jax.sharding import PartitionSpec as P

D = 1152
NH = 4
HD = 256
WINDOW = 512


EPS = 1e-06
ROPE_BASE = 10000.0
NEG_FILL = -1e30


def rms_norm(values, gain_vec):
    return values * lax.rsqrt(jnp.mean(values * values, axis=-1, keepdims=True) + EPS) * gain_vec


MESH = pl.DeviceIdType.MESH
NT = (((1,), (1,)), ((), ()))
NN = (((1,), (0,)), ((), ()))
TN = (((0,), (0,)), ((), ()))
GELU_C = 0.7978845608028654
GELU_A = 0.044715


def dot32(left, right, dims):
    return lax.dot_general(left, right, dims, preferred_element_type=jnp.float32)


def ffn_kernel(
    normed_ref, mid_ref, cot_ref, gain_ref, w_hbm,
    out_ref, gn_ref, ggain_ref, gff_hbm,
    wg, wu, wd, seq, gseq, act_a, act_b, hid, dgate, dup, part, keep, base,
    d2d_snd, d2d_in, ici_snd, ici_in, dw,
    w_sem, o_sem, ag_s, ag_r, rd_s, rd_r, ri_s, ri_r,
):
    rows = normed_ref.shape[0]
    units = wg.shape[0]
    share = units // w_hbm.shape[0]
    tile = 256
    me = lax.axis_index("ctx")
    chip, core = me // 2, lax.rem(me, 2)
    partner = {"ctx": chip * 2 + 1 - core}
    chips = {k: {"ctx": lax.rem(chip + k, 4) * 2 + core} for k in (1, 2, 3)}
    order = (0, 1, 3, 2)

    loads = [
        pltpu.make_async_copy(
            w_hbm.at[f, pl.ds(i * share, share), :], dst.at[pl.ds(f * share, share), :], w_sem.at[i, f]
        )
        for i, dst in enumerate((wg, wu, wd))
        for f in range(w_hbm.shape[0])
    ]
    for load in loads:
        load.start()

    barrier = pltpu.get_barrier_semaphore()
    for peer in (partner, chips[1], chips[2], chips[3]):
        pl.semaphore_signal(barrier, inc=1, device_id=peer, device_id_type=MESH)
    pl.semaphore_wait(barrier, 4)

    started = []

    def send(src, dst, s_sem, r_sem, peer):
        copy = pltpu.make_async_remote_copy(
            src_ref=src, dst_ref=dst, send_sem=s_sem, recv_sem=r_sem,
            device_id=peer, device_id_type=MESH,
        )
        copy.start()
        started.append(copy)
        return copy

    def mine(k):
        return pl.ds(k * 2 * rows, rows)

    def other(k):
        return pl.ds(k * 2 * rows + rows, rows)

    def pair(k):
        return pl.ds(k * 2 * rows, 2 * rows)

    def spread(buf, ph):
        own = buf.at[mine(0)]
        got = {}
        for k in (1, 3):
            back = 4 - k
            got[back] = send(own, buf.at[mine(back)], ag_s.at[ph, k], ag_r.at[ph, back], chips[k])
        got[0] = send(own, buf.at[other(0)], ag_s.at[ph, 0], ag_r.at[ph, 0], partner)
        return got

    def half_of(k, h, offset=0):
        return pl.ds(k * 2 * rows + offset + h * (rows // 2), rows // 2)

    def relay(buf, ph, got, k):
        got[k].wait_recv()
        h = 0 if k == 3 else 1
        got[2, h] = send(
            buf.at[half_of(k, h)], buf.at[half_of(2, h)],
            ag_s.at[ph, 2 + 2 * h], ag_r.at[ph, 2 + 2 * h], chips[4 - k],
        )
        got[k] = send(
            buf.at[mine(k)], buf.at[other(k)], ag_s.at[ph, 4 + k], ag_r.at[ph, 4 + k], partner
        )

    def relay_far(buf, ph, got):
        for h in (0, 1):
            got[2, h].wait_recv()
            got[2, h] = send(
                buf.at[half_of(2, h)], buf.at[half_of(2, h, rows)],
                ag_s.at[ph, 6 + 2 * h], ag_r.at[ph, 6 + 2 * h], partner,
            )

    def swap(ph, k):
        d2d_snd[ph, k] = part[pl.ds(rows, rows), :].astype(jnp.bfloat16)
        keep[order.index(k) % 2] = part[pl.ds(0, rows), :]
        return send(d2d_snd.at[ph, k], d2d_in.at[ph, k], rd_s.at[ph, k], rd_r.at[ph, k], partner)

    def sum_out(ph, k, copy):
        copy.wait_recv()
        total = keep[order.index(k) % 2] + d2d_in[ph, k].astype(jnp.float32)
        if k == 0:
            base[...] = total
            return None
        ici_snd[ph, k - 1] = total.astype(jnp.bfloat16)
        back = 4 - k
        return send(
            ici_snd.at[ph, k - 1], ici_in.at[ph, back - 1], ri_s.at[ph, k], ri_r.at[ph, back],
            chips[k],
        )

    def phase(buf, ph, work):
        got = spread(buf, ph)
        if ph == 0:
            for load in loads:
                load.wait()
        sums = {}
        copy = waiting = None
        for k in order:
            if k == 1:
                relay(buf, ph, got, 1)
                relay(buf, ph, got, 3)
            if k == 2:
                relay_far(buf, ph, got)
                got[2, 0].wait_recv()
                got[2, 1].wait_recv()
            else:
                got[k].wait_recv()
            if waiting is not None and k == 2:
                sums[waiting] = sum_out(ph, waiting, copy)
                waiting = None
            work(k)
            if waiting is not None:
                sums[waiting] = sum_out(ph, waiting, copy)
            copy, waiting = swap(ph, k), k
        sums[waiting] = sum_out(ph, waiting, copy)
        return sums

    def collect(ph, sums):
        total = base[...]
        for k in (1, 3, 2):
            sums[k].wait_recv()
        for k in (1, 2, 3):
            total = total + ici_in[ph, k - 1].astype(jnp.float32)
        return total

    def forward(k):
        def one(t, carry):
            cols = pl.ds(pl.multiple_of(t * tile, tile), tile)
            block = seq[pair(k), :]
            gate = dot32(block, wg[cols, :], NT)
            up = dot32(block, wu[cols, :], NT)
            square = gate * gate
            th = jnp.tanh(GELU_C * gate * (1.0 + GELU_A * square))
            half = 0.5 * (1.0 + th)
            gelu = gate * half
            slope = half + (0.5 * GELU_C) * gate * (1.0 - th * th) * (1.0 + 3.0 * GELU_A * square)
            hid[pair(k), cols] = (gelu * up).astype(jnp.bfloat16)
            act_a[pair(k), cols] = up * slope
            act_b[pair(k), cols] = gelu
            return carry

        lax.fori_loop(0, units // tile, one, 0)
        part[...] = dot32(hid[pair(k), :], wd[...], NN)

    seq[mine(0), :] = normed_ref[...]
    sums = phase(seq, 0, forward)
    mlp = collect(0, sums)
    r = lax.rsqrt(jnp.mean(mlp * mlp, axis=-1, keepdims=True) + EPS)
    n = mlp * r
    gain = gain_ref[3:4, :]
    out_ref[...] = (mid_ref[...] + n * gain).astype(jnp.bfloat16)
    dy = cot_ref[...].astype(jnp.float32)
    ggain_ref[...] = jnp.sum(dy * n, axis=0, keepdims=True)
    dyg = dy * gain
    dv = r * (dyg - n * jnp.mean(dyg * n, axis=-1, keepdims=True))
    gseq[mine(0), :] = dv.astype(jnp.bfloat16)

    def backward(k):
        def one(t, carry):
            cols = pl.ds(pl.multiple_of(t * tile, tile), tile)
            gh = dot32(gseq[pair(k), :], wd[cols, :], NT)
            dgate[pair(k), cols] = (gh * act_a[pair(k), cols]).astype(jnp.bfloat16)
            dup[pair(k), cols] = (gh * act_b[pair(k), cols]).astype(jnp.bfloat16)
            return carry

        lax.fori_loop(0, units // tile, one, 0)
        part[...] = dot32(dgate[pair(k), :], wg[...], NN) + dot32(dup[pair(k), :], wu[...], NN)

    sums = phase(gseq, 1, backward)
    stores = []
    for i, (left, right) in enumerate(((dgate, seq), (dup, seq), (hid, gseq))):
        def one(t, carry, i=i, left=left, right=right):
            cols = pl.ds(pl.multiple_of(t * tile, tile), tile)
            group = tile // share
            dw[pl.ds(t * group, group), pl.ds(i * share, share), :] = (
                dot32(left[:, cols], right[...], TN).reshape(group, share, -1).astype(jnp.bfloat16)
            )
            return carry

        lax.fori_loop(0, units // tile, one, 0)
        third = pl.ds(i * share, share)
        stores.append(
            pltpu.make_async_copy(dw.at[:, third, :], gff_hbm.at[:, third, :], o_sem.at[i])
        )
        stores[-1].start()
    gn_ref[...] = collect(1, sums)
    for copy in started:
        copy.wait_send()
    for store in stores:
        store.wait()


def ffn(normed_two, mid, cot, gain, weights):
    rows = normed_two.shape[0]
    owners, lines = weights.shape[:2]
    units = owners * lines // 3
    seq_rows = rows * 8
    bf, f32 = jnp.bfloat16, jnp.float32
    vm = pl.BlockSpec(memory_space=pltpu.VMEM)
    hbm = pl.BlockSpec(memory_space=pl.ANY)
    dma = pltpu.SemaphoreType.DMA
    return pl.pallas_call(
        ffn_kernel,
        out_shape=(
            jax.ShapeDtypeStruct((rows, D), bf),
            jax.ShapeDtypeStruct((rows, D), f32),
            jax.ShapeDtypeStruct((1, D), f32),
            jax.ShapeDtypeStruct(weights.shape, bf),
        ),
        in_specs=[vm] * 4 + [hbm],
        out_specs=(vm, vm, vm, hbm),
        scratch_shapes=[
            pltpu.VMEM((units, D), bf),
            pltpu.VMEM((units, D), bf),
            pltpu.VMEM((units, D), bf),
            pltpu.VMEM((seq_rows, D), bf),
            pltpu.VMEM((seq_rows, D), bf),
            pltpu.VMEM((seq_rows, units), f32),
            pltpu.VMEM((seq_rows, units), f32),
            pltpu.VMEM((seq_rows, units), bf),
            pltpu.VMEM((seq_rows, units), bf),
            pltpu.VMEM((seq_rows, units), bf),
            pltpu.VMEM((2 * rows, D), f32),
            pltpu.VMEM((2, rows, D), f32),
            pltpu.VMEM((rows, D), f32),
            pltpu.VMEM((2, 4, rows, D), bf),
            pltpu.VMEM((2, 4, rows, D), bf),
            pltpu.VMEM((2, 3, rows, D), bf),
            pltpu.VMEM((2, 3, rows, D), bf),
            pltpu.VMEM(weights.shape, bf),
            dma((3, owners)), dma((3,)),
            dma((2, 10)), dma((2, 10)),
            dma((2, 4)), dma((2, 4)),
            dma((2, 4)), dma((2, 4)),
        ],
        compiler_params=pltpu.CompilerParams(
            collective_id=1, has_side_effects=True, vmem_limit_bytes=62 * 1024 * 1024
        ),
        cost_estimate=pl.CostEstimate(
            flops=18 * seq_rows * units * D, bytes_accessed=14 * units * D, transcendentals=0
        ),
    )(normed_two, mid, cot, gain, weights)


def place():
    fsdp = lax.axis_index("fsdp")
    ctx = lax.axis_index("ctx")
    y, z = fsdp // 4, lax.rem(fsdp, 4)
    chip, core = ctx // 2, lax.rem(ctx, 2)
    return y, z, chip, core


def shape_of(y, z, core):
    first = (1 - core) * y + core * z
    second = (1 - core) * z + core * y

    def block(i, j):
        return (1 - core) * (4 * i + j) + core * (4 * j + i)

    return first, second, block


def remote(src, dst, s_sem, r_sem, peer):
    return pltpu.make_async_remote_copy(
        src_ref=src, dst_ref=dst, send_sem=s_sem, recv_sem=r_sem,
        device_id=peer, device_id_type=MESH,
    )


def greet(peers, meanwhile=None):
    barrier = pltpu.get_barrier_semaphore()
    for peer in peers:
        pl.semaphore_signal(barrier, inc=1, device_id=peer, device_id_type=MESH)
    if meanwhile is not None:
        meanwhile()
    pl.semaphore_wait(barrier, len(peers))


def rms_back(values, grad, gain):
    r = lax.rsqrt(jnp.mean(values * values, axis=-1, keepdims=True) + EPS)
    n = values * r
    dyg = grad * gain
    return (
        r * (dyg - n * jnp.mean(dyg * n, axis=-1, keepdims=True)),
        jnp.sum(grad * n, axis=0, keepdims=True),
    )


def stack_heads(values):
    return jnp.concatenate([values[:, h * HD : (h + 1) * HD] for h in range(NH)], axis=0)


def turn_back(grad, cos_table, sin_table):
    left, right = grad[:, : HD // 2], grad[:, HD // 2 :]
    return jnp.concatenate(
        [left * cos_table + right * sin_table, right * cos_table - left * sin_table], axis=1
    )


def front_kernel(
    qkv_own, gain_own, qk_own, wo_ref, gate_hbm, up_hbm, down_hbm, tok_ref, seg_line, table_ref,
    qkv_hbm, wo_hbm, ffn_all, gains_ref, qk_ref, normed_ref, proj_ref, q_ref, pair_ref, att_ref,
    attn_ref, mid_ref, low_ref, bias_ref, turn_ref,
    ffn_ref, window, win_sem, qkv_ref, placing, qkv_all, qkv_out, wo_all, seg_ref, seg_in,
    l_sem, s1, r1, s2, r2, sd, rd, s1f, r1f, s2f, r2f, skv, rkv, ssg, rsg,
):
    f32, bf = jnp.float32, jnp.bfloat16
    y, z, chip, core = place()
    a, b, block = shape_of(y, z, core)
    _, _, block_there = shape_of(y, z, 1 - core)
    q_rows, width = qkv_ref.shape
    o_rows = wo_ref.shape[0]
    q_half, o_half = width // 2, o_rows // 2
    partner = {"ctx": chip * 2 + 1 - core}
    me = chip * 2 + core
    rows = tok_ref.shape[0]
    reach = pair_ref.shape[0] // rows - 1
    members = 2 * (lax.axis_size("ctx") // 2)

    def member(k):
        return {"ctx": lax.rem(me + k, members)}

    seg_ref[...] = jnp.broadcast_to(seg_line[...], seg_ref.shape)

    def views(f, half):
        return (
            qkv_all.at[
                pl.ds(pl.multiple_of(f * q_rows, 16), q_rows),
                pl.ds(pl.multiple_of(half * q_half, 128), q_half),
            ],
            wo_all.at[pl.ds(pl.multiple_of(f * o_rows + half * o_half, 16), o_half), :],
        )

    mine = (
        qkv_ref.at[:, pl.ds(pl.multiple_of(core * q_half, 128), q_half)],
        wo_ref.at[pl.ds(pl.multiple_of(core * o_half, 16), o_half), :],
    )
    here = block(a, b)
    lines, tall = gate_hbm.shape[0] // members, window.shape[1]
    begin = lines * me // 16 * 16 - me // (members - 1) * 16
    skip = lines * me - begin
    windows = [
        pltpu.make_async_copy(
            src.at[pl.ds(pl.multiple_of(begin, 16), tall), :], window.at[i], win_sem.at[i]
        )
        for i, src in enumerate((gate_hbm, up_hbm, down_hbm))
    ]
    for copy in windows:
        copy.start()

    def stage_ffn():
        share = ffn_ref.shape[0] // 3
        inside = lax.broadcasted_iota(jnp.int32, (share, 1), 0) < lines
        for i, copy in enumerate(windows):
            copy.wait()
            moved = pltpu.roll(window[i].astype(f32), lax.rem(tall - skip, tall), 0)[:share]
            ffn_ref[i * share : (i + 1) * share, :] = jnp.where(inside, moved, 0.0).astype(bf)

    def stage_shard():
        owner = lax.axis_index("fsdp")
        placing[...] = jnp.zeros_like(placing)
        lines, own = gain_own.shape
        placing[:lines, :own] = gain_own[...].astype(f32)
        placed = pltpu.roll(placing[...], owner * own, 1)
        placing[...] = jnp.zeros_like(placing)
        more, own = qk_own.shape
        placing[lines : lines + more, :own] = qk_own[...].astype(f32)
        placed = placed + pltpu.roll(placing[...], owner * own, 1)
        qkv_ref[...] = jnp.concatenate([qkv_own[...].astype(f32), placed], axis=0).astype(bf)

    locals_ = [
        pltpu.make_async_copy(
            qkv_ref, qkv_all.at[pl.ds(pl.multiple_of(here * q_rows, 16), q_rows), :], l_sem.at[0]
        ),
        pltpu.make_async_copy(
            wo_ref, wo_all.at[pl.ds(pl.multiple_of(here * o_rows, 16), o_rows), :], l_sem.at[1]
        ),
        pltpu.make_async_copy(ffn_ref, ffn_all.at[here], l_sem.at[2]),
        pltpu.make_async_copy(table_ref.at[me], turn_ref, l_sem.at[3]),
    ]
    for copy in (locals_[1], locals_[3]):
        copy.start()

    def first_peer(k):
        return {"fsdp": block(lax.rem(a + k, 4), b)}

    def second_peer(k):
        return {"fsdp": block(a, lax.rem(b + k, 4))}

    greet(
        [first_peer(k) for k in (1, 2, 3)]
        + [second_peer(k) for k in (1, 2, 3)]
        + [member(k) for k in range(1, members)],
        stage_shard,
    )
    locals_[0].start()

    def seg_send(d):
        return remote(
            seg_ref, seg_in.at[reach - d], ssg.at[d - 1], rsg.at[d - 1], member(d)
        )

    def ffn_one(k):
        return remote(ffn_ref, ffn_all.at[here], s1f.at[k], r1f.at[4 - k], first_peer(k))

    def ffn_block(j, m):
        return ffn_all.at[block(lax.rem(a + j, 4), lax.rem(b + m, 4))]

    def ffn_two(j, k):
        dst = ffn_block(j, 0)
        src = dst if j else ffn_ref
        return remote(src, dst, s2f.at[j, k], r2f.at[j, 4 - k], second_peer(k))

    def ffn_pass(j):
        dst, k = (ffn_block(j, 3), 1) if j < 2 else (ffn_block(j, 1), 3)
        return remote(dst, dst, s2f.at[j, 2], r2f.at[j, 2], second_peer(k))

    def ffn_got(j, m):
        dst = ffn_block(j, m)
        sems = (s1f.at[j], r1f.at[j]) if m == 0 else (s2f.at[j, m], r2f.at[j, m])
        return remote(dst, dst, *sems, partner)

    def hop_one(k, t):
        return remote(mine[t], views(here, core)[t], s1.at[k, t], r1.at[4 - k, t], first_peer(k))

    def hop_two(j, k, t):
        f = block(lax.rem(a + j, 4), b)
        dst = views(f, core)[t]
        src = dst if j else mine[t]
        return remote(src, dst, s2.at[j, k, t], r2.at[j, 4 - k, t], second_peer(k))

    def arrive_one(j, t):
        dst = views(block(lax.rem(a + j, 4), b), core)[t]
        return remote(dst, dst, s1.at[j, t], r1.at[j, t], partner)

    def arrive_two(j, m, t):
        dst = views(block(lax.rem(a + j, 4), lax.rem(b + m, 4)), core)[t]
        return remote(dst, dst, s2.at[j, m, t], r2.at[j, m, t], partner)

    def cross(j, m, t):
        dst = views(block(lax.rem(a + j, 4), lax.rem(b + m, 4)), core)[t]
        return remote(dst, dst, sd.at[j, m, t], rd.at[j, m, t], partner)

    def arrive_cross(j, m, t):
        dst = views(block_there(lax.rem(b + j, 4), lax.rem(a + m, 4)), 1 - core)[t]
        return remote(dst, dst, sd.at[j, m, t], rd.at[j, m, t], partner)

    both = (0, 1)
    for k in (1, 3, 2):
        for t in both:
            hop_one(k, t).start()
    def hop_pass(j, t):
        m, k = (3, 1) if j < 2 else (1, 3)
        dst = views(block(lax.rem(a + j, 4), lax.rem(b + m, 4)), core)[t]
        return remote(dst, dst, s2.at[j, 2, t], r2.at[j, 2, t], second_peer(k))

    for k in (1, 3):
        for t in both:
            hop_two(0, k, t).start()
    stage_ffn()
    locals_[2].start()
    for j in (1, 3, 2):
        for t in both:
            arrive_one(j, t).wait_recv()
            for k in (1, 3):
                hop_two(j, k, t).start()
            cross(j, 0, t).start()

    for d in range(1, reach + 1):
        seg_send(d).start()
    for k in (1, 3, 2):
        ffn_one(k).start()
    for k in (1, 3):
        ffn_two(0, k).start()

    for j in (0, 1, 3, 2):
        for m in (3, 1) if j < 2 else (1, 3):
            for t in both:
                arrive_two(j, m, t).wait_recv()
                if m == (3 if j < 2 else 1):
                    hop_pass(j, t).start()
                cross(j, m, t).start()
    for j in (0, 1, 3, 2):
        for t in both:
            arrive_two(j, 2, t).wait_recv()
            cross(j, 2, t).start()

    def land(i, carry):
        m, j = i // 4, lax.rem(i, 4)
        for t in both:
            arrive_cross(j, m, t).wait_recv()
            cross(j, m, t).wait_send()
        return carry

    lax.fori_loop(1, 16, land, 0)
    for copy in locals_[:2]:
        copy.wait()
    for t in both:
        for k in (1, 2, 3):
            hop_one(k, t).wait_send()
        for j in range(4):
            hop_pass(j, t).wait_send()
            for k in (1, 3):
                hop_two(j, k, t).wait_send()
    saves = [
        pltpu.make_async_copy(qkv_out, qkv_hbm, l_sem.at[4]),
        pltpu.make_async_copy(wo_all, wo_hbm, l_sem.at[5]),
    ]
    saves[1].start()

    keep = qkv_out.shape[0] // 16
    extra = jnp.zeros((q_rows - keep, width), f32)
    for f in range(0, 16, 2):
        left = qkv_all[pl.ds(f * q_rows, q_rows), :].astype(f32)
        right = qkv_all[pl.ds((f + 1) * q_rows, q_rows), :].astype(f32)
        qkv_out[pl.ds(f * keep, 2 * keep), :] = jnp.concatenate(
            [left[:keep], right[:keep]], axis=0
        ).astype(bf)
        extra = extra + left[keep:] + right[keep:]
    saves[0].start()
    gains = extra[:4, :D]
    gains_ref[...] = gains
    qk_ref[...] = extra[4:6, :HD]

    stream = tok_ref[...].astype(f32)
    normed_ref[...] = rms_norm(stream, gains[0:1]).astype(bf)
    proj_ref[...] = dot32(normed_ref[...], qkv_out[...], NN)
    locals_[3].wait()
    cos_table, sin_table = turn_ref[:, : HD // 2], turn_ref[:, HD // 2 :]

    def turn(values, gain, cos_part, sin_part):
        values = rms_norm(values, gain)
        left, right = values[:, : HD // 2], values[:, HD // 2 :]
        return jnp.concatenate(
            [left * cos_part - right * sin_part, right * cos_part + left * sin_part], axis=1
        ).astype(bf)

    own = pl.ds(reach * rows, rows)
    pair_ref[own, :HD] = turn(
        proj_ref[:, NH * HD : NH * HD + HD], extra[5:6, :HD], cos_table, sin_table
    )
    pair_ref[own, HD:] = proj_ref[:, NH * HD + HD :].astype(bf)

    def kv_send(d):
        return remote(
            pair_ref.at[own],
            pair_ref.at[pl.ds((reach - d) * rows, rows)],
            skv.at[d - 1], rkv.at[d - 1], member(d),
        )

    for d in range(1, reach + 1):
        kv_send(d).start()
    for j in (1, 3, 2):
        ffn_got(j, 0).wait_recv()
        for k in (1, 3):
            ffn_two(j, k).start()
    queries = turn(
        stack_heads(proj_ref[:, : NH * HD]),
        extra[4:5, :HD],
        jnp.concatenate([cos_table] * NH, axis=0),
        jnp.concatenate([sin_table] * NH, axis=0),
    )
    for h in range(NH):
        q_ref[:, h * HD : (h + 1) * HD] = queries[h * rows : (h + 1) * rows]

    for d in range(1, reach + 1):
        seg_send(d).wait_recv()
    seg_in[reach] = seg_ref[...]
    key_seg = jnp.concatenate([seg_in[p][0:1, :] for p in range(reach + 1)], axis=1)
    shape = (rows, (reach + 1) * rows)
    spacing = (
        reach * rows + lax.broadcasted_iota(jnp.int32, shape, 0)
        - lax.broadcasted_iota(jnp.int32, shape, 1)
    )
    begun = lax.broadcasted_iota(jnp.int32, shape, 1) + (me - reach) * rows >= 0
    wide = jnp.broadcast_to(seg_line[...], (rows, rows)).astype(f32)
    query_seg = jnp.concatenate([wide.T] * (reach + 1), axis=1)
    allowed = (
        (spacing >= 0) & (spacing < WINDOW) & begun & (query_seg == key_seg.astype(f32))
    )
    bias_ref[...] = jnp.where(allowed, 0.0, NEG_FILL)
    def ffn_onward(j):
        ffn_got(j, 3 if j < 2 else 1).wait_recv()
        ffn_pass(j).start()

    ffn_onward(0)
    for d in range(1, reach + 1):
        kv_send(d).wait_recv()
    scores = dot32(queries, pair_ref[:, :HD], NT) * (HD ** (-0.5)) + jnp.concatenate(
        [bias_ref[...]] * NH, axis=0
    )
    expo = jnp.exp(scores - jnp.max(scores, axis=-1, keepdims=True))
    probs = expo * (1.0 / jnp.sum(expo, axis=-1, keepdims=True))
    heads = dot32(probs.astype(bf), pair_ref[:, HD:], NN).astype(bf)
    for h in range(NH):
        att_ref[:, h * HD : (h + 1) * HD] = heads[h * rows : (h + 1) * rows]
    ffn_onward(1)
    ffn_onward(3)
    attn = dot32(att_ref[...], wo_all[...], NN)
    attn_ref[...] = attn
    mid = stream + rms_norm(attn, gains[1:2])
    mid_ref[...] = mid
    low_ref[...] = rms_norm(mid, gains[2:3]).astype(bf)

    ffn_onward(2)
    for copy in saves + locals_[2:3]:
        copy.wait()
    for j in range(4):
        ffn_got(j, 1 if j < 2 else 3).wait_recv()
        ffn_got(j, 2).wait_recv()
    for j in range(4):
        ffn_pass(j).wait_send()
        for k in (1, 3):
            ffn_two(j, k).wait_send()
    for k in (1, 2, 3):
        ffn_one(k).wait_send()
    for d in range(1, reach + 1):
        seg_send(d).wait_send()
        kv_send(d).wait_send()


def front(qkv_own, gain_own, qk_own, wo_shard, ffn_own, padded, tokens, seg_line, table):
    f32, bf = jnp.float32, jnp.bfloat16
    vm = pl.BlockSpec(memory_space=pltpu.VMEM)
    hbm = pl.BlockSpec(memory_space=pl.ANY)
    dma = pltpu.SemaphoreType.DMA
    keep, width = qkv_own.shape
    q_rows = keep + 8
    o_rows, o_width = wo_shard.shape
    rows = tokens.shape[0]
    reach = min(-(-(WINDOW - 1) // rows), lax.axis_size("ctx") - 1)
    pairs = (reach + 1) * rows
    shapes = (
        ((16 * keep, width), bf),
        ((16 * o_rows, o_width), bf),
        ((16, 3 * padded, D), bf),
        ((4, D), f32),
        ((2, HD), f32),
        ((rows, D), bf),
        ((rows, width), f32),
        ((rows, NH * HD), bf),
        ((pairs, 2 * HD), bf),
        ((rows, NH * HD), bf),
        ((rows, D), f32),
        ((rows, D), f32),
        ((rows, D), bf),
        ((rows, pairs), f32),
        ((rows, HD), f32),
    )
    return pl.pallas_call(
        front_kernel,
        out_shape=tuple(jax.ShapeDtypeStruct(*s) for s in shapes),
        in_specs=[vm, vm, vm, vm, hbm, hbm, hbm, vm, vm, hbm],
        out_specs=(hbm,) * 3 + (vm,) * (len(shapes) - 3),
        scratch_shapes=[
            pltpu.VMEM((3 * padded, D), bf),
            pltpu.VMEM((3, padded + 16, D), bf),
            dma((3,)),
            pltpu.VMEM((q_rows, width), bf),
            pltpu.VMEM((8, width), f32),
            pltpu.VMEM((16 * q_rows, width), bf),
            pltpu.VMEM((16 * keep, width), bf),
            pltpu.VMEM((16 * o_rows, o_width), bf),
            pltpu.VMEM((8, rows), jnp.int32),
            pltpu.VMEM((reach + 1, 8, rows), jnp.int32),
            dma((6,)),
            dma((4, 2)), dma((4, 2)),
            dma((4, 4, 2)), dma((4, 4, 2)),
            dma((4, 4, 2)), dma((4, 4, 2)),
            dma((4,)), dma((4,)),
            dma((4, 4)), dma((4, 4)),
            dma((reach,)), dma((reach,)),
            dma((reach,)), dma((reach,)),
        ],
        compiler_params=pltpu.CompilerParams(
            collective_id=2, has_side_effects=True, vmem_limit_bytes=62 * 1024 * 1024
        ),
        cost_estimate=pl.CostEstimate(
            flops=6 * rows * width * D, bytes_accessed=64 * q_rows * width, transcendentals=0
        ),
    )(qkv_own, gain_own, qk_own, wo_shard, *ffn_own, tokens, seg_line, table)


def back_entry(count, gff, *refs):
    sources, refs = refs[:count], refs[count:]
    hbm_and_out, refs = refs[:7], refs[7:]
    held, v_sem, rest = refs[:count], refs[count], refs[count + 1 :]
    loads = [
        pltpu.make_async_copy(src, dst, v_sem.at[i]) for i, (src, dst) in enumerate(zip(sources, held))
    ]
    for load in loads:
        load.start()
    back_kernel(loads, gff, *held, *hbm_and_out, *rest)


def back_kernel(
    loads, gff, gn_ref, mid_ref, attn_ref, cot_ref, tok_ref, gains_ref, qk_ref, proj_ref, q_ref,
    pair_ref, att_ref, normed_ref, turn_ref, bias_ref, g3_ref, qkv_hbm, wo_hbm,
    gt_ref, oq_out, tail_out, oo_ref, all_ff,
    qkv_ref, wo_ref, oq_ref, own_ff, far_own, far_in, in1_ff, t_ff, in2_ff, kv_snd, kv_in, gmid, gpair, gproj, tail,
    stage, go, dq, do, sq, so, fq, fo, iq1, io1, tq, to, iq2, io2, xq, xo,
    l_sem, sfar, rfar, s1f, r1f, s2f, r2f, sag, rag, skv, rkv,
    sd, rd, sfa, rfa, s1, r1, s2, r2, sx, rx, sf, rf,
):
    y, z, chip, core = place()
    a, b, block = shape_of(y, z, core)
    _, _, block_there = shape_of(y, z, 1 - core)
    me = chip * 2 + core
    rows = gn_ref.shape[0]
    q_rows, width = oq_ref.shape
    keep = normed_ref.shape[1] // 16
    o_rows = oo_ref.shape[0]
    q_half, o_half = width // 2, o_rows // 2
    chips = xq.shape[0]
    members = 2 * chips
    reach = kv_in.shape[0]
    scale = HD ** (-0.5)
    f32, bf = jnp.float32, jnp.bfloat16
    partner = {"ctx": chip * 2 + 1 - core}

    def first_peer(k):
        return {"fsdp": block(lax.rem(a + k, 4), b)}

    def second_peer(k):
        return {"fsdp": block(a, lax.rem(b + k, 4))}

    def chip_peer(k):
        return {"ctx": lax.rem(chip + k, chips) * 2 + core}

    def member(k):
        return {"ctx": lax.rem(me + k, members)}

    def q_cols(half):
        return pl.ds(pl.multiple_of(half * q_half, 128), q_half)

    def o_lines(half):
        return pl.ds(pl.multiple_of(half * o_half, 16), o_half)

    def line(k):
        return lax.rem(a + k, 4)

    own_loads = [
        pltpu.make_async_copy(gff.at[block(a, j)], own_ff.at[j], l_sem.at[j]) for j in range(4)
    ] + [
        pltpu.make_async_copy(
            gff.at[block(line(1 if j < 2 else 3), j)], far_own.at[j], l_sem.at[4 + j]
        )
        for j in range(4)
    ]
    weight_loads = [
        pltpu.make_async_copy(wo_hbm, wo_ref, l_sem.at[8]),
        pltpu.make_async_copy(qkv_hbm, qkv_ref, l_sem.at[9]),
    ]
    for copy in own_loads + weight_loads:
        copy.start()
    greet(
        [first_peer(k) for k in (1, 2, 3)]
        + [second_peer(k) for k in (1, 2, 3)]
        + [member(k) for k in range(1, members)]
    )

    def ff_far(j):
        k = 1 if j < 2 else 3
        return remote(
            gff.at[block(line(2), j)], far_in.at[j], sfar.at[j], rfar.at[j], first_peer(k)
        )

    def ff_near(k, j):
        side = 0 if k == 1 else 1
        direct = (j >= 2) == (k == 1)
        src = gff.at[block(line(k), j)] if direct else far_own.at[j]
        return remote(src, in1_ff.at[side, j], s1f.at[side, j], r1f.at[side, j], first_peer(k))

    for j in (0, 2, 1, 3):
        ff_far(j).start()
    for k, j in ((1, 2), (3, 0), (1, 3), (3, 1)):
        ff_near(k, j).start()

    def pass_far(js):
        for j in js:
            ff_far(j).wait_recv()
            own_loads[4 + j].wait()
            far_own[j] = (far_own[j].astype(f32) + far_in[j].astype(f32)).astype(bf)
            ff_near(1 if j < 2 else 3, j).start()

    for copy in loads + weight_loads[:1]:
        copy.wait()

    grad_final = cot_ref[...].astype(f32)
    part, gain_two = rms_back(mid_ref[...], gn_ref[...], gains_ref[2:3, :])
    grad_mid = grad_final + part
    gmid[...] = grad_mid
    grad_attn, gain_one = rms_back(attn_ref[...], grad_mid, gains_ref[1:2, :])
    grad_attn_low = grad_attn.astype(bf)
    grad_attended = dot32(grad_attn_low, wo_ref[...], NT).astype(bf)

    def out_tile(t, carry):
        cols = pl.ds(pl.multiple_of(t * 256, 256), 256)
        go[pl.ds(t * 4, 4)] = (
            dot32(att_ref[:, cols], grad_attn_low, TN).reshape(4, 64, D).astype(bf)
        )
        return carry

    lax.fori_loop(0, NH * HD // 256, out_tile, 0)

    def away(i, t):
        k, j = lax.rem(i // 4 + 2, 4), lax.rem(i, 4)
        there = lax.rem(b + k, 4)
        f = block_there(there, j)
        slot = there * 4 + j
        if t == 0:
            src, dst = stage.at[f, :, q_cols(1 - core)], dq.at[slot]
        else:
            src, dst = go.at[f, o_lines(1 - core), :], do.at[slot]
        return remote(src, dst, sd.at[i, t], rd.at[i, t], partner)

    def home(i, t):
        k, j = lax.rem(i // 4 + 2, 4), lax.rem(i, 4)
        slot = lax.rem(a + k, 4) * 4 + j
        dst = (dq, do)[t].at[slot]
        return remote(dst, dst, sd.at[i, t], rd.at[i, t], partner)

    def start_away(t):
        def one(i, carry):
            away(i, t).start()
            return carry

        lax.fori_loop(0, 16, one, 0)

    start_away(1)

    keys, vals = pair_ref[:, :HD], pair_ref[:, HD:]
    queries = stack_heads(q_ref[...])
    grad_heads = stack_heads(grad_attended)
    scores = dot32(queries, keys, NT) * scale + jnp.concatenate([bias_ref[...]] * NH, axis=0)
    expo = jnp.exp(scores - jnp.max(scores, axis=-1, keepdims=True))
    probs = expo * (1.0 / jnp.sum(expo, axis=-1, keepdims=True))
    grad_probs = dot32(grad_heads, vals, NT)
    row_total = jnp.sum(probs * grad_probs, axis=-1, keepdims=True)
    grad_scores = (probs * (grad_probs - row_total)).astype(bf)
    gpair[:, HD:] = dot32(probs.astype(bf), grad_heads, TN)
    gpair[:, :HD] = dot32(grad_scores, queries, TN) * scale

    def kv_send(d):
        return remote(
            kv_snd.at[d - 1], kv_in.at[d - 1], skv.at[d - 1], rkv.at[d - 1], member(members - d)
        )

    for d in range(1, reach + 1):
        kv_snd[d - 1] = gpair[pl.ds((reach - d) * rows, rows), :].astype(bf)
        kv_send(d).start()

    pass_far((0, 2))
    cos_table, sin_table = turn_ref[:, : HD // 2], turn_ref[:, HD // 2 :]
    cos_all = jnp.concatenate([cos_table] * NH, axis=0)
    sin_all = jnp.concatenate([sin_table] * NH, axis=0)
    grad_queries = dot32(grad_scores, keys, NN) * scale
    grad_q, qk_gain_q = rms_back(
        stack_heads(proj_ref[:, : NH * HD]),
        turn_back(grad_queries, cos_all, sin_all),
        qk_ref[0:1, :],
    )
    for h in range(NH):
        gproj[:, h * HD : (h + 1) * HD] = grad_q[h * rows : (h + 1) * rows].astype(bf)

    def pair_of(k, h):
        return pl.ds(line(k) * 4 + 2 * h, 2)

    def sum_far(h, t):
        src, dst = ((sq, fq), (so, fo))[t]
        return remote(
            src.at[pair_of(2, h)], dst.at[pl.ds(2 * h, 2)],
            sfa.at[h, t], rfa.at[h, t], first_peer(3 if h else 1),
        )

    def sum_near(k, h, t):
        src, dst = ((sq, iq1), (so, io1))[t]
        side = 0 if k == 1 else 1
        return remote(
            src.at[pair_of(k, h)], dst.at[side, pl.ds(2 * h, 2)],
            s1.at[side, h, t], r1.at[side, h, t], first_peer(k),
        )

    def fold_cores(t):
        for k in (2, 3, 1, 0):
            def add(j, carry, k=k):
                slot = line(k) * 4 + j
                f = block(line(k), j)
                home((k + 2) % 4 * 4 + j, t).wait_recv()
                if t == 0:
                    sq[slot] = (
                        stage[f, :, q_cols(core)].astype(f32) + dq[slot].astype(f32)
                    ).astype(bf)
                else:
                    so[slot] = (
                        go[f, o_lines(core), :].astype(f32) + do[slot].astype(f32)
                    ).astype(bf)
                return carry

            lax.fori_loop(0, 4, add, 0)
            if k == 2:
                sum_far(0, t).start()
                sum_far(1, t).start()
            elif k:
                sum_near(k, 0 if k == 3 else 1, t).start()

    def fold_far(t):
        acc, far = ((sq, fq), (so, fo))[t]
        for h, k in ((0, 1), (1, 3)):
            sum_far(h, t).wait_recv()
            acc[pair_of(k, h)] = (
                acc[pair_of(k, h)].astype(f32) + far[2 * h : 2 * h + 2].astype(f32)
            ).astype(bf)
            sum_near(k, h, t).start()

    pass_far((1, 3))

    total = gpair[pl.ds(reach * rows, rows), :]
    for d in range(1, reach + 1):
        kv_send(d).wait_recv()
        total = total + kv_in[d - 1].astype(f32)
    grad_k, qk_gain_k = rms_back(
        proj_ref[:, NH * HD : NH * HD + HD],
        turn_back(total[:, :HD], cos_table, sin_table),
        qk_ref[1:2, :],
    )
    gproj[:, NH * HD : NH * HD + HD] = grad_k.astype(bf)
    gproj[:, NH * HD + HD :] = total[:, HD:].astype(bf)
    for copy in weight_loads[1:]:
        copy.wait()
    stream = tok_ref[...].astype(f32)
    grad_in, gain_zero = rms_back(stream, dot32(gproj[...], qkv_ref[...], NT), gains_ref[0:1, :])
    gt_ref[...] = gmid[...] + grad_in
    tail[...] = jnp.zeros_like(tail)
    for i, total_gain in enumerate((gain_zero, gain_one, gain_two, g3_ref[...])):
        tail[i : i + 1, :D] = total_gain
    tail[4:5, :HD] = qk_gain_q
    tail[5:6, :HD] = qk_gain_k

    def qkv_tile(t, carry):
        cols = pl.ds(pl.multiple_of(t * 256, 256), 256)
        res = dot32(normed_ref[...], gproj[:, cols], TN)
        low = tail[:, cols]
        for f in range(16):
            stage[f, :, cols] = jnp.concatenate(
                [res[f * keep : (f + 1) * keep], low], axis=0
            ).astype(bf)
        return carry

    lax.fori_loop(0, width // 256, qkv_tile, 0)
    start_away(0)

    for copy in own_loads[:4]:
        copy.wait()

    def ff_two(k):
        return remote(
            t_ff.at[lax.rem(b + k, 4)], in2_ff.at[3 - k], s2f.at[k], r2f.at[4 - k], second_peer(k)
        )

    for k in (2, 1, 3, 0):
        j = lax.rem(b + k, 4)
        for m in (0, 1):
            dst = in1_ff.at[m, j]
            remote(dst, dst, s1f.at[m, j], r1f.at[m, j], partner).wait_recv()
        total = own_ff[j].astype(f32)
        for m in (0, 1):
            total = total + in1_ff[m, j].astype(f32)
        t_ff[j] = total.astype(bf)
        if k:
            ff_two(k).start()

    fold_cores(1)
    fold_cores(0)
    fold_far(1)
    fold_far(0)

    def hop_two(k, t):
        src, dst = ((tq, iq2), (to, io2))[t]
        return remote(
            src.at[lax.rem(b + k, 4)], dst.at[3 - k], s2.at[k, t], r2.at[4 - k, t], second_peer(k)
        )

    for k in (1, 3, 2):
        ff_two(4 - k).wait_recv()
    total = t_ff[b].astype(f32)
    for m in range(3):
        total = total + in2_ff[m].astype(f32)
    all_ff[me] = total.astype(bf)

    half = all_ff.shape[1] // 2

    def ff_slot(k, there=0):
        return lax.rem(chip + k, chips) * 2 + (1 - core if there else core)

    def ff_all(k):
        peer = chip_peer(k) if k else partner
        return remote(
            all_ff.at[me], all_ff.at[me], sag.at[k], rag.at[(chips - k) % chips], peer
        )

    def ff_from(k):
        dst = all_ff.at[ff_slot(k)]
        return remote(dst, dst, sag.at[k], rag.at[k], partner)

    def ff_half(k, h, there=0):
        return all_ff.at[ff_slot(k, there), pl.ds(h * half, half), :]

    def ff_on(k):
        h = 0 if k == 3 else 1
        dst = ff_half(k, h)
        return remote(dst, dst, sag.at[8 + h], rag.at[8 + h], chip_peer(4 - k))

    def ff_far_got(h):
        dst = ff_half(2, h)
        return remote(dst, dst, sag.at[8 + h], rag.at[8 + h], partner)

    def ff_cross(k, h=None, there=0):
        if h is None:
            dst, i = all_ff.at[ff_slot(k, there)], 4 + k
        else:
            dst, i = ff_half(2, h, there), 10 + h
        return remote(dst, dst, sag.at[i], rag.at[i], partner)

    for k in (1, 3, 0):
        ff_all(k).start()

    for t in (1, 0):
        own, got, dst = ((sq, iq1, tq), (so, io1, to))[t]
        for k in (1, 3):
            for h in (0, 1):
                sum_near(k, h, t).wait_recv()
        for k in (2, 1, 3, 0):
            j = lax.rem(b + k, 4)
            total = own[a * 4 + j].astype(f32)
            for m in (0, 1):
                total = total + got[m, j].astype(f32)
            dst[j] = total.astype(bf)
            if k:
                hop_two(k, t).start()

    for k in (1, 3):
        ff_from(k).wait_recv()
        ff_on(k).start()
        ff_cross(k).start()

    def hop_chip(k, t):
        buf = (xq, xo)[t]
        return remote(
            buf.at[chip], buf.at[chip], sx.at[k, t], rx.at[chips - k, t], chip_peer(k)
        )

    for t in (1, 0):
        own, got, dst = ((tq, iq2, xq), (to, io2, xo))[t]
        for k in (1, 3, 2):
            hop_two(4 - k, t).wait_recv()
        total = own[b].astype(f32)
        for m in range(3):
            total = total + got[m].astype(f32)
        dst[chip] = total.astype(bf)
        for k in range(1, chips):
            hop_chip(k, t).start()

    def last(t, half):
        part = (oq_ref.at[:, q_cols(half)], oo_ref.at[o_lines(half), :])[t]
        return remote(part, part, sf.at[t], rf.at[t], partner)

    for h in (0, 1):
        ff_far_got(h).wait_recv()
        ff_cross(2, h).start()

    for t in (1, 0):
        buf = (xq, xo)[t]
        for k in range(1, chips):
            dst = buf.at[lax.rem(chip + k, chips)]
            remote(dst, dst, sx.at[k, t], rx.at[k, t], partner).wait_recv()
        total = buf[0].astype(f32)
        for m in range(1, chips):
            total = total + buf[m].astype(f32)
        if t == 0:
            oq_ref[:, q_cols(core)] = total
        else:
            oo_ref[o_lines(core), :] = total
        last(t, core).start()

    everywhere = all_ff.at[ff_slot(0, 1)]
    remote(everywhere, everywhere, sag.at[0], rag.at[0], partner).wait_recv()
    for k in (1, 3):
        ff_cross(k, there=1).wait_recv()
    for h in (0, 1):
        ff_cross(2, h, there=1).wait_recv()

    def end_away(i, carry):
        for t in (0, 1):
            away(i, t).wait_send()
        return carry

    lax.fori_loop(0, 16, end_away, 0)
    for j in range(4):
        ff_far(j).wait_send()
        ff_near(1, j).wait_send()
        ff_near(3, j).wait_send()
    for k in (1, 2, 3):
        ff_two(k).wait_send()
    for d in range(1, reach + 1):
        kv_send(d).wait_send()
    for k in (1, 3, 0):
        ff_all(k).wait_send()
    for k in (1, 3):
        ff_on(k).wait_send()
        ff_cross(k).wait_send()
    for h in (0, 1):
        ff_cross(2, h).wait_send()
    for t in (0, 1):
        for h in (0, 1):
            sum_far(h, t).wait_send()
            sum_near(1, h, t).wait_send()
            sum_near(3, h, t).wait_send()
        for k in (1, 2, 3):
            hop_two(k, t).wait_send()
        for k in range(1, chips):
            hop_chip(k, t).wait_send()
        last(t, core).wait_send()
        last(t, 1 - core).wait_recv()
    oq_out[...] = oq_ref[:keep, :]
    tail_out[...] = oq_ref[keep:, :]


def backward_rest(gff, values, weights, keep):
    f32, bf = jnp.float32, jnp.bfloat16
    vm = pl.BlockSpec(memory_space=pltpu.VMEM)
    hbm = pl.BlockSpec(memory_space=pl.ANY)
    dma = pltpu.SemaphoreType.DMA
    rows = values[0].shape[0]
    owners, ff_rows = gff.shape[:2]
    q_rows, width = keep + 8, (NH + 2) * HD
    o_rows, o_width = NH * HD // owners, D
    q_half, o_half = width // 2, o_rows // 2
    chips = lax.axis_size("ctx") // 2
    pairs = values[9].shape[0]
    reach = pairs // rows - 1

    def two(*lead):
        return [pltpu.VMEM(lead + (q_rows, q_half), bf), pltpu.VMEM(lead + (o_half, o_width), bf)]

    def ff(*lead):
        return pltpu.VMEM(lead + (ff_rows, D), bf)

    return pl.pallas_call(
        functools.partial(back_entry, len(values)),
        out_shape=(
            jax.ShapeDtypeStruct((rows, D), f32),
            jax.ShapeDtypeStruct((keep, width), f32),
            jax.ShapeDtypeStruct((8, width), f32),
            jax.ShapeDtypeStruct((o_rows, o_width), f32),
            jax.ShapeDtypeStruct((2 * chips, ff_rows, D), bf),
        ),
        in_specs=[hbm] * (3 + len(values)),
        out_specs=(vm,) * 5,
        scratch_shapes=[
            *(pltpu.VMEM(v.shape, v.dtype) for v in values),
            dma((len(values),)),
            pltpu.VMEM((16 * keep, width), bf),
            pltpu.VMEM((16 * o_rows, o_width), bf),
            pltpu.VMEM((q_rows, width), f32),
            ff(4), ff(4), ff(4), ff(2, 4), ff(4), ff(3),
            pltpu.VMEM((reach, rows, 2 * HD), bf),
            pltpu.VMEM((reach, rows, 2 * HD), bf),
            pltpu.VMEM((rows, D), f32),
            pltpu.VMEM((pairs, 2 * HD), f32),
            pltpu.VMEM((rows, width), bf),
            pltpu.VMEM((8, width), f32),
            pltpu.VMEM((16, q_rows, width), bf),
            pltpu.VMEM((16, o_rows, o_width), bf),
            *two(16), *two(16), *two(4), *two(2, 4), *two(4), *two(3), *two(chips),
            dma((10,)),
            dma((4,)), dma((4,)),
            dma((2, 4)), dma((2, 4)),
            dma((4,)), dma((4,)),
            dma((12,)), dma((12,)),
            dma((reach,)), dma((reach,)),
            dma((16, 2)), dma((16, 2)),
            dma((2, 2)), dma((2, 2)),
            dma((2, 2, 2)), dma((2, 2, 2)),
            dma((4, 2)), dma((4, 2)),
            dma((4, 2)), dma((4, 2)),
            dma((2,)), dma((2,)),
        ],
        compiler_params=pltpu.CompilerParams(
            collective_id=3, has_side_effects=True, vmem_limit_bytes=62 * 1024 * 1024
        ),
        cost_estimate=pl.CostEstimate(
            flops=12 * rows * width * D, bytes_accessed=64 * ff_rows * D, transcendentals=0
        ),
    )(gff, *values, *weights)


def finish_kernel(*refs):
    count = (len(refs) - 7) // 2
    all_ref, tail_ref, sources = refs[0], refs[1], refs[2 : 2 + count]
    weights, gains, qk = refs[2 + count : 5 + count], refs[5 + count], refs[6 + count]
    for src, dst in zip(sources, refs[7 + count :]):
        dst[...] = src[...]
    owner = lax.axis_index("fsdp")
    width = tail_ref.shape[1]
    for first, dst in ((0, gains), (4, qk)):
        lines, own = dst.shape
        shift = lax.rem(width - owner * own, width)
        dst[...] = pltpu.roll(tail_ref[...], shift, 1)[first : first + lines, :own]
    members = all_ref.shape[0]
    share = all_ref.shape[1] // 3
    lines = weights[0].shape[0] // members
    for i, dst in enumerate(weights):
        for m in range(members):
            dst[m * lines : (m + 1) * lines, :] = all_ref[
                m, i * share : (i + 1) * share, :
            ].astype(jnp.float32)[:lines]


def finish(all_ff, tail, lines, gain_lines, qk_lines, *rest):
    vm = pl.BlockSpec(memory_space=pltpu.VMEM)
    f32 = jnp.float32
    results = ((lines, D),) * 3 + (gain_lines, qk_lines)
    return pl.pallas_call(
        finish_kernel,
        out_shape=tuple(jax.ShapeDtypeStruct(s, f32) for s in results)
        + tuple(jax.ShapeDtypeStruct(r.shape, r.dtype) for r in rest),
        in_specs=[vm] * (2 + len(rest)),
        out_specs=(vm,) * (5 + len(rest)),
        compiler_params=pltpu.CompilerParams(vmem_limit_bytes=62 * 1024 * 1024),
    )(all_ff, tail, *rest)


def on_device(
    tokens,
    norm_gains,
    qk_gains,
    qkv_weight,
    out_weight,
    gate_weight,
    up_weight,
    down_weight,
    segments,
    cotangent,
):
    local_len = tokens.shape[1]
    ctx_size = lax.axis_size("ctx")
    own_rows = gate_weight.shape[0]
    slice_rows = own_rows // ctx_size
    padded = -(-slice_rows // 16) * 16
    keep = qkv_weight.shape[0]
    gain_lines, qk_lines = norm_gains.shape, qk_gains.shape
    places = np.arange(ctx_size * local_len, dtype=np.float32)
    rates = (ROPE_BASE ** (-(2.0 * np.arange(HD // 2)) / HD)).astype(np.float32)
    angles = (places[:, None] * rates).astype(np.float64)
    table = jnp.asarray(
        np.concatenate([np.cos(angles), np.sin(angles)], axis=1)
        .astype(np.float32)
        .reshape(ctx_size, local_len, HD)
    )
    flat = tokens.reshape(local_len, D)
    cot = cotangent.reshape(local_len, D)
    (
        qkv_full, out_full, ffn_full, gains_all, qk_all, normed, projected, queries, pair_all,
        attended, attn, mid, normed_two, bias, turn_table,
    ) = front(
        qkv_weight,
        norm_gains,
        qk_gains,
        out_weight,
        (gate_weight, up_weight, down_weight),
        padded,
        flat,
        segments,
        table,
    )
    output, grad_normed_two, grad_gain_three, ffn_grads = ffn(
        normed_two, mid, cot, gains_all, ffn_full
    )
    grad_tokens, total_qkv, tail, total_out, all_ff = backward_rest(
        ffn_grads,
        (
            grad_normed_two, mid, attn, cot, flat, gains_all, qk_all, projected, queries,
            pair_all, attended, normed, turn_table, bias, grad_gain_three,
        ),
        (qkv_full, out_full),
        keep,
    )
    (
        total_gate, total_up, total_down, total_gains, total_qk,
        grad_tokens, total_qkv, total_out, output,
    ) = finish(
        all_ff, tail, own_rows, gain_lines, qk_lines, grad_tokens, total_qkv, total_out, output
    )
    return (
        output.reshape(tokens.shape),
        grad_tokens.reshape(tokens.shape),
        total_gains,
        total_qk,
        total_qkv,
        total_out,
        total_gate,
        total_up,
        total_down,
    )


def solution(mesh):
    in_specs = (
        P("fsdp", "ctx", None),
        P(None, "fsdp"),
        P(None, "fsdp"),
        P("fsdp", None),
        P("fsdp", None),
        P("fsdp", None),
        P("fsdp", None),
        P("fsdp", None),
        P("fsdp", "ctx"),
        P("fsdp", "ctx", None),
    )
    out_specs = (
        P("fsdp", "ctx", None),
        P("fsdp", "ctx", None),
        P(None, "fsdp"),
        P(None, "fsdp"),
        P("fsdp", None),
        P("fsdp", None),
        P("fsdp", None),
        P("fsdp", None),
        P("fsdp", None),
    )
    return jax.shard_map(
        on_device, mesh=mesh, in_specs=in_specs, out_specs=out_specs, check_vma=False
    )
```
